32 devices in a mesh: dp: 8 (over z, y), section: 4 (over x, core).
Axes of the slice: x: 2, y: 2, z: 4, core: 2. Of those that a mesh axis runs over, the one named last changes fastest.
Arguments:
- frames: bfloat16 [32, 168, 512], P('dp'), may hold values from -6 to 6
- actions: int32 [32, 168], P('dp'), may hold values from 0 to 16
- deltas: int32 [32, 168, 4], P('dp'), may hold values from 0 to 1023
- kinds: int32 [32], P('dp'), may hold values from 0 to 1
- codebook: bfloat16 [1024, 512], replicated, may hold values from -3 to 3
- action_table: bfloat16 [17, 512], replicated, may hold values from -3 to 3
- position_table: bfloat16 [126, 512], replicated, may hold values from -3 to 3
- norm1_gain: float32 [2, 512], replicated, may hold values from 0.5 to 1.5
- norm1_bias: float32 [2, 512], replicated, may hold values from -1.25 to 1.25
- qkv_weight: bfloat16 [2, 512, 1536], replicated, may hold values from -0.25 to 0.25
- query_bias: float32 [2, 512], replicated, may hold values from -1.25 to 1.25
- value_bias: float32 [2, 512], replicated, may hold values from -1.25 to 1.25
- out_weight: bfloat16 [2, 512, 512], replicated, may hold values from -1 to 1
- out_bias: float32 [2, 512], replicated, may hold values from -1.25 to 1.25
- norm2_gain: float32 [2, 512], replicated, may hold values from 0.5 to 1.5
- norm2_bias: float32 [2, 512], replicated, may hold values from -1.25 to 1.25
- up_weight: bfloat16 [2, 512, 2048], replicated, may hold values from -0.25 to 0.25
- up_bias: float32 [2, 2048], replicated, may hold values from -1.25 to 1.25
- down_weight: bfloat16 [2, 2048, 512], replicated, may hold values from -0.125 to 0.125
- down_bias: float32 [2, 512], replicated, may hold values from -1.25 to 1.25
- final_gain: float32 [512], replicated, may hold values from 0.5 to 1.5
- final_bias: float32 [512], replicated, may hold values from -1.25 to 1.25
- cotangent: bfloat16 [32, 1008, 512], P('dp'), may hold values from -8 to 8
Outputs:
- activations: float32 [32, 1008, 512], P(('dp', 'section'))
- frame_grad: float32 [32, 168, 512], P(('dp', 'section'))
- codebook_grad: float32 [1024, 512], P(None, 'dp')
- action_grad: float32 [17, 512], P(None, 'dp')
- position_grad: float32 [126, 512], P(None, 'dp')
- norm1_gain_grad: float32 [2, 512], P(None, 'dp')
- norm1_bias_grad: float32 [2, 512], P(None, 'dp')
- qkv_grad: float32 [2, 512, 1536], P(None, 'dp')
- query_bias_grad: float32 [2, 512], P(None, 'dp')
- value_bias_grad: float32 [2, 512], P(None, 'dp')
- out_weight_grad: float32 [2, 512, 512], P(None, 'dp')
- out_bias_grad: float32 [2, 512], P(None, 'dp')
- norm2_gain_grad: float32 [2, 512], P(None, 'dp')
- norm2_bias_grad: float32 [2, 512], P(None, 'dp')
- up_weight_grad: float32 [2, 512, 2048], P(None, 'dp')
- up_bias_grad: float32 [2, 2048], P(None, 'dp')
- down_weight_grad: float32 [2, 2048, 512], P(None, None, 'dp')
- down_bias_grad: float32 [2, 512], P(None, 'dp')
- final_gain_grad: float32 [512], P('dp')
- final_bias_grad: float32 [512], P('dp')
The draws below stay inside these ranges and needn't reach their ends.
Inputs may be any that keep to these rules, and one draw needn't show every extreme that they name: `kinds`: 1 marks a buffer of 8 sequences of 21 steps, 0 one of 21 sequences of 8 steps.
All inputs are finite; a program needn't handle non-finite values.
Results may differ from the reference program's by a relative error of at most 0.019.
Values may be sent and summed in bfloat16 or wider, within the bound.
No kernel may reach another device: no remote copies, remote signals or barrier semaphores. Data moves between devices by JAX's collectives and lax.ppermute only.
A program may use at most 448 MiB of HBM per device.

```python
import math
import jax
import jax.numpy as jnp
import numpy as np
from jax import lax

D = 512
HEADS = 8
HEAD_DIM = 64
FF = 2048
CODES = 1024
ACTIONS = 17
DELTAS = 4
SHORT_STEPS = 8
LONG_STEPS = 21
SLOTS = 6
STEPS = 168
TOK = 1008
POSITIONS = 126
BUFFERS = 32


def with_ends(entries, rng, smallest, top_value):
    longest = entries.shape.index(max(entries.shape))
    spots = []
    for shift in (0, 1):
        where = [jax.random.randint(jax.random.fold_in(rng, axis), (), 0, length) for axis, length in enumerate(entries.shape)]
        where[longest] = (where[longest] + shift) % entries.shape[longest]
        spots.append(tuple(where))
    return entries.at[spots[0]].set(smallest).at[spots[1]].set(top_value)


def raised(entries, own_key, source, target, shards_of, factor):
    def block_of(dim):
        return (jnp.arange(entries.shape[dim]) // (entries.shape[dim] // shards_of)).reshape((-1,) + (1,) * (entries.ndim - 1 - dim))

    first = jax.random.permutation(own_key, shards_of)[block_of(target)]
    second = (block_of(target) + shards_of // 2) % shards_of
    return jnp.where((block_of(source) == first) | (block_of(source) == second), factor * entries, entries)


def steps_of(stream_key, shape, pieces, least, top_value):
    loudness = 1.0
    for axis_at, shards_of in pieces:
        draws = jax.random.uniform(jax.random.fold_in(jax.random.fold_in(stream_key, 6), axis_at), (shards_of,), jnp.float32, least / len(pieces), top_value / len(pieces))
        loudness = loudness * jnp.repeat(jnp.exp(draws), shape[axis_at] // shards_of).reshape((-1,) + (1,) * (len(shape) - 1 - axis_at))
    return loudness


def cumulative_ranks(number_of, slope):
    weights = [(1 << 20) // math.isqrt(grade ** slope) + 1 for grade in range(1, number_of + 1)]
    scale = 1 + sum(weights) // (1 << 30)
    return np.cumsum(np.array([max(1, weight // scale) for weight in weights]))


def ranked(own_key, dims, count, skew):
    grid = cumulative_ranks(count, skew)
    pick = jax.random.randint(jax.random.fold_in(own_key, 1), dims, 0, int(grid[count - 1]))
    standing = jnp.searchsorted(jnp.asarray(grid, jnp.int32), pick, side="right")
    return jax.random.permutation(jax.random.fold_in(own_key, 2), count)[standing].astype(jnp.int32)


def bell_draw(key, dims, scale, reach, shards=(), kind=jnp.bfloat16):
    values = scale * jax.random.normal(key, dims, jnp.float32)
    if shards:
        values = values * steps_of(key, dims, shards, -0.22, 0.18)
    return jnp.clip(values, -reach, reach).astype(kind)


def heavy_noise(key, dims, scale, limit, cuts, heavy, kind=jnp.bfloat16):
    result = scale * jax.random.normal(key, dims, jnp.float32)
    if cuts:
        result = result * steps_of(key, dims, cuts, -0.22, 0.18)
    return jnp.clip(raised(result, jax.random.fold_in(key, 3), *heavy), -limit, limit).astype(kind)


def setup_inputs(seed: int = 0) -> dict:
    arg_keys = jax.random.split(jax.random.key(seed), 24)
    frames = bell_draw(arg_keys[0], (BUFFERS, STEPS, D), 1.0, 6.0, ((0, 8),))
    actions = with_ends(jax.random.randint(arg_keys[1], (BUFFERS, STEPS), 0, ACTIONS), jax.random.fold_in(arg_keys[1], 1), 0, ACTIONS - 1).astype(jnp.int32)
    deltas = with_ends(ranked(arg_keys[2], (BUFFERS, STEPS, DELTAS), CODES, 1), jax.random.fold_in(arg_keys[2], 3), 0, CODES - 1).astype(jnp.int32)
    kinds = with_ends(jax.random.randint(arg_keys[3], (BUFFERS,), 0, 2), jax.random.fold_in(arg_keys[3], 1), 0, 1).astype(jnp.int32)
    codebook = bell_draw(arg_keys[4], (CODES, D), 0.5, 3.0)
    action_table = bell_draw(arg_keys[5], (ACTIONS, D), 0.5, 3.0)
    position_table = bell_draw(arg_keys[6], (POSITIONS, D), 0.5, 3.0)
    norm1_gain = jnp.clip(1.0 + 0.1 * jax.random.normal(arg_keys[7], (2, D), jnp.float32), 0.5, 1.5)
    norm1_bias = bell_draw(arg_keys[8], (2, D), 0.2, 1.25, (), jnp.float32)
    qkv_weight = bell_draw(arg_keys[9], (2, D, 3 * D), D ** -0.5, 0.25)
    query_bias = bell_draw(arg_keys[10], (2, D), 0.2, 1.25, (), jnp.float32)
    value_bias = bell_draw(arg_keys[11], (2, D), 0.2, 1.25, (), jnp.float32)
    out_weight = bell_draw(arg_keys[12], (2, D, D), (D // 16) ** -0.5, 1.0)
    out_bias = bell_draw(arg_keys[13], (2, D), 0.2, 1.25, (), jnp.float32)
    norm2_gain = jnp.clip(1.0 + 0.1 * jax.random.normal(arg_keys[14], (2, D), jnp.float32), 0.5, 1.5)
    norm2_bias = bell_draw(arg_keys[15], (2, D), 0.2, 1.25, (), jnp.float32)
    up_weight = bell_draw(arg_keys[16], (2, D, FF), D ** -0.5, 0.25)
    up_bias = bell_draw(arg_keys[17], (2, FF), 0.2, 1.25, (), jnp.float32)
    down_weight = bell_draw(arg_keys[18], (2, FF, D), FF ** -0.5, 0.125)
    down_bias = bell_draw(arg_keys[19], (2, D), 0.2, 1.25, (), jnp.float32)
    final_gain = jnp.clip(1.0 + 0.1 * jax.random.normal(arg_keys[20], (D,), jnp.float32), 0.5, 1.5)
    final_bias = bell_draw(arg_keys[21], (D,), 0.2, 1.25, (), jnp.float32)
    cotangent = heavy_noise(arg_keys[22], (BUFFERS, TOK, D), 1.0, 8.0, ((0, 8),), (0, 2, 8, 2.0))
    return {"frames": frames, "actions": actions, "deltas": deltas, "kinds": kinds, "codebook": codebook, "action_table": action_table, "position_table": position_table, "norm1_gain": norm1_gain, "norm1_bias": norm1_bias, "qkv_weight": qkv_weight, "query_bias": query_bias, "value_bias": value_bias, "out_weight": out_weight, "out_bias": out_bias, "norm2_gain": norm2_gain, "norm2_bias": norm2_bias, "up_weight": up_weight, "up_bias": up_bias, "down_weight": down_weight, "down_bias": down_bias, "final_gain": final_gain, "final_bias": final_bias, "cotangent": cotangent}


HIGHEST = lax.Precision.HIGHEST
EPSILON = 1e-05
MASKED = -1e+30

@jax.custom_vjp
def low(v):
    return lax.optimization_barrier(v.astype(jnp.bfloat16)).astype(jnp.float32)

@jax.custom_vjp
def low_back(v):
    return v

def low_keep(v):
    return (low(v), None)

def low_pass(kept, grad):
    return (grad,)

def back_keep(v):
    return (v, None)

def back_low(kept, grad):
    return (low(grad),)
low.defvjp(low_keep, low_pass)
low_back.defvjp(back_keep, back_low)

def rounded(value):
    return low_back(low(value))

def matmul(left, right):
    return jnp.dot(left, right, precision=HIGHEST)

def norm_apply(hidden, gain, bias):
    center = hidden - lax.optimization_barrier(jnp.mean(hidden, axis=-1, keepdims=True))
    spread = lax.optimization_barrier(jnp.mean(center * center, axis=-1, keepdims=True))
    return center * lax.rsqrt(spread + EPSILON) * gain + bias

def token_layout(kind_value):
    span = jnp.where(kind_value == 1, LONG_STEPS, SHORT_STEPS).astype(jnp.int32)
    step_index = jnp.arange(STEPS, dtype=jnp.int32)
    slot_index = jnp.arange(SLOTS, dtype=jnp.int32)
    position = ((step_index % span)[:, None] * SLOTS + slot_index[None, :]).reshape(-1)
    token_step = jnp.repeat(step_index, SLOTS)
    member = token_step // span
    allowed = (member[:, None] == member[None, :]) & (token_step[None, :] <= token_step[:, None])
    return (position, allowed)

def embed_tokens(tables, frame_rows, action_ids, delta_ids, position):
    codebook, action_table, position_table = tables
    action_rows = action_table[action_ids]
    delta_rows = codebook[delta_ids]
    tokens = jnp.concatenate([frame_rows[:, None, :], action_rows[:, None, :], delta_rows], axis=1).reshape(TOK, D)
    return rounded(tokens + position_table[position])

def attention(qkv, allowed):
    queries = qkv[:, :D].reshape(TOK, HEADS, HEAD_DIM)
    key_part = qkv[:, D:2 * D].reshape(TOK, HEADS, HEAD_DIM)
    value_part = qkv[:, 2 * D:].reshape(TOK, HEADS, HEAD_DIM)
    scores = jnp.einsum('qhd,khd->hqk', queries, key_part, precision=HIGHEST) * HEAD_DIM ** (-0.5)
    scores = low_back(jnp.where(allowed[None], scores, MASKED))
    probs = low(jax.nn.softmax(scores, axis=-1))
    mixed = jnp.einsum('hqk,khd->qhd', probs, value_part, precision=HIGHEST)
    return rounded(mixed.reshape(TOK, D))

def layer_apply(hidden, weights, allowed):
    gain_first, bias_first, qkv_matrix, query_shift, value_shift, out_matrix, out_shift, gain_second, bias_second, up_matrix, up_shift, down_matrix, down_shift = weights
    normed = low(norm_apply(hidden, gain_first, bias_first))
    shift = jnp.concatenate([query_shift, jnp.zeros_like(query_shift), value_shift])
    qkv = rounded(matmul(normed, qkv_matrix) + shift)
    mixed = attention(qkv, allowed)
    middle = hidden + low_back(matmul(mixed, out_matrix) + out_shift)
    normed_two = low(norm_apply(middle, gain_second, bias_second))
    pre_act = low_back(matmul(normed_two, up_matrix) + up_shift)
    act_value = low(jax.nn.gelu(pre_act, approximate=False))
    return rounded(middle + low_back(matmul(act_value, down_matrix) + down_shift))

def buffer_apply(params, frame_rows, action_ids, delta_ids, kind_value):
    tables, layers, finals = params
    position, allowed = token_layout(kind_value)
    hidden = embed_tokens(tables, frame_rows, action_ids, delta_ids, position)
    for depth in range(2):
        hidden = layer_apply(hidden, tuple((weight[depth] for weight in layers)), allowed)
    return norm_apply(hidden, finals[0], finals[1])

def reference(frames, actions, deltas, kinds, codebook, action_table, position_table, norm1_gain, norm1_bias, qkv_weight, query_bias, value_bias, out_weight, out_bias, norm2_gain, norm2_bias, up_weight, up_bias, down_weight, down_bias, final_gain, final_bias, cotangent):
    tables = tuple((table.astype(jnp.float32) for table in (codebook, action_table, position_table)))
    layers = tuple((weight.astype(jnp.float32) for weight in (norm1_gain, norm1_bias, qkv_weight, query_bias, value_bias, out_weight, out_bias, norm2_gain, norm2_bias, up_weight, up_bias, down_weight, down_bias)))
    finals = (final_gain.astype(jnp.float32), final_bias.astype(jnp.float32))

    def forward(params, frame_all):

        def one_buffer(buffer_item):
            return buffer_apply(params, buffer_item[0], buffer_item[1], buffer_item[2], buffer_item[3])
        return lax.map(jax.checkpoint(one_buffer), (frame_all, actions, deltas, kinds))
    outputs, pullback = jax.vjp(forward, (tables, layers, finals), frames.astype(jnp.float32))
    param_grads, frame_grads = pullback(cotangent.astype(jnp.float32))
    table_grads, layer_grads, final_grads = param_grads
    return (outputs, frame_grads, table_grads[0], table_grads[1], table_grads[2], layer_grads[0], layer_grads[1], layer_grads[2], layer_grads[3], layer_grads[4], layer_grads[5], layer_grads[6], layer_grads[7], layer_grads[8], layer_grads[9], layer_grads[10], layer_grads[11], layer_grads[12], final_grads[0], final_grads[1])
```

```python
from functools import partial

import jax
import jax.numpy as jnp
from jax import lax
from jax.sharding import PartitionSpec as P

HEADS = 8
SHORT_STEPS = 8
LONG_STEPS = 21


EPSILON = 1e-05
MASKED = -1e30
GRAD_DIMS = (1, 1, 1, 1, 1, 1, 1, 1, 1, 1, 1, 1, 1, 1, 2, 1, 0, 0)


def for_sending(array):
    return jax.tree.map(lambda a: a.astype(jnp.bfloat16) if a.dtype == jnp.float32 else a, array)


def passed_along(array, axis, by):
    size = lax.axis_size(axis)
    pairs = [(i, i + by) for i in range(size) if 0 <= i + by < size]
    return lax.ppermute(array, axis, pairs)


def norm_apply(hidden, gain, bias):
    center = hidden - jnp.mean(hidden, axis=-1, keepdims=True)
    spread = jnp.mean(center * center, axis=-1, keepdims=True)
    return center * lax.rsqrt(spread + EPSILON) * gain + bias


def plain_product(left, right):
    return jnp.dot(left, right, preferred_element_type=jnp.float32)


def left_product(left, right):
    return lax.dot_general(
        left, right, (((0,), (0,)), ((), ())), preferred_element_type=jnp.float32
    )


def right_product(left, right):
    return lax.dot_general(
        left, right, (((1,), (1,)), ((), ())), preferred_element_type=jnp.float32
    )


def token_layout(kind_value, steps, slots):
    span = jnp.where(kind_value == 1, LONG_STEPS, SHORT_STEPS).astype(jnp.int32)
    step_index = jnp.arange(steps, dtype=jnp.int32)
    slot_index = jnp.arange(slots, dtype=jnp.int32)
    position = ((step_index % span)[:, None] * slots + slot_index[None, :]).reshape(-1)
    token_step = jnp.repeat(step_index, slots)
    member = token_step // span
    allowed = (member[:, None] == member[None, :]) & (token_step[None, :] <= token_step[:, None])
    return (position, allowed)


def lookup_tables(tables, action_ids, delta_ids, position):
    codebook, action_table, position_table = tables
    action_hot = (
        action_ids[:, None] == jnp.arange(action_table.shape[0], dtype=jnp.int32)[None, :]
    ).astype(jnp.bfloat16)
    delta_hot = (
        delta_ids.reshape(-1)[:, None] == jnp.arange(codebook.shape[0], dtype=jnp.int32)[None, :]
    ).astype(jnp.bfloat16)
    place_hot = (
        position[:, None] == jnp.arange(position_table.shape[0], dtype=jnp.int32)[None, :]
    ).astype(jnp.bfloat16)
    return (action_hot, delta_hot, place_hot)


def embed_forward(tables, frame_rows, action_ids, delta_ids, position):
    codebook, action_table, position_table = tables
    action_hot, delta_hot, place_hot = lookup_tables(tables, action_ids, delta_ids, position)
    steps, width = frame_rows.shape
    action_rows = plain_product(action_hot, action_table)
    delta_rows = plain_product(delta_hot, codebook).reshape(steps, -1, width)
    tokens = jnp.concatenate(
        [frame_rows.astype(jnp.float32)[:, None], action_rows[:, None], delta_rows], axis=1
    ).reshape(-1, width)
    return (tokens + plain_product(place_hot, position_table)).astype(jnp.bfloat16)


def embed_backward(tables, action_ids, delta_ids, position, grad_bits):
    action_hot, delta_hot, place_hot = lookup_tables(tables, action_ids, delta_ids, position)
    rows, width = grad_bits.shape
    steps = action_ids.shape[0]
    per_slot = grad_bits.reshape(steps, rows // steps, width)
    frame_grad = per_slot[:, 0].astype(jnp.float32)
    grad_actions = left_product(action_hot, per_slot[:, 1])
    grad_codes = left_product(delta_hot, per_slot[:, 2:].reshape(-1, width))
    grad_places = left_product(place_hot, grad_bits)
    return (frame_grad, (grad_codes, grad_actions, grad_places))


def split_heads(qkv_bits, heads):
    rows = qkv_bits.shape[0]
    width = qkv_bits.shape[1] // 3
    head_dim = width // heads
    queries = qkv_bits[:, :width].reshape(rows, heads, head_dim)
    key_part = qkv_bits[:, width : 2 * width].reshape(rows, heads, head_dim)
    value_part = qkv_bits[:, 2 * width :].reshape(rows, heads, head_dim)
    return (queries, key_part, value_part)


def attention_probs(queries, key_part, allowed):
    scale = queries.shape[2] ** (-0.5)
    scores = (
        jnp.einsum("qhd,khd->hqk", queries, key_part, preferred_element_type=jnp.float32) * scale
    )
    scores = jnp.where(allowed[None], scores, MASKED)
    shifted = jnp.exp(scores - jnp.max(scores, axis=-1, keepdims=True))
    return shifted / jnp.sum(shifted, axis=-1, keepdims=True)


def layer_forward(hidden_bits, weights, allowed):
    (
        gain_first,
        bias_first,
        qkv_matrix,
        query_shift,
        value_shift,
        out_matrix,
        out_shift,
        gain_second,
        bias_second,
        up_matrix,
        up_shift,
        down_matrix,
        down_shift,
    ) = weights
    rows, width = hidden_bits.shape
    hidden = hidden_bits.astype(jnp.float32)
    normed = norm_apply(hidden, gain_first, bias_first).astype(jnp.bfloat16)
    shift = jnp.concatenate([query_shift, jnp.zeros_like(query_shift), value_shift])
    qkv_bits = (plain_product(normed, qkv_matrix) + shift).astype(jnp.bfloat16)
    queries, key_part, value_part = split_heads(qkv_bits, HEADS)
    probs = attention_probs(queries, key_part, allowed)
    mixed = jnp.einsum(
        "hqk,khd->qhd", probs.astype(jnp.bfloat16), value_part, preferred_element_type=jnp.float32
    )
    mixed_bits = mixed.reshape(rows, width).astype(jnp.bfloat16)
    middle = hidden + (plain_product(mixed_bits, out_matrix) + out_shift)
    normed_two = norm_apply(middle, gain_second, bias_second).astype(jnp.bfloat16)
    pre_act = plain_product(normed_two, up_matrix) + up_shift
    act_bits = jax.nn.gelu(pre_act, approximate=False).astype(jnp.bfloat16)
    output = middle + (plain_product(act_bits, down_matrix) + down_shift)
    return (output.astype(jnp.bfloat16), (hidden_bits, qkv_bits, mixed_bits, middle, pre_act))


def layer_backward(cache, weights, allowed, grad_bits):
    hidden_bits, qkv_bits, mixed_bits, middle, pre_act = cache
    (
        gain_first,
        bias_first,
        qkv_matrix,
        query_shift,
        value_shift,
        out_matrix,
        out_shift,
        gain_second,
        bias_second,
        up_matrix,
        up_shift,
        down_matrix,
        down_shift,
    ) = weights
    rows, width = hidden_bits.shape
    hidden = hidden_bits.astype(jnp.float32)
    act_value, gelu_pull = jax.vjp(partial(jax.nn.gelu, approximate=False), pre_act)
    act_bits = act_value.astype(jnp.bfloat16)
    normed_two = norm_apply(middle, gain_second, bias_second).astype(jnp.bfloat16)
    grad_down = left_product(act_bits, grad_bits)
    grad_down_shift = jnp.sum(grad_bits, axis=0, dtype=jnp.float32)
    grad_act = right_product(grad_bits, down_matrix)
    grad_pre_bits = gelu_pull(grad_act)[0].astype(jnp.bfloat16)
    grad_up = left_product(normed_two, grad_pre_bits)
    grad_up_shift = jnp.sum(grad_pre_bits, axis=0, dtype=jnp.float32)
    grad_normed_two = right_product(grad_pre_bits, up_matrix)
    second_pull = jax.vjp(norm_apply, middle, gain_second, bias_second)[1]
    grad_from_two, grad_gain_second, grad_bias_second = second_pull(grad_normed_two)
    grad_middle = grad_bits.astype(jnp.float32) + grad_from_two
    grad_middle_bits = grad_middle.astype(jnp.bfloat16)
    grad_out = left_product(mixed_bits, grad_middle_bits)
    grad_out_shift = jnp.sum(grad_middle_bits, axis=0, dtype=jnp.float32)
    queries, key_part, value_part = split_heads(qkv_bits, HEADS)
    scale = queries.shape[2] ** (-0.5)
    grad_mixed_bits = (
        right_product(grad_middle_bits, out_matrix).astype(jnp.bfloat16).reshape(queries.shape)
    )
    probs = attention_probs(queries, key_part, allowed)
    grad_probs = jnp.einsum(
        "qhd,khd->hqk", grad_mixed_bits, value_part, preferred_element_type=jnp.float32
    )
    grad_values = jnp.einsum(
        "hqk,qhd->khd",
        probs.astype(jnp.bfloat16),
        grad_mixed_bits,
        preferred_element_type=jnp.float32,
    )
    inner = jnp.sum(grad_probs * probs, axis=-1, keepdims=True)
    grad_scores = (probs * (grad_probs - inner)).astype(jnp.bfloat16)
    grad_queries = (
        jnp.einsum("hqk,khd->qhd", grad_scores, key_part, preferred_element_type=jnp.float32)
        * scale
    )
    grad_keys = (
        jnp.einsum("hqk,qhd->khd", grad_scores, queries, preferred_element_type=jnp.float32) * scale
    )
    grad_qkv_bits = jnp.concatenate(
        [
            grad_queries.reshape(rows, width),
            grad_keys.reshape(rows, width),
            grad_values.reshape(rows, width),
        ],
        axis=1,
    ).astype(jnp.bfloat16)
    normed = norm_apply(hidden, gain_first, bias_first).astype(jnp.bfloat16)
    grad_qkv = left_product(normed, grad_qkv_bits)
    grad_columns = jnp.sum(grad_qkv_bits, axis=0, dtype=jnp.float32)
    grad_normed = right_product(grad_qkv_bits, qkv_matrix)
    first_pull = jax.vjp(norm_apply, hidden, gain_first, bias_first)[1]
    grad_from_one, grad_gain_first, grad_bias_first = first_pull(grad_normed)
    grad_input = (grad_middle + grad_from_one).astype(jnp.bfloat16)
    terms = (
        grad_gain_first,
        grad_bias_first,
        grad_qkv,
        grad_columns[:width],
        grad_columns[2 * width :],
        grad_out,
        grad_out_shift,
        grad_gain_second,
        grad_bias_second,
        grad_up,
        grad_up_shift,
        grad_down,
        grad_down_shift,
    )
    return (grad_input, terms)


def reduced(matrix):
    shard = lax.psum_scatter(matrix.astype(jnp.bfloat16), ("dp", "section"), scatter_dimension=0, tiled=True)
    return lax.all_gather(shard, "section", axis=0, tiled=True).astype(jnp.float32)


def local(
    frames,
    actions,
    deltas,
    kinds,
    codebook,
    action_table,
    position_table,
    norm1_gain,
    norm1_bias,
    qkv_weight,
    query_bias,
    value_bias,
    out_weight,
    out_bias,
    norm2_gain,
    norm2_bias,
    up_weight,
    up_bias,
    down_weight,
    down_bias,
    final_gain,
    final_bias,
    cotangent,
):
    micro, steps, width = frames.shape
    rows = cotangent.shape[1]
    slots = rows // steps
    sections = lax.axis_size("section")
    section = lax.axis_index("section")
    per = micro // sections
    tables = (codebook, action_table, position_table)
    layer_stack = (
        norm1_gain,
        norm1_bias,
        qkv_weight,
        query_bias,
        value_bias,
        out_weight,
        out_bias,
        norm2_gain,
        norm2_bias,
        up_weight,
        up_bias,
        down_weight,
        down_bias,
    )

    def layer_weights(depth):
        return tuple((weight[depth] for weight in layer_stack))

    outputs, frame_grads = [], []
    layer_terms = [None, None]
    table_terms, final_terms = None, None

    def plus(total, terms):
        return terms if total is None else tuple(a + b for a, b in zip(total, terms))

    for part in range(per):
        slot = section * per + part
        position, allowed = token_layout(kinds[slot], steps, slots)
        hidden = embed_forward(tables, frames[slot], actions[slot], deltas[slot], position)
        caches = []
        for depth in range(2):
            hidden, cache = layer_forward(hidden, layer_weights(depth), allowed)
            caches.append(cache)
        output, pull = jax.vjp(norm_apply, hidden.astype(jnp.float32), final_gain, final_bias)
        grad_hidden, grad_gain, grad_bias = pull(cotangent[slot].astype(jnp.float32))
        final_terms = plus(final_terms, (grad_gain, grad_bias))
        grad = grad_hidden.astype(jnp.bfloat16)
        for depth in (1, 0):
            grad, terms = layer_backward(caches[depth], layer_weights(depth), allowed, grad)
            layer_terms[depth] = plus(layer_terms[depth], terms)
        frame_grad, terms = embed_backward(tables, actions[slot], deltas[slot], position, grad)
        table_terms = plus(table_terms, terms)
        outputs.append(output)
        frame_grads.append(frame_grad)

    big = {}
    for depth in (1, 0):
        terms = layer_terms[depth]
        big[depth] = [reduced(terms[k]) for k in (9, 2, 5)] + [reduced(terms[11].T)]
    codes = [reduced(t.T) for t in table_terms]
    small = [
        jnp.stack([layer_terms[0][k], layer_terms[1][k]], axis=1).reshape(width, -1) if k != 10
        else jnp.concatenate([layer_terms[d][k].reshape(width, -1) for d in (0, 1)], axis=1)
        for k in (0, 1, 3, 4, 6, 7, 8, 10, 12)
    ] + [t[:, None] for t in final_terms]
    widths = [s.shape[1] for s in small]
    joined = reduced(jnp.concatenate(small, axis=1))
    pieces = []
    start = 0
    for w in widths:
        pieces.append(joined[:, start : start + w])
        start += w

    def vec(piece):
        half = piece.shape[1] // 2
        return jnp.stack([piece[:, :half].reshape(-1), piece[:, half:].reshape(-1)])

    gain1, bias1, qb, vb, outb, gain2, bias2, upb, downb, fg, fb = pieces
    both = [jnp.stack([big[0][k], big[1][k]]) for k in range(4)]
    return (
        jnp.stack(outputs),
        jnp.stack(frame_grads),
        codes[0].T,
        codes[1].T,
        codes[2].T,
        vec(gain1),
        vec(bias1),
        both[1],
        vec(qb),
        vec(vb),
        both[2],
        vec(outb),
        vec(gain2),
        vec(bias2),
        both[0],
        vec(upb),
        both[3].transpose(0, 2, 1),
        vec(downb),
        fg[:, 0],
        fb[:, 0],
    )


def solution(mesh):
    return jax.shard_map(
        local,
        mesh=mesh,
        in_specs=(
            P("dp", None, None),
            P("dp", None),
            P("dp", None, None),
            P("dp"),
            P(),
            P(),
            P(),
            P(),
            P(),
            P(),
            P(),
            P(),
            P(),
            P(),
            P(),
            P(),
            P(),
            P(),
            P(),
            P(),
            P(),
            P(),
            P("dp", None, None),
        ),
        out_specs=(
            P(("dp", "section"), None, None),
            P(("dp", "section"), None, None),
            P(None, "dp"),
            P(None, "dp"),
            P(None, "dp"),
            P(None, "dp"),
            P(None, "dp"),
            P(None, "dp", None),
            P(None, "dp"),
            P(None, "dp"),
            P(None, "dp", None),
            P(None, "dp"),
            P(None, "dp"),
            P(None, "dp"),
            P(None, "dp", None),
            P(None, "dp"),
            P(None, None, "dp"),
            P(None, "dp"),
            P("dp"),
            P("dp"),
        ),
        check_vma=False,
    )
```

```python
from functools import partial

import jax
import jax.numpy as jnp
from jax import lax
from jax.experimental import pallas as pl
from jax.experimental.pallas import tpu as pltpu
from jax.sharding import PartitionSpec as P

HEADS = 8
SHORT_STEPS = 8
LONG_STEPS = 21
EPSILON = 1e-05
MASKED = -1e30
TILE = 128
ROWS = 256
CHUNK = 512
BF = jnp.bfloat16
F32 = jnp.float32

NN = (((1,), (0,)), ((), ()))
NT = (((1,), (1,)), ((), ()))
TN = (((0,), (0,)), ((), ()))


def product(left, right, form=NN):
    return lax.dot_general(left, right, form, preferred_element_type=F32)


def normalized(x):
    center = x - jnp.mean(x, axis=-1, keepdims=True)
    spread = jnp.mean(center * center, axis=-1, keepdims=True)
    scale = lax.rsqrt(spread + EPSILON)
    return center * scale, scale


def norm_back(grad, xhat, scale, gain):
    inner = grad * gain
    first = jnp.mean(inner, axis=-1, keepdims=True)
    second = jnp.mean(inner * xhat, axis=-1, keepdims=True)
    back = (inner - first - xhat * second) * scale
    return back, jnp.sum(grad * xhat, axis=0, keepdims=True), jnp.sum(grad, axis=0, keepdims=True)


def gelu_pair(u):
    t = 1.0 / (1.0 + jnp.abs(u) * (0.3275911 * 0.7071067811865476))
    e = jnp.exp(u * u * -0.5)
    poly = t * (0.127414796 + t * (-0.142248368 + t * (0.7107068705 + t * (-0.7265760135 + t * 0.5307027145))))
    half = poly * e
    cdf = jnp.where(u >= 0, 1.0 - half, half)
    return u * cdf, cdf + u * (e * 0.3989422804014327)


def row_tile(m):
    return pl.ds(pl.multiple_of(m * ROWS, ROWS), ROWS)


def lane_halves():
    lane = lax.broadcasted_iota(jnp.int32, (1, TILE), 1)
    low = (lane < TILE // 2).astype(F32)
    return low.astype(BF), (1.0 - low).astype(BF)


def both_heads(x, low, high):
    return jnp.concatenate([x * low, x * high], axis=0)


def side_by_side(x):
    return jnp.concatenate([x[:TILE], x[TILE:]], axis=1)


def write_mask(mask, stride):
    row = lax.broadcasted_iota(jnp.int32, (2 * TILE, TILE), 0)
    row = jnp.where(row >= TILE, row - TILE, row).astype(F32) + 0.5
    col = lax.broadcasted_iota(jnp.int32, (2 * TILE, TILE), 1).astype(F32) + 0.5
    step = jnp.floor(col * (1.0 / 6.0)) <= jnp.floor(row * (1.0 / 6.0))
    member = jnp.floor(col * (1.0 / 48.0)) == jnp.floor(row * (1.0 / 48.0))
    long = jnp.where(step, 0.0, MASKED)
    short = jnp.where(member, long, MASKED)
    mask[...] = jnp.where(stride == TILE, long, short)


def fetch(source, target, sem):
    copy = pltpu.make_async_copy(source, target, sem)
    copy.start()
    return copy


def attention_forward(qkv, probs, mixed, mask, stride, windows, width):
    low, high = lane_halves()

    @pl.loop(0, windows)
    def _(t):
        rows = pl.ds(pl.multiple_of(t * stride, 32), TILE)
        kept = pl.ds(pl.multiple_of(t * 2 * TILE, 2 * TILE), 2 * TILE)
        for pair in range(width // TILE):
            at = pair * TILE
            queries = qkv[rows, at : at + TILE]
            keys = qkv[rows, width + at : width + at + TILE]
            values = qkv[rows, 2 * width + at : 2 * width + at + TILE]
            scores = product(both_heads(queries, low, high), keys, NT) + mask[...]
            shifted = jnp.exp(scores - jnp.max(scores, axis=-1, keepdims=True))
            p = (shifted * (1.0 / jnp.sum(shifted, axis=-1, keepdims=True))).astype(BF)
            probs[pair, kept, :] = p
            mixed[rows, at : at + TILE] = product(side_by_side(p), both_heads(values, low, high)).astype(BF)


def forward_kernel(
    scalars, index, frames, codebook, action_table, position_table,
    gain1, bias1, qkv_w, query_bias, value_bias, out_w, out_bias, gain2, bias2,
    up_w, up_bias, down_w, down_bias, final_gain, final_bias, cotangent,
    activations, grad_out, final_grads, hidden_out, qkv_out, probs_out, mixed_out, middle_out, act_out, slope_out,
    table, qkv_v, out_v, up_v, down_v, hidden, qkv, probs, mixed, middle, act, slope, mask, result, cot,
    weight_sem, save_sem, tile_sem, result_sem,
):
    stride = scalars[1]
    windows = scalars[2]
    width = hidden.shape[-1]
    total = hidden.shape[1]
    hidden_units = up_bias.shape[1]
    tiles = total // ROWS
    loads = []
    for depth in range(2):
        loads.append([
            fetch(qkv_w.at[depth], qkv_v.at[depth], weight_sem.at[depth, 0]),
            fetch(out_w.at[depth], out_v.at[depth], weight_sem.at[depth, 1]),
            fetch(up_w.at[depth], up_v.at[depth], weight_sem.at[depth, 2]),
            fetch(down_w.at[depth], down_v.at[depth], weight_sem.at[depth, 3]),
        ])
    write_mask(mask, stride)
    positions = position_table.shape[0]
    action_count = action_table.shape[0]
    table[...] = jnp.zeros_like(table)
    table[:positions] = position_table[...]
    table[TILE : TILE + action_count] = action_table[...]
    qkv[:, total:, :] = jnp.zeros((2, qkv.shape[1] - total, qkv.shape[2]), BF)

    codes = codebook.shape[0]
    steps = frames.shape[1]

    @pl.loop(0, tiles)
    def _(m):
        rows = row_tile(m)
        code_hot = (lax.broadcasted_iota(jnp.int32, (codes, ROWS), 0) == index[0:1, rows]).astype(F32).astype(BF)
        line = lax.broadcasted_iota(jnp.int32, (2 * TILE, ROWS), 0)
        small_hot = ((line == index[1:2, rows]) | (line == index[2:3, rows])).astype(F32).astype(BF)
        frame_hot = (lax.broadcasted_iota(jnp.int32, (steps, ROWS), 0) == index[3:4, rows]).astype(F32).astype(BF)
        value = product(code_hot, codebook[...], TN) + product(small_hot, table[...], TN)
        value = value + product(frame_hot, frames[0], TN)
        hidden[0, rows, :] = value.astype(BF)

    saves = []
    for depth in range(2):
        saves.append(fetch(hidden.at[depth], hidden_out.at[depth], save_sem.at[depth, 0]))
        loads[depth][0].wait()

        @pl.loop(0, tiles)
        def _(m):
            rows = row_tile(m)
            xhat, _ = normalized(hidden[depth, rows, :].astype(F32))
            normed = (xhat * gain1[depth : depth + 1, :] + bias1[depth : depth + 1, :]).astype(BF)
            q = product(normed, qkv_v[depth, :, :width]) + query_bias[depth : depth + 1, :]
            qkv[depth, rows, :width] = (q.astype(BF).astype(F32) * 0.125).astype(BF)
            qkv[depth, rows, width : 2 * width] = product(normed, qkv_v[depth, :, width : 2 * width]).astype(BF)
            v = product(normed, qkv_v[depth, :, 2 * width :]) + value_bias[depth : depth + 1, :]
            qkv[depth, rows, 2 * width :] = v.astype(BF)

        saves.append(fetch(qkv.at[depth, pl.ds(0, total)], qkv_out.at[depth], save_sem.at[depth, 1]))
        attention_forward(qkv.at[depth], probs.at[depth], mixed.at[depth], mask, stride, windows, width)
        saves.append(fetch(probs.at[depth], probs_out.at[depth], save_sem.at[depth, 2]))
        saves.append(fetch(mixed.at[depth, pl.ds(0, total)], mixed_out.at[depth], save_sem.at[depth, 3]))
        for load in loads[depth][1:]:
            load.wait()

        def tile_copies(m, slot):
            rows = row_tile(m)
            return (
                pltpu.make_async_copy(act.at[slot], act_out.at[depth, rows], tile_sem.at[0, slot]),
                pltpu.make_async_copy(slope.at[slot], slope_out.at[depth, rows], tile_sem.at[1, slot]),
            )

        @pl.loop(0, tiles)
        def _(m):
            rows = row_tile(m)
            slot = lax.rem(m, 2)
            mid = hidden[depth, rows, :].astype(F32) + (
                product(mixed[depth, rows, :], out_v[depth]) + out_bias[depth : depth + 1, :]
            )
            middle[depth, rows, :] = mid
            xhat, _ = normalized(mid)
            normed = (xhat * gain2[depth : depth + 1, :] + bias2[depth : depth + 1, :]).astype(BF)

            @pl.when(m >= 2)
            def _():
                for copy in tile_copies(m - 2, slot):
                    copy.wait()

            added = jnp.zeros((ROWS, width), F32)
            for f in range(0, hidden_units, CHUNK):
                u = product(normed, up_v[depth, :, f : f + CHUNK]) + up_bias[depth : depth + 1, f : f + CHUNK]
                z, d = gelu_pair(u)
                z = z.astype(BF)
                act[slot, :, f : f + CHUNK] = z
                slope[slot, :, f : f + CHUNK] = d.astype(BF)
                added = added + product(z, down_v[depth, f : f + CHUNK, :])
            hidden[depth + 1, rows, :] = (mid + (added + down_bias[depth : depth + 1, :])).astype(BF)
            for copy in tile_copies(m, slot):
                copy.start()

        saves.append(fetch(middle.at[depth], middle_out.at[depth], save_sem.at[depth, 4]))
        for m in (tiles - 2, tiles - 1):
            for copy in tile_copies(m, m % 2):
                copy.wait()

    real = cotangent.shape[1]
    cot[:real] = cotangent[0].astype(F32)
    cot[real:] = jnp.zeros((cot.shape[0] - real, width), F32)
    final_grads[...] = jnp.zeros_like(final_grads)

    def finish(step):
        for g in range(total // TILE):
            xhat, scale = normalized(hidden[2, g * TILE : (g + 1) * TILE, :].astype(F32))
            result[g * step : g * step + TILE, :] = xhat * final_gain[...] + final_bias[...]
            arriving = cot[g * step : g * step + TILE, :]
            if step < TILE:
                line = lax.broadcasted_iota(jnp.int32, (TILE, 1), 0)
                arriving = jnp.where(line < step, arriving, 0.0)
            back, gain_sum, bias_sum = norm_back(arriving, xhat, scale, final_gain[...])
            grad_out[g * TILE : (g + 1) * TILE, :] = back.astype(BF)
            final_grads[0:1, :] += gain_sum
            final_grads[1:2, :] += bias_sum

    @pl.when(stride == TILE)
    def _():
        finish(LONG_STEPS * 6)

    @pl.when(stride != TILE)
    def _():
        finish(TILE)

    out = fetch(result.at[pl.ds(0, real)], activations, result_sem)
    for save in saves:
        save.wait()
    out.wait()


def mlp_back_kernel(
    depth, scalars, grad, middle, slope, act, mixed, up_w, down_w, out_w, gain2, bias2,
    first, second, grad_middle, grad_mixed, vectors, wide,
    slope_v, act_v, mixed_v, up_v, down_v, out_v, middle_v, normed, grad_pre, rounded,
    sems, tile_sems,
):
    core = scalars[3]
    total, width = grad.shape
    hidden_units = act_v.shape[1]
    tiles = total // ROWS
    down = fetch(down_w.at[depth], down_v, sems.at[0])
    slopes = [fetch(slope.at[depth, pl.ds(m * ROWS, ROWS)], slope_v.at[pl.ds(m * ROWS, ROWS)], tile_sems.at[m]) for m in range(1)]
    up = fetch(up_w.at[depth], up_v, sems.at[1])
    mid = fetch(middle.at[depth], middle_v, sems.at[2])
    out = fetch(out_w.at[depth], out_v, sems.at[3])
    slopes += [fetch(slope.at[depth, pl.ds(m * ROWS, ROWS)], slope_v.at[pl.ds(m * ROWS, ROWS)], tile_sems.at[m]) for m in range(1, tiles)]
    acts = fetch(act.at[depth], act_v, sems.at[4])
    mix = fetch(mixed.at[depth], mixed_v, sems.at[5])
    vectors[...] = jnp.zeros_like(vectors)
    wide[...] = jnp.zeros_like(wide)
    down.wait()
    for m in range(tiles):
        rows = slice(m * ROWS, (m + 1) * ROWS)
        slopes[m].wait()
        g = grad[rows, :]
        if m == 0:
            up.wait()
        back = jnp.zeros((ROWS, width), F32)
        for f in range(0, hidden_units, CHUNK):
            grad_act = product(g, down_v[f : f + CHUNK, :], NT)
            pre = grad_act * slope_v[rows, f : f + CHUNK].astype(F32)
            pre = pre.astype(BF)
            grad_pre[rows, f : f + CHUNK] = pre
            wide[0:1, f : f + CHUNK] += jnp.sum(pre.astype(F32), axis=0, keepdims=True)
            back = back + product(pre, up_v[:, f : f + CHUNK], NT)
        if m == 0:
            mid.wait()
            out.wait()
        xhat, scale = normalized(middle_v[rows, :])
        normed[rows, :] = (xhat * gain2[depth : depth + 1, :] + bias2[depth : depth + 1, :]).astype(BF)
        through, gain_sum, bias_sum = norm_back(back, xhat, scale, gain2[depth : depth + 1, :])
        g = g.astype(F32)
        total_grad = g + through
        grad_middle[rows, :] = total_grad
        r = total_grad.astype(BF)
        rounded[rows, :] = r
        vectors[0:1, :] += gain_sum
        vectors[1:2, :] += bias_sum
        vectors[2:3, :] += jnp.sum(g, axis=0, keepdims=True)
        vectors[3:4, :] += jnp.sum(r.astype(F32), axis=0, keepdims=True)
        grad_mixed[rows, :] = product(r, out_v[...], NT).astype(BF)
    acts.wait()
    mix.wait()

    half = hidden_units // 2
    quarter = half // 2
    for part in range(2):
        mine = core if part == 0 else 1 - core
        for path in range(2):
            out = (first, second)[path]
            cols = pl.ds(pl.multiple_of(mine * half + path * quarter, quarter), quarter)
            out[part, :, :quarter] = product(normed[...], grad_pre[:, cols], TN).astype(BF)
            out[part, :, quarter:half] = product(grad[...], act_v[:, cols], TN).astype(BF)
            cols = pl.ds(pl.multiple_of(mine * (width // 2) + path * (width // 4), width // 4), width // 4)
            out[part, :, half:] = product(mixed_v[...], rounded[:, cols], TN).astype(BF)


def attention_backward(qkv, probs, grad_mixed, grad_qkv, stride, windows, width):
    low, high = lane_halves()

    @pl.loop(0, windows)
    def _(t):
        rows = pl.ds(pl.multiple_of(t * stride, 32), TILE)
        kept = pl.ds(pl.multiple_of(t * 2 * TILE, 2 * TILE), 2 * TILE)
        for pair in range(width // TILE):
            at = pair * TILE
            queries = both_heads(qkv[rows, at : at + TILE], low, high)
            keys = qkv[rows, width + at : width + at + TILE]
            values = qkv[rows, 2 * width + at : 2 * width + at + TILE]
            arriving = both_heads(grad_mixed[rows, at : at + TILE], low, high)
            p = probs[pair, kept, :]
            wide_p = p.astype(F32)
            grad_p = product(arriving, values, NT)
            inner = jnp.sum(grad_p * wide_p, axis=-1, keepdims=True)
            grad_s = (wide_p * (grad_p - inner)).astype(BF)
            grad_q = product(side_by_side(grad_s), both_heads(keys, low, high)) * 0.125
            grad_qkv[rows, at : at + TILE] = grad_q.astype(BF)
            grad_qkv[rows, width + at : width + at + TILE] = product(grad_s, queries, TN).astype(BF)
            grad_qkv[rows, 2 * width + at : 2 * width + at + TILE] = product(p, arriving, TN).astype(BF)


def attention_back_kernel(
    depth, scalars, hidden, qkv, probs, grad_mixed, grad_middle, qkv_w, gain1, bias1,
    first, second, grad_in, vectors,
    hidden_v, qkv_v, probs_v, mixed_v, middle_v, weight_v, grad_qkv, normed, sems,
):
    stride = scalars[1]
    windows = scalars[2]
    core = scalars[3]
    total, width = grad_in.shape
    tiles = total // ROWS
    loads = [
        fetch(qkv.at[depth], qkv_v.at[pl.ds(0, total)], sems.at[0]),
        fetch(grad_mixed, mixed_v.at[pl.ds(0, total)], sems.at[1]),
        fetch(probs.at[depth], probs_v, sems.at[2]),
    ]
    later = [
        fetch(qkv_w.at[depth], weight_v, sems.at[3]),
        fetch(hidden.at[depth], hidden_v, sems.at[4]),
        fetch(grad_middle, middle_v, sems.at[5]),
    ]
    extra = qkv_v.shape[0] - total
    qkv_v[total:, :] = jnp.zeros((extra, 3 * width), BF)
    mixed_v[total:, :] = jnp.zeros((extra, width), BF)
    vectors[...] = jnp.zeros_like(vectors)
    for load in loads:
        load.wait()
    attention_backward(qkv_v, probs_v, mixed_v, grad_qkv, stride, windows, width)
    for load in later:
        load.wait()

    @pl.loop(0, tiles)
    def _(m):
        rows = row_tile(m)
        back = jnp.zeros((ROWS, width), F32)
        for f in range(0, 3 * width, width):
            back = back + product(grad_qkv[rows, f : f + width], weight_v[:, f : f + width], NT)
        xhat, scale = normalized(hidden_v[rows, :].astype(F32))
        normed[rows, :] = (xhat * gain1[depth : depth + 1, :] + bias1[depth : depth + 1, :]).astype(BF)
        through, gain_sum, bias_sum = norm_back(back, xhat, scale, gain1[depth : depth + 1, :])
        grad_in[rows, :] = (middle_v[rows, :] + through).astype(BF)
        vectors[0:1, :] += gain_sum
        vectors[1:2, :] += bias_sum
        vectors[2:3, :] += jnp.sum(grad_qkv[rows, :width].astype(F32), axis=0, keepdims=True)
        vectors[3:4, :] += jnp.sum(grad_qkv[rows, 2 * width :].astype(F32), axis=0, keepdims=True)

    quarter = 3 * width // 4
    for part in range(2):
        mine = core if part == 0 else 1 - core
        for path in range(2):
            cols = pl.ds(pl.multiple_of(mine * 2 * quarter + path * quarter, quarter), quarter)
            (first, second)[path][part] = product(normed[...], grad_qkv[:total, cols], TN).astype(BF)


def table_back_kernel(scalars, index, grad, first, second, frame_grad, turned):
    core = scalars[3]
    total, width = grad.shape
    quarter = second.shape[2]
    steps = frame_grad.shape[0]
    turned[...] = grad[...].T
    for part in range(2):
        mine = core if part == 0 else 1 - core
        for path in range(2):
            line = lax.broadcasted_iota(jnp.int32, (quarter, total), 0) + (mine * 2 * quarter + path * quarter)
            hot = (line == index[0:1, :]).astype(F32).astype(BF)
            (first, second)[path][part, :, :quarter] = product(turned[...], hot, NT).astype(BF)
        line = lax.broadcasted_iota(jnp.int32, (TILE, total), 0) + mine * TILE
        hot = ((line == index[1:2, :]) | (line == index[2:3, :])).astype(F32).astype(BF)
        first[part, :, quarter:] = product(turned[...], hot, NT).astype(BF)
    hot = (lax.broadcasted_iota(jnp.int32, (steps, total), 0) == index[3:4, :]).astype(F32).astype(BF)
    frame_grad[...] = product(hot, grad[...])


VMEM = pl.BlockSpec(memory_space=pltpu.VMEM)
ANY = pl.BlockSpec(memory_space=pl.ANY)
SMEM = pl.BlockSpec(memory_space=pltpu.SMEM)


def cost(flops, moved, others=0):
    return pl.CostEstimate(flops=int(flops), bytes_accessed=int(moved), transcendentals=int(others))


def run_forward(scalars, index, frames, codebook, action_table, position_table, layers, finals, cotangent):
    gain1, bias1, qkv_w, query_bias, value_bias, out_w, out_bias, gain2, bias2, up_w, up_bias, down_w, down_bias = layers
    width = codebook.shape[1]
    units = up_bias.shape[1]
    steps = frames.shape[1]
    real = cotangent.shape[1]
    total = index.shape[1]
    reach = total + TILE // 2
    windows = 11
    shape = jax.ShapeDtypeStruct
    whole = lambda a: pl.BlockSpec(a.shape, lambda i, s, n=a.ndim: (0,) * n)
    mine = lambda a: pl.BlockSpec((1,) + a.shape[1:], lambda i, s: (s[0], 0, 0))
    outs = [
        (shape((real, width), F32), ANY),
        (shape((total, width), BF), None),
        (shape((8, width), F32), None),
        (shape((2, total, width), BF), ANY),
        (shape((2, total, 3 * width), BF), ANY),
        (shape((2, width // TILE, windows * 2 * TILE, TILE), BF), ANY),
        (shape((2, total, width), BF), ANY),
        (shape((2, total, width), F32), ANY),
        (shape((2, total, units), BF), ANY),
        (shape((2, total, units), BF), ANY),
    ]
    args = [
        (index, None), (frames, mine(frames)), (codebook, None), (action_table, None), (position_table, None),
        (gain1, None), (bias1, None), (qkv_w, ANY), (query_bias, None), (value_bias, None), (out_w, ANY),
        (out_bias, None), (gain2, None), (bias2, None), (up_w, ANY), (up_bias, None), (down_w, ANY), (down_bias, None),
        (finals[0][None], None), (finals[1][None], None), (cotangent, mine(cotangent)),
    ]
    scratch = [
        pltpu.VMEM((2 * TILE, width), BF),
        pltpu.VMEM(qkv_w.shape, BF), pltpu.VMEM(out_w.shape, BF), pltpu.VMEM(up_w.shape, BF), pltpu.VMEM(down_w.shape, BF),
        pltpu.VMEM((3, total, width), BF),
        pltpu.VMEM((2, reach, 3 * width), BF),
        pltpu.VMEM((2, width // TILE, windows * 2 * TILE, TILE), BF),
        pltpu.VMEM((2, reach, width), BF),
        pltpu.VMEM((2, total, width), F32),
        pltpu.VMEM((2, ROWS, units), BF),
        pltpu.VMEM((2, ROWS, units), BF),
        pltpu.VMEM((2 * TILE, TILE), F32),
        pltpu.VMEM((total, width), F32),
        pltpu.VMEM((total, width), F32),
        pltpu.SemaphoreType.DMA((2, 4)),
        pltpu.SemaphoreType.DMA((2, 5)),
        pltpu.SemaphoreType.DMA((2, 2)),
        pltpu.SemaphoreType.DMA,
    ]
    return pl.pallas_call(
        forward_kernel,
        out_shape=[o for o, _ in outs],
        grid_spec=pltpu.PrefetchScalarGridSpec(
            num_scalar_prefetch=1,
            grid=(1,),
            in_specs=[spec or whole(a) for a, spec in args],
            out_specs=[spec or whole(o) for o, spec in outs],
            scratch_shapes=scratch,
        ),
        compiler_params=pltpu.CompilerParams(vmem_limit_bytes=58 << 20),
        cost_estimate=cost(14e9, 50e6, 4e6),
        name="forward",
    )(scalars, *[a for a, _ in args])


def run_mlp_back(depth, scalars, grad, saved, layers):
    hidden, qkv, probs, mixed, middle, act, slope = saved
    gain1, bias1, qkv_w, query_bias, value_bias, out_w, out_bias, gain2, bias2, up_w, up_bias, down_w, down_bias = layers
    total, width = grad.shape
    units = up_bias.shape[1]
    shape = jax.ShapeDtypeStruct
    return pl.pallas_call(
        partial(mlp_back_kernel, depth),
        out_shape=[
            shape((2, width, (units + width // 2) // 2), BF), shape((2, width, (units + width // 2) // 2), BF),
            shape((total, width), F32), shape((total, width), BF), shape((8, width), F32), shape((8, units), F32),
        ],
        in_specs=[SMEM, VMEM] + [ANY] * 7 + [VMEM] * 2,
        out_specs=[VMEM] * 6,
        scratch_shapes=[
            pltpu.VMEM((total, units), BF), pltpu.VMEM((total, units), BF), pltpu.VMEM((total, width), BF),
            pltpu.VMEM((width, units), BF), pltpu.VMEM((units, width), BF), pltpu.VMEM((width, width), BF),
            pltpu.VMEM((total, width), F32), pltpu.VMEM((total, width), BF), pltpu.VMEM((total, units), BF),
            pltpu.VMEM((total, width), BF),
            pltpu.SemaphoreType.DMA((6,)), pltpu.SemaphoreType.DMA((total // ROWS,)),
        ],
        compiler_params=pltpu.CompilerParams(vmem_limit_bytes=58 << 20),
        cost_estimate=cost(10e9, 24e6),
        name="mlp_back",
    )(scalars, grad, middle, slope, act, mixed, up_w, down_w, out_w, gain2, bias2)


def run_attention_back(depth, scalars, grad_mixed, grad_middle, saved, layers):
    hidden, qkv, probs, mixed, middle, act, slope = saved
    gain1, bias1, qkv_w = layers[:3]
    total, width = grad_mixed.shape
    reach = total + TILE // 2
    shape = jax.ShapeDtypeStruct
    return pl.pallas_call(
        partial(attention_back_kernel, depth),
        out_shape=[
            shape((2, width, 3 * width // 4), BF), shape((2, width, 3 * width // 4), BF),
            shape((total, width), BF), shape((8, width), F32),
        ],
        in_specs=[SMEM] + [ANY] * 6 + [VMEM] * 2,
        out_specs=[VMEM] * 4,
        scratch_shapes=[
            pltpu.VMEM((total, width), BF), pltpu.VMEM((reach, 3 * width), BF), pltpu.VMEM(probs.shape[1:], BF),
            pltpu.VMEM((reach, width), BF), pltpu.VMEM((total, width), F32), pltpu.VMEM(qkv_w.shape[1:], BF),
            pltpu.VMEM((reach, 3 * width), BF), pltpu.VMEM((total, width), BF),
            pltpu.SemaphoreType.DMA((6,)),
        ],
        compiler_params=pltpu.CompilerParams(vmem_limit_bytes=58 << 20),
        cost_estimate=cost(8e9, 16e6),
        name="attention_back",
    )(scalars, hidden, qkv, probs, grad_mixed, grad_middle, qkv_w, gain1, bias1)


def run_table_back(scalars, index, grad, codes, steps):
    total, width = grad.shape
    shape = jax.ShapeDtypeStruct
    return pl.pallas_call(
        table_back_kernel,
        out_shape=[
            shape((2, width, codes // 4 + TILE), BF), shape((2, width, codes // 4), BF), shape((steps, width), F32),
        ],
        in_specs=[SMEM] + [VMEM] * 2,
        out_specs=[VMEM] * 3,
        scratch_shapes=[pltpu.VMEM((width, total), BF)],
        compiler_params=pltpu.CompilerParams(vmem_limit_bytes=40 << 20),
        cost_estimate=cost(3e9, 6e6),
        name="table_back",
    )(scalars, index, grad)


def padded_index(action_ids, delta_ids, kind, total):
    steps, deltas = delta_ids.shape
    slots = deltas + 2
    none = lambda n: jnp.full((steps, n), -1, jnp.int32)
    step = jnp.arange(steps, dtype=jnp.int32)[:, None]
    code = jnp.concatenate([none(2), delta_ids], axis=1).reshape(-1)
    action = jnp.concatenate([none(1), action_ids[:, None] + TILE, none(deltas)], axis=1).reshape(-1)
    frame = jnp.concatenate([step, none(slots - 1)], axis=1).reshape(-1)
    token = jnp.arange(steps * slots, dtype=jnp.int32)
    span = jnp.where(kind == 1, LONG_STEPS, SHORT_STEPS) * slots
    natural = jnp.stack([code, token % span, action, frame])
    long = LONG_STEPS * slots
    apart = jnp.pad(natural.reshape(4, -1, long), ((0, 0), (0, 0), (0, TILE - long)), constant_values=-1).reshape(4, -1)
    close = jnp.pad(natural, ((0, 0), (0, total - natural.shape[1])), constant_values=-1)
    return jnp.pad(jnp.where(kind == 1, apart, close), ((0, 4), (0, 0)), constant_values=-1)


def swap(array, axis, bit):
    size = lax.axis_size(axis)
    return lax.ppermute(array, axis, [(i, i ^ (1 << bit)) for i in range(size)])


def bits_of(axis):
    return lax.axis_size(axis).bit_length() - 1


def own_bit(axis, bit):
    return (lax.axis_index(axis) >> bit) & 1


def take(array, dim, which):
    return lax.dynamic_index_in_dim(array, which, dim, keepdims=False)


def total_of(terms):
    return sum(term.astype(F32) for term in terms)


def settled(array):
    return lax.optimization_barrier(array.astype(BF))


def scattered(terms, order):
    count = bits_of("dp")
    rows, columns = terms[0].shape
    terms = [t.reshape((2,) * count + (rows >> count, columns)) for t in terms]
    left = list(range(count - 1, -1, -1))
    for bit in order:
        dim = left.index(bit)
        left.remove(bit)
        own = own_bit("dp", bit)
        arrived = swap(settled(total_of([take(t, dim, 1 - own) for t in terms])), "dp", bit)
        terms = [take(t, dim, own) for t in terms] + [arrived]
    return terms


def reduced(first, second):
    count = bits_of("dp")
    more = range(1, bits_of("section"))
    first = [first[0], swap(first[1], "section", 0)]
    second = [second[0], swap(second[1], "section", 0)]
    first = scattered(first, list(range(count)))
    for bit in more:
        sent = settled(total_of(first))
        first = [sent, swap(sent, "section", bit)]
    first = settled(total_of(first))
    for bit in more:
        rows, columns = second[0].shape
        own = own_bit("section", bit)
        second = [t.reshape(1 << count, 2, (rows >> count) // 2, columns) for t in second]
        arrived = swap(settled(total_of([take(t, 1, 1 - own) for t in second])), "section", bit)
        second = [t.reshape(rows // 2, columns) for t in [take(t, 1, own) for t in second] + [arrived]]
    second = scattered(second, list(range(1, count)) + [0])
    second = settled(total_of(second))
    for bit in reversed(more):
        other = swap(second, "section", bit)
        second = jnp.where(own_bit("section", bit) == 0, jnp.concatenate([second, other]), jnp.concatenate([other, second]))
    sent = jnp.concatenate([first, second], axis=1)
    other = swap(sent, "section", 0)
    core = own_bit("section", 0)
    low, high = jnp.where(core == 0, sent, other), jnp.where(core == 0, other, sent)
    split = first.shape[1]
    return jnp.stack([low[:, :split], high[:, :split]]), jnp.stack([low[:, split:], high[:, split:]])


def summed_everywhere(array):
    for axis in ("section", "dp"):
        for bit in range(bits_of(axis)):
            array = array + swap(array, axis, bit)
    return array


def joined(first, second, start, size):
    return jnp.concatenate([p[h, :, start : start + size] for h in range(2) for p in (first, second)], axis=1).astype(F32)


def local(
    frames, actions, deltas, kinds, codebook, action_table, position_table, norm1_gain, norm1_bias, qkv_weight,
    query_bias, value_bias, out_weight, out_bias, norm2_gain, norm2_bias, up_weight, up_bias, down_weight, down_bias,
    final_gain, final_bias, cotangent,
):
    micro, steps, width = frames.shape
    units = up_weight.shape[2]
    codes = codebook.shape[0]
    slot = lax.axis_index("section") * micro // lax.axis_size("section")
    kind = kinds[slot]
    layers = (
        norm1_gain, norm1_bias, qkv_weight, query_bias, value_bias, out_weight, out_bias, norm2_gain, norm2_bias,
        up_weight, up_bias, down_weight, down_bias,
    )
    total = -(-cotangent.shape[1] // ROWS) * ROWS
    index = padded_index(actions[slot], deltas[slot], kind, total)
    scalars = jnp.stack([
        slot, jnp.where(kind == 1, TILE, 96), jnp.where(kind == 1, total // TILE, 11), own_bit("section", 0)
    ]).astype(jnp.int32)
    activations, grad, final_grads, *saved = run_forward(
        scalars, index, frames, codebook, action_table, position_table, layers, (final_gain, final_bias), cotangent
    )
    feed, attend, vectors = [None, None], [None, None], [None, None]
    for depth in (1, 0):
        first, second, middle, mixed, vec2, wide = run_mlp_back(depth, scalars, grad, saved, layers)
        feed[depth] = reduced(first, second)
        first, second, grad, vec1 = run_attention_back(depth, scalars, mixed, middle, saved, layers)
        attend[depth] = reduced(first, second)
        vectors[depth] = jnp.concatenate([vec1[:4], vec2[:4], wide[0].reshape(-1, width)])
    first, second, frame_grad = run_table_back(scalars, index, grad, codes, steps)
    tables = reduced(first, second)

    every = summed_everywhere(jnp.concatenate([vectors[0], vectors[1], final_grads[:2]]))
    group = lax.axis_index("dp")
    groups = lax.axis_size("dp")

    def part(array):
        size = array.shape[-1] // groups
        return lax.dynamic_slice_in_dim(array, group * size, size, array.ndim - 1)

    per = vectors[0].shape[0]
    stacked = jnp.stack([every[:per], every[per : 2 * per]])
    gain1, bias1, query, value, gain2, bias2, down_b, out_b = [part(stacked[:, k]) for k in range(8)]
    up_b = part(stacked[:, 8:].reshape(2, units))
    quarter = units // 4
    up = jnp.stack([joined(*feed[d], 0, quarter) for d in range(2)])
    down = jnp.stack([joined(*feed[d], quarter, quarter).T for d in range(2)])
    out = jnp.stack([joined(*feed[d], 2 * quarter, width // 4) for d in range(2)])
    qkv = jnp.stack([joined(*attend[d], 0, 3 * width // 4) for d in range(2)])
    code = joined(*tables, 0, codes // 4).T
    small = tables[0][:, :, codes // 4 :].astype(F32)
    return (
        activations[None], frame_grad[None], code, small[1, :, : action_table.shape[0]].T,
        small[0, :, : position_table.shape[0]].T, gain1, bias1, qkv, query, value, out, out_b, gain2, bias2, up, up_b,
        down, down_b, part(every[2 * per]), part(every[2 * per + 1]),
    )


def solution(mesh):
    rows, one = P("dp", None, None), P(None, "dp")
    weight = P(None, "dp", None)
    both = P(("dp", "section"), None, None)
    return jax.shard_map(
        local,
        mesh=mesh,
        in_specs=(rows, P("dp", None), rows, P("dp")) + (P(),) * 18 + (rows,),
        out_specs=(
            both, both, one, one, one, one, one, weight, one, one, weight, one, one, one, weight, one,
            P(None, None, "dp"), one, P("dp"), P("dp"),
        ),
        check_vma=False,
    )
```

```python
from functools import partial

import jax
import jax.numpy as jnp
from jax import lax
from jax.experimental import pallas as pl
from jax.experimental.pallas import tpu as pltpu
from jax.sharding import PartitionSpec as P

HEADS = 8
SHORT_STEPS = 8
LONG_STEPS = 21
EPSILON = 1e-05
MASKED = -1e30
TILE = 128
ROWS = 256
CHUNK = 512
STRIP = 256
VECTORS = 32
BF = jnp.bfloat16
F32 = jnp.float32

NN = (((1,), (0,)), ((), ()))
NT = (((1,), (1,)), ((), ()))
TN = (((0,), (0,)), ((), ()))


def product(left, right, form=NN):
    return lax.dot_general(left, right, form, preferred_element_type=F32)


def normalized(x):
    center = x - jnp.mean(x, axis=-1, keepdims=True)
    spread = jnp.mean(center * center, axis=-1, keepdims=True)
    scale = lax.rsqrt(spread + EPSILON)
    return center * scale, scale


def norm_back(grad, xhat, scale, gain):
    inner = grad * gain
    first = jnp.mean(inner, axis=-1, keepdims=True)
    second = jnp.mean(inner * xhat, axis=-1, keepdims=True)
    back = (inner - first - xhat * second) * scale
    return back, jnp.sum(grad * xhat, axis=0, keepdims=True), jnp.sum(grad, axis=0, keepdims=True)


def gelu_pair(u):
    cdf = 0.5 + 0.5 * lax.erf(u * 0.7071067811865476)
    e = jnp.exp2(u * u * (-0.5 * 1.4426950408889634))
    return u * cdf, cdf + u * (e * 0.3989422804014327)


def row_tile(m):
    return pl.ds(pl.multiple_of(m * ROWS, ROWS), ROWS)


def lane_halves():
    lane = lax.broadcasted_iota(jnp.int32, (1, TILE), 1)
    low = (lane < TILE // 2).astype(F32)
    return low.astype(BF), (1.0 - low).astype(BF)


def both_heads(x, low, high):
    return jnp.concatenate([x * low, x * high], axis=0)


def side_by_side(x):
    return jnp.concatenate([x[:TILE], x[TILE:]], axis=1)


def write_mask(mask, stride):
    row = lax.broadcasted_iota(jnp.int32, (2 * TILE, TILE), 0)
    row = jnp.where(row >= TILE, row - TILE, row).astype(F32) + 0.5
    col = lax.broadcasted_iota(jnp.int32, (2 * TILE, TILE), 1).astype(F32) + 0.5
    step = jnp.floor(col * (1.0 / 6.0)) <= jnp.floor(row * (1.0 / 6.0))
    member = jnp.floor(col * (1.0 / 48.0)) == jnp.floor(row * (1.0 / 48.0))
    long = jnp.where(step, 0.0, MASKED)
    short = jnp.where(member, long, MASKED)
    mask[...] = jnp.where(stride == TILE, long, short)


def fetch(source, target, sem):
    copy = pltpu.make_async_copy(source, target, sem)
    copy.start()
    return copy


def attention_forward(qkv, probs, mixed, mask, stride, windows, width):
    low, high = lane_halves()

    @pl.loop(0, windows)
    def _(t):
        rows = pl.ds(pl.multiple_of(t * stride, 32), TILE)
        kept = pl.ds(pl.multiple_of(t * 2 * TILE, 2 * TILE), 2 * TILE)
        pairs = range(width // TILE)
        cut = lambda k, pair: qkv[rows, k * width + pair * TILE : k * width + (pair + 1) * TILE]
        scores = [product(both_heads(cut(0, pair), low, high), cut(1, pair), NT) + mask[...] for pair in pairs]
        shifted = [jnp.exp(s - jnp.max(s, axis=-1, keepdims=True)) for s in scores]
        p = [(s * (1.0 / jnp.sum(s, axis=-1, keepdims=True))).astype(BF) for s in shifted]
        for pair in pairs:
            probs[pair, kept, :] = p[pair]
        out = [product(side_by_side(p[pair]), both_heads(cut(2, pair), low, high)) for pair in pairs]
        for pair in pairs:
            mixed[rows, pair * TILE : (pair + 1) * TILE] = out[pair].astype(BF)


def forward_kernel(
    scalars, index, frames, codebook, action_table, position_table,
    gain1, bias1, qkv_w, query_bias, value_bias, out_w, out_bias, gain2, bias2,
    up_w, up_bias, down_w, down_bias, final_gain, final_bias, cotangent,
    activations, grad_out, final_grads, hidden_out, qkv_out, probs_out, mixed_out, middle_out, act_out, slope_out,
    table, qkv_v, out_v, up_v, down_v, hidden, qkv, probs, mixed, middle, act, slope, mask, result, cot,
    weight_sem, save_sem, tile_sem, result_sem,
):
    stride = scalars[1]
    windows = scalars[2]
    width = hidden.shape[-1]
    total = hidden.shape[1]
    hidden_units = up_bias.shape[1]
    tiles = total // ROWS
    loads = []
    for depth in range(2):
        loads.append([
            fetch(qkv_w.at[depth], qkv_v.at[depth], weight_sem.at[depth, 0]),
            fetch(out_w.at[depth], out_v.at[depth], weight_sem.at[depth, 1]),
            fetch(up_w.at[depth], up_v.at[depth], weight_sem.at[depth, 2]),
            fetch(down_w.at[depth], down_v.at[depth], weight_sem.at[depth, 3]),
        ])
    write_mask(mask, stride)
    positions = position_table.shape[0]
    action_count = action_table.shape[0]
    table[...] = jnp.zeros_like(table)
    table[:positions] = position_table[...]
    table[TILE : TILE + action_count] = action_table[...]
    qkv[:, total:, :] = jnp.zeros((2, qkv.shape[1] - total, qkv.shape[2]), BF)

    codes = codebook.shape[0]
    steps = frames.shape[1]

    @pl.loop(0, tiles)
    def _(m):
        rows = row_tile(m)
        code_hot = (lax.broadcasted_iota(jnp.int32, (codes, ROWS), 0) == index[0:1, rows]).astype(F32).astype(BF)
        line = lax.broadcasted_iota(jnp.int32, (2 * TILE, ROWS), 0)
        small_hot = ((line == index[1:2, rows]) | (line == index[2:3, rows])).astype(F32).astype(BF)
        frame_hot = (lax.broadcasted_iota(jnp.int32, (steps, ROWS), 0) == index[3:4, rows]).astype(F32).astype(BF)
        value = product(code_hot, codebook[...], TN) + product(small_hot, table[...], TN)
        value = value + product(frame_hot, frames[0], TN)
        hidden[0, rows, :] = value.astype(BF)

    saves = []
    for depth in range(2):
        saves.append(fetch(hidden.at[depth], hidden_out.at[depth], save_sem.at[depth, 0]))
        loads[depth][0].wait()

        def normed_tile(m):
            xhat, _ = normalized(hidden[depth, m * ROWS : (m + 1) * ROWS, :].astype(F32))
            return (xhat * gain1[depth : depth + 1, :] + bias1[depth : depth + 1, :]).astype(BF)

        ready = normed_tile(0)
        for m in range(tiles):
            rows = slice(m * ROWS, (m + 1) * ROWS)
            normed = ready
            if m + 1 < tiles:
                ready = normed_tile(m + 1)
            q = product(normed, qkv_v[depth, :, :width]) + query_bias[depth : depth + 1, :]
            k = product(normed, qkv_v[depth, :, width : 2 * width])
            v = product(normed, qkv_v[depth, :, 2 * width :]) + value_bias[depth : depth + 1, :]
            qkv[depth, rows, :width] = (q.astype(BF).astype(F32) * 0.125).astype(BF)
            qkv[depth, rows, width : 2 * width] = k.astype(BF)
            qkv[depth, rows, 2 * width :] = v.astype(BF)

        saves.append(fetch(qkv.at[depth, pl.ds(0, total)], qkv_out.at[depth], save_sem.at[depth, 1]))
        attention_forward(qkv.at[depth], probs.at[depth], mixed.at[depth], mask, stride, windows, width)
        saves.append(fetch(probs.at[depth], probs_out.at[depth], save_sem.at[depth, 2]))
        saves.append(fetch(mixed.at[depth, pl.ds(0, total)], mixed_out.at[depth], save_sem.at[depth, 3]))
        for load in loads[depth][1:]:
            load.wait()

        def tile_copies(m, slot):
            rows = row_tile(m)
            return (
                pltpu.make_async_copy(act.at[slot], act_out.at[depth, rows], tile_sem.at[0, slot]),
                pltpu.make_async_copy(slope.at[slot], slope_out.at[depth, rows], tile_sem.at[1, slot]),
            )

        @pl.loop(0, tiles)
        def _(m):
            rows = row_tile(m)
            slot = lax.rem(m, 2)
            mid = hidden[depth, rows, :].astype(F32) + (
                product(mixed[depth, rows, :], out_v[depth]) + out_bias[depth : depth + 1, :]
            )
            middle[depth, rows, :] = mid
            xhat, _ = normalized(mid)
            normed = (xhat * gain2[depth : depth + 1, :] + bias2[depth : depth + 1, :]).astype(BF)

            @pl.when(m >= 2)
            def _():
                for copy in tile_copies(m - 2, slot):
                    copy.wait()

            parts = list(range(0, hidden_units, STRIP))
            up = lambda f: product(normed, up_v[depth, :, f : f + STRIP]) + up_bias[depth : depth + 1, f : f + STRIP]
            u = up(0)
            added = jnp.zeros((ROWS, width), F32)
            previous = None
            for f in parts:
                following = up(f + STRIP) if f + STRIP < hidden_units else None
                if previous is not None:
                    added = added + product(previous, down_v[depth, f - STRIP : f, :])
                z, d = gelu_pair(u)
                previous = z.astype(BF)
                act[slot, :, f : f + STRIP] = previous
                slope[slot, :, f : f + STRIP] = d.astype(BF)
                u = following
            added = added + product(previous, down_v[depth, hidden_units - STRIP :, :])
            hidden[depth + 1, rows, :] = (mid + (added + down_bias[depth : depth + 1, :])).astype(BF)
            for copy in tile_copies(m, slot):
                copy.start()

        saves.append(fetch(middle.at[depth], middle_out.at[depth], save_sem.at[depth, 4]))
        for m in (tiles - 2, tiles - 1):
            for copy in tile_copies(m, m % 2):
                copy.wait()

    real = cotangent.shape[1]
    cot[:real] = cotangent[0].astype(F32)
    cot[real:] = jnp.zeros((cot.shape[0] - real, width), F32)
    final_grads[...] = jnp.zeros_like(final_grads)

    def finish(step):
        for g in range(total // TILE):
            xhat, scale = normalized(hidden[2, g * TILE : (g + 1) * TILE, :].astype(F32))
            result[g * step : g * step + TILE, :] = xhat * final_gain[...] + final_bias[...]
            arriving = cot[g * step : g * step + TILE, :]
            if step < TILE:
                line = lax.broadcasted_iota(jnp.int32, (TILE, 1), 0)
                arriving = jnp.where(line < step, arriving, 0.0)
            back, gain_sum, bias_sum = norm_back(arriving, xhat, scale, final_gain[...])
            grad_out[g * TILE : (g + 1) * TILE, :] = back.astype(BF)
            final_grads[0:1, :] += gain_sum
            final_grads[1:2, :] += bias_sum

    @pl.when(stride == TILE)
    def _():
        finish(LONG_STEPS * 6)

    @pl.when(stride != TILE)
    def _():
        finish(TILE)

    out = fetch(result.at[pl.ds(0, real)], activations, result_sem)
    for save in saves:
        save.wait()
    out.wait()


def mlp_data_back(depth, loads, grad, grad_middle, grad_mixed, vectors, wide, slope_v, up_v, down_v, out_v, middle_v, normed, grad_pre, rounded, gain2, bias2):
    total, width = grad.shape
    hidden_units = grad_pre.shape[1]
    down, slopes, up, mid, out = loads
    vectors[...] = jnp.zeros_like(vectors)
    wide[...] = jnp.zeros_like(wide)
    down.wait()
    for m in range(total // ROWS):
        rows = slice(m * ROWS, (m + 1) * ROWS)
        slopes[m].wait()
        g = grad[rows, :]
        if m == 0:
            up.wait()
        back = jnp.zeros((ROWS, width), F32)
        for f in range(0, hidden_units, CHUNK):
            grad_act = product(g, down_v[f : f + CHUNK, :], NT)
            pre = grad_act * slope_v[rows, f : f + CHUNK].astype(F32)
            pre = pre.astype(BF)
            grad_pre[rows, f : f + CHUNK] = pre
            wide[0:1, f : f + CHUNK] += jnp.sum(pre.astype(F32), axis=0, keepdims=True)
            back = back + product(pre, up_v[:, f : f + CHUNK], NT)
        if m == 0:
            mid.wait()
            out.wait()
        xhat, scale = normalized(middle_v[rows, :])
        normed[rows, :] = (xhat * gain2[depth : depth + 1, :] + bias2[depth : depth + 1, :]).astype(BF)
        through, gain_sum, bias_sum = norm_back(back, xhat, scale, gain2[depth : depth + 1, :])
        g = g.astype(F32)
        total_grad = g + through
        grad_middle[rows, :] = total_grad
        r = total_grad.astype(BF)
        rounded[rows, :] = r
        vectors[0:1, :] += gain_sum
        vectors[1:2, :] += bias_sum
        vectors[2:3, :] += jnp.sum(g, axis=0, keepdims=True)
        vectors[3:4, :] += jnp.sum(r.astype(F32), axis=0, keepdims=True)
        grad_mixed[rows, :] = product(r, out_v[...], NT).astype(BF)


def mlp_weight_back(core, loads, mine, theirs, grad, act_v, mixed_v, normed, grad_pre, rounded):
    width = grad.shape[1]
    half = grad_pre.shape[1] // 2
    quarter = half // 2
    path_width = half + width // 4
    for part in range(2):
        out = (mine, theirs)[part]
        which = core if part == 0 else 1 - core
        for path in range(2):
            at = path * path_width
            cols = pl.ds(pl.multiple_of(which * half + path * quarter, quarter), quarter)
            out[:, at : at + quarter] = product(normed[...], grad_pre[:, cols], TN).astype(BF)
            if part + path == 0:
                for load in loads:
                    load.wait()
            out[:, at + quarter : at + half] = product(grad[...], act_v[:, cols], TN).astype(BF)
            cols = pl.ds(pl.multiple_of(which * (width // 2) + path * (width // 4), width // 4), width // 4)
            out[:, at + half : at + path_width] = product(mixed_v[...], rounded[:, cols], TN).astype(BF)


def mlp_loads(depth, slope, up_w, down_w, middle, out_w, slope_v, up_v, down_v, middle_v, out_v, sems, tile_sems):
    tiles = slope_v.shape[0] // ROWS

    def slope_tile(m):
        rows = pl.ds(m * ROWS, ROWS)
        return fetch(slope.at[depth, rows], slope_v.at[rows], tile_sems.at[m])

    down = fetch(down_w.at[depth], down_v, sems.at[0])
    slopes = [slope_tile(0)]
    up = fetch(up_w.at[depth], up_v, sems.at[1])
    mid = fetch(middle.at[depth], middle_v, sems.at[2])
    out = fetch(out_w.at[depth], out_v, sems.at[3])
    slopes += [slope_tile(m) for m in range(1, tiles)]
    return down, slopes, up, mid, out


def mlp_back_kernel(depth, tokens, scalars, grad, middle, slope, act, mixed, up_w, down_w, out_w, gain2, bias2, *rest):
    (mine, theirs, grad_middle, grad_mixed, vectors, wide,
     slope_v, act_v, mixed_v, up_v, down_v, out_v, middle_v, normed, grad_pre, rounded,
     sems, tile_sems) = rest[tokens:]
    loads = mlp_loads(depth, slope, up_w, down_w, middle, out_w, slope_v, up_v, down_v, middle_v, out_v, sems, tile_sems)
    later = [fetch(act.at[depth], act_v, sems.at[4]), fetch(mixed.at[depth], mixed_v, sems.at[5])]
    mlp_data_back(
        depth, loads, grad, grad_middle, grad_mixed, vectors, wide, slope_v, up_v, down_v, out_v, middle_v, normed,
        grad_pre, rounded, gain2, bias2,
    )
    mlp_weight_back(scalars[3], later, mine, theirs, grad, act_v, mixed_v, normed, grad_pre, rounded)


def mlp_data_kernel(depth, tokens, grad, middle, slope, up_w, down_w, out_w, gain2, bias2, *rest):
    (grad_middle, grad_mixed, vectors, wide, normed, grad_pre, rounded,
     slope_v, up_v, down_v, out_v, middle_v, sems, tile_sems) = rest[tokens:]
    loads = mlp_loads(depth, slope, up_w, down_w, middle, out_w, slope_v, up_v, down_v, middle_v, out_v, sems, tile_sems)
    mlp_data_back(
        depth, loads, grad, grad_middle, grad_mixed, vectors, wide, slope_v, up_v, down_v, out_v, middle_v, normed,
        grad_pre, rounded, gain2, bias2,
    )


def mlp_weight_kernel(depth, tokens, scalars, grad, act, mixed, normed, grad_pre, rounded, *rest):
    mine, theirs, act_v, mixed_v, normed_v, pre_v, rounded_v, sems = rest[tokens:]
    first = [fetch(normed, normed_v, sems.at[0]), fetch(grad_pre, pre_v, sems.at[1])]
    later = [
        fetch(act.at[depth], act_v, sems.at[2]), fetch(mixed.at[depth], mixed_v, sems.at[3]),
        fetch(rounded, rounded_v, sems.at[4]),
    ]
    for load in first:
        load.wait()
    mlp_weight_back(scalars[3], later, mine, theirs, grad, act_v, mixed_v, normed_v, pre_v, rounded_v)


def attention_backward(qkv, probs, grad_mixed, grad_qkv, stride, windows, width):
    low, high = lane_halves()

    @pl.loop(0, windows)
    def _(t):
        rows = pl.ds(pl.multiple_of(t * stride, 32), TILE)
        kept = pl.ds(pl.multiple_of(t * 2 * TILE, 2 * TILE), 2 * TILE)
        pairs = range(width // TILE)
        cut = lambda k, pair: qkv[rows, k * width + pair * TILE : k * width + (pair + 1) * TILE]
        arriving = [both_heads(grad_mixed[rows, pair * TILE : (pair + 1) * TILE], low, high) for pair in pairs]
        grad_p = [product(arriving[pair], cut(2, pair), NT) for pair in pairs]
        p = [probs[pair, kept, :] for pair in pairs]
        grad_v = [product(p[pair], arriving[pair], TN) for pair in pairs]
        inner = [jnp.sum(grad_p[pair] * p[pair].astype(F32), axis=-1, keepdims=True) for pair in pairs]
        grad_s = [(p[pair].astype(F32) * (grad_p[pair] - inner[pair])).astype(BF) for pair in pairs]
        grad_q = [product(side_by_side(grad_s[pair]), both_heads(cut(1, pair), low, high)) * 0.125 for pair in pairs]
        grad_k = [product(grad_s[pair], both_heads(cut(0, pair), low, high), TN) for pair in pairs]
        for k, grads in enumerate((grad_q, grad_k, grad_v)):
            for pair in pairs:
                grad_qkv[rows, k * width + pair * TILE : k * width + (pair + 1) * TILE] = grads[pair].astype(BF)


def qkv_back(depth, core, grad_qkv, hidden_v, middle_v, weight_v, gain1, bias1, grad_in, normed, vectors, mine, theirs, path_width):
    total, width = hidden_v.shape

    @pl.loop(0, total // ROWS)
    def _(m):
        rows = row_tile(m)
        back = jnp.zeros((ROWS, width), F32)
        for f in range(0, 3 * width, width):
            back = back + product(grad_qkv[rows, f : f + width], weight_v[:, f : f + width], NT)
        xhat, scale = normalized(hidden_v[rows, :].astype(F32))
        normed[rows, :] = (xhat * gain1[depth : depth + 1, :] + bias1[depth : depth + 1, :]).astype(BF)
        through, gain_sum, bias_sum = norm_back(back, xhat, scale, gain1[depth : depth + 1, :])
        grad_in[rows, :] = (middle_v[rows, :] + through).astype(BF)
        vectors[0:1, :] += gain_sum
        vectors[1:2, :] += bias_sum
        vectors[2:3, :] += jnp.sum(grad_qkv[rows, :width].astype(F32), axis=0, keepdims=True)
        vectors[3:4, :] += jnp.sum(grad_qkv[rows, 2 * width :].astype(F32), axis=0, keepdims=True)

    quarter = 3 * width // 4
    for part in range(2):
        which = core if part == 0 else 1 - core
        for path in range(2):
            cols = pl.ds(pl.multiple_of(which * 2 * quarter + path * quarter, quarter), quarter)
            at = path * path_width
            (mine, theirs)[part][:, at : at + quarter] = product(normed[...], grad_qkv[:total, cols], TN).astype(BF)


def attention_load(depth, qkv, probs, grad_mixed, qkv_v, probs_v, mixed_v, sems):
    total = grad_mixed.shape[0]
    loads = [
        fetch(qkv.at[depth], qkv_v.at[pl.ds(0, total)], sems.at[0]),
        fetch(grad_mixed, mixed_v.at[pl.ds(0, total)], sems.at[1]),
        fetch(probs.at[depth], probs_v, sems.at[2]),
    ]
    qkv_v[total:, :] = jnp.zeros((qkv_v.shape[0] - total, qkv_v.shape[1]), BF)
    mixed_v[total:, :] = jnp.zeros((mixed_v.shape[0] - total, mixed_v.shape[1]), BF)
    return loads


def attention_back_kernel(
    depth, tokens, scalars, hidden, qkv, probs, grad_mixed, grad_middle, qkv_w, gain1, bias1, *rest,
):
    (mine, theirs, grad_in, vectors,
     hidden_v, middle_v, weight_v, normed, qkv_v, probs_v, mixed_v, grad_qkv, sems) = rest[tokens:]
    loads = attention_load(depth, qkv, probs, grad_mixed, qkv_v, probs_v, mixed_v, sems)
    later = [
        fetch(qkv_w.at[depth], weight_v, sems.at[3]),
        fetch(hidden.at[depth], hidden_v, sems.at[4]),
        fetch(grad_middle, middle_v, sems.at[5]),
    ]
    vectors[...] = jnp.zeros_like(vectors)
    for load in loads:
        load.wait()
    attention_backward(qkv_v, probs_v, mixed_v, grad_qkv, scalars[1], scalars[2], grad_in.shape[1])
    for load in later:
        load.wait()
    qkv_back(
        depth, scalars[3], grad_qkv, hidden_v, middle_v, weight_v, gain1, bias1, grad_in, normed, vectors, mine, theirs,
        mine.shape[1] // 2,
    )


def attention_part_kernel(depth, part, parts, tokens, scalars, qkv, probs, grad_mixed, *rest):
    out, qkv_v, probs_v, mixed_v, grad_qkv, sems, out_sem = rest[tokens:]
    total, whole = grad_mixed.shape
    width = whole // parts
    pairs = probs_v.shape[0]
    inside = pl.ds(0, total)
    loads = [
        fetch(qkv.at[depth, :, pl.ds(k * whole + part * width, width)], qkv_v.at[inside, pl.ds(k * width, width)], sems.at[k])
        for k in range(3)
    ]
    loads.append(fetch(grad_mixed.at[:, pl.ds(part * width, width)], mixed_v.at[inside], sems.at[3]))
    loads.append(fetch(probs.at[depth, pl.ds(part * pairs, pairs)], probs_v, sems.at[4]))
    qkv_v[total:, :] = jnp.zeros((qkv_v.shape[0] - total, qkv_v.shape[1]), BF)
    mixed_v[total:, :] = jnp.zeros((mixed_v.shape[0] - total, mixed_v.shape[1]), BF)
    for load in loads:
        load.wait()
    attention_backward(qkv_v, probs_v, mixed_v, grad_qkv, scalars[1], scalars[2], width)
    fetch(grad_qkv.at[inside], out, out_sem).wait()


def table_kernel(
    depth, tokens, groups, scalars, grad_low, grad_high, hidden, grad_middle, qkv_w, gain1, bias1,
    index, final_grads, feed1, wide1, attend1, feed0, wide0, *rest,
):
    (mine, theirs, frame_grad, grad_in, turned, vectors, stage, hidden_v, normed, grad_qkv, weight_v, middle_v, sems) = rest[tokens:]
    total, width = grad_in.shape
    half = width // 2
    loads = [
        fetch(low_high.at[:, pl.ds(k * half, half)], grad_qkv.at[:, pl.ds(k * width + n * half, half)], sems.at[3 * n + k])
        for k in range(3) for n, low_high in enumerate((grad_low, grad_high))
    ]
    loads.append(fetch(qkv_w.at[depth], weight_v, sems.at[6]))
    loads.append(fetch(hidden.at[depth], hidden_v, sems.at[7]))
    loads.append(fetch(grad_middle, middle_v, sems.at[8]))
    core = scalars[3]
    steps = frame_grad.shape[0]
    quarter = 3 * width // 4
    first_width = (mine.shape[1] + TILE) // 2
    code_width = mine.shape[1] - first_width - quarter
    vectors[...] = jnp.zeros_like(vectors)
    for load in loads:
        load.wait()
    qkv_back(
        depth, core, grad_qkv, hidden_v, middle_v, weight_v, gain1, bias1, grad_in, normed, vectors, mine, theirs,
        first_width,
    )

    stage[...] = jnp.zeros_like(stage)
    for k, block in enumerate((feed0, vectors, feed1, attend1, final_grads)):
        stage[VECTORS + 8 * k : VECTORS + 8 * k + 8, :] = block[...]
    each = width // groups
    for k, wide in enumerate((wide0, wide1)):
        for group in range(groups):
            for c in range(4):
                start = group * 4 * each + c * each
                at = VECTORS + 40 + 8 * k + c
                stage[at : at + 1, group * each : group * each + each] = wide[0:1, start : start + each]

    turned[...] = grad_in[...].T
    for part in range(2):
        out = (mine, theirs)[part]
        which = core if part == 0 else 1 - core
        for path in range(2):
            line = lax.broadcasted_iota(jnp.int32, (code_width, total), 0) + (which * 2 * code_width + path * code_width)
            hot = (line == index[0:1, :]).astype(F32).astype(BF)
            at = path * first_width + quarter
            out[:, at : at + code_width] = product(turned[...], hot, NT).astype(BF)
        line = lax.broadcasted_iota(jnp.int32, (TILE, total), 0) + which * TILE
        hot = ((line == index[1:2, :]) | (line == index[2:3, :])).astype(F32).astype(BF)
        small = product(turned[...], hot, NT) + stage[...].T * which.astype(F32)
        out[:, first_width - TILE : first_width] = small.astype(BF)
    hot = (lax.broadcasted_iota(jnp.int32, (steps, total), 0) == index[3:4, :]).astype(F32).astype(BF)
    frame_grad[...] = product(hot, grad_in[...])


VMEM = pl.BlockSpec(memory_space=pltpu.VMEM)
ANY = pl.BlockSpec(memory_space=pl.ANY)
SMEM = pl.BlockSpec(memory_space=pltpu.SMEM)


def cost(flops, moved, others=0):
    return pl.CostEstimate(flops=int(flops), bytes_accessed=int(moved), transcendentals=int(others))


def run_forward(scalars, index, frames, codebook, action_table, position_table, layers, finals, cotangent):
    gain1, bias1, qkv_w, query_bias, value_bias, out_w, out_bias, gain2, bias2, up_w, up_bias, down_w, down_bias = layers
    width = codebook.shape[1]
    units = up_bias.shape[1]
    steps = frames.shape[1]
    real = cotangent.shape[1]
    total = index.shape[1]
    reach = total + TILE // 2
    windows = 11
    shape = jax.ShapeDtypeStruct
    whole = lambda a: pl.BlockSpec(a.shape, lambda i, s, n=a.ndim: (0,) * n)
    mine = lambda a: pl.BlockSpec((1,) + a.shape[1:], lambda i, s: (s[0], 0, 0))
    outs = [
        (shape((real, width), F32), ANY),
        (shape((total, width), BF), None),
        (shape((8, width), F32), None),
        (shape((2, total, width), BF), ANY),
        (shape((2, total, 3 * width), BF), ANY),
        (shape((2, width // TILE, windows * 2 * TILE, TILE), BF), ANY),
        (shape((2, total, width), BF), ANY),
        (shape((2, total, width), F32), ANY),
        (shape((2, total, units), BF), ANY),
        (shape((2, total, units), BF), ANY),
    ]
    args = [
        (index, None), (frames, mine(frames)), (codebook, None), (action_table, None), (position_table, None),
        (gain1, None), (bias1, None), (qkv_w, ANY), (query_bias, None), (value_bias, None), (out_w, ANY),
        (out_bias, None), (gain2, None), (bias2, None), (up_w, ANY), (up_bias, None), (down_w, ANY), (down_bias, None),
        (finals[0][None], None), (finals[1][None], None), (cotangent, mine(cotangent)),
    ]
    scratch = [
        pltpu.VMEM((2 * TILE, width), BF),
        pltpu.VMEM(qkv_w.shape, BF), pltpu.VMEM(out_w.shape, BF), pltpu.VMEM(up_w.shape, BF), pltpu.VMEM(down_w.shape, BF),
        pltpu.VMEM((3, total, width), BF),
        pltpu.VMEM((2, reach, 3 * width), BF),
        pltpu.VMEM((2, width // TILE, windows * 2 * TILE, TILE), BF),
        pltpu.VMEM((2, reach, width), BF),
        pltpu.VMEM((2, total, width), F32),
        pltpu.VMEM((2, ROWS, units), BF),
        pltpu.VMEM((2, ROWS, units), BF),
        pltpu.VMEM((2 * TILE, TILE), F32),
        pltpu.VMEM((total, width), F32),
        pltpu.VMEM((total, width), F32),
        pltpu.SemaphoreType.DMA((2, 4)),
        pltpu.SemaphoreType.DMA((2, 5)),
        pltpu.SemaphoreType.DMA((2, 2)),
        pltpu.SemaphoreType.DMA,
    ]
    return pl.pallas_call(
        forward_kernel,
        out_shape=[o for o, _ in outs],
        grid_spec=pltpu.PrefetchScalarGridSpec(
            num_scalar_prefetch=1,
            grid=(1,),
            in_specs=[spec or whole(a) for a, spec in args],
            out_specs=[spec or whole(o) for o, spec in outs],
            scratch_shapes=scratch,
        ),
        compiler_params=pltpu.CompilerParams(vmem_limit_bytes=58 << 20),
        cost_estimate=cost(14e9, 50e6, 4e6),
        name="forward",
    )(scalars, *[a for a, _ in args])


def run_mlp_back(depth, scalars, grad, saved, layers, after=()):
    hidden, qkv, probs, mixed, middle, act, slope = saved
    gain1, bias1, qkv_w, query_bias, value_bias, out_w, out_bias, gain2, bias2, up_w, up_bias, down_w, down_bias = layers
    total, width = grad.shape
    units = up_bias.shape[1]
    shape = jax.ShapeDtypeStruct
    return pl.pallas_call(
        partial(mlp_back_kernel, depth, len(after)),
        out_shape=[
            shape((width, units + width // 2), BF), shape((width, units + width // 2), BF),
            shape((total, width), F32), shape((total, width), BF), shape((8, width), F32), shape((8, units), F32),
        ],
        in_specs=[SMEM, VMEM] + [ANY] * 7 + [VMEM] * 2 + [ANY] * len(after),
        out_specs=[VMEM] * 6,
        scratch_shapes=[
            pltpu.VMEM((total, units), BF), pltpu.VMEM((total, units), BF), pltpu.VMEM((total, width), BF),
            pltpu.VMEM((width, units), BF), pltpu.VMEM((units, width), BF), pltpu.VMEM((width, width), BF),
            pltpu.VMEM((total, width), F32), pltpu.VMEM((total, width), BF), pltpu.VMEM((total, units), BF),
            pltpu.VMEM((total, width), BF),
            pltpu.SemaphoreType.DMA((6,)), pltpu.SemaphoreType.DMA((total // ROWS,)),
        ],
        compiler_params=pltpu.CompilerParams(vmem_limit_bytes=50 << 20),
        cost_estimate=cost(10e9, 24e6),
        name="mlp_back",
    )(scalars, grad, middle, slope, act, mixed, up_w, down_w, out_w, gain2, bias2, *after)


def run_mlp_data(depth, grad, saved, layers, after):
    hidden, qkv, probs, mixed, middle, act, slope = saved
    gain1, bias1, qkv_w, query_bias, value_bias, out_w, out_bias, gain2, bias2, up_w, up_bias, down_w, down_bias = layers
    total, width = grad.shape
    units = up_bias.shape[1]
    shape = jax.ShapeDtypeStruct
    return pl.pallas_call(
        partial(mlp_data_kernel, depth, len(after)),
        out_shape=[
            shape((total, width), F32), shape((total, width), BF), shape((8, width), F32), shape((8, units), F32),
            shape((total, width), BF), shape((total, units), BF), shape((total, width), BF),
        ],
        in_specs=[VMEM] + [ANY] * 5 + [VMEM] * 2 + [ANY] * len(after),
        out_specs=[VMEM] * 7,
        scratch_shapes=[
            pltpu.VMEM((total, units), BF),
            pltpu.VMEM((width, units), BF), pltpu.VMEM((units, width), BF), pltpu.VMEM((width, width), BF),
            pltpu.VMEM((total, width), F32),
            pltpu.SemaphoreType.DMA((4,)), pltpu.SemaphoreType.DMA((total // ROWS,)),
        ],
        compiler_params=pltpu.CompilerParams(vmem_limit_bytes=40 << 20),
        cost_estimate=cost(10e9, 16e6),
        name="mlp_data",
    )(grad, middle, slope, up_w, down_w, out_w, gain2, bias2, *after)


def run_mlp_weight(depth, scalars, grad, saved, normed, grad_pre, rounded, after):
    hidden, qkv, probs, mixed, middle, act, slope = saved
    total, width = grad.shape
    units = grad_pre.shape[1]
    shape = jax.ShapeDtypeStruct
    return pl.pallas_call(
        partial(mlp_weight_kernel, depth, len(after)),
        out_shape=[shape((width, units + width // 2), BF), shape((width, units + width // 2), BF)],
        in_specs=[SMEM, VMEM] + [ANY] * 5 + [ANY] * len(after),
        out_specs=[VMEM] * 2,
        scratch_shapes=[
            pltpu.VMEM((total, units), BF), pltpu.VMEM((total, width), BF), pltpu.VMEM((total, width), BF),
            pltpu.VMEM((total, units), BF), pltpu.VMEM((total, width), BF),
            pltpu.SemaphoreType.DMA((5,)),
        ],
        compiler_params=pltpu.CompilerParams(vmem_limit_bytes=40 << 20),
        cost_estimate=cost(8e9, 16e6),
        name="mlp_weight",
    )(scalars, grad, act, mixed, normed, grad_pre, rounded, *after)


def window_scratch(total, width, probs):
    reach = total + TILE // 2
    return [
        pltpu.VMEM((reach, 3 * width), BF), pltpu.VMEM(probs.shape[1:], BF),
        pltpu.VMEM((reach, width), BF), pltpu.VMEM((reach, 3 * width), BF),
    ]


def run_attention_back(depth, scalars, grad_mixed, grad_middle, saved, layers, after):
    hidden, qkv, probs, mixed, middle, act, slope = saved
    gain1, bias1, qkv_w = layers[:3]
    total, width = grad_mixed.shape
    shape = jax.ShapeDtypeStruct
    return pl.pallas_call(
        partial(attention_back_kernel, depth, len(after)),
        out_shape=[
            shape((width, 3 * width // 2), BF), shape((width, 3 * width // 2), BF),
            shape((total, width), BF), shape((8, width), F32),
        ],
        in_specs=[SMEM] + [ANY] * 6 + [VMEM] * 2 + [ANY] * len(after),
        out_specs=[VMEM] * 4,
        scratch_shapes=[
            pltpu.VMEM((total, width), BF), pltpu.VMEM((total, width), F32), pltpu.VMEM(qkv_w.shape[1:], BF),
            pltpu.VMEM((total, width), BF), *window_scratch(total, width, probs),
            pltpu.SemaphoreType.DMA((6,)),
        ],
        compiler_params=pltpu.CompilerParams(vmem_limit_bytes=50 << 20),
        cost_estimate=cost(16e9, 24e6),
        name="attention_back",
    )(scalars, hidden, qkv, probs, grad_mixed, grad_middle, qkv_w, gain1, bias1, *after)


def run_attention_part(depth, part, parts, scalars, grad_mixed, saved, after):
    hidden, qkv, probs, mixed, middle, act, slope = saved
    total, width = grad_mixed.shape
    width = width // parts
    reach = total + TILE // 2
    return pl.pallas_call(
        partial(attention_part_kernel, depth, part, parts, len(after)),
        out_shape=jax.ShapeDtypeStruct((total, 3 * width), BF),
        in_specs=[SMEM] + [ANY] * 3 + [ANY] * len(after),
        out_specs=ANY,
        scratch_shapes=[
            pltpu.VMEM((reach, 3 * width), BF), pltpu.VMEM((width // TILE,) + probs.shape[2:], BF),
            pltpu.VMEM((reach, width), BF), pltpu.VMEM((reach, 3 * width), BF),
            pltpu.SemaphoreType.DMA((5,)), pltpu.SemaphoreType.DMA,
        ],
        compiler_params=pltpu.CompilerParams(vmem_limit_bytes=40 << 20),
        cost_estimate=cost(8e9, 8e6),
        name="attention_part",
    )(scalars, qkv, probs, grad_mixed, *after)


def run_table(depth, scalars, grad_low, grad_high, grad_middle, saved, layers, index, vectors, codes, steps, groups, after):
    hidden, qkv, probs, mixed, middle, act, slope = saved
    gain1, bias1, qkv_w = layers[:3]
    total, width = grad_middle.shape
    columns = 3 * width // 2 + codes // 2 + TILE
    shape = jax.ShapeDtypeStruct
    return pl.pallas_call(
        partial(table_kernel, depth, len(after), groups),
        out_shape=[shape((width, columns), BF), shape((width, columns), BF), shape((steps, width), F32)],
        in_specs=[SMEM] + [ANY] * 5 + [VMEM] * 2 + [VMEM] * 7 + [ANY] * len(after),
        out_specs=[VMEM] * 3,
        scratch_shapes=[
            pltpu.VMEM((total, width), BF), pltpu.VMEM((width, total), BF), pltpu.VMEM((8, width), F32),
            pltpu.VMEM((TILE, width), F32), pltpu.VMEM((total, width), BF), pltpu.VMEM((total, width), BF),
            pltpu.VMEM((total, 3 * width), BF), pltpu.VMEM(qkv_w.shape[1:], BF), pltpu.VMEM((total, width), F32),
            pltpu.SemaphoreType.DMA((9,)),
        ],
        compiler_params=pltpu.CompilerParams(vmem_limit_bytes=40 << 20),
        cost_estimate=cost(8e9, 12e6),
        name="tables",
    )(scalars, grad_low, grad_high, hidden, grad_middle, qkv_w, gain1, bias1, index, *vectors, *after)


def padded_index(action_ids, delta_ids, kind, total):
    steps, deltas = delta_ids.shape
    slots = deltas + 2
    none = lambda n: jnp.full((steps, n), -1, jnp.int32)
    step = jnp.arange(steps, dtype=jnp.int32)[:, None]
    code = jnp.concatenate([none(2), delta_ids], axis=1).reshape(-1)
    action = jnp.concatenate([none(1), action_ids[:, None] + TILE, none(deltas)], axis=1).reshape(-1)
    frame = jnp.concatenate([step, none(slots - 1)], axis=1).reshape(-1)
    token = jnp.arange(steps * slots, dtype=jnp.int32)
    span = jnp.where(kind == 1, LONG_STEPS, SHORT_STEPS) * slots
    natural = jnp.stack([code, token % span, action, frame])
    long = LONG_STEPS * slots
    apart = jnp.pad(natural.reshape(4, -1, long), ((0, 0), (0, 0), (0, TILE - long)), constant_values=-1).reshape(4, -1)
    close = jnp.pad(natural, ((0, 0), (0, total - natural.shape[1])), constant_values=-1)
    return jnp.pad(jnp.where(kind == 1, apart, close), ((0, 4), (0, 0)), constant_values=-1)


def swap(array, axis, bit):
    size = lax.axis_size(axis)
    return lax.ppermute(array, axis, [(i, i ^ (1 << bit)) for i in range(size)])


def bits_of(axis):
    return lax.axis_size(axis).bit_length() - 1


def own_bit(axis, bit):
    return (lax.axis_index(axis) >> bit) & 1


def take(array, dim, which):
    return lax.dynamic_index_in_dim(array, which, dim, keepdims=False)


def total_of(terms):
    return sum(term.astype(F32) for term in terms)


def settled(array):
    return lax.optimization_barrier(array.astype(BF))


def tied(array, token):
    return lax.optimization_barrier((array, token))[0]


def columns_sum(terms):
    pieces = [t for t in terms if isinstance(t, list)]
    whole = [t for t in terms if not isinstance(t, list)]
    total = None
    if pieces:
        total = jnp.concatenate([total_of(column) for column in zip(*pieces)], axis=-1)
    for t in whole:
        total = t.astype(F32) if total is None else total + t.astype(F32)
    return total


def each(function, terms):
    return [[function(p) for p in t] if isinstance(t, list) else function(t) for t in terms]


class Chunk:
    def __init__(self):
        self.count = bits_of("dp")
        self.more = list(range(1, bits_of("section")))
        self.pieces = []
        self.paths = None
        self.sent = []

    def add(self, mine, theirs, split):
        self.pieces.append([mine, swap(theirs, "section", 0), split])

    def hold(self, token):
        if self.paths is None:
            for piece in self.pieces:
                piece[1] = tied(piece[1], token)
        else:
            for terms in self.paths:
                terms[-1] = tied(terms[-1], token)

    def send(self, total, axis, bit):
        sent = settled(total)
        self.sent.append(sent)
        return swap(sent, axis, bit)

    def halved(self, terms, dim, axis, bit):
        own = own_bit(axis, bit)
        arrived = self.send(columns_sum(each(lambda t: take(t, dim, 1 - own), terms)), axis, bit)
        return each(lambda t: take(t, dim, own), terms) + [arrived]

    def halve_group(self, path, bit):
        dim = self.left[path].index(bit)
        self.left[path].remove(bit)
        self.paths[path] = self.halved(self.paths[path], dim, "dp", bit)

    def one(self):
        self.sent = []
        rows = self.pieces[0][0].shape[0]
        ways = (2,) * self.count
        self.left = [list(range(self.count - 1, -1, -1)) for _ in range(2)]
        first = [[p[k][:, : p[2]] for p in self.pieces] for k in range(2)]
        second = [[p[k][:, p[2] :] for p in self.pieces] for k in range(2)]
        first = each(lambda t: t.reshape(ways + (rows >> self.count, t.shape[-1])), first)
        for bit in self.more:
            half = rows // 2
            second = each(lambda t: t.reshape(1 << self.count, 2, half >> self.count, t.shape[-1]), second)
            second = each(lambda t: t.reshape(half, t.shape[-1]), self.halved(second, 1, "section", bit))
            rows = half
        second = each(lambda t: t.reshape(ways + (rows >> self.count, t.shape[-1])), second)
        self.paths = [first, second]
        self.halve_group(0, 0)
        return self

    def step(self, first, second):
        self.sent = []
        if first is not None:
            self.halve_group(0, first)
        else:
            for bit in self.more:
                sent = settled(columns_sum(self.paths[0]))
                self.sent.append(sent)
                self.paths[0] = [sent, swap(sent, "section", bit)]
        self.halve_group(1, second)
        return self

    def finish(self):
        first = settled(columns_sum(self.paths[0]))
        second = self.paths[1]
        self.sent = []
        for bit in reversed(self.more):
            sent = settled(columns_sum(second))
            self.sent.append(sent)
            other = swap(sent, "section", bit)
            own = own_bit("section", bit)
            second = [jnp.where(own == 0, jnp.concatenate([sent, other]), jnp.concatenate([other, sent]))]
        second = settled(columns_sum(second))
        sent = jnp.concatenate([first, second], axis=1)
        other = swap(sent, "section", 0)
        core = own_bit("section", 0)
        low, high = jnp.where(core == 0, sent, other), jnp.where(core == 0, other, sent)
        split = first.shape[1]
        self.results = []
        at = [0, split]
        for mine, _, cut in self.pieces:
            sizes = (cut, mine.shape[1] - cut)
            self.results.append([jnp.stack([low[:, a : a + n], high[:, a : a + n]]) for a, n in zip(at, sizes)])
            at = [a + n for a, n in zip(at, sizes)]


def joined(parts, start, size):
    return jnp.concatenate([p[h, :, start : start + size] for h in range(2) for p in parts], axis=1).astype(F32)


def local(
    frames, actions, deltas, kinds, codebook, action_table, position_table, norm1_gain, norm1_bias, qkv_weight,
    query_bias, value_bias, out_weight, out_bias, norm2_gain, norm2_bias, up_weight, up_bias, down_weight, down_bias,
    final_gain, final_bias, cotangent,
):
    micro, steps, width = frames.shape
    units = up_weight.shape[2]
    codes = codebook.shape[0]
    slot = lax.axis_index("section") * micro // lax.axis_size("section")
    kind = kinds[slot]
    layers = (
        norm1_gain, norm1_bias, qkv_weight, query_bias, value_bias, out_weight, out_bias, norm2_gain, norm2_bias,
        up_weight, up_bias, down_weight, down_bias,
    )
    total = -(-cotangent.shape[1] // ROWS) * ROWS
    index = padded_index(actions[slot], deltas[slot], kind, total)
    scalars = jnp.stack([
        slot, jnp.where(kind == 1, TILE, 96), jnp.where(kind == 1, total // TILE, 11), own_bit("section", 0)
    ]).astype(jnp.int32)
    activations, grad, final_grads, *saved = run_forward(
        scalars, index, frames, codebook, action_table, position_table, layers, (final_gain, final_bias), cotangent
    )
    groups = lax.axis_size("dp")
    count = bits_of("dp")
    path = units // 2 + width // 4
    split = 3 * width // 4
    chunk1, chunk2, chunk3 = Chunk(), Chunk(), Chunk()
    plan = list(zip(list(range(1, count)) + [None], range(count)))
    mine, theirs, middle, mixed, feed1, wide1 = run_mlp_back(1, scalars, grad, saved, layers)
    chunk1.add(mine, theirs, path)
    mine, theirs, grad, attend1 = run_attention_back(1, scalars, mixed, middle, saved, layers, [])
    chunk1.hold(attend1)
    chunk2.add(mine, theirs, split)
    chunk1.one()
    middle, mixed, feed0, wide0, normed, grad_pre, rounded = run_mlp_data(0, grad, saved, layers, chunk1.sent)
    chunk1.hold(normed)
    chunk1.step(*plan[0])
    mine, theirs = run_mlp_weight(0, scalars, grad, saved, normed, grad_pre, rounded, chunk1.sent)
    chunk1.hold(theirs)
    chunk2.hold(theirs)
    chunk2.add(mine, theirs, path)
    chunk1.step(*plan[1])
    grad_low = run_attention_part(0, 0, 2, scalars, mixed, saved, chunk1.sent)
    chunk1.hold(grad_low)
    chunk2.hold(grad_low)
    chunk2.one()
    chunk1.step(*plan[2])
    grad_high = run_attention_part(0, 1, 2, scalars, mixed, saved, chunk2.sent + chunk1.sent)
    chunk1.hold(grad_high)
    vectors = (final_grads, feed1, wide1, attend1, feed0, wide0)
    mine, theirs, frame_grad = run_table(
        0, scalars, grad_low, grad_high, middle, saved, layers, index, vectors, codes, steps, groups, []
    )
    chunk3.add(mine, theirs, split + codes // 4 + TILE)
    chunk2.hold(frame_grad)
    chunk1.hold(chunk2.paths[0][-1])
    chunk1.hold(chunk2.paths[1][-1])
    chunk2.step(*plan[0])
    for token in chunk2.sent:
        chunk3.hold(token)
    chunk3.one()
    for token in chunk3.sent:
        chunk2.hold(token)
        chunk1.hold(token)
    for pair in plan[3:]:
        chunk1.step(*pair)
    chunk1.finish()
    for k in range(1, count + 1):
        if k < count:
            chunk2.step(*plan[k])
        else:
            chunk2.finish()
        for token in chunk2.sent:
            chunk3.hold(token)
        chunk3.step(*plan[k - 1])
        if k < count:
            for token in chunk3.sent:
                chunk2.hold(token)
    chunk3.finish()
    feed = (chunk2.results[1], chunk1.results[0])
    attend = (chunk3.results[0], chunk2.results[0])
    tables = chunk3.results[0]
    quarter = units // 4
    up = jnp.stack([joined(feed[d], 0, quarter) for d in range(2)])
    down = jnp.stack([joined(feed[d], quarter, quarter).T for d in range(2)])
    out = jnp.stack([joined(feed[d], 2 * quarter, width // 4) for d in range(2)])
    qkv = jnp.stack([joined(attend[d], 0, 3 * width // 4) for d in range(2)])
    code = joined(tables, 3 * width // 4, codes // 4).T
    small = tables[0][:, :, -TILE:].astype(F32)
    vec = small[1, :, VECTORS:].T

    def pair(k):
        return jnp.stack([vec[k], vec[k + 16]])

    down_b, out_b = pair(2), pair(3)
    up_b = jnp.stack([vec[40 + 8 * d : 44 + 8 * d].reshape(-1) for d in range(2)])
    return (
        activations[None], frame_grad[None], code, small[1, :, : action_table.shape[0]].T,
        small[0, :, : position_table.shape[0]].T, pair(8), pair(9), qkv, pair(10), pair(11), out, out_b, pair(0), pair(1),
        up, up_b, down, down_b, vec[32], vec[33],
    )


def solution(mesh):
    rows, one = P("dp", None, None), P(None, "dp")
    weight = P(None, "dp", None)
    both = P(("dp", "section"), None, None)
    return jax.shard_map(
        local,
        mesh=mesh,
        in_specs=(rows, P("dp", None), rows, P("dp")) + (P(),) * 18 + (rows,),
        out_specs=(
            both, both, one, one, one, one, one, weight, one, one, weight, one, one, one, weight, one,
            P(None, None, "dp"), one, P("dp"), P("dp"),
        ),
        check_vma=False,
    )
```

```python
from functools import partial

import jax
import jax.numpy as jnp
from jax import lax
from jax.experimental import pallas as pl
from jax.experimental.pallas import tpu as pltpu
from jax.sharding import PartitionSpec as P

HEADS = 8
SHORT_STEPS = 8
LONG_STEPS = 21
EPSILON = 1e-05
MASKED = -1e30
TILE = 128
ROWS = 256
CHUNK = 512
STRIP = 256
VECTORS = 32
WINDOWS = 11
BF = jnp.bfloat16
F32 = jnp.float32

NN = (((1,), (0,)), ((), ()))
NT = (((1,), (1,)), ((), ()))
TN = (((0,), (0,)), ((), ()))


def product(left, right, form=NN):
    return lax.dot_general(left, right, form, preferred_element_type=F32)


def normalized(x):
    center = x - jnp.mean(x, axis=-1, keepdims=True)
    spread = jnp.mean(center * center, axis=-1, keepdims=True)
    scale = lax.rsqrt(spread + EPSILON)
    return center * scale, scale


def norm_back(grad, xhat, scale, gain):
    inner = grad * gain
    first = jnp.mean(inner, axis=-1, keepdims=True)
    second = jnp.mean(inner * xhat, axis=-1, keepdims=True)
    back = (inner - first - xhat * second) * scale
    return back, jnp.sum(grad * xhat, axis=0, keepdims=True), jnp.sum(grad, axis=0, keepdims=True)


def gelu_pair(u):
    cdf = 0.5 + 0.5 * lax.erf(u * 0.7071067811865476)
    e = jnp.exp2(u * u * (-0.5 * 1.4426950408889634))
    return u * cdf, cdf + u * (e * 0.3989422804014327)


def row_tile(m):
    return pl.ds(pl.multiple_of(m * ROWS, ROWS), ROWS)


def lane_halves():
    lane = lax.broadcasted_iota(jnp.int32, (1, TILE), 1)
    low = (lane < TILE // 2).astype(F32)
    return low.astype(BF), (1.0 - low).astype(BF)


def both_heads(x, low, high):
    return jnp.concatenate([x * low, x * high], axis=0)


def side_by_side(x):
    return jnp.concatenate([x[:TILE], x[TILE:]], axis=1)


def write_mask(mask, stride):
    row = lax.broadcasted_iota(jnp.int32, (2 * TILE, TILE), 0)
    row = jnp.where(row >= TILE, row - TILE, row).astype(F32) + 0.5
    col = lax.broadcasted_iota(jnp.int32, (2 * TILE, TILE), 1).astype(F32) + 0.5
    step = jnp.floor(col * (1.0 / 6.0)) <= jnp.floor(row * (1.0 / 6.0))
    member = jnp.floor(col * (1.0 / 48.0)) == jnp.floor(row * (1.0 / 48.0))
    long = jnp.where(step, 0.0, MASKED)
    short = jnp.where(member, long, MASKED)
    mask[...] = jnp.where(stride == TILE, long, short)


def placed(scalars, total):
    long = scalars[2 + scalars[0]] == 1
    return jnp.where(long, TILE, 2 * SHORT_STEPS * 6), jnp.where(long, total // TILE, WINDOWS)


def fetch(source, target, sem):
    copy = pltpu.make_async_copy(source, target, sem)
    copy.start()
    return copy


def attention_forward(qkv, probs, mixed, mask, stride, windows, width):
    low, high = lane_halves()

    @pl.loop(0, windows)
    def _(t):
        rows = pl.ds(pl.multiple_of(t * stride, 32), TILE)
        kept = pl.ds(pl.multiple_of(t * 2 * TILE, 2 * TILE), 2 * TILE)
        pairs = range(width // TILE)
        cut = lambda k, pair: qkv[rows, k * width + pair * TILE : k * width + (pair + 1) * TILE]
        scores = [product(both_heads(cut(0, pair), low, high), cut(1, pair), NT) + mask[...] for pair in pairs]
        shifted = [jnp.exp(s - jnp.max(s, axis=-1, keepdims=True)) for s in scores]
        p = [(s * (1.0 / jnp.sum(s, axis=-1, keepdims=True))).astype(BF) for s in shifted]
        for pair in pairs:
            probs[pair, kept, :] = p[pair]
        out = [product(side_by_side(p[pair]), both_heads(cut(2, pair), low, high)) for pair in pairs]
        for pair in pairs:
            mixed[rows, pair * TILE : (pair + 1) * TILE] = out[pair].astype(BF)


def build_index(index, actions, deltas, long):
    steps = actions.shape[-1]
    total = index.shape[1]
    step = lax.broadcasted_iota(jnp.int32, (steps, total), 0).astype(F32)
    start = step * 6.0 + jnp.where(long, 2.0, 0.0) * jnp.floor((step + 0.5) * (1.0 / LONG_STEPS))
    slot = lax.broadcasted_iota(jnp.int32, (steps, total), 1).astype(F32) - start
    line = lax.broadcasted_iota(jnp.int32, (8, steps), 0)

    def rows(**values):
        out = jnp.zeros((8, steps), F32)
        for name, value in values.items():
            out = jnp.where(line == int(name[1:]), value, out)
        return out.astype(BF)

    def spread(value, j):
        return product(value, (slot == float(j)).astype(F32).astype(BF))

    count = lax.broadcasted_iota(jnp.int32, (8, steps), 1).astype(F32)
    found = spread(rows(r5=count, r6=1.0), 0) + spread(rows(r3=actions[0].astype(F32), r4=1.0), 1)
    for j in range(deltas.shape[1]):
        code = deltas[0, j : j + 1, :].astype(F32)
        high = jnp.floor(code * (1.0 / 32.0))
        found = found + spread(rows(r0=high, r1=code - 32.0 * high, r2=1.0), 2 + j)
    found = found.astype(jnp.int32)
    none = jnp.full((1, total), -1, jnp.int32)
    row = lax.broadcasted_iota(jnp.int32, (1, total), 1)
    real = row.astype(F32) + 0.5
    apart = row - TILE * jnp.floor(real * (1.0 / TILE)).astype(jnp.int32)
    apart = jnp.where(apart < LONG_STEPS * 6, apart, none)
    close = row - SHORT_STEPS * 6 * jnp.floor(real * (1.0 / (SHORT_STEPS * 6))).astype(jnp.int32)
    close = jnp.where(row < steps * 6, close, none)
    index[0:1, :] = jnp.where(found[2:3] == 1, found[0:1] * 32 + found[1:2], none)
    index[1:2, :] = jnp.where(long, apart, close)
    index[2:3, :] = jnp.where(found[4:5] == 1, found[3:4] + TILE, none)
    index[3:4, :] = jnp.where(found[6:7] == 1, found[5:6], none)
    index[4:8, :] = jnp.full((4, total), -1, jnp.int32)


def forward_kernel(
    places, scalars, actions, deltas, frames, codebook, action_table, position_table,
    gain1, bias1, qkv_w, query_bias, value_bias, out_w, out_bias, gain2, bias2,
    up_w, up_bias, down_w, down_bias, final_gain, final_bias, cotangent,
    activations, index, final_grads, vectors, wide,
    hidden_out, qkv_out, probs_out, mixed_out, middle_out, act_out, slope_out,
    grad_middle_out, grad_mixed_out, mine_out, theirs_out,
    table, qkv_v, out_v, up_v, down_v, hidden, qkv, probs, mixed, middle, act, slope, mask, result, cot,
    grad, grad_mixed, normed_two, rounded, grad_pre, mine, theirs,
    weight_sem, save_sem, tile_sem, result_sem, part_sem,
):
    core = scalars[1]
    width = hidden.shape[-1]
    total = hidden.shape[1]
    stride, windows = placed(scalars, total)
    hidden_units = up_bias.shape[1]
    tiles = total // ROWS
    loads = []
    for depth in range(2):
        loads.append([
            fetch(qkv_w.at[depth], qkv_v.at[depth], weight_sem.at[depth, 0]),
            fetch(out_w.at[depth], out_v.at[depth], weight_sem.at[depth, 1]),
            fetch(up_w.at[depth], up_v.at[depth], weight_sem.at[depth, 2]),
            fetch(down_w.at[depth], down_v.at[depth], weight_sem.at[depth, 3]),
        ])
    write_mask(mask, stride)
    build_index(index, actions, deltas, stride == TILE)
    positions = position_table.shape[0]
    action_count = action_table.shape[0]
    table[...] = jnp.zeros_like(table)
    table[:positions] = position_table[...]
    table[TILE : TILE + action_count] = action_table[...]
    qkv[total:, :] = jnp.zeros((qkv.shape[0] - total, qkv.shape[1]), BF)

    codes = codebook.shape[0]
    steps = frames.shape[1]

    @pl.loop(0, tiles)
    def _(m):
        rows = row_tile(m)
        code_hot = (lax.broadcasted_iota(jnp.int32, (codes, ROWS), 0) == index[0:1, rows]).astype(F32).astype(BF)
        line = lax.broadcasted_iota(jnp.int32, (2 * TILE, ROWS), 0)
        small_hot = ((line == index[1:2, rows]) | (line == index[2:3, rows])).astype(F32).astype(BF)
        frame_hot = (lax.broadcasted_iota(jnp.int32, (steps, ROWS), 0) == index[3:4, rows]).astype(F32).astype(BF)
        value = product(code_hot, codebook[...], TN) + product(small_hot, table[...], TN)
        value = value + product(frame_hot, frames[0], TN)
        hidden[0, rows, :] = value.astype(BF)

    def tile_copies(m):
        rows = row_tile(m)
        return (
            pltpu.make_async_copy(act.at[rows], act_out.at[rows], tile_sem.at[0, m]),
            pltpu.make_async_copy(slope.at[rows], slope_out.at[rows], tile_sem.at[1, m]),
        )

    saves = {}
    started = []

    def save(name, source, target):
        saves[name] = fetch(source, target, save_sem.at[len(started)])
        started.append(name)

    inside = pl.ds(0, total)
    for depth in range(2):
        save(("hidden", depth), hidden.at[depth], hidden_out.at[depth])
        loads[depth][0].wait()
        if depth:
            saves.pop(("qkv", 0)).wait()

        def normed_tile(m):
            xhat, _ = normalized(hidden[depth, m * ROWS : (m + 1) * ROWS, :].astype(F32))
            return (xhat * gain1[depth : depth + 1, :] + bias1[depth : depth + 1, :]).astype(BF)

        ready = normed_tile(0)
        for m in range(tiles):
            rows = slice(m * ROWS, (m + 1) * ROWS)
            normed = ready
            if m + 1 < tiles:
                ready = normed_tile(m + 1)
            q = product(normed, qkv_v[depth, :, :width]) + query_bias[depth : depth + 1, :]
            k = product(normed, qkv_v[depth, :, width : 2 * width])
            v = product(normed, qkv_v[depth, :, 2 * width :]) + value_bias[depth : depth + 1, :]
            qkv[rows, :width] = (q.astype(BF).astype(F32) * 0.125).astype(BF)
            qkv[rows, width : 2 * width] = k.astype(BF)
            qkv[rows, 2 * width :] = v.astype(BF)

        save(("qkv", depth), qkv.at[inside], qkv_out.at[depth])
        if depth:
            saves.pop(("probs", 0)).wait()
            saves.pop(("mixed", 0)).wait()
        attention_forward(qkv, probs, mixed, mask, stride, windows, width)
        save(("probs", depth), probs, probs_out.at[depth])
        if not depth:
            save(("mixed", depth), mixed.at[inside], mixed_out)
        for load in loads[depth][1:]:
            load.wait()
        if depth:
            saves.pop(("middle", 0)).wait()

        @pl.loop(0, tiles)
        def _(m):
            rows = row_tile(m)
            mid = hidden[depth, rows, :].astype(F32) + (
                product(mixed[rows, :], out_v[depth]) + out_bias[depth : depth + 1, :]
            )
            middle[rows, :] = mid
            xhat, _ = normalized(mid)
            normed = (xhat * gain2[depth : depth + 1, :] + bias2[depth : depth + 1, :]).astype(BF)
            if depth:
                normed_two[rows, :] = normed
                for copy in tile_copies(m):
                    copy.wait()
            parts = list(range(0, hidden_units, STRIP))
            up = lambda f: product(normed, up_v[depth, :, f : f + STRIP]) + up_bias[depth : depth + 1, f : f + STRIP]
            u = up(0)
            added = jnp.zeros((ROWS, width), F32)
            previous = None
            for f in parts:
                following = up(f + STRIP) if f + STRIP < hidden_units else None
                if previous is not None:
                    added = added + product(previous, down_v[depth, f - STRIP : f, :])
                z, d = gelu_pair(u)
                previous = z.astype(BF)
                act[rows, f : f + STRIP] = previous
                slope[rows, f : f + STRIP] = d.astype(BF)
                u = following
            added = added + product(previous, down_v[depth, hidden_units - STRIP :, :])
            hidden[depth + 1, rows, :] = (mid + (added + down_bias[depth : depth + 1, :])).astype(BF)
            if not depth:
                for copy in tile_copies(m):
                    copy.start()

        if not depth:
            save(("middle", depth), middle, middle_out)

    real = cotangent.shape[1]
    cot[:real] = cotangent[0].astype(F32)
    cot[real:] = jnp.zeros((cot.shape[0] - real, width), F32)
    final_grads[...] = jnp.zeros_like(final_grads)

    def finish(step):
        for g in range(total // TILE):
            xhat, scale = normalized(hidden[2, g * TILE : (g + 1) * TILE, :].astype(F32))
            result[g * step : g * step + TILE, :] = xhat * final_gain[...] + final_bias[...]
            arriving = cot[g * step : g * step + TILE, :]
            if step < TILE:
                line = lax.broadcasted_iota(jnp.int32, (TILE, 1), 0)
                arriving = jnp.where(line < step, arriving, 0.0)
            back, gain_sum, bias_sum = norm_back(arriving, xhat, scale, final_gain[...])
            grad[g * TILE : (g + 1) * TILE, :] = back.astype(BF)
            final_grads[0:1, :] += gain_sum
            final_grads[1:2, :] += bias_sum

    @pl.when(stride == TILE)
    def _():
        finish(LONG_STEPS * 6)

    @pl.when(stride != TILE)
    def _():
        finish(TILE)

    saves["out"] = fetch(result.at[pl.ds(0, real)], activations, result_sem)
    grad_middle = cot
    mlp_data_back(
        1, None, grad, grad_middle, grad_mixed, vectors, wide, slope, up_v.at[1], down_v.at[1], out_v.at[1], middle,
        normed_two, grad_pre, rounded, gain2, bias2,
    )
    save("grad_middle", grad_middle, grad_middle_out)
    save("grad_mixed", grad_mixed, grad_mixed_out)
    saves["parts"] = mlp_weight_back(
        core, places, (), mine, theirs, grad, act, mixed.at[inside], normed_two, grad_pre, rounded,
        (mine_out, theirs_out, part_sem),
    )
    for copy in saves.values():
        copy.wait()


def mlp_data_back(depth, loads, grad, grad_middle, grad_mixed, vectors, wide, slope_v, up_v, down_v, out_v, middle_v, normed, grad_pre, rounded, gain2, bias2):
    total, width = grad.shape
    hidden_units = grad_pre.shape[1]
    vectors[...] = jnp.zeros_like(vectors)
    wide[...] = jnp.zeros_like(wide)
    if loads:
        down, slopes, up, mid, out = loads
        down.wait()
    for m in range(total // ROWS):
        rows = slice(m * ROWS, (m + 1) * ROWS)
        g = grad[rows, :]
        if loads:
            slopes[m].wait()
        if loads and m == 0:
            up.wait()
        back = jnp.zeros((ROWS, width), F32)
        for f in range(0, hidden_units, CHUNK):
            grad_act = product(g, down_v[f : f + CHUNK, :], NT)
            pre = grad_act * slope_v[rows, f : f + CHUNK].astype(F32)
            pre = pre.astype(BF)
            grad_pre[rows, f : f + CHUNK] = pre
            wide[0:1, f : f + CHUNK] += jnp.sum(pre.astype(F32), axis=0, keepdims=True)
            back = back + product(pre, up_v[:, f : f + CHUNK], NT)
        if loads and m == 0:
            mid.wait()
            out.wait()
        xhat, scale = normalized(middle_v[rows, :])
        if loads:
            normed[rows, :] = (xhat * gain2[depth : depth + 1, :] + bias2[depth : depth + 1, :]).astype(BF)
        through, gain_sum, bias_sum = norm_back(back, xhat, scale, gain2[depth : depth + 1, :])
        g = g.astype(F32)
        total_grad = g + through
        grad_middle[rows, :] = total_grad
        r = total_grad.astype(BF)
        rounded[rows, :] = r
        vectors[0:1, :] += gain_sum
        vectors[1:2, :] += bias_sum
        vectors[2:3, :] += jnp.sum(g, axis=0, keepdims=True)
        vectors[3:4, :] += jnp.sum(r.astype(F32), axis=0, keepdims=True)
        grad_mixed[rows, :] = product(r, out_v[...], NT).astype(BF)


def store_units(out, at, value, which, places):
    width = value.shape[1]
    if places is None:
        out[:, at : at + width] = value.astype(BF)
        return
    first, second = places
    rows = value.shape[0] // len(first)
    for unit in range(len(first)):
        place = first[unit] + which * (second[unit] - first[unit])
        out[pl.ds(pl.multiple_of(place * rows, rows), rows), at : at + width] = value[unit * rows : (unit + 1) * rows].astype(BF)


class Several:
    def __init__(self, copies):
        self.copies = copies

    def wait(self):
        for copy in self.copies:
            copy.wait()


def mlp_weight_back(core, places, loads, mine, theirs, grad, act_v, mixed_v, normed, grad_pre, rounded, outside=None):
    width = grad.shape[1]
    half = grad_pre.shape[1] // 2
    copies = []

    def made(part, at, size):
        if outside:
            cols = pl.ds(at, size)
            copies.append(fetch((mine, theirs)[part].at[:, cols], outside[part].at[:, cols], outside[2].at[len(copies)]))

    for part in range(2):
        out = (mine, theirs)[part]
        which = core if part == 0 else 1 - core
        for at in range(0, half, CHUNK):
            cols = pl.ds(pl.multiple_of(which * half + at, CHUNK), CHUNK)
            store_units(out, at, product(normed[...], grad_pre[:, cols], TN), which, places)
        made(part, 0, half)
        if part == 0:
            for load in loads:
                load.wait()
        for at in range(0, half, CHUNK):
            cols = pl.ds(pl.multiple_of(which * half + at, CHUNK), CHUNK)
            store_units(out, half + at, product(grad[...], act_v[:, cols], TN), which, places)
        made(part, half, half)
        cols = pl.ds(pl.multiple_of(which * (width // 2), width // 2), width // 2)
        store_units(out, 2 * half, product(mixed_v[...], rounded[:, cols], TN), which, places)
        made(part, 2 * half, width // 2)
    return Several(copies)


def mlp_loads(depth, slope, up_w, down_w, middle, out_w, slope_v, up_v, down_v, middle_v, out_v, sems, tile_sems):
    tiles = slope_v.shape[0] // ROWS

    def slope_tile(m):
        rows = pl.ds(m * ROWS, ROWS)
        return fetch(slope.at[rows], slope_v.at[rows], tile_sems.at[m])

    down = fetch(down_w.at[depth], down_v, sems.at[0])
    slopes = [slope_tile(0)]
    up = fetch(up_w.at[depth], up_v, sems.at[1])
    mid = fetch(middle, middle_v, sems.at[2])
    out = fetch(out_w.at[depth], out_v, sems.at[3])
    slopes += [slope_tile(m) for m in range(1, tiles)]
    return down, slopes, up, mid, out


def mlp_data_kernel(depth, tokens, grad, middle, slope, up_w, down_w, out_w, gain2, bias2, *rest):
    (grad_middle, grad_mixed, vectors, wide, normed, grad_pre, rounded,
     slope_v, up_v, down_v, out_v, middle_v, sems, tile_sems) = rest[tokens:]
    loads = mlp_loads(depth, slope, up_w, down_w, middle, out_w, slope_v, up_v, down_v, middle_v, out_v, sems, tile_sems)
    mlp_data_back(
        depth, loads, grad, grad_middle, grad_mixed, vectors, wide, slope_v, up_v, down_v, out_v, middle_v, normed,
        grad_pre, rounded, gain2, bias2,
    )


def mlp_weight_kernel(depth, tokens, places, scalars, grad, act, mixed, normed, grad_pre, rounded, *rest):
    mine, theirs, act_v, mixed_v, normed_v, pre_v, rounded_v, sems = rest[tokens:]
    first = [fetch(normed, normed_v, sems.at[0]), fetch(grad_pre, pre_v, sems.at[1])]
    later = [
        fetch(act, act_v, sems.at[2]), fetch(mixed, mixed_v, sems.at[3]),
        fetch(rounded, rounded_v, sems.at[4]),
    ]
    for load in first:
        load.wait()
    mlp_weight_back(scalars[1], places, later, mine, theirs, grad, act_v, mixed_v, normed_v, pre_v, rounded_v)


def attention_backward(qkv, probs, grad_mixed, grad_qkv, stride, windows, width):
    low, high = lane_halves()

    @pl.loop(0, windows)
    def _(t):
        rows = pl.ds(pl.multiple_of(t * stride, 32), TILE)
        kept = pl.ds(pl.multiple_of(t * 2 * TILE, 2 * TILE), 2 * TILE)
        pairs = range(width // TILE)
        cut = lambda k, pair: qkv[rows, k * width + pair * TILE : k * width + (pair + 1) * TILE]
        arriving = [both_heads(grad_mixed[rows, pair * TILE : (pair + 1) * TILE], low, high) for pair in pairs]
        grad_p = [product(arriving[pair], cut(2, pair), NT) for pair in pairs]
        p = [probs[pair, kept, :] for pair in pairs]
        grad_v = [product(p[pair], arriving[pair], TN) for pair in pairs]
        inner = [jnp.sum(grad_p[pair] * p[pair].astype(F32), axis=-1, keepdims=True) for pair in pairs]
        grad_s = [(p[pair].astype(F32) * (grad_p[pair] - inner[pair])).astype(BF) for pair in pairs]
        grad_q = [product(side_by_side(grad_s[pair]), both_heads(cut(1, pair), low, high)) * 0.125 for pair in pairs]
        grad_k = [product(grad_s[pair], both_heads(cut(0, pair), low, high), TN) for pair in pairs]
        for k, grads in enumerate((grad_q, grad_k, grad_v)):
            for pair in pairs:
                grad_qkv[rows, k * width + pair * TILE : k * width + (pair + 1) * TILE] = grads[pair].astype(BF)


def qkv_back(depth, core, places, grad_qkv, hidden_v, middle_v, weight_v, gain1, bias1, grad_in, normed, vectors, mine, theirs):
    total, width = hidden_v.shape

    @pl.loop(0, total // ROWS)
    def _(m):
        rows = row_tile(m)
        back = jnp.zeros((ROWS, width), F32)
        for f in range(0, 3 * width, width):
            back = back + product(grad_qkv[rows, f : f + width], weight_v[:, f : f + width], NT)
        xhat, scale = normalized(hidden_v[rows, :].astype(F32))
        normed[rows, :] = (xhat * gain1[depth : depth + 1, :] + bias1[depth : depth + 1, :]).astype(BF)
        through, gain_sum, bias_sum = norm_back(back, xhat, scale, gain1[depth : depth + 1, :])
        grad_in[rows, :] = (middle_v[rows, :] + through).astype(BF)
        vectors[0:1, :] += gain_sum
        vectors[1:2, :] += bias_sum
        vectors[2:3, :] += jnp.sum(grad_qkv[rows, :width].astype(F32), axis=0, keepdims=True)
        vectors[3:4, :] += jnp.sum(grad_qkv[rows, 2 * width :].astype(F32), axis=0, keepdims=True)

    half = 3 * width // 2
    for part in range(2):
        which = core if part == 0 else 1 - core
        cols = pl.ds(pl.multiple_of(which * half, half), half)
        store_units((mine, theirs)[part], 0, product(normed[...], grad_qkv[:total, cols], TN), which, places)


def attention_load(depth, qkv, probs, grad_mixed, qkv_v, probs_v, mixed_v, sems):
    total = grad_mixed.shape[0]
    loads = [
        fetch(qkv.at[depth], qkv_v.at[pl.ds(0, total)], sems.at[0]),
        fetch(grad_mixed, mixed_v.at[pl.ds(0, total)], sems.at[1]),
        fetch(probs.at[depth], probs_v, sems.at[2]),
    ]
    qkv_v[total:, :] = jnp.zeros((qkv_v.shape[0] - total, qkv_v.shape[1]), BF)
    mixed_v[total:, :] = jnp.zeros((mixed_v.shape[0] - total, mixed_v.shape[1]), BF)
    return loads


def attention_back_kernel(
    depth, tokens, places, scalars, hidden, qkv, probs, grad_mixed, grad_middle, qkv_w, gain1, bias1, *rest,
):
    (mine, theirs, grad_in, vectors,
     hidden_v, middle_v, weight_v, normed, qkv_v, probs_v, mixed_v, grad_qkv, sems) = rest[tokens:]
    loads = attention_load(depth, qkv, probs, grad_mixed, qkv_v, probs_v, mixed_v, sems)
    later = [
        fetch(qkv_w.at[depth], weight_v, sems.at[3]),
        fetch(hidden.at[depth], hidden_v, sems.at[4]),
        fetch(grad_middle, middle_v, sems.at[5]),
    ]
    vectors[...] = jnp.zeros_like(vectors)
    for load in loads:
        load.wait()
    attention_backward(qkv_v, probs_v, mixed_v, grad_qkv, *placed(scalars, grad_in.shape[0]), grad_in.shape[1])
    for load in later:
        load.wait()
    qkv_back(
        depth, scalars[1], places, grad_qkv, hidden_v, middle_v, weight_v, gain1, bias1, grad_in, normed, vectors, mine,
        theirs,
    )


def attention_part_kernel(depth, part, parts, tokens, scalars, qkv, probs, grad_mixed, *rest):
    out, qkv_v, probs_v, mixed_v, grad_qkv, sems, out_sem = rest[tokens:]
    total, whole = grad_mixed.shape
    width = whole // parts
    pairs = probs_v.shape[0]
    inside = pl.ds(0, total)
    loads = [
        fetch(qkv.at[depth, :, pl.ds(k * whole + part * width, width)], qkv_v.at[inside, pl.ds(k * width, width)], sems.at[k])
        for k in range(3)
    ]
    loads.append(fetch(grad_mixed.at[:, pl.ds(part * width, width)], mixed_v.at[inside], sems.at[3]))
    loads.append(fetch(probs.at[depth, pl.ds(part * pairs, pairs)], probs_v, sems.at[4]))
    qkv_v[total:, :] = jnp.zeros((qkv_v.shape[0] - total, qkv_v.shape[1]), BF)
    mixed_v[total:, :] = jnp.zeros((mixed_v.shape[0] - total, mixed_v.shape[1]), BF)
    for load in loads:
        load.wait()
    attention_backward(qkv_v, probs_v, mixed_v, grad_qkv, *placed(scalars, total), width)
    fetch(grad_qkv.at[inside], out, out_sem).wait()


def table_kernel(
    depth, tokens, places, groups, scalars, grad_low, grad_high, hidden, grad_middle, qkv_w, gain1, bias1,
    index, final_grads, feed1, wide1, attend1, feed0, wide0, *rest,
):
    (mine, theirs, frame_grad, grad_in, turned, vectors, stage, hidden_v, normed, grad_qkv, weight_v, middle_v, sems) = rest[tokens:]
    total, width = grad_in.shape
    half = width // 2
    loads = [
        fetch(low_high.at[:, pl.ds(k * half, half)], grad_qkv.at[:, pl.ds(k * width + n * half, half)], sems.at[3 * n + k])
        for k in range(3) for n, low_high in enumerate((grad_low, grad_high))
    ]
    loads.append(fetch(qkv_w.at[depth], weight_v, sems.at[6]))
    loads.append(fetch(hidden.at[depth], hidden_v, sems.at[7]))
    loads.append(fetch(grad_middle, middle_v, sems.at[8]))
    core = scalars[1]
    steps = frame_grad.shape[0]
    qkv_width = 3 * width // 2
    code_width = mine.shape[1] - qkv_width - TILE
    vectors[...] = jnp.zeros_like(vectors)
    for load in loads:
        load.wait()
    qkv_back(
        depth, core, places, grad_qkv, hidden_v, middle_v, weight_v, gain1, bias1, grad_in, normed, vectors, mine, theirs,
    )

    stage[...] = jnp.zeros_like(stage)
    for k, block in enumerate((feed0, vectors, feed1, attend1, final_grads)):
        stage[VECTORS + 8 * k : VECTORS + 8 * k + 8, :] = block[...]
    each = width // groups
    for k, wide in enumerate((wide0, wide1)):
        for group in range(groups):
            for c in range(4):
                start = group * 4 * each + c * each
                at = VECTORS + 40 + 8 * k + c
                stage[at : at + 1, group * each : group * each + each] = wide[0:1, start : start + each]

    turned[...] = grad_in[...].T
    for part in range(2):
        out = (mine, theirs)[part]
        which = core if part == 0 else 1 - core
        line = lax.broadcasted_iota(jnp.int32, (code_width, total), 0) + which * code_width
        hot = (line == index[0:1, :]).astype(F32).astype(BF)
        store_units(out, qkv_width, product(turned[...], hot, NT), which, places)
        line = lax.broadcasted_iota(jnp.int32, (TILE, total), 0) + which * TILE
        hot = ((line == index[1:2, :]) | (line == index[2:3, :])).astype(F32).astype(BF)
        small = product(turned[...], hot, NT) + stage[...].T * which.astype(F32)
        store_units(out, qkv_width + code_width, small, which, places)
    hot = (lax.broadcasted_iota(jnp.int32, (steps, total), 0) == index[3:4, :]).astype(F32).astype(BF)
    frame_grad[...] = product(hot, grad_in[...])


VMEM = pl.BlockSpec(memory_space=pltpu.VMEM)
ANY = pl.BlockSpec(memory_space=pl.ANY)
SMEM = pl.BlockSpec(memory_space=pltpu.SMEM)


def cost(flops, moved, others=0):
    return pl.CostEstimate(flops=int(8 * flops), bytes_accessed=int(moved), transcendentals=int(others))


def run_forward(places, scalars, actions, deltas, frames, codebook, action_table, position_table, layers, finals, cotangent):
    gain1, bias1, qkv_w, query_bias, value_bias, out_w, out_bias, gain2, bias2, up_w, up_bias, down_w, down_bias = layers
    width = codebook.shape[1]
    units = up_bias.shape[1]
    real = cotangent.shape[1]
    total = -(-real // ROWS) * ROWS
    reach = total + TILE // 2
    columns = units + width // 2
    shape = jax.ShapeDtypeStruct
    once = dict(pipeline_mode=pl.Buffered(1))
    whole = lambda a: pl.BlockSpec(a.shape, lambda i, s, n=a.ndim: (0,) * n, **once)
    mine = lambda a: pl.BlockSpec((1,) + a.shape[1:], lambda i, s: (s[0], 0, 0), **once)
    kept = (width // TILE, WINDOWS * 2 * TILE, TILE)
    outs = [
        (shape((real, width), F32), ANY),
        (shape((8, total), jnp.int32), None),
        (shape((8, width), F32), None), (shape((8, width), F32), None), (shape((8, units), F32), None),
        (shape((2, total, width), BF), ANY),
        (shape((2, total, 3 * width), BF), ANY),
        (shape((2,) + kept, BF), ANY),
        (shape((total, width), BF), ANY),
        (shape((total, width), F32), ANY),
        (shape((total, units), BF), ANY),
        (shape((total, units), BF), ANY),
        (shape((total, width), F32), ANY), (shape((total, width), BF), ANY),
        (shape((width, columns), BF), ANY), (shape((width, columns), BF), ANY),
    ]
    args = [
        (actions, mine(actions)), (deltas, mine(deltas)), (frames, mine(frames)),
        (codebook, None), (action_table, None), (position_table, None),
        (gain1, None), (bias1, None), (qkv_w, ANY), (query_bias, None), (value_bias, None), (out_w, ANY),
        (out_bias, None), (gain2, None), (bias2, None), (up_w, ANY), (up_bias, None), (down_w, ANY), (down_bias, None),
        (finals[0][None], None), (finals[1][None], None), (cotangent, mine(cotangent)),
    ]
    scratch = [
        pltpu.VMEM((2 * TILE, width), BF),
        pltpu.VMEM(qkv_w.shape, BF), pltpu.VMEM(out_w.shape, BF), pltpu.VMEM(up_w.shape, BF), pltpu.VMEM(down_w.shape, BF),
        pltpu.VMEM((3, total, width), BF), pltpu.VMEM((reach, 3 * width), BF), pltpu.VMEM(kept, BF),
        pltpu.VMEM((reach, width), BF), pltpu.VMEM((total, width), F32),
        pltpu.VMEM((total, units), BF), pltpu.VMEM((total, units), BF), pltpu.VMEM((2 * TILE, TILE), F32),
        pltpu.VMEM((total, width), F32), pltpu.VMEM((total, width), F32),
        pltpu.VMEM((total, width), BF), pltpu.VMEM((total, width), BF), pltpu.VMEM((total, width), BF),
        pltpu.VMEM((total, width), BF), pltpu.VMEM((total, units), BF),
        pltpu.VMEM((width, columns), BF), pltpu.VMEM((width, columns), BF),
        pltpu.SemaphoreType.DMA((2, 4)), pltpu.SemaphoreType.DMA((16,)), pltpu.SemaphoreType.DMA((2, total // ROWS)),
        pltpu.SemaphoreType.DMA, pltpu.SemaphoreType.DMA((6,)),
    ]
    return pl.pallas_call(
        partial(forward_kernel, places),
        out_shape=[o for o, _ in outs],
        grid_spec=pltpu.PrefetchScalarGridSpec(
            num_scalar_prefetch=1,
            grid=(1,),
            in_specs=[spec or whole(a) for a, spec in args],
            out_specs=[spec or whole(o) for o, spec in outs],
            scratch_shapes=scratch,
        ),
        compiler_params=pltpu.CompilerParams(vmem_limit_bytes=62 << 20),
        cost_estimate=cost(24e9, 50e6, 4e6),
        name="forward",
    )(scalars, *[a for a, _ in args])


def run_mlp_data(depth, grad, saved, layers, after):
    hidden, qkv, probs, mixed, middle, act, slope = saved
    gain1, bias1, qkv_w, query_bias, value_bias, out_w, out_bias, gain2, bias2, up_w, up_bias, down_w, down_bias = layers
    total, width = grad.shape
    units = up_bias.shape[1]
    shape = jax.ShapeDtypeStruct
    return pl.pallas_call(
        partial(mlp_data_kernel, depth, len(after)),
        out_shape=[
            shape((total, width), F32), shape((total, width), BF), shape((8, width), F32), shape((8, units), F32),
            shape((total, width), BF), shape((total, units), BF), shape((total, width), BF),
        ],
        in_specs=[VMEM] + [ANY] * 5 + [VMEM] * 2 + [ANY] * len(after),
        out_specs=[VMEM] * 7,
        scratch_shapes=[
            pltpu.VMEM((total, units), BF),
            pltpu.VMEM((width, units), BF), pltpu.VMEM((units, width), BF), pltpu.VMEM((width, width), BF),
            pltpu.VMEM((total, width), F32),
            pltpu.SemaphoreType.DMA((4,)), pltpu.SemaphoreType.DMA((total // ROWS,)),
        ],
        compiler_params=pltpu.CompilerParams(vmem_limit_bytes=40 << 20),
        cost_estimate=cost(10e9, 16e6),
        name="mlp_data",
    )(grad, middle, slope, up_w, down_w, out_w, gain2, bias2, *after)


def run_mlp_weight(depth, places, scalars, grad, saved, normed, grad_pre, rounded, after):
    hidden, qkv, probs, mixed, middle, act, slope = saved
    total, width = grad.shape
    units = grad_pre.shape[1]
    shape = jax.ShapeDtypeStruct
    return pl.pallas_call(
        partial(mlp_weight_kernel, depth, len(after), places),
        out_shape=[shape((width, units + width // 2), BF), shape((width, units + width // 2), BF)],
        in_specs=[SMEM, VMEM] + [ANY] * 5 + [ANY] * len(after),
        out_specs=[VMEM] * 2,
        scratch_shapes=[
            pltpu.VMEM((total, units), BF), pltpu.VMEM((total, width), BF), pltpu.VMEM((total, width), BF),
            pltpu.VMEM((total, units), BF), pltpu.VMEM((total, width), BF),
            pltpu.SemaphoreType.DMA((5,)),
        ],
        compiler_params=pltpu.CompilerParams(vmem_limit_bytes=40 << 20),
        cost_estimate=cost(8e9, 16e6),
        name="mlp_weight",
    )(scalars, grad, act, mixed, normed, grad_pre, rounded, *after)


def window_scratch(total, width, probs):
    reach = total + TILE // 2
    return [
        pltpu.VMEM((reach, 3 * width), BF), pltpu.VMEM(probs.shape[1:], BF),
        pltpu.VMEM((reach, width), BF), pltpu.VMEM((reach, 3 * width), BF),
    ]


def run_attention_back(depth, places, scalars, grad_mixed, grad_middle, saved, layers, after):
    hidden, qkv, probs, mixed, middle, act, slope = saved
    gain1, bias1, qkv_w = layers[:3]
    total, width = grad_mixed.shape
    shape = jax.ShapeDtypeStruct
    return pl.pallas_call(
        partial(attention_back_kernel, depth, len(after), places),
        out_shape=[
            shape((width, 3 * width // 2), BF), shape((width, 3 * width // 2), BF),
            shape((total, width), BF), shape((8, width), F32),
        ],
        in_specs=[SMEM] + [ANY] * 6 + [VMEM] * 2 + [ANY] * len(after),
        out_specs=[VMEM] * 4,
        scratch_shapes=[
            pltpu.VMEM((total, width), BF), pltpu.VMEM((total, width), F32), pltpu.VMEM(qkv_w.shape[1:], BF),
            pltpu.VMEM((total, width), BF), *window_scratch(total, width, probs),
            pltpu.SemaphoreType.DMA((6,)),
        ],
        compiler_params=pltpu.CompilerParams(vmem_limit_bytes=50 << 20),
        cost_estimate=cost(16e9, 24e6),
        name="attention_back",
    )(scalars, hidden, qkv, probs, grad_mixed, grad_middle, qkv_w, gain1, bias1, *after)


def run_attention_part(depth, part, parts, scalars, grad_mixed, saved, after):
    hidden, qkv, probs, mixed, middle, act, slope = saved
    total, width = grad_mixed.shape
    width = width // parts
    reach = total + TILE // 2
    return pl.pallas_call(
        partial(attention_part_kernel, depth, part, parts, len(after)),
        out_shape=jax.ShapeDtypeStruct((total, 3 * width), BF),
        in_specs=[SMEM] + [ANY] * 3 + [ANY] * len(after),
        out_specs=ANY,
        scratch_shapes=[
            pltpu.VMEM((reach, 3 * width), BF), pltpu.VMEM((width // TILE,) + probs.shape[2:], BF),
            pltpu.VMEM((reach, width), BF), pltpu.VMEM((reach, 3 * width), BF),
            pltpu.SemaphoreType.DMA((5,)), pltpu.SemaphoreType.DMA,
        ],
        compiler_params=pltpu.CompilerParams(vmem_limit_bytes=40 << 20),
        cost_estimate=cost(8e9, 8e6),
        name="attention_part",
    )(scalars, qkv, probs, grad_mixed, *after)


def run_table(depth, places, scalars, grad_low, grad_high, grad_middle, saved, layers, index, vectors, codes, steps, groups, after):
    hidden, qkv, probs, mixed, middle, act, slope = saved
    gain1, bias1, qkv_w = layers[:3]
    total, width = grad_middle.shape
    columns = 3 * width // 2 + codes // 2 + TILE
    shape = jax.ShapeDtypeStruct
    return pl.pallas_call(
        partial(table_kernel, depth, len(after), places, groups),
        out_shape=[shape((width, columns), BF), shape((width, columns), BF), shape((steps, width), F32)],
        in_specs=[SMEM] + [ANY] * 5 + [VMEM] * 2 + [VMEM] * 7 + [ANY] * len(after),
        out_specs=[VMEM] * 3,
        scratch_shapes=[
            pltpu.VMEM((total, width), BF), pltpu.VMEM((width, total), BF), pltpu.VMEM((8, width), F32),
            pltpu.VMEM((TILE, width), F32), pltpu.VMEM((total, width), BF), pltpu.VMEM((total, width), BF),
            pltpu.VMEM((total, 3 * width), BF), pltpu.VMEM(qkv_w.shape[1:], BF), pltpu.VMEM((total, width), F32),
            pltpu.SemaphoreType.DMA((9,)),
        ],
        compiler_params=pltpu.CompilerParams(vmem_limit_bytes=40 << 20),
        cost_estimate=cost(8e9, 12e6),
        name="tables",
    )(scalars, grad_low, grad_high, hidden, grad_middle, qkv_w, gain1, bias1, index, *vectors, *after)


def swap(array, axis, bit):
    size = lax.axis_size(axis)
    return lax.ppermute(array, axis, [(i, i ^ (1 << bit)) for i in range(size)])


def bits_of(axis):
    return lax.axis_size(axis).bit_length() - 1


def own_bit(axis, bit):
    return (lax.axis_index(axis) >> bit) & 1


def take(array, dim, which):
    return lax.dynamic_index_in_dim(array, which, dim, keepdims=False)


def total_of(terms):
    return sum(term.astype(F32) for term in terms)


def settled(array):
    return lax.optimization_barrier(array.astype(BF))


def tied(array, token):
    return lax.optimization_barrier((array, token))[0]


def unit_places(count):
    first, second = [], []
    for unit in range(2 << count):
        bits = [(unit >> (1 + bit)) & 1 for bit in range(count)]
        for order, places in ((bits + [unit & 1], first), ([unit & 1] + bits, second)):
            place = 0
            for bit in order:
                place = 2 * place + bit
            places.append(place)
    return first, second


def reordered(array, which, count):
    rows, columns = array.shape
    ways = array.reshape((2,) * (count + 1) + (rows >> (count + 1), columns))
    dims = list(range(count - 1, -1, -1))
    first = ways.transpose(dims + [count, count + 1, count + 2])
    second = ways.transpose([count] + dims + [count + 1, count + 2])
    return jnp.where(which == 0, first, second).reshape(rows, columns)


class Chunk:
    def __init__(self, places):
        self.count = bits_of("dp")
        self.places = places
        self.pieces = []
        self.terms = []
        self.core = own_bit("section", 0)

    def add(self, mine, theirs):
        if self.places is None:
            mine, theirs = reordered(mine, self.core, self.count), reordered(theirs, 1 - self.core, self.count)
        self.pieces.append([mine, swap(theirs, "section", 0)])

    def hold(self, token):
        if self.terms:
            self.terms[-1] = tied(self.terms[-1], token)
        else:
            for piece in self.pieces:
                piece[1] = tied(piece[1], token)

    def step(self):
        if not self.terms:
            self.left = self.pieces[0][0].shape[0]
        k = len(self.terms)
        bits = [own_bit("dp", bit) for bit in range(self.count)]
        across = own_bit("section", 1)
        own = jnp.where(self.core == 0, (bits + [across])[k], ([across] + bits)[k])
        half = self.left // 2
        cut = lambda t, which: lax.dynamic_slice_in_dim(t, which * half, half, 0)
        if not self.terms:
            self.parts = [[[mine, arrived] for mine, arrived in self.pieces]]
        parts = self.parts[-1]
        sum_of = jnp.concatenate([total_of([cut(t, 1 - own) for t in part]) for part in parts], axis=1)
        for term in self.terms:
            sum_of = sum_of + cut(term, 1 - own).astype(F32)
        self.sent = settled(sum_of)
        sections = lax.axis_size("section")
        pairs = []
        for source in range(lax.axis_size("dp") * sections):
            at = k if source & 1 == 0 else (k - 1) % (self.count + 1)
            bit = sections << at if at < self.count else 2
            pairs.append((source, source ^ bit))
        self.parts = [[[cut(t, own) for t in part] for part in parts]]
        self.terms = [cut(t, own) for t in self.terms] + [lax.ppermute(self.sent, ("dp", "section"), pairs)]
        self.left = half
        return self

    def across(self):
        total = jnp.concatenate([total_of(part) for part in self.parts[-1]], axis=1)
        for term in self.terms:
            total = total + term.astype(F32)
        self.sent = settled(total)
        self.terms = [swap(self.sent, "section", 1)]

    def finish(self):
        other = self.terms[-1]
        rows = jnp.where(
            own_bit("section", 1) == 0, jnp.concatenate([self.sent, other]), jnp.concatenate([other, self.sent])
        )
        rows = lax.optimization_barrier(rows)
        arrived = swap(rows, "section", 0)
        both = jnp.stack([jnp.where(self.core == 0, rows, arrived), jnp.where(self.core == 0, arrived, rows)])
        self.results = []
        at = 0
        for mine, _ in self.pieces:
            self.results.append(both[:, :, at : at + mine.shape[1]])
            at += mine.shape[1]


def joined(result, start, size):
    return jnp.concatenate([result[core, :, start : start + size] for core in range(2)], axis=1).astype(F32)


def local(
    frames, actions, deltas, kinds, codebook, action_table, position_table, norm1_gain, norm1_bias, qkv_weight,
    query_bias, value_bias, out_weight, out_bias, norm2_gain, norm2_bias, up_weight, up_bias, down_weight, down_bias,
    final_gain, final_bias, cotangent,
):
    micro, steps, width = frames.shape
    units = up_weight.shape[2]
    codes = codebook.shape[0]
    slot = lax.axis_index("section") * micro // lax.axis_size("section")
    layers = (
        norm1_gain, norm1_bias, qkv_weight, query_bias, value_bias, out_weight, out_bias, norm2_gain, norm2_bias,
        up_weight, up_bias, down_weight, down_bias,
    )
    scalars = jnp.concatenate([jnp.stack([slot, own_bit("section", 0)]).astype(jnp.int32), kinds])
    groups = lax.axis_size("dp")
    count = bits_of("dp")
    places = unit_places(count) if width >> (count + 1) >= 16 else None
    chunk1, chunk2, chunk3 = Chunk(places), Chunk(places), Chunk(places)
    activations, index, final_grads, feed1, wide1, *saved, middle, mixed, mine, theirs = run_forward(
        places, scalars, actions[:, None], deltas.transpose(0, 2, 1), frames, codebook, action_table, position_table,
        layers, (final_gain, final_bias), cotangent,
    )
    chunk1.add(mine, theirs)
    mine, theirs, grad, attend1 = run_attention_back(1, places, scalars, mixed, middle, saved, layers, [])
    chunk1.hold(attend1)
    chunk2.add(mine, theirs)
    chunk1.step()
    middle, mixed, feed0, wide0, normed, grad_pre, rounded = run_mlp_data(0, grad, saved, layers, [chunk1.sent])
    chunk1.hold(normed)
    chunk1.step()
    mine, theirs = run_mlp_weight(0, places, scalars, grad, saved, normed, grad_pre, rounded, [chunk1.sent])
    chunk1.hold(theirs)
    chunk2.hold(theirs)
    chunk2.add(mine, theirs)
    chunk1.step()
    grad_low = run_attention_part(0, 0, 2, scalars, mixed, saved, [chunk1.sent])
    chunk1.hold(grad_low)
    chunk2.hold(grad_low)
    chunk2.step()
    chunk1.step()
    grad_high = run_attention_part(0, 1, 2, scalars, mixed, saved, [chunk2.sent, chunk1.sent])
    chunk1.hold(grad_high)
    for _ in range(3, count):
        chunk1.step()
    chunk1.across()
    vectors = (final_grads, feed1, wide1, attend1, feed0, wide0)
    mine, theirs, frame_grad = run_table(
        0, places, scalars, grad_low, grad_high, middle, saved, layers, index, vectors, codes, steps, groups, [chunk1.sent]
    )
    chunk3.add(mine, theirs)
    chunk2.hold(frame_grad)
    chunk1.hold(chunk2.terms[-1])
    chunk2.step()
    chunk3.hold(chunk2.sent)
    chunk3.step()
    chunk2.hold(chunk3.sent)
    chunk1.hold(chunk3.sent)
    chunk1.finish()
    for k in range(2, count + 3):
        if k <= count:
            chunk2.step()
        elif k == count + 1:
            chunk2.across()
        else:
            chunk2.finish()
        chunk3.hold(chunk2.sent)
        if k <= count + 1:
            chunk3.step()
        else:
            chunk3.across()
        if k <= count + 1:
            chunk2.hold(chunk3.sent)
    chunk3.finish()
    feed = (chunk2.results[1], chunk1.results[0])
    attend = (chunk3.results[0], chunk2.results[0])
    tables = chunk3.results[0]
    half = units // 2
    up = jnp.stack([joined(feed[d], 0, half) for d in range(2)])
    down = jnp.stack([joined(feed[d], half, half).T for d in range(2)])
    out = jnp.stack([joined(feed[d], 2 * half, width // 2) for d in range(2)])
    qkv = jnp.stack([joined(attend[d], 0, 3 * width // 2) for d in range(2)])
    code = joined(tables, 3 * width // 2, codes // 2).T
    small = tables[:, :, -TILE:].astype(F32)
    vec = small[1, :, VECTORS:].T

    def pair(k):
        return jnp.stack([vec[k], vec[k + 16]])

    down_b, out_b = pair(2), pair(3)
    up_b = jnp.stack([vec[40 + 8 * d : 44 + 8 * d].reshape(-1) for d in range(2)])
    return (
        activations[None], frame_grad[None], code, small[1, :, : action_table.shape[0]].T,
        small[0, :, : position_table.shape[0]].T, pair(8), pair(9), qkv, pair(10), pair(11), out, out_b, pair(0), pair(1),
        up, up_b, down, down_b, vec[32], vec[33],
    )


def solution(mesh):
    rows, one = P("dp", None, None), P(None, "dp")
    weight = P(None, "dp", None)
    both = P(("dp", "section"), None, None)
    return jax.shard_map(
        local,
        mesh=mesh,
        in_specs=(rows, P("dp", None), rows, P("dp")) + (P(),) * 18 + (rows,),
        out_specs=(
            both, both, one, one, one, one, one, weight, one, one, weight, one, one, one, weight, one,
            P(None, None, "dp"), one, P("dp"), P("dp"),
        ),
        check_vma=False,
    )
```

```python
from functools import partial

import jax
import jax.numpy as jnp
from jax import lax
from jax.experimental import pallas as pl
from jax.experimental.pallas import tpu as pltpu
from jax.sharding import PartitionSpec as P

HEADS = 8
SHORT_STEPS = 8
LONG_STEPS = 21
EPSILON = 1e-05
MASKED = -1e30
TILE = 128
ROWS = 256
CHUNK = 512
STRIP = 256
VECTORS = 32
WINDOWS = 11
BF = jnp.bfloat16
F32 = jnp.float32

NN = (((1,), (0,)), ((), ()))
NT = (((1,), (1,)), ((), ()))
TN = (((0,), (0,)), ((), ()))


def product(left, right, form=NN):
    return lax.dot_general(left, right, form, preferred_element_type=F32)


def normalized(x):
    center = x - jnp.mean(x, axis=-1, keepdims=True)
    spread = jnp.mean(center * center, axis=-1, keepdims=True)
    scale = lax.rsqrt(spread + EPSILON)
    return center * scale, scale


def norm_back(grad, xhat, scale, gain):
    inner = grad * gain
    first = jnp.mean(inner, axis=-1, keepdims=True)
    second = jnp.mean(inner * xhat, axis=-1, keepdims=True)
    back = (inner - first - xhat * second) * scale
    return back, jnp.sum(grad * xhat, axis=0, keepdims=True), jnp.sum(grad, axis=0, keepdims=True)


def gelu_pair(u):
    cdf = 0.5 + 0.5 * lax.erf(u * 0.7071067811865476)
    e = jnp.exp2(u * u * (-0.5 * 1.4426950408889634))
    return u * cdf, cdf + u * (e * 0.3989422804014327)


def row_tile(m):
    return pl.ds(pl.multiple_of(m * ROWS, ROWS), ROWS)


def lane_halves():
    lane = lax.broadcasted_iota(jnp.int32, (1, TILE), 1)
    low = (lane < TILE // 2).astype(F32)
    return low.astype(BF), (1.0 - low).astype(BF)


def both_heads(x, low, high):
    return jnp.concatenate([x * low, x * high], axis=0)


def side_by_side(x):
    return jnp.concatenate([x[:TILE], x[TILE:]], axis=1)


def write_mask(mask, stride):
    row = lax.broadcasted_iota(jnp.int32, (2 * TILE, TILE), 0)
    row = jnp.where(row >= TILE, row - TILE, row).astype(F32) + 0.5
    col = lax.broadcasted_iota(jnp.int32, (2 * TILE, TILE), 1).astype(F32) + 0.5
    step = jnp.floor(col * (1.0 / 6.0)) <= jnp.floor(row * (1.0 / 6.0))
    member = jnp.floor(col * (1.0 / 48.0)) == jnp.floor(row * (1.0 / 48.0))
    long = jnp.where(step, 0.0, MASKED)
    short = jnp.where(member, long, MASKED)
    mask[...] = jnp.where(stride == TILE, long, short)


def placed(scalars, total):
    long = scalars[2 + scalars[0]] == 1
    return jnp.where(long, TILE, 2 * SHORT_STEPS * 6), jnp.where(long, total // TILE, WINDOWS)


def fetch(source, target, sem):
    copy = pltpu.make_async_copy(source, target, sem)
    copy.start()
    return copy


def attention_forward(qkv, probs, mixed, mask, stride, windows, width):
    low, high = lane_halves()

    @pl.loop(0, windows)
    def _(t):
        rows = pl.ds(pl.multiple_of(t * stride, 32), TILE)
        kept = pl.ds(pl.multiple_of(t * 2 * TILE, 2 * TILE), 2 * TILE)
        pairs = range(width // TILE)
        cut = lambda k, pair: qkv[rows, k * width + pair * TILE : k * width + (pair + 1) * TILE]
        scores = [product(both_heads(cut(0, pair), low, high), cut(1, pair), NT) + mask[...] for pair in pairs]
        shifted = [jnp.exp(s - jnp.max(s, axis=-1, keepdims=True)) for s in scores]
        p = [(s * (1.0 / jnp.sum(s, axis=-1, keepdims=True))).astype(BF) for s in shifted]
        for pair in pairs:
            probs[pair, kept, :] = p[pair]
        out = [product(side_by_side(p[pair]), both_heads(cut(2, pair), low, high)) for pair in pairs]
        for pair in pairs:
            mixed[rows, pair * TILE : (pair + 1) * TILE] = out[pair].astype(BF)


def build_index(index, actions, deltas, long):
    steps = actions.shape[-1]
    total = index.shape[1]
    step = lax.broadcasted_iota(jnp.int32, (steps, total), 0).astype(F32)
    start = step * 6.0 + jnp.where(long, 2.0, 0.0) * jnp.floor((step + 0.5) * (1.0 / LONG_STEPS))
    slot = lax.broadcasted_iota(jnp.int32, (steps, total), 1).astype(F32) - start
    line = lax.broadcasted_iota(jnp.int32, (8, steps), 0)

    def rows(**values):
        out = jnp.zeros((8, steps), F32)
        for name, value in values.items():
            out = jnp.where(line == int(name[1:]), value, out)
        return out.astype(BF)

    def spread(value, j):
        return product(value, (slot == float(j)).astype(F32).astype(BF))

    count = lax.broadcasted_iota(jnp.int32, (8, steps), 1).astype(F32)
    found = spread(rows(r5=count, r6=1.0), 0) + spread(rows(r3=actions[0].astype(F32), r4=1.0), 1)
    for j in range(deltas.shape[1]):
        code = deltas[0, j : j + 1, :].astype(F32)
        high = jnp.floor(code * (1.0 / 32.0))
        found = found + spread(rows(r0=high, r1=code - 32.0 * high, r2=1.0), 2 + j)
    found = found.astype(jnp.int32)
    none = jnp.full((1, total), -1, jnp.int32)
    row = lax.broadcasted_iota(jnp.int32, (1, total), 1)
    real = row.astype(F32) + 0.5
    apart = row - TILE * jnp.floor(real * (1.0 / TILE)).astype(jnp.int32)
    apart = jnp.where(apart < LONG_STEPS * 6, apart, none)
    close = row - SHORT_STEPS * 6 * jnp.floor(real * (1.0 / (SHORT_STEPS * 6))).astype(jnp.int32)
    close = jnp.where(row < steps * 6, close, none)
    index[0:1, :] = jnp.where(found[2:3] == 1, found[0:1] * 32 + found[1:2], none)
    index[1:2, :] = jnp.where(long, apart, close)
    index[2:3, :] = jnp.where(found[4:5] == 1, found[3:4] + TILE, none)
    index[3:4, :] = jnp.where(found[6:7] == 1, found[5:6], none)
    index[4:8, :] = jnp.full((4, total), -1, jnp.int32)


def forward_kernel(
    places, scalars, actions, deltas, frames, codebook, action_table, position_table,
    gain1, bias1, qkv_w, query_bias, value_bias, out_w, out_bias, gain2, bias2,
    up_w, up_bias, down_w, down_bias, final_gain, final_bias, cotangent,
    activations, index, final_grads, vectors, wide,
    hidden_out, qkv_out, probs_out, mixed_out, middle_out, act_out, slope_out,
    grad_middle_out, grad_mixed_out, mine_out, theirs_out,
    table, qkv_v, out_v, up_v, down_v, hidden, qkv, probs, mixed, middle, act, slope, mask, result, cot,
    grad, grad_mixed, normed_two, rounded, grad_pre, mine, theirs,
    weight_sem, save_sem, tile_sem, result_sem, part_sem,
):
    core = scalars[1]
    width = hidden.shape[-1]
    total = hidden.shape[1]
    stride, windows = placed(scalars, total)
    hidden_units = up_bias.shape[1]
    tiles = total // ROWS
    loads = []
    for depth in range(2):
        loads.append([
            fetch(qkv_w.at[depth], qkv_v.at[depth], weight_sem.at[depth, 0]),
            fetch(out_w.at[depth], out_v.at[depth], weight_sem.at[depth, 1]),
            fetch(up_w.at[depth], up_v.at[depth], weight_sem.at[depth, 2]),
            fetch(down_w.at[depth], down_v.at[depth], weight_sem.at[depth, 3]),
        ])
    write_mask(mask, stride)
    build_index(index, actions, deltas, stride == TILE)
    positions = position_table.shape[0]
    action_count = action_table.shape[0]
    table[...] = jnp.zeros_like(table)
    table[:positions] = position_table[...]
    table[TILE : TILE + action_count] = action_table[...]
    qkv[total:, :] = jnp.zeros((qkv.shape[0] - total, qkv.shape[1]), BF)

    codes = codebook.shape[0]
    steps = frames.shape[1]

    @pl.loop(0, tiles)
    def _(m):
        rows = row_tile(m)
        code_hot = (lax.broadcasted_iota(jnp.int32, (codes, ROWS), 0) == index[0:1, rows]).astype(F32).astype(BF)
        line = lax.broadcasted_iota(jnp.int32, (2 * TILE, ROWS), 0)
        small_hot = ((line == index[1:2, rows]) | (line == index[2:3, rows])).astype(F32).astype(BF)
        frame_hot = (lax.broadcasted_iota(jnp.int32, (steps, ROWS), 0) == index[3:4, rows]).astype(F32).astype(BF)
        value = product(code_hot, codebook[...], TN) + product(small_hot, table[...], TN)
        value = value + product(frame_hot, frames[0], TN)
        hidden[0, rows, :] = value.astype(BF)

    def tile_copies(m):
        rows = row_tile(m)
        return (
            pltpu.make_async_copy(act.at[rows], act_out.at[rows], tile_sem.at[0, m]),
            pltpu.make_async_copy(slope.at[rows], slope_out.at[rows], tile_sem.at[1, m]),
        )

    saves = {}
    started = []

    def save(name, source, target):
        saves[name] = fetch(source, target, save_sem.at[len(started)])
        started.append(name)

    inside = pl.ds(0, total)
    for depth in range(2):
        save(("hidden", depth), hidden.at[depth], hidden_out.at[depth])
        loads[depth][0].wait()
        if depth:
            saves.pop(("qkv", 0)).wait()

        def normed_tile(m):
            xhat, _ = normalized(hidden[depth, m * ROWS : (m + 1) * ROWS, :].astype(F32))
            return (xhat * gain1[depth : depth + 1, :] + bias1[depth : depth + 1, :]).astype(BF)

        ready = normed_tile(0)
        for m in range(tiles):
            rows = slice(m * ROWS, (m + 1) * ROWS)
            normed = ready
            if m + 1 < tiles:
                ready = normed_tile(m + 1)
            q = product(normed, qkv_v[depth, :, :width]) + query_bias[depth : depth + 1, :]
            k = product(normed, qkv_v[depth, :, width : 2 * width])
            v = product(normed, qkv_v[depth, :, 2 * width :]) + value_bias[depth : depth + 1, :]
            qkv[rows, :width] = (q.astype(BF).astype(F32) * 0.125).astype(BF)
            qkv[rows, width : 2 * width] = k.astype(BF)
            qkv[rows, 2 * width :] = v.astype(BF)

        save(("qkv", depth), qkv.at[inside], qkv_out.at[depth])
        if depth:
            saves.pop(("probs", 0)).wait()
            saves.pop(("mixed", 0)).wait()
        attention_forward(qkv, probs, mixed, mask, stride, windows, width)
        save(("probs", depth), probs, probs_out.at[depth])
        if not depth:
            save(("mixed", depth), mixed.at[inside], mixed_out)
        for load in loads[depth][1:]:
            load.wait()
        if depth:
            saves.pop(("middle", 0)).wait()

        @pl.loop(0, tiles)
        def _(m):
            rows = row_tile(m)
            mid = hidden[depth, rows, :].astype(F32) + (
                product(mixed[rows, :], out_v[depth]) + out_bias[depth : depth + 1, :]
            )
            middle[rows, :] = mid
            xhat, _ = normalized(mid)
            normed = (xhat * gain2[depth : depth + 1, :] + bias2[depth : depth + 1, :]).astype(BF)
            if depth:
                normed_two[rows, :] = normed
                for copy in tile_copies(m):
                    copy.wait()
            parts = list(range(0, hidden_units, STRIP))
            up = lambda f: product(normed, up_v[depth, :, f : f + STRIP]) + up_bias[depth : depth + 1, f : f + STRIP]
            u = up(0)
            added = jnp.zeros((ROWS, width), F32)
            previous = None
            for f in parts:
                following = up(f + STRIP) if f + STRIP < hidden_units else None
                if previous is not None:
                    added = added + product(previous, down_v[depth, f - STRIP : f, :])
                z, d = gelu_pair(u)
                previous = z.astype(BF)
                act[rows, f : f + STRIP] = previous
                slope[rows, f : f + STRIP] = d.astype(BF)
                u = following
            added = added + product(previous, down_v[depth, hidden_units - STRIP :, :])
            hidden[depth + 1, rows, :] = (mid + (added + down_bias[depth : depth + 1, :])).astype(BF)
            if not depth:
                for copy in tile_copies(m):
                    copy.start()

        if not depth:
            save(("middle", depth), middle, middle_out)

    real = cotangent.shape[1]
    cot[:real] = cotangent[0].astype(F32)
    cot[real:] = jnp.zeros((cot.shape[0] - real, width), F32)
    final_grads[...] = jnp.zeros_like(final_grads)

    def finish(step):
        for g in range(total // TILE):
            xhat, scale = normalized(hidden[2, g * TILE : (g + 1) * TILE, :].astype(F32))
            result[g * step : g * step + TILE, :] = xhat * final_gain[...] + final_bias[...]
            arriving = cot[g * step : g * step + TILE, :]
            if step < TILE:
                line = lax.broadcasted_iota(jnp.int32, (TILE, 1), 0)
                arriving = jnp.where(line < step, arriving, 0.0)
            back, gain_sum, bias_sum = norm_back(arriving, xhat, scale, final_gain[...])
            grad[g * TILE : (g + 1) * TILE, :] = back.astype(BF)
            final_grads[0:1, :] += gain_sum
            final_grads[1:2, :] += bias_sum

    @pl.when(stride == TILE)
    def _():
        finish(LONG_STEPS * 6)

    @pl.when(stride != TILE)
    def _():
        finish(TILE)

    saves["out"] = fetch(result.at[pl.ds(0, real)], activations, result_sem)
    grad_middle = cot
    mlp_data_back(
        1, None, grad, grad_middle, grad_mixed, vectors, wide, slope, up_v.at[1], down_v.at[1], out_v.at[1], middle,
        normed_two, grad_pre, rounded, gain2, bias2,
    )
    save("grad_middle", grad_middle, grad_middle_out)
    save("grad_mixed", grad_mixed, grad_mixed_out)
    saves["parts"] = mlp_weight_back(
        core, places, (), mine, theirs, grad, act, mixed.at[inside], normed_two, grad_pre, rounded,
        (mine_out, theirs_out, part_sem),
    )
    for copy in saves.values():
        copy.wait()


def mlp_data_back(depth, loads, grad, grad_middle, grad_mixed, vectors, wide, slope_v, up_v, down_v, out_v, middle_v, normed, grad_pre, rounded, gain2, bias2):
    total, width = grad.shape
    hidden_units = grad_pre.shape[1]
    vectors[...] = jnp.zeros_like(vectors)
    wide[...] = jnp.zeros_like(wide)
    if loads:
        down, slopes, up, mid, out = loads
        down.wait()
    for m in range(total // ROWS):
        rows = slice(m * ROWS, (m + 1) * ROWS)
        g = grad[rows, :]
        if loads:
            slopes[m].wait()
        if loads and m == 0:
            up.wait()
        back = jnp.zeros((ROWS, width), F32)
        for f in range(0, hidden_units, CHUNK):
            grad_act = product(g, down_v[f : f + CHUNK, :], NT)
            pre = grad_act * slope_v[rows, f : f + CHUNK].astype(F32)
            pre = pre.astype(BF)
            grad_pre[rows, f : f + CHUNK] = pre
            wide[0:1, f : f + CHUNK] += jnp.sum(pre.astype(F32), axis=0, keepdims=True)
            back = back + product(pre, up_v[:, f : f + CHUNK], NT)
        if loads and m == 0:
            mid.wait()
            out.wait()
        xhat, scale = normalized(middle_v[rows, :])
        if loads:
            normed[rows, :] = (xhat * gain2[depth : depth + 1, :] + bias2[depth : depth + 1, :]).astype(BF)
        through, gain_sum, bias_sum = norm_back(back, xhat, scale, gain2[depth : depth + 1, :])
        g = g.astype(F32)
        total_grad = g + through
        grad_middle[rows, :] = total_grad
        r = total_grad.astype(BF)
        rounded[rows, :] = r
        vectors[0:1, :] += gain_sum
        vectors[1:2, :] += bias_sum
        vectors[2:3, :] += jnp.sum(g, axis=0, keepdims=True)
        vectors[3:4, :] += jnp.sum(r.astype(F32), axis=0, keepdims=True)
        grad_mixed[rows, :] = product(r, out_v[...], NT).astype(BF)


def store_units(out, at, value, which, places):
    width = value.shape[1]
    if places is None:
        out[:, at : at + width] = value.astype(BF)
        return
    first, second = places
    rows = value.shape[0] // len(first)
    for unit in range(len(first)):
        place = first[unit] + which * (second[unit] - first[unit])
        out[pl.ds(pl.multiple_of(place * rows, rows), rows), at : at + width] = value[unit * rows : (unit + 1) * rows].astype(BF)


class Several:
    def __init__(self, copies):
        self.copies = copies

    def wait(self):
        for copy in self.copies:
            copy.wait()


def mlp_weight_back(core, places, loads, mine, theirs, grad, act_v, mixed_v, normed, grad_pre, rounded, outside=None):
    width = grad.shape[1]
    half = grad_pre.shape[1] // 2
    copies = []

    def made(part, at, size):
        if outside:
            cols = pl.ds(at, size)
            copies.append(fetch((mine, theirs)[part].at[:, cols], outside[part].at[:, cols], outside[2].at[len(copies)]))

    for part in range(2):
        out = (mine, theirs)[part]
        which = core if part == 0 else 1 - core
        for at in range(0, half, CHUNK):
            cols = pl.ds(pl.multiple_of(which * half + at, CHUNK), CHUNK)
            store_units(out, at, product(normed[...], grad_pre[:, cols], TN), which, places)
        made(part, 0, half)
        if part == 0:
            for load in loads:
                load.wait()
        for at in range(0, half, CHUNK):
            cols = pl.ds(pl.multiple_of(which * half + at, CHUNK), CHUNK)
            store_units(out, half + at, product(grad[...], act_v[:, cols], TN), which, places)
        made(part, half, half)
        cols = pl.ds(pl.multiple_of(which * (width // 2), width // 2), width // 2)
        store_units(out, 2 * half, product(mixed_v[...], rounded[:, cols], TN), which, places)
        made(part, 2 * half, width // 2)
    return Several(copies)


def mlp_loads(depth, slope, up_w, down_w, middle, out_w, slope_v, up_v, down_v, middle_v, out_v, sems, tile_sems):
    tiles = slope_v.shape[0] // ROWS

    def slope_tile(m):
        rows = pl.ds(m * ROWS, ROWS)
        return fetch(slope.at[rows], slope_v.at[rows], tile_sems.at[m])

    down = fetch(down_w.at[depth], down_v, sems.at[0])
    slopes = [slope_tile(0)]
    up = fetch(up_w.at[depth], up_v, sems.at[1])
    mid = fetch(middle, middle_v, sems.at[2])
    out = fetch(out_w.at[depth], out_v, sems.at[3])
    slopes += [slope_tile(m) for m in range(1, tiles)]
    return down, slopes, up, mid, out


def mlp_data_kernel(depth, tokens, grad, middle, slope, up_w, down_w, out_w, gain2, bias2, *rest):
    (grad_middle, grad_mixed, vectors, wide, normed, grad_pre, rounded,
     slope_v, up_v, down_v, out_v, middle_v, sems, tile_sems) = rest[tokens:]
    loads = mlp_loads(depth, slope, up_w, down_w, middle, out_w, slope_v, up_v, down_v, middle_v, out_v, sems, tile_sems)
    mlp_data_back(
        depth, loads, grad, grad_middle, grad_mixed, vectors, wide, slope_v, up_v, down_v, out_v, middle_v, normed,
        grad_pre, rounded, gain2, bias2,
    )


def mlp_weight_kernel(depth, tokens, places, scalars, grad, act, mixed, normed, grad_pre, rounded, *rest):
    mine, theirs, act_v, mixed_v, normed_v, pre_v, rounded_v, sems = rest[tokens:]
    first = [fetch(normed, normed_v, sems.at[0]), fetch(grad_pre, pre_v, sems.at[1])]
    later = [
        fetch(act, act_v, sems.at[2]), fetch(mixed, mixed_v, sems.at[3]),
        fetch(rounded, rounded_v, sems.at[4]),
    ]
    for load in first:
        load.wait()
    mlp_weight_back(scalars[1], places, later, mine, theirs, grad, act_v, mixed_v, normed_v, pre_v, rounded_v)


def attention_backward(qkv, probs, grad_mixed, grad_qkv, stride, windows, width, whole=None, at=0):
    whole = whole or width
    low, high = lane_halves()

    @pl.loop(0, windows)
    def _(t):
        rows = pl.ds(pl.multiple_of(t * stride, 32), TILE)
        kept = pl.ds(pl.multiple_of(t * 2 * TILE, 2 * TILE), 2 * TILE)
        pairs = range(width // TILE)
        cut = lambda k, pair: qkv[rows, k * width + pair * TILE : k * width + (pair + 1) * TILE]
        arriving = [both_heads(grad_mixed[rows, pair * TILE : (pair + 1) * TILE], low, high) for pair in pairs]
        grad_p = [product(arriving[pair], cut(2, pair), NT) for pair in pairs]
        p = [probs[pair, kept, :] for pair in pairs]
        grad_v = [product(p[pair], arriving[pair], TN) for pair in pairs]
        inner = [jnp.sum(grad_p[pair] * p[pair].astype(F32), axis=-1, keepdims=True) for pair in pairs]
        grad_s = [(p[pair].astype(F32) * (grad_p[pair] - inner[pair])).astype(BF) for pair in pairs]
        grad_q = [product(side_by_side(grad_s[pair]), both_heads(cut(1, pair), low, high)) * 0.125 for pair in pairs]
        grad_k = [product(grad_s[pair], both_heads(cut(0, pair), low, high), TN) for pair in pairs]
        for k, grads in enumerate((grad_q, grad_k, grad_v)):
            for pair in pairs:
                start = k * whole + at + pair * TILE
                grad_qkv[rows, start : start + TILE] = grads[pair].astype(BF)


def qkv_back(depth, core, places, grad_qkv, hidden_v, middle_v, weight_v, gain1, bias1, grad_in, normed, vectors, mine, theirs):
    total, width = hidden_v.shape

    @pl.loop(0, total // ROWS)
    def _(m):
        rows = row_tile(m)
        back = jnp.zeros((ROWS, width), F32)
        for f in range(0, 3 * width, width):
            back = back + product(grad_qkv[rows, f : f + width], weight_v[:, f : f + width], NT)
        xhat, scale = normalized(hidden_v[rows, :].astype(F32))
        normed[rows, :] = (xhat * gain1[depth : depth + 1, :] + bias1[depth : depth + 1, :]).astype(BF)
        through, gain_sum, bias_sum = norm_back(back, xhat, scale, gain1[depth : depth + 1, :])
        grad_in[rows, :] = (middle_v[rows, :] + through).astype(BF)
        vectors[0:1, :] += gain_sum
        vectors[1:2, :] += bias_sum
        vectors[2:3, :] += jnp.sum(grad_qkv[rows, :width].astype(F32), axis=0, keepdims=True)
        vectors[3:4, :] += jnp.sum(grad_qkv[rows, 2 * width :].astype(F32), axis=0, keepdims=True)

    half = 3 * width // 2
    for part in range(2):
        which = core if part == 0 else 1 - core
        cols = pl.ds(pl.multiple_of(which * half, half), half)
        store_units((mine, theirs)[part], 0, product(normed[...], grad_qkv[:total, cols], TN), which, places)


def attention_load(depth, qkv, probs, grad_mixed, qkv_v, probs_v, mixed_v, sems):
    total = grad_mixed.shape[0]
    loads = [
        fetch(qkv.at[depth], qkv_v.at[pl.ds(0, total)], sems.at[0]),
        fetch(grad_mixed, mixed_v.at[pl.ds(0, total)], sems.at[1]),
        fetch(probs.at[depth], probs_v, sems.at[2]),
    ]
    qkv_v[total:, :] = jnp.zeros((qkv_v.shape[0] - total, qkv_v.shape[1]), BF)
    mixed_v[total:, :] = jnp.zeros((mixed_v.shape[0] - total, mixed_v.shape[1]), BF)
    return loads


def attention_back_kernel(
    depth, tokens, places, scalars, hidden, qkv, probs, grad_mixed, grad_middle, qkv_w, gain1, bias1, *rest,
):
    (mine, theirs, grad_in, vectors,
     hidden_v, middle_v, weight_v, normed, qkv_v, probs_v, mixed_v, grad_qkv, sems) = rest[tokens:]
    loads = attention_load(depth, qkv, probs, grad_mixed, qkv_v, probs_v, mixed_v, sems)
    later = [
        fetch(qkv_w.at[depth], weight_v, sems.at[3]),
        fetch(hidden.at[depth], hidden_v, sems.at[4]),
        fetch(grad_middle, middle_v, sems.at[5]),
    ]
    vectors[...] = jnp.zeros_like(vectors)
    for load in loads:
        load.wait()
    attention_backward(qkv_v, probs_v, mixed_v, grad_qkv, *placed(scalars, grad_in.shape[0]), grad_in.shape[1])
    for load in later:
        load.wait()
    qkv_back(
        depth, scalars[1], places, grad_qkv, hidden_v, middle_v, weight_v, gain1, bias1, grad_in, normed, vectors, mine,
        theirs,
    )


def part_loads(depth, part, parts, qkv, probs, grad_mixed, qkv_v, probs_v, mixed_v, sems):
    total, whole = grad_mixed.shape
    width = whole // parts
    pairs = probs_v.shape[0]
    inside = pl.ds(0, total)
    loads = [
        fetch(qkv.at[depth, :, pl.ds(k * whole + part * width, width)], qkv_v.at[inside, pl.ds(k * width, width)], sems.at[k])
        for k in range(3)
    ]
    loads.append(fetch(grad_mixed.at[:, pl.ds(part * width, width)], mixed_v.at[inside], sems.at[3]))
    loads.append(fetch(probs.at[depth, pl.ds(part * pairs, pairs)], probs_v, sems.at[4]))
    qkv_v[total:, :] = jnp.zeros((qkv_v.shape[0] - total, qkv_v.shape[1]), BF)
    mixed_v[total:, :] = jnp.zeros((mixed_v.shape[0] - total, mixed_v.shape[1]), BF)
    return loads


def attention_part_kernel(depth, part, parts, tokens, scalars, qkv, probs, grad_mixed, *rest):
    out, qkv_v, probs_v, mixed_v, grad_qkv, sems, out_sem = rest[tokens:]
    total, whole = grad_mixed.shape
    for load in part_loads(depth, part, parts, qkv, probs, grad_mixed, qkv_v, probs_v, mixed_v, sems):
        load.wait()
    attention_backward(qkv_v, probs_v, mixed_v, grad_qkv, *placed(scalars, total), whole // parts)
    fetch(grad_qkv.at[pl.ds(0, total)], out, out_sem).wait()


def table_kernel(
    depth, tokens, places, groups, scalars, qkv, probs, grad_mixed, grad_low, hidden, grad_middle, qkv_w, gain1, bias1,
    index, final_grads, feed1, wide1, attend1, feed0, wide0, *rest,
):
    (mine, theirs, frame_grad, grad_in, turned, vectors, stage, hidden_v, normed, grad_qkv, weight_v, middle_v,
     qkv_v, probs_v, mixed_v, sems, part_sems) = rest[tokens:]
    total, width = grad_in.shape
    half = width // 2
    first = part_loads(depth, 1, 2, qkv, probs, grad_mixed, qkv_v, probs_v, mixed_v, part_sems)
    inside = pl.ds(0, total)
    loads = [
        fetch(grad_low.at[:, pl.ds(k * half, half)], grad_qkv.at[inside, pl.ds(k * width, half)], sems.at[k])
        for k in range(3)
    ]
    loads.append(fetch(qkv_w.at[depth], weight_v, sems.at[3]))
    loads.append(fetch(hidden.at[depth], hidden_v, sems.at[4]))
    loads.append(fetch(grad_middle, middle_v, sems.at[5]))
    core = scalars[1]
    steps = frame_grad.shape[0]
    qkv_width = 3 * width // 2
    code_width = mine.shape[1] - qkv_width - TILE
    vectors[...] = jnp.zeros_like(vectors)
    for load in first:
        load.wait()
    attention_backward(qkv_v, probs_v, mixed_v, grad_qkv, *placed(scalars, total), half, width, half)
    for load in loads:
        load.wait()
    qkv_back(
        depth, core, places, grad_qkv, hidden_v, middle_v, weight_v, gain1, bias1, grad_in, normed, vectors, mine, theirs,
    )

    stage[...] = jnp.zeros_like(stage)
    for k, block in enumerate((feed0, vectors, feed1, attend1, final_grads)):
        stage[VECTORS + 8 * k : VECTORS + 8 * k + 8, :] = block[...]
    each = width // groups
    for k, wide in enumerate((wide0, wide1)):
        for group in range(groups):
            for c in range(4):
                start = group * 4 * each + c * each
                at = VECTORS + 40 + 8 * k + c
                stage[at : at + 1, group * each : group * each + each] = wide[0:1, start : start + each]

    turned[...] = grad_in[...].T
    for part in range(2):
        out = (mine, theirs)[part]
        which = core if part == 0 else 1 - core
        line = lax.broadcasted_iota(jnp.int32, (code_width, total), 0) + which * code_width
        hot = (line == index[0:1, :]).astype(F32).astype(BF)
        store_units(out, qkv_width, product(turned[...], hot, NT), which, places)
        line = lax.broadcasted_iota(jnp.int32, (TILE, total), 0) + which * TILE
        hot = ((line == index[1:2, :]) | (line == index[2:3, :])).astype(F32).astype(BF)
        small = product(turned[...], hot, NT) + stage[...].T * which.astype(F32)
        store_units(out, qkv_width + code_width, small, which, places)
    hot = (lax.broadcasted_iota(jnp.int32, (steps, total), 0) == index[3:4, :]).astype(F32).astype(BF)
    frame_grad[...] = product(hot, grad_in[...])


def output_kernel(where, scalars, *refs):
    count = 1 + max(chunk for chunk, _ in where.values())
    sources = refs[: 2 * count]
    (code, action, position, gain1, bias1, qkv, query, value, out, out_bias, gain2, bias2, up, up_bias, down, down_bias,
     final_gain, final_bias) = refs[2 * count : -1]
    square = refs[-1]
    rows, units = up.shape[1:]
    half = units // 2
    small = qkv.shape[2] // 2 + code.shape[1] // 2

    def emit(own):
        def part(name, core, across, start, size):
            chunk, at = where[name]
            lines = slice((across ^ (own >> 1)) * rows // 2, ((across ^ (own >> 1)) + 1) * rows // 2)
            return sources[2 * chunk + (core ^ (own & 1))][lines, at + start : at + start + size].astype(F32)

        def place(target, name, start):
            size = target.shape[-1] // 2
            for across in range(2):
                lines = slice(across * rows // 2, (across + 1) * rows // 2)
                for core in range(2):
                    target[lines, core * size : (core + 1) * size] = part(name, core, across, start, size)

        for depth in range(2):
            place(up.at[depth], ("feed", depth), 0)
            place(down.at[depth], ("feed", depth), half)
            place(out.at[depth], ("feed", depth), units)
            place(qkv.at[depth], ("attend", depth), 0)
        place(code, ("attend", 0), qkv.shape[2] // 2)
        square[...] = jnp.zeros_like(square)
        for across in range(2):
            lines = slice(across * rows // 2, (across + 1) * rows // 2)
            position[lines, :] = part(("attend", 0), 0, across, small, TILE)[:, : position.shape[1]]
            square[lines, :] = part(("attend", 0), 1, across, small, TILE)
        lines = square[...].T[:, :rows]
        action[...] = lines[: action.shape[0]]

        def line(k):
            return lines[VECTORS + k : VECTORS + k + 1]

        for depth in range(2):
            at = slice(depth, depth + 1)
            base = 16 * depth
            for k, target in enumerate((gain2, bias2, down_bias, out_bias)):
                target[at, :] = line(base + k)
            for k, target in enumerate((gain1, bias1, query, value)):
                target[at, :] = line(base + 8 + k)
            for c in range(4):
                up_bias[at, c * rows : (c + 1) * rows] = line(40 + 8 * depth + c)
        final_gain[...] = line(32)
        final_bias[...] = line(33)

    for own in range(4):
        pl.when(scalars[scalars.shape[0] - 1] == own)(partial(emit, own))


VMEM = pl.BlockSpec(memory_space=pltpu.VMEM)
ANY = pl.BlockSpec(memory_space=pl.ANY)
SMEM = pl.BlockSpec(memory_space=pltpu.SMEM)


def cost(flops, moved, others=0):
    return pl.CostEstimate(flops=int(8 * flops), bytes_accessed=int(moved), transcendentals=int(others))


def run_forward(places, scalars, actions, deltas, frames, codebook, action_table, position_table, layers, finals, cotangent):
    gain1, bias1, qkv_w, query_bias, value_bias, out_w, out_bias, gain2, bias2, up_w, up_bias, down_w, down_bias = layers
    width = codebook.shape[1]
    units = up_bias.shape[1]
    real = cotangent.shape[1]
    total = -(-real // ROWS) * ROWS
    reach = total + TILE // 2
    columns = units + width // 2
    shape = jax.ShapeDtypeStruct
    once = dict(pipeline_mode=pl.Buffered(1))
    whole = lambda a: pl.BlockSpec(a.shape, lambda i, s, n=a.ndim: (0,) * n, **once)
    mine = lambda a: pl.BlockSpec((1,) + a.shape[1:], lambda i, s: (s[0], 0, 0), **once)
    kept = (width // TILE, WINDOWS * 2 * TILE, TILE)
    outs = [
        (shape((real, width), F32), ANY),
        (shape((8, total), jnp.int32), None),
        (shape((8, width), F32), None), (shape((8, width), F32), None), (shape((8, units), F32), None),
        (shape((2, total, width), BF), ANY),
        (shape((2, total, 3 * width), BF), ANY),
        (shape((2,) + kept, BF), ANY),
        (shape((total, width), BF), ANY),
        (shape((total, width), F32), ANY),
        (shape((total, units), BF), ANY),
        (shape((total, units), BF), ANY),
        (shape((total, width), F32), ANY), (shape((total, width), BF), ANY),
        (shape((width, columns), BF), ANY), (shape((width, columns), BF), ANY),
    ]
    args = [
        (actions, mine(actions)), (deltas, mine(deltas)), (frames, mine(frames)),
        (codebook, None), (action_table, None), (position_table, None),
        (gain1, None), (bias1, None), (qkv_w, ANY), (query_bias, None), (value_bias, None), (out_w, ANY),
        (out_bias, None), (gain2, None), (bias2, None), (up_w, ANY), (up_bias, None), (down_w, ANY), (down_bias, None),
        (finals[0][None], None), (finals[1][None], None), (cotangent, mine(cotangent)),
    ]
    scratch = [
        pltpu.VMEM((2 * TILE, width), BF),
        pltpu.VMEM(qkv_w.shape, BF), pltpu.VMEM(out_w.shape, BF), pltpu.VMEM(up_w.shape, BF), pltpu.VMEM(down_w.shape, BF),
        pltpu.VMEM((3, total, width), BF), pltpu.VMEM((reach, 3 * width), BF), pltpu.VMEM(kept, BF),
        pltpu.VMEM((reach, width), BF), pltpu.VMEM((total, width), F32),
        pltpu.VMEM((total, units), BF), pltpu.VMEM((total, units), BF), pltpu.VMEM((2 * TILE, TILE), F32),
        pltpu.VMEM((total, width), F32), pltpu.VMEM((total, width), F32),
        pltpu.VMEM((total, width), BF), pltpu.VMEM((total, width), BF), pltpu.VMEM((total, width), BF),
        pltpu.VMEM((total, width), BF), pltpu.VMEM((total, units), BF),
        pltpu.VMEM((width, columns), BF), pltpu.VMEM((width, columns), BF),
        pltpu.SemaphoreType.DMA((2, 4)), pltpu.SemaphoreType.DMA((16,)), pltpu.SemaphoreType.DMA((2, total // ROWS)),
        pltpu.SemaphoreType.DMA, pltpu.SemaphoreType.DMA((6,)),
    ]
    return pl.pallas_call(
        partial(forward_kernel, places),
        out_shape=[o for o, _ in outs],
        grid_spec=pltpu.PrefetchScalarGridSpec(
            num_scalar_prefetch=1,
            grid=(1,),
            in_specs=[spec or whole(a) for a, spec in args],
            out_specs=[spec or whole(o) for o, spec in outs],
            scratch_shapes=scratch,
        ),
        compiler_params=pltpu.CompilerParams(vmem_limit_bytes=62 << 20),
        cost_estimate=cost(24e9, 50e6, 4e6),
        name="forward",
    )(scalars, *[a for a, _ in args])


def run_mlp_data(depth, grad, saved, layers, after):
    hidden, qkv, probs, mixed, middle, act, slope = saved
    gain1, bias1, qkv_w, query_bias, value_bias, out_w, out_bias, gain2, bias2, up_w, up_bias, down_w, down_bias = layers
    total, width = grad.shape
    units = up_bias.shape[1]
    shape = jax.ShapeDtypeStruct
    return pl.pallas_call(
        partial(mlp_data_kernel, depth, len(after)),
        out_shape=[
            shape((total, width), F32), shape((total, width), BF), shape((8, width), F32), shape((8, units), F32),
            shape((total, width), BF), shape((total, units), BF), shape((total, width), BF),
        ],
        in_specs=[VMEM] + [ANY] * 5 + [VMEM] * 2 + [ANY] * len(after),
        out_specs=[VMEM] * 7,
        scratch_shapes=[
            pltpu.VMEM((total, units), BF),
            pltpu.VMEM((width, units), BF), pltpu.VMEM((units, width), BF), pltpu.VMEM((width, width), BF),
            pltpu.VMEM((total, width), F32),
            pltpu.SemaphoreType.DMA((4,)), pltpu.SemaphoreType.DMA((total // ROWS,)),
        ],
        compiler_params=pltpu.CompilerParams(vmem_limit_bytes=40 << 20),
        cost_estimate=cost(10e9, 16e6),
        name="mlp_data",
    )(grad, middle, slope, up_w, down_w, out_w, gain2, bias2, *after)


def run_mlp_weight(depth, places, scalars, grad, saved, normed, grad_pre, rounded, after):
    hidden, qkv, probs, mixed, middle, act, slope = saved
    total, width = grad.shape
    units = grad_pre.shape[1]
    shape = jax.ShapeDtypeStruct
    return pl.pallas_call(
        partial(mlp_weight_kernel, depth, len(after), places),
        out_shape=[shape((width, units + width // 2), BF), shape((width, units + width // 2), BF)],
        in_specs=[SMEM, VMEM] + [ANY] * 5 + [ANY] * len(after),
        out_specs=[VMEM] * 2,
        scratch_shapes=[
            pltpu.VMEM((total, units), BF), pltpu.VMEM((total, width), BF), pltpu.VMEM((total, width), BF),
            pltpu.VMEM((total, units), BF), pltpu.VMEM((total, width), BF),
            pltpu.SemaphoreType.DMA((5,)),
        ],
        compiler_params=pltpu.CompilerParams(vmem_limit_bytes=40 << 20),
        cost_estimate=cost(8e9, 16e6),
        name="mlp_weight",
    )(scalars, grad, act, mixed, normed, grad_pre, rounded, *after)


def window_scratch(total, width, probs):
    reach = total + TILE // 2
    return [
        pltpu.VMEM((reach, 3 * width), BF), pltpu.VMEM(probs.shape[1:], BF),
        pltpu.VMEM((reach, width), BF), pltpu.VMEM((reach, 3 * width), BF),
    ]


def run_attention_back(depth, places, scalars, grad_mixed, grad_middle, saved, layers, after):
    hidden, qkv, probs, mixed, middle, act, slope = saved
    gain1, bias1, qkv_w = layers[:3]
    total, width = grad_mixed.shape
    shape = jax.ShapeDtypeStruct
    return pl.pallas_call(
        partial(attention_back_kernel, depth, len(after), places),
        out_shape=[
            shape((width, 3 * width // 2), BF), shape((width, 3 * width // 2), BF),
            shape((total, width), BF), shape((8, width), F32),
        ],
        in_specs=[SMEM] + [ANY] * 6 + [VMEM] * 2 + [ANY] * len(after),
        out_specs=[VMEM] * 4,
        scratch_shapes=[
            pltpu.VMEM((total, width), BF), pltpu.VMEM((total, width), F32), pltpu.VMEM(qkv_w.shape[1:], BF),
            pltpu.VMEM((total, width), BF), *window_scratch(total, width, probs),
            pltpu.SemaphoreType.DMA((6,)),
        ],
        compiler_params=pltpu.CompilerParams(vmem_limit_bytes=50 << 20),
        cost_estimate=cost(16e9, 24e6),
        name="attention_back",
    )(scalars, hidden, qkv, probs, grad_mixed, grad_middle, qkv_w, gain1, bias1, *after)


def run_attention_part(depth, part, parts, scalars, grad_mixed, saved, after):
    hidden, qkv, probs, mixed, middle, act, slope = saved
    total, width = grad_mixed.shape
    width = width // parts
    reach = total + TILE // 2
    return pl.pallas_call(
        partial(attention_part_kernel, depth, part, parts, len(after)),
        out_shape=jax.ShapeDtypeStruct((total, 3 * width), BF),
        in_specs=[SMEM] + [ANY] * 3 + [ANY] * len(after),
        out_specs=ANY,
        scratch_shapes=[
            pltpu.VMEM((reach, 3 * width), BF), pltpu.VMEM((width // TILE,) + probs.shape[2:], BF),
            pltpu.VMEM((reach, width), BF), pltpu.VMEM((reach, 3 * width), BF),
            pltpu.SemaphoreType.DMA((5,)), pltpu.SemaphoreType.DMA,
        ],
        compiler_params=pltpu.CompilerParams(vmem_limit_bytes=40 << 20),
        cost_estimate=cost(8e9, 8e6),
        name="attention_part",
    )(scalars, qkv, probs, grad_mixed, *after)


def run_table(depth, places, scalars, grad_mixed, grad_low, grad_middle, saved, layers, index, vectors, codes, steps, groups, after):
    hidden, qkv, probs, mixed, middle, act, slope = saved
    gain1, bias1, qkv_w = layers[:3]
    total, width = grad_middle.shape
    reach = total + TILE // 2
    columns = 3 * width // 2 + codes // 2 + TILE
    shape = jax.ShapeDtypeStruct
    return pl.pallas_call(
        partial(table_kernel, depth, len(after), places, groups),
        out_shape=[shape((width, columns), BF), shape((width, columns), BF), shape((steps, width), F32)],
        in_specs=[SMEM] + [ANY] * 7 + [VMEM] * 2 + [VMEM] * 7 + [ANY] * len(after),
        out_specs=[VMEM] * 3,
        scratch_shapes=[
            pltpu.VMEM((total, width), BF), pltpu.VMEM((width, total), BF), pltpu.VMEM((8, width), F32),
            pltpu.VMEM((TILE, width), F32), pltpu.VMEM((total, width), BF), pltpu.VMEM((total, width), BF),
            pltpu.VMEM((reach, 3 * width), BF), pltpu.VMEM(qkv_w.shape[1:], BF), pltpu.VMEM((total, width), F32),
            pltpu.VMEM((reach, 3 * width // 2), BF), pltpu.VMEM((probs.shape[1] // 2,) + probs.shape[2:], BF),
            pltpu.VMEM((reach, width // 2), BF),
            pltpu.SemaphoreType.DMA((6,)), pltpu.SemaphoreType.DMA((5,)),
        ],
        compiler_params=pltpu.CompilerParams(vmem_limit_bytes=40 << 20),
        cost_estimate=cost(12e9, 12e6),
        name="tables",
    )(scalars, qkv, probs, grad_mixed, grad_low, hidden, grad_middle, qkv_w, gain1, bias1, index, *vectors, *after)


def run_output(where, scalars, sources, width, units, codes, actions, positions):
    rows = sources[0].shape[0]
    wide, line = (2, rows), (1, rows)
    shapes = [
        (rows, codes), (actions, rows), (rows, positions), wide, wide, (2, rows, 3 * width), wide, wide, (2, rows, width),
        wide, wide, wide, (2, rows, units), (2, 4 * rows), (2, rows, units), wide, line, line,
    ]
    return pl.pallas_call(
        partial(output_kernel, where),
        out_shape=[jax.ShapeDtypeStruct(s, F32) for s in shapes],
        in_specs=[SMEM] + [VMEM] * len(sources),
        out_specs=[VMEM] * len(shapes),
        scratch_shapes=[pltpu.VMEM((TILE, TILE), F32)],
        compiler_params=pltpu.CompilerParams(vmem_limit_bytes=30 << 20),
        cost_estimate=cost(1e6, 6e6),
        name="outputs",
    )(scalars, *sources)


def meet(array, axis, by):
    size = lax.axis_size(axis)
    return lax.ppermute(array, axis, [(i, i ^ by) for i in range(size)])


def swap(array, axis, bit):
    return meet(array, axis, 1 << bit)


def bits_of(axis):
    return lax.axis_size(axis).bit_length() - 1


def own_bit(axis, bit):
    return (lax.axis_index(axis) >> bit) & 1


def take(array, dim, which):
    return lax.dynamic_index_in_dim(array, which, dim, keepdims=False)


def total_of(terms):
    return sum(term.astype(F32) for term in terms)


def settled(array):
    return lax.optimization_barrier(array.astype(BF))


def tied(array, token):
    return lax.optimization_barrier((array, token))[0]


def unit_places(count):
    first, second = [], []
    for unit in range(2 << count):
        bits = [(unit >> (1 + bit)) & 1 for bit in range(count)]
        for order, places in ((bits + [unit & 1], first), ([unit & 1] + bits, second)):
            place = 0
            for bit in order:
                place = 2 * place + bit
            places.append(place)
    return first, second


def reordered(array, which, count):
    rows, columns = array.shape
    ways = array.reshape((2,) * (count + 1) + (rows >> (count + 1), columns))
    dims = list(range(count - 1, -1, -1))
    first = ways.transpose(dims + [count, count + 1, count + 2])
    second = ways.transpose([count] + dims + [count + 1, count + 2])
    return jnp.where(which == 0, first, second).reshape(rows, columns)


class Chunk:
    def __init__(self, places):
        self.count = bits_of("dp")
        self.places = places
        self.pieces = []
        self.terms = []
        self.core = own_bit("section", 0)

    def add(self, mine, theirs):
        if self.places is None:
            mine, theirs = reordered(mine, self.core, self.count), reordered(theirs, 1 - self.core, self.count)
        self.pieces.append([mine, swap(theirs, "section", 0)])

    def hold(self, token):
        if self.terms:
            self.terms[-1] = tied(self.terms[-1], token)
        else:
            for piece in self.pieces:
                piece[1] = tied(piece[1], token)

    def step(self):
        if not self.terms:
            self.left = self.pieces[0][0].shape[0]
        k = len(self.terms)
        bits = [own_bit("dp", bit) for bit in range(self.count)]
        across = own_bit("section", 1)
        own = jnp.where(self.core == 0, (bits + [across])[k], ([across] + bits)[k])
        half = self.left // 2
        cut = lambda t, which: lax.dynamic_slice_in_dim(t, which * half, half, 0)
        if not self.terms:
            self.parts = [[[mine, arrived] for mine, arrived in self.pieces]]
        parts = self.parts[-1]
        sum_of = jnp.concatenate([total_of([cut(t, 1 - own) for t in part]) for part in parts], axis=1)
        for term in self.terms:
            sum_of = sum_of + cut(term, 1 - own).astype(F32)
        self.sent = settled(sum_of)
        sections = lax.axis_size("section")
        pairs = []
        for source in range(lax.axis_size("dp") * sections):
            at = k if source & 1 == 0 else (k - 1) % (self.count + 1)
            bit = sections << at if at < self.count else 2
            pairs.append((source, source ^ bit))
        self.parts = [[[cut(t, own) for t in part] for part in parts]]
        self.terms = [cut(t, own) for t in self.terms] + [lax.ppermute(self.sent, ("dp", "section"), pairs)]
        self.left = half
        return self

    def across(self):
        total = jnp.concatenate([total_of(part) for part in self.parts[-1]], axis=1)
        for term in self.terms:
            total = total + term.astype(F32)
        self.sent = settled(total)
        other = swap(self.sent, "section", 1)
        self.terms = [self.sent, other]

    def finish(self):
        rows = settled(jnp.concatenate(self.terms))
        arrived = swap(rows, "section", 0)
        return [rows, arrived]


def local(
    frames, actions, deltas, kinds, codebook, action_table, position_table, norm1_gain, norm1_bias, qkv_weight,
    query_bias, value_bias, out_weight, out_bias, norm2_gain, norm2_bias, up_weight, up_bias, down_weight, down_bias,
    final_gain, final_bias, cotangent,
):
    micro, steps, width = frames.shape
    units = up_weight.shape[2]
    codes = codebook.shape[0]
    slot = lax.axis_index("section") * micro // lax.axis_size("section")
    layers = (
        norm1_gain, norm1_bias, qkv_weight, query_bias, value_bias, out_weight, out_bias, norm2_gain, norm2_bias,
        up_weight, up_bias, down_weight, down_bias,
    )
    section = lax.axis_index("section")
    scalars = jnp.concatenate([jnp.stack([slot, section & 1]), kinds, section[None]]).astype(jnp.int32)
    groups = lax.axis_size("dp")
    count = bits_of("dp")
    places = unit_places(count) if width >> (count + 1) >= 16 else None
    chunk1, chunk2, chunk3 = Chunk(places), Chunk(places), Chunk(places)
    activations, index, final_grads, feed1, wide1, *saved, middle, mixed, mine, theirs = run_forward(
        places, scalars, actions[:, None], deltas.transpose(0, 2, 1), frames, codebook, action_table, position_table,
        layers, (final_gain, final_bias), cotangent,
    )
    chunk1.add(mine, theirs)
    mine, theirs, grad, attend1 = run_attention_back(1, places, scalars, mixed, middle, saved, layers, [])
    chunk1.hold(attend1)
    chunk2.add(mine, theirs)
    chunk1.step()
    middle, mixed, feed0, wide0, normed, grad_pre, rounded = run_mlp_data(0, grad, saved, layers, [chunk1.sent])
    chunk1.hold(normed)
    chunk1.step()
    mine, theirs = run_mlp_weight(0, places, scalars, grad, saved, normed, grad_pre, rounded, [chunk1.sent])
    chunk1.hold(theirs)
    chunk2.hold(theirs)
    chunk2.add(mine, theirs)
    chunk1.step()
    grad_low = run_attention_part(0, 0, 2, scalars, mixed, saved, [chunk1.sent])
    chunk1.hold(grad_low)
    chunk2.hold(grad_low)
    chunk2.step()
    chunk1.step()
    vectors = (final_grads, feed1, wide1, attend1, feed0, wide0)
    mine, theirs, frame_grad = run_table(
        0, places, scalars, mixed, grad_low, middle, saved, layers, index, vectors, codes, steps, groups,
        [chunk2.sent, chunk1.sent],
    )
    chunk3.add(mine, theirs)
    chunk2.hold(frame_grad)
    chunk1.hold(chunk2.terms[-1])
    chunk2.step()
    chunk3.hold(chunk2.sent)
    chunk3.step()
    chunk2.hold(chunk3.sent)
    chunk1.hold(chunk3.sent)
    for _ in range(3, count):
        chunk1.step()
    chunk1.across()
    for k in range(2, count + 3):
        if k <= count:
            chunk2.step()
        elif k == count + 1:
            chunk2.across()
        else:
            sources += chunk2.finish()
        chunk3.hold(chunk2.sent)
        if k == 2:
            chunk3.hold(chunk1.terms[-1])
            sources = chunk1.finish()
        if k <= count + 1:
            chunk3.step()
            chunk2.hold(chunk3.sent)
        else:
            chunk3.across()
    sources += chunk3.finish()
    split = 3 * width // 2
    where = {("feed", 1): (0, 0), ("attend", 1): (1, 0), ("feed", 0): (1, split), ("attend", 0): (2, 0)}
    (code, action, position, gain1, bias1, qkv, query, value, out, out_b, gain2, bias2, up, up_b, down, down_b, last_gain,
     last_bias) = run_output(
        where, scalars, sources, width, units, codes, action_table.shape[0], position_table.shape[0]
    )
    return (
        activations[None], frame_grad[None], code.T, action, position.T, gain1, bias1, qkv, query, value, out, out_b,
        gain2, bias2, up, up_b, down.transpose(0, 2, 1), down_b, last_gain[0], last_bias[0],
    )


def solution(mesh):
    rows, one = P("dp", None, None), P(None, "dp")
    weight = P(None, "dp", None)
    both = P(("dp", "section"), None, None)
    return jax.shard_map(
        local,
        mesh=mesh,
        in_specs=(rows, P("dp", None), rows, P("dp")) + (P(),) * 18 + (rows,),
        out_specs=(
            both, both, one, one, one, one, one, weight, one, one, weight, one, one, one, weight, one,
            P(None, None, "dp"), one, P("dp"), P("dp"),
        ),
        check_vma=False,
    )
```

```python
from functools import partial

import jax
import jax.numpy as jnp
from jax import lax
from jax.experimental import pallas as pl
from jax.experimental.pallas import tpu as pltpu
from jax.sharding import PartitionSpec as P

HEADS = 8
SHORT_STEPS = 8
LONG_STEPS = 21
EPSILON = 1e-05
MASKED = -1e30
TILE = 128
ROWS = 512
CHUNK = 512
STRIP = 256
VECTORS = 32
WINDOWS = 12
PER = 2
BF = jnp.bfloat16
F32 = jnp.float32

NN = (((1,), (0,)), ((), ()))
NT = (((1,), (1,)), ((), ()))
TN = (((0,), (0,)), ((), ()))


def product(left, right, form=NN):
    return lax.dot_general(left, right, form, preferred_element_type=F32)


def normalized(x):
    center = x - jnp.mean(x, axis=-1, keepdims=True)
    spread = jnp.mean(center * center, axis=-1, keepdims=True)
    scale = lax.rsqrt(spread + EPSILON)
    return center * scale, scale


def norm_back(grad, xhat, scale, gain):
    inner = grad * gain
    first = jnp.mean(inner, axis=-1, keepdims=True)
    second = jnp.mean(inner * xhat, axis=-1, keepdims=True)
    back = (inner - first - xhat * second) * scale
    return back, jnp.sum(grad * xhat, axis=0, keepdims=True), jnp.sum(grad, axis=0, keepdims=True)


def gelu_pair(u):
    cdf = 0.5 + 0.5 * lax.erf(u * 0.7071067811865476)
    e = jnp.exp2(u * u * (-0.5 * 1.4426950408889634))
    return u * cdf, cdf + u * (e * 0.3989422804014327)


def row_tile(m):
    return pl.ds(pl.multiple_of(m * ROWS, ROWS), ROWS)


def lane_halves():
    lane = lax.broadcasted_iota(jnp.int32, (1, TILE), 1)
    low = (lane < TILE // 2).astype(F32)
    return low.astype(BF), (1.0 - low).astype(BF)


def both_heads(x, low, high):
    return jnp.concatenate([x * low, x * high], axis=0)


def side_by_side(x):
    return jnp.concatenate([x[:TILE], x[TILE:]], axis=1)


def write_mask(mask, stride):
    row = lax.broadcasted_iota(jnp.int32, (2 * TILE, TILE), 0)
    row = jnp.where(row >= TILE, row - TILE, row).astype(F32) + 0.5
    col = lax.broadcasted_iota(jnp.int32, (2 * TILE, TILE), 1).astype(F32) + 0.5
    step = jnp.floor(col * (1.0 / 6.0)) <= jnp.floor(row * (1.0 / 6.0))
    member = jnp.floor(col * (1.0 / 48.0)) == jnp.floor(row * (1.0 / 48.0))
    long = jnp.where(step, 0.0, MASKED)
    short = jnp.where(member, long, MASKED)
    mask[...] = jnp.where(stride == TILE, long, short)


def placed(scalars, total):
    long = scalars[2 + scalars[0]] == 1
    return jnp.where(long, TILE, 2 * SHORT_STEPS * 6), jnp.where(long, total // TILE, WINDOWS)


def fetch(source, target, sem):
    copy = pltpu.make_async_copy(source, target, sem)
    copy.start()
    return copy


def attention_forward(qkv, probs, mixed, mask, stride, windows, width):
    low, high = lane_halves()

    @pl.loop(0, windows // PER)
    def _(step):
        units = [(n, pair) for n in range(PER) for pair in range(width // TILE)]
        starts = [pl.multiple_of((PER * step + n) * stride, 32) for n in range(PER)]
        rows = [pl.ds(start, TILE) for start in starts]
        cut = lambda k, n, pair: qkv[rows[n], k * width + pair * TILE : k * width + (pair + 1) * TILE]
        scores = [product(both_heads(cut(0, n, pair), low, high), cut(1, n, pair), NT) + mask[...] for n, pair in units]
        shifted = [jnp.exp(s - jnp.max(s, axis=-1, keepdims=True)) for s in scores]
        p = [(s * (1.0 / jnp.sum(s, axis=-1, keepdims=True))).astype(BF) for s in shifted]
        for (n, pair), value in zip(units, p):
            kept = pl.ds(pl.multiple_of((PER * step + n) * 2 * TILE, 2 * TILE), 2 * TILE)
            probs[pair, kept, :] = value
        out = [product(side_by_side(value), both_heads(cut(2, n, pair), low, high)) for (n, pair), value in zip(units, p)]
        for (n, pair), value in zip(units, out):
            mixed[rows[n], pair * TILE : (pair + 1) * TILE] = value.astype(BF)


def build_index(index, actions, deltas, long):
    steps = actions.shape[-1]
    total = index.shape[1]
    step = lax.broadcasted_iota(jnp.int32, (steps, total), 0).astype(F32)
    start = step * 6.0 + jnp.where(long, 2.0, 0.0) * jnp.floor((step + 0.5) * (1.0 / LONG_STEPS))
    slot = lax.broadcasted_iota(jnp.int32, (steps, total), 1).astype(F32) - start
    line = lax.broadcasted_iota(jnp.int32, (8, steps), 0)

    def rows(**values):
        out = jnp.zeros((8, steps), F32)
        for name, value in values.items():
            out = jnp.where(line == int(name[1:]), value, out)
        return out.astype(BF)

    def spread(value, j):
        return product(value, (slot == float(j)).astype(F32).astype(BF))

    count = lax.broadcasted_iota(jnp.int32, (8, steps), 1).astype(F32)
    found = spread(rows(r5=count, r6=1.0), 0) + spread(rows(r3=actions[0].astype(F32), r4=1.0), 1)
    for j in range(deltas.shape[1]):
        code = deltas[0, j : j + 1, :].astype(F32)
        high = jnp.floor(code * (1.0 / 32.0))
        found = found + spread(rows(r0=high, r1=code - 32.0 * high, r2=1.0), 2 + j)
    found = found.astype(jnp.int32)
    none = jnp.full((1, total), -1, jnp.int32)
    row = lax.broadcasted_iota(jnp.int32, (1, total), 1)
    real = row.astype(F32) + 0.5
    apart = row - TILE * jnp.floor(real * (1.0 / TILE)).astype(jnp.int32)
    apart = jnp.where(apart < LONG_STEPS * 6, apart, none)
    close = row - SHORT_STEPS * 6 * jnp.floor(real * (1.0 / (SHORT_STEPS * 6))).astype(jnp.int32)
    close = jnp.where(row < steps * 6, close, none)
    index[0:1, :] = jnp.where(found[2:3] == 1, found[0:1] * 32 + found[1:2], none)
    index[1:2, :] = jnp.where(long, apart, close)
    index[2:3, :] = jnp.where(found[4:5] == 1, found[3:4] + TILE, none)
    index[3:4, :] = jnp.where(found[6:7] == 1, found[5:6], none)
    index[4:8, :] = jnp.full((4, total), -1, jnp.int32)


def forward_kernel(
    places, scalars, actions, deltas, frames, codebook, action_table, position_table,
    gain1, bias1, qkv_w, query_bias, value_bias, out_w, out_bias, gain2, bias2,
    up_w, up_bias, down_w, down_bias, final_gain, final_bias, cotangent,
    activations, index, final_grads, vectors, wide,
    hidden_out, qkv_out, probs_out, mixed_out, middle_out, act_out, slope_out,
    grad_middle_out, grad_mixed_out, mine_out, theirs_out,
    table, qkv_v, out_v, up_v, down_v, hidden, qkv, probs, mixed, middle, act, slope, mask, result, cot,
    grad, grad_mixed, normed_two, rounded, grad_pre, mine, theirs,
    weight_sem, save_sem, tile_sem, result_sem, part_sem,
):
    core = scalars[1]
    width = hidden.shape[-1]
    total = hidden.shape[1]
    stride, windows = placed(scalars, total)
    hidden_units = up_bias.shape[1]
    tiles = total // ROWS
    loads = []
    for depth in range(2):
        loads.append([
            fetch(qkv_w.at[depth], qkv_v.at[depth], weight_sem.at[depth, 0]),
            fetch(out_w.at[depth], out_v.at[depth], weight_sem.at[depth, 1]),
            fetch(up_w.at[depth], up_v.at[depth], weight_sem.at[depth, 2]),
            fetch(down_w.at[depth], down_v.at[depth], weight_sem.at[depth, 3]),
        ])
    write_mask(mask, stride)
    build_index(index, actions, deltas, stride == TILE)
    positions = position_table.shape[0]
    action_count = action_table.shape[0]
    table[...] = jnp.zeros_like(table)
    table[:positions] = position_table[...]
    table[TILE : TILE + action_count] = action_table[...]
    qkv[total:, :] = jnp.zeros((qkv.shape[0] - total, qkv.shape[1]), BF)

    codes = codebook.shape[0]
    steps = frames.shape[1]

    @pl.loop(0, tiles)
    def _(m):
        rows = row_tile(m)
        code_hot = (lax.broadcasted_iota(jnp.int32, (codes, ROWS), 0) == index[0:1, rows]).astype(F32).astype(BF)
        line = lax.broadcasted_iota(jnp.int32, (2 * TILE, ROWS), 0)
        small_hot = ((line == index[1:2, rows]) | (line == index[2:3, rows])).astype(F32).astype(BF)
        frame_hot = (lax.broadcasted_iota(jnp.int32, (steps, ROWS), 0) == index[3:4, rows]).astype(F32).astype(BF)
        value = product(code_hot, codebook[...], TN) + product(small_hot, table[...], TN)
        value = value + product(frame_hot, frames[0], TN)
        hidden[0, rows, :] = value.astype(BF)

    def tile_copies(m):
        rows = row_tile(m)
        return (
            pltpu.make_async_copy(act.at[rows], act_out.at[rows], tile_sem.at[0, m]),
            pltpu.make_async_copy(slope.at[rows], slope_out.at[rows], tile_sem.at[1, m]),
        )

    saves = {}
    started = []

    def save(name, source, target):
        saves[name] = fetch(source, target, save_sem.at[len(started)])
        started.append(name)

    inside = pl.ds(0, total)
    for depth in range(2):
        save(("hidden", depth), hidden.at[depth], hidden_out.at[depth])
        loads[depth][0].wait()
        if depth:
            saves.pop(("qkv", 0)).wait()

        def normed_tile(m):
            xhat, _ = normalized(hidden[depth, m * ROWS : (m + 1) * ROWS, :].astype(F32))
            return (xhat * gain1[depth : depth + 1, :] + bias1[depth : depth + 1, :]).astype(BF)

        ready = normed_tile(0)
        for m in range(tiles):
            rows = slice(m * ROWS, (m + 1) * ROWS)
            normed = ready
            if m + 1 < tiles:
                ready = normed_tile(m + 1)
            q = product(normed, qkv_v[depth, :, :width]) + query_bias[depth : depth + 1, :]
            k = product(normed, qkv_v[depth, :, width : 2 * width])
            v = product(normed, qkv_v[depth, :, 2 * width :]) + value_bias[depth : depth + 1, :]
            qkv[rows, :width] = (q.astype(BF).astype(F32) * 0.125).astype(BF)
            qkv[rows, width : 2 * width] = k.astype(BF)
            qkv[rows, 2 * width :] = v.astype(BF)

        save(("qkv", depth), qkv.at[inside], qkv_out.at[depth])
        if depth:
            saves.pop(("probs", 0)).wait()
            saves.pop(("mixed", 0)).wait()
        attention_forward(qkv, probs, mixed, mask, stride, windows, width)
        save(("probs", depth), probs, probs_out.at[depth])
        if not depth:
            save(("mixed", depth), mixed.at[inside], mixed_out)
        for load in loads[depth][1:]:
            load.wait()
        if depth:
            saves.pop(("middle", 0)).wait()

        @pl.loop(0, tiles)
        def _(m):
            rows = row_tile(m)
            mid = hidden[depth, rows, :].astype(F32) + (
                product(mixed[rows, :], out_v[depth]) + out_bias[depth : depth + 1, :]
            )
            middle[rows, :] = mid
            xhat, _ = normalized(mid)
            normed = (xhat * gain2[depth : depth + 1, :] + bias2[depth : depth + 1, :]).astype(BF)
            if depth:
                normed_two[rows, :] = normed
                for copy in tile_copies(m):
                    copy.wait()
            parts = list(range(0, hidden_units, STRIP))
            up = lambda f: product(normed, up_v[depth, :, f : f + STRIP]) + up_bias[depth : depth + 1, f : f + STRIP]
            u = up(0)
            added = jnp.zeros((ROWS, width), F32)
            previous = None
            for f in parts:
                following = up(f + STRIP) if f + STRIP < hidden_units else None
                if previous is not None:
                    added = added + product(previous, down_v[depth, f - STRIP : f, :])
                z, d = gelu_pair(u)
                previous = z.astype(BF)
                act[rows, f : f + STRIP] = previous
                slope[rows, f : f + STRIP] = d.astype(BF)
                u = following
            added = added + product(previous, down_v[depth, hidden_units - STRIP :, :])
            hidden[depth + 1, rows, :] = (mid + (added + down_bias[depth : depth + 1, :])).astype(BF)
            if not depth:
                for copy in tile_copies(m):
                    copy.start()

        if not depth:
            save(("middle", depth), middle, middle_out)

    real = cotangent.shape[1]
    cot[:real] = cotangent[0].astype(F32)
    cot[real:] = jnp.zeros((cot.shape[0] - real, width), F32)
    final_grads[...] = jnp.zeros_like(final_grads)

    def finish(step):
        for g in range(total // TILE):
            xhat, scale = normalized(hidden[2, g * TILE : (g + 1) * TILE, :].astype(F32))
            result[g * step : g * step + TILE, :] = xhat * final_gain[...] + final_bias[...]
            arriving = cot[g * step : g * step + TILE, :]
            if step < TILE:
                line = lax.broadcasted_iota(jnp.int32, (TILE, 1), 0)
                arriving = jnp.where(line < step, arriving, 0.0)
            back, gain_sum, bias_sum = norm_back(arriving, xhat, scale, final_gain[...])
            grad[g * TILE : (g + 1) * TILE, :] = back.astype(BF)
            final_grads[0:1, :] += gain_sum
            final_grads[1:2, :] += bias_sum

    @pl.when(stride == TILE)
    def _():
        finish(LONG_STEPS * 6)

    @pl.when(stride != TILE)
    def _():
        finish(TILE)

    saves["out"] = fetch(result.at[pl.ds(0, real)], activations, result_sem)
    grad_middle = cot
    mlp_data_back(
        1, None, grad, grad_middle, grad_mixed, vectors, wide, slope, up_v.at[1], down_v.at[1], out_v.at[1], middle,
        normed_two, grad_pre, rounded, gain2, bias2,
    )
    save("grad_middle", grad_middle, grad_middle_out)
    save("grad_mixed", grad_mixed, grad_mixed_out)
    saves["parts"] = mlp_weight_back(
        core, places, (), mine, theirs, grad, act, mixed.at[inside], normed_two, grad_pre, rounded,
        (mine_out, theirs_out, part_sem),
    )
    for copy in saves.values():
        copy.wait()


def mlp_data_back(depth, loads, grad, grad_middle, grad_mixed, vectors, wide, slope_v, up_v, down_v, out_v, middle_v, normed, grad_pre, rounded, gain2, bias2):
    total, width = grad.shape
    hidden_units = grad_pre.shape[1]
    vectors[...] = jnp.zeros_like(vectors)
    wide[...] = jnp.zeros_like(wide)
    if loads:
        down, slopes, up, mid, out = loads
        down.wait()
    for m in range(total // ROWS):
        rows = slice(m * ROWS, (m + 1) * ROWS)
        g = grad[rows, :]
        if loads:
            slopes[m].wait()
        if loads and m == 0:
            up.wait()
        back = jnp.zeros((ROWS, width), F32)
        ahead = product(g, down_v[:CHUNK, :], NT)
        for f in range(0, hidden_units, CHUNK):
            grad_act = ahead
            if f + CHUNK < hidden_units:
                ahead = product(g, down_v[f + CHUNK : f + 2 * CHUNK, :], NT)
            pre = (grad_act * slope_v[rows, f : f + CHUNK].astype(F32)).astype(BF)
            grad_pre[rows, f : f + CHUNK] = pre
            wide[0:1, f : f + CHUNK] += jnp.sum(pre.astype(F32), axis=0, keepdims=True)
            back = back + product(pre, up_v[:, f : f + CHUNK], NT)
        if loads and m == 0:
            mid.wait()
            out.wait()
        xhat, scale = normalized(middle_v[rows, :])
        if loads:
            normed[rows, :] = (xhat * gain2[depth : depth + 1, :] + bias2[depth : depth + 1, :]).astype(BF)
        through, gain_sum, bias_sum = norm_back(back, xhat, scale, gain2[depth : depth + 1, :])
        g = g.astype(F32)
        total_grad = g + through
        grad_middle[rows, :] = total_grad
        r = total_grad.astype(BF)
        rounded[rows, :] = r
        vectors[0:1, :] += gain_sum
        vectors[1:2, :] += bias_sum
        vectors[2:3, :] += jnp.sum(g, axis=0, keepdims=True)
        vectors[3:4, :] += jnp.sum(r.astype(F32), axis=0, keepdims=True)
        grad_mixed[rows, :] = product(r, out_v[...], NT).astype(BF)


def store_units(out, at, value, which, places):
    width = value.shape[1]
    if places is None:
        out[:, at : at + width] = value.astype(BF)
        return
    first, second = places
    rows = value.shape[0] // len(first)
    for unit in range(len(first)):
        place = first[unit] + which * (second[unit] - first[unit])
        out[pl.ds(pl.multiple_of(place * rows, rows), rows), at : at + width] = value[unit * rows : (unit + 1) * rows].astype(BF)


class Several:
    def __init__(self, copies):
        self.copies = copies

    def wait(self):
        for copy in self.copies:
            copy.wait()


def mlp_weight_back(core, places, loads, mine, theirs, grad, act_v, mixed_v, normed, grad_pre, rounded, outside=None):
    width = grad.shape[1]
    half = grad_pre.shape[1] // 2
    copies = []

    def made(part, at, size):
        if outside:
            cols = pl.ds(at, size)
            copies.append(fetch((mine, theirs)[part].at[:, cols], outside[part].at[:, cols], outside[2].at[len(copies)]))

    for part in range(2):
        out = (mine, theirs)[part]
        which = core if part == 0 else 1 - core
        for at in range(0, half, CHUNK):
            cols = pl.ds(pl.multiple_of(which * half + at, CHUNK), CHUNK)
            store_units(out, at, product(normed[...], grad_pre[:, cols], TN), which, places)
        made(part, 0, half)
        if part == 0:
            for load in loads:
                load.wait()
        for at in range(0, half, CHUNK):
            cols = pl.ds(pl.multiple_of(which * half + at, CHUNK), CHUNK)
            store_units(out, half + at, product(grad[...], act_v[:, cols], TN), which, places)
        made(part, half, half)
        cols = pl.ds(pl.multiple_of(which * (width // 2), width // 2), width // 2)
        store_units(out, 2 * half, product(mixed_v[...], rounded[:, cols], TN), which, places)
        made(part, 2 * half, width // 2)
    return Several(copies)


def mlp_loads(depth, slope, up_w, down_w, middle, out_w, slope_v, up_v, down_v, middle_v, out_v, sems, tile_sems):
    tiles = slope_v.shape[0] // ROWS

    def slope_tile(m):
        rows = pl.ds(m * ROWS, ROWS)
        return fetch(slope.at[rows], slope_v.at[rows], tile_sems.at[m])

    down = fetch(down_w.at[depth], down_v, sems.at[0])
    slopes = [slope_tile(0)]
    up = fetch(up_w.at[depth], up_v, sems.at[1])
    mid = fetch(middle, middle_v, sems.at[2])
    out = fetch(out_w.at[depth], out_v, sems.at[3])
    slopes += [slope_tile(m) for m in range(1, tiles)]
    return down, slopes, up, mid, out


def mlp_data_kernel(depth, tokens, grad, middle, slope, up_w, down_w, out_w, gain2, bias2, *rest):
    (grad_middle, grad_mixed, vectors, wide, normed, grad_pre, rounded,
     slope_v, up_v, down_v, out_v, middle_v, sems, tile_sems) = rest[tokens:]
    loads = mlp_loads(depth, slope, up_w, down_w, middle, out_w, slope_v, up_v, down_v, middle_v, out_v, sems, tile_sems)
    mlp_data_back(
        depth, loads, grad, grad_middle, grad_mixed, vectors, wide, slope_v, up_v, down_v, out_v, middle_v, normed,
        grad_pre, rounded, gain2, bias2,
    )


def mlp_weight_kernel(depth, tokens, places, scalars, grad, act, mixed, normed, grad_pre, rounded, *rest):
    mine, theirs, act_v, mixed_v, normed_v, pre_v, rounded_v, sems = rest[tokens:]
    first = [fetch(normed, normed_v, sems.at[0]), fetch(grad_pre, pre_v, sems.at[1])]
    later = [
        fetch(act, act_v, sems.at[2]), fetch(mixed, mixed_v, sems.at[3]),
        fetch(rounded, rounded_v, sems.at[4]),
    ]
    for load in first:
        load.wait()
    mlp_weight_back(scalars[1], places, later, mine, theirs, grad, act_v, mixed_v, normed_v, pre_v, rounded_v)


def attention_backward(qkv, probs, grad_mixed, grad_qkv, stride, windows, width, whole=None, at=0):
    whole = whole or width
    low, high = lane_halves()

    per = PER * TILE * 4 // width

    @pl.loop(0, windows // per)
    def _(step):
        units = [(n, pair) for n in range(per) for pair in range(width // TILE)]
        rows = [pl.ds(pl.multiple_of((per * step + n) * stride, 32), TILE) for n in range(per)]
        kept = [pl.ds(pl.multiple_of((per * step + n) * 2 * TILE, 2 * TILE), 2 * TILE) for n in range(per)]
        count = range(len(units))
        cut = lambda k, n, pair: qkv[rows[n], k * width + pair * TILE : k * width + (pair + 1) * TILE]
        arriving = [both_heads(grad_mixed[rows[n], pair * TILE : (pair + 1) * TILE], low, high) for n, pair in units]
        grad_p = [product(arriving[i], cut(2, *units[i]), NT) for i in count]
        p = [probs[pair, kept[n], :] for n, pair in units]
        grad_v = [product(p[i], arriving[i], TN) for i in count]
        inner = [jnp.sum(grad_p[i] * p[i].astype(F32), axis=-1, keepdims=True) for i in count]
        grad_s = [(p[i].astype(F32) * (grad_p[i] - inner[i])).astype(BF) for i in count]
        grad_q = [product(side_by_side(grad_s[i]), both_heads(cut(1, *units[i]), low, high)) * 0.125 for i in count]
        grad_k = [product(grad_s[i], both_heads(cut(0, *units[i]), low, high), TN) for i in count]
        for k, grads in enumerate((grad_q, grad_k, grad_v)):
            for (n, pair), value in zip(units, grads):
                start = k * whole + at + pair * TILE
                grad_qkv[rows[n], start : start + TILE] = value.astype(BF)


def qkv_back(depth, core, places, grad_qkv, hidden_v, middle_v, weight_v, gain1, bias1, grad_in, normed, vectors, mine, theirs):
    total, width = hidden_v.shape

    @pl.loop(0, total // ROWS)
    def _(m):
        rows = row_tile(m)
        back = jnp.zeros((ROWS, width), F32)
        for f in range(0, 3 * width, width):
            back = back + product(grad_qkv[rows, f : f + width], weight_v[:, f : f + width], NT)
        xhat, scale = normalized(hidden_v[rows, :].astype(F32))
        normed[rows, :] = (xhat * gain1[depth : depth + 1, :] + bias1[depth : depth + 1, :]).astype(BF)
        through, gain_sum, bias_sum = norm_back(back, xhat, scale, gain1[depth : depth + 1, :])
        grad_in[rows, :] = (middle_v[rows, :] + through).astype(BF)
        vectors[0:1, :] += gain_sum
        vectors[1:2, :] += bias_sum
        vectors[2:3, :] += jnp.sum(grad_qkv[rows, :width].astype(F32), axis=0, keepdims=True)
        vectors[3:4, :] += jnp.sum(grad_qkv[rows, 2 * width :].astype(F32), axis=0, keepdims=True)

    half = 3 * width // 2
    for part in range(2):
        which = core if part == 0 else 1 - core
        cols = pl.ds(pl.multiple_of(which * half, half), half)
        store_units((mine, theirs)[part], 0, product(normed[...], grad_qkv[:total, cols], TN), which, places)


def attention_load(depth, qkv, probs, grad_mixed, qkv_v, probs_v, mixed_v, sems):
    total = grad_mixed.shape[0]
    loads = [
        fetch(qkv.at[depth], qkv_v.at[pl.ds(0, total)], sems.at[0]),
        fetch(grad_mixed, mixed_v.at[pl.ds(0, total)], sems.at[1]),
        fetch(probs.at[depth], probs_v, sems.at[2]),
    ]
    qkv_v[total:, :] = jnp.zeros((qkv_v.shape[0] - total, qkv_v.shape[1]), BF)
    mixed_v[total:, :] = jnp.zeros((mixed_v.shape[0] - total, mixed_v.shape[1]), BF)
    return loads


def attention_back_kernel(
    depth, tokens, places, scalars, hidden, qkv, probs, grad_mixed, grad_middle, qkv_w, gain1, bias1, *rest,
):
    (mine, theirs, grad_in, vectors,
     hidden_v, middle_v, weight_v, normed, qkv_v, probs_v, mixed_v, grad_qkv, sems) = rest[tokens:]
    loads = attention_load(depth, qkv, probs, grad_mixed, qkv_v, probs_v, mixed_v, sems)
    later = [
        fetch(qkv_w.at[depth], weight_v, sems.at[3]),
        fetch(hidden.at[depth], hidden_v, sems.at[4]),
        fetch(grad_middle, middle_v, sems.at[5]),
    ]
    vectors[...] = jnp.zeros_like(vectors)
    for load in loads:
        load.wait()
    attention_backward(qkv_v, probs_v, mixed_v, grad_qkv, *placed(scalars, grad_in.shape[0]), grad_in.shape[1])
    for load in later:
        load.wait()
    qkv_back(
        depth, scalars[1], places, grad_qkv, hidden_v, middle_v, weight_v, gain1, bias1, grad_in, normed, vectors, mine,
        theirs,
    )


def part_loads(depth, part, parts, qkv, probs, grad_mixed, qkv_v, probs_v, mixed_v, sems):
    total, whole = grad_mixed.shape
    width = whole // parts
    pairs = probs_v.shape[0]
    inside = pl.ds(0, total)
    loads = [
        fetch(qkv.at[depth, :, pl.ds(k * whole + part * width, width)], qkv_v.at[inside, pl.ds(k * width, width)], sems.at[k])
        for k in range(3)
    ]
    loads.append(fetch(grad_mixed.at[:, pl.ds(part * width, width)], mixed_v.at[inside], sems.at[3]))
    loads.append(fetch(probs.at[depth, pl.ds(part * pairs, pairs)], probs_v, sems.at[4]))
    qkv_v[total:, :] = jnp.zeros((qkv_v.shape[0] - total, qkv_v.shape[1]), BF)
    mixed_v[total:, :] = jnp.zeros((mixed_v.shape[0] - total, mixed_v.shape[1]), BF)
    return loads


def attention_part_kernel(depth, part, parts, tokens, scalars, qkv, probs, grad_mixed, *rest):
    out, qkv_v, probs_v, mixed_v, grad_qkv, sems, out_sem = rest[tokens:]
    total, whole = grad_mixed.shape
    for load in part_loads(depth, part, parts, qkv, probs, grad_mixed, qkv_v, probs_v, mixed_v, sems):
        load.wait()
    attention_backward(qkv_v, probs_v, mixed_v, grad_qkv, *placed(scalars, total), whole // parts)
    fetch(grad_qkv.at[pl.ds(0, total)], out, out_sem).wait()


def table_kernel(
    depth, tokens, places, groups, scalars, qkv, probs, grad_mixed, grad_low, hidden, grad_middle, qkv_w, gain1, bias1,
    index, final_grads, feed1, wide1, attend1, feed0, wide0, *rest,
):
    (mine, theirs, frame_grad, grad_in, turned, vectors, stage, hidden_v, normed, grad_qkv, weight_v, middle_v,
     qkv_v, probs_v, mixed_v, sems, part_sems) = rest[tokens:]
    total, width = grad_in.shape
    half = width // 2
    first = part_loads(depth, 1, 2, qkv, probs, grad_mixed, qkv_v, probs_v, mixed_v, part_sems)
    inside = pl.ds(0, total)
    loads = [
        fetch(grad_low.at[:, pl.ds(k * half, half)], grad_qkv.at[inside, pl.ds(k * width, half)], sems.at[k])
        for k in range(3)
    ]
    loads.append(fetch(qkv_w.at[depth], weight_v, sems.at[3]))
    loads.append(fetch(hidden.at[depth], hidden_v, sems.at[4]))
    loads.append(fetch(grad_middle, middle_v, sems.at[5]))
    core = scalars[1]
    steps = frame_grad.shape[0]
    qkv_width = 3 * width // 2
    code_width = mine.shape[1] - qkv_width - TILE
    vectors[...] = jnp.zeros_like(vectors)
    for load in first:
        load.wait()
    attention_backward(qkv_v, probs_v, mixed_v, grad_qkv, *placed(scalars, total), half, width, half)
    for load in loads:
        load.wait()
    qkv_back(
        depth, core, places, grad_qkv, hidden_v, middle_v, weight_v, gain1, bias1, grad_in, normed, vectors, mine, theirs,
    )

    stage[...] = jnp.zeros_like(stage)
    for k, block in enumerate((feed0, vectors, feed1, attend1, final_grads)):
        stage[VECTORS + 8 * k : VECTORS + 8 * k + 8, :] = block[...]
    each = width // groups
    for k, wide in enumerate((wide0, wide1)):
        for group in range(groups):
            for c in range(4):
                start = group * 4 * each + c * each
                at = VECTORS + 40 + 8 * k + c
                stage[at : at + 1, group * each : group * each + each] = wide[0:1, start : start + each]

    turned[...] = grad_in[...].T
    for part in range(2):
        out = (mine, theirs)[part]
        which = core if part == 0 else 1 - core
        line = lax.broadcasted_iota(jnp.int32, (code_width, total), 0) + which * code_width
        hot = (line == index[0:1, :]).astype(F32).astype(BF)
        store_units(out, qkv_width, product(turned[...], hot, NT), which, places)
        line = lax.broadcasted_iota(jnp.int32, (TILE, total), 0) + which * TILE
        hot = ((line == index[1:2, :]) | (line == index[2:3, :])).astype(F32).astype(BF)
        small = product(turned[...], hot, NT) + stage[...].T * which.astype(F32)
        store_units(out, qkv_width + code_width, small, which, places)
    hot = (lax.broadcasted_iota(jnp.int32, (steps, total), 0) == index[3:4, :]).astype(F32).astype(BF)
    frame_grad[...] = product(hot, grad_in[...])


def output_kernel(where, scalars, *refs):
    count = 1 + max(chunk for chunk, _ in where.values())
    sources = refs[: 2 * count]
    (code, action, position, gain1, bias1, qkv, query, value, out, out_bias, gain2, bias2, up, up_bias, down, down_bias,
     final_gain, final_bias) = refs[2 * count : -1]
    square = refs[-1]
    rows, units = up.shape[1:]
    half = units // 2
    small = qkv.shape[2] // 2 + code.shape[1] // 2

    def emit(own):
        def part(name, core, across, start, size):
            chunk, at = where[name]
            lines = slice((across ^ (own >> 1)) * rows // 2, ((across ^ (own >> 1)) + 1) * rows // 2)
            return sources[2 * chunk + (core ^ (own & 1))][lines, at + start : at + start + size].astype(F32)

        def place(target, name, start):
            size = target.shape[-1] // 2
            for across in range(2):
                lines = slice(across * rows // 2, (across + 1) * rows // 2)
                for core in range(2):
                    target[lines, core * size : (core + 1) * size] = part(name, core, across, start, size)

        for depth in range(2):
            place(up.at[depth], ("feed", depth), 0)
            place(down.at[depth], ("feed", depth), half)
            place(out.at[depth], ("feed", depth), units)
            place(qkv.at[depth], ("attend", depth), 0)
        place(code, ("attend", 0), qkv.shape[2] // 2)
        square[...] = jnp.zeros_like(square)
        for across in range(2):
            lines = slice(across * rows // 2, (across + 1) * rows // 2)
            position[lines, :] = part(("attend", 0), 0, across, small, TILE)[:, : position.shape[1]]
            square[lines, :] = part(("attend", 0), 1, across, small, TILE)
        lines = square[...].T[:, :rows]
        action[...] = lines[: action.shape[0]]

        def line(k):
            return lines[VECTORS + k : VECTORS + k + 1]

        for depth in range(2):
            at = slice(depth, depth + 1)
            base = 16 * depth
            for k, target in enumerate((gain2, bias2, down_bias, out_bias)):
                target[at, :] = line(base + k)
            for k, target in enumerate((gain1, bias1, query, value)):
                target[at, :] = line(base + 8 + k)
            for c in range(4):
                up_bias[at, c * rows : (c + 1) * rows] = line(40 + 8 * depth + c)
        final_gain[...] = line(32)
        final_bias[...] = line(33)

    for own in range(4):
        pl.when(scalars[scalars.shape[0] - 1] == own)(partial(emit, own))


VMEM = pl.BlockSpec(memory_space=pltpu.VMEM)
ANY = pl.BlockSpec(memory_space=pl.ANY)
SMEM = pl.BlockSpec(memory_space=pltpu.SMEM)


def cost(flops, moved, others=0):
    return pl.CostEstimate(flops=int(8 * flops), bytes_accessed=int(moved), transcendentals=int(others))


def run_forward(places, scalars, actions, deltas, frames, codebook, action_table, position_table, layers, finals, cotangent):
    gain1, bias1, qkv_w, query_bias, value_bias, out_w, out_bias, gain2, bias2, up_w, up_bias, down_w, down_bias = layers
    width = codebook.shape[1]
    units = up_bias.shape[1]
    real = cotangent.shape[1]
    total = -(-real // ROWS) * ROWS
    reach = total + TILE + 32
    columns = units + width // 2
    shape = jax.ShapeDtypeStruct
    once = dict(pipeline_mode=pl.Buffered(1))
    whole = lambda a: pl.BlockSpec(a.shape, lambda i, s, n=a.ndim: (0,) * n, **once)
    mine = lambda a: pl.BlockSpec((1,) + a.shape[1:], lambda i, s: (s[0], 0, 0), **once)
    kept = (width // TILE, WINDOWS * 2 * TILE, TILE)
    outs = [
        (shape((real, width), F32), ANY),
        (shape((8, total), jnp.int32), None),
        (shape((8, width), F32), None), (shape((8, width), F32), None), (shape((8, units), F32), None),
        (shape((2, total, width), BF), ANY),
        (shape((2, total, 3 * width), BF), ANY),
        (shape((2,) + kept, BF), ANY),
        (shape((total, width), BF), ANY),
        (shape((total, width), F32), ANY),
        (shape((total, units), BF), ANY),
        (shape((total, units), BF), ANY),
        (shape((total, width), F32), ANY), (shape((total, width), BF), ANY),
        (shape((width, columns), BF), ANY), (shape((width, columns), BF), ANY),
    ]
    args = [
        (actions, mine(actions)), (deltas, mine(deltas)), (frames, mine(frames)),
        (codebook, None), (action_table, None), (position_table, None),
        (gain1, None), (bias1, None), (qkv_w, ANY), (query_bias, None), (value_bias, None), (out_w, ANY),
        (out_bias, None), (gain2, None), (bias2, None), (up_w, ANY), (up_bias, None), (down_w, ANY), (down_bias, None),
        (finals[0][None], None), (finals[1][None], None), (cotangent, mine(cotangent)),
    ]
    scratch = [
        pltpu.VMEM((2 * TILE, width), BF),
        pltpu.VMEM(qkv_w.shape, BF), pltpu.VMEM(out_w.shape, BF), pltpu.VMEM(up_w.shape, BF), pltpu.VMEM(down_w.shape, BF),
        pltpu.VMEM((3, total, width), BF), pltpu.VMEM((reach, 3 * width), BF), pltpu.VMEM(kept, BF),
        pltpu.VMEM((reach, width), BF), pltpu.VMEM((total, width), F32),
        pltpu.VMEM((total, units), BF), pltpu.VMEM((total, units), BF), pltpu.VMEM((2 * TILE, TILE), F32),
        pltpu.VMEM((total, width), F32), pltpu.VMEM((total, width), F32),
        pltpu.VMEM((total, width), BF), pltpu.VMEM((total, width), BF), pltpu.VMEM((total, width), BF),
        pltpu.VMEM((total, width), BF), pltpu.VMEM((total, units), BF),
        pltpu.VMEM((width, columns), BF), pltpu.VMEM((width, columns), BF),
        pltpu.SemaphoreType.DMA((2, 4)), pltpu.SemaphoreType.DMA((16,)), pltpu.SemaphoreType.DMA((2, total // ROWS)),
        pltpu.SemaphoreType.DMA, pltpu.SemaphoreType.DMA((6,)),
    ]
    return pl.pallas_call(
        partial(forward_kernel, places),
        out_shape=[o for o, _ in outs],
        grid_spec=pltpu.PrefetchScalarGridSpec(
            num_scalar_prefetch=1,
            grid=(1,),
            in_specs=[spec or whole(a) for a, spec in args],
            out_specs=[spec or whole(o) for o, spec in outs],
            scratch_shapes=scratch,
        ),
        compiler_params=pltpu.CompilerParams(vmem_limit_bytes=62 << 20),
        cost_estimate=cost(24e9, 50e6, 4e6),
        name="forward",
    )(scalars, *[a for a, _ in args])


def run_mlp_data(depth, grad, saved, layers, after):
    hidden, qkv, probs, mixed, middle, act, slope = saved
    gain1, bias1, qkv_w, query_bias, value_bias, out_w, out_bias, gain2, bias2, up_w, up_bias, down_w, down_bias = layers
    total, width = grad.shape
    units = up_bias.shape[1]
    shape = jax.ShapeDtypeStruct
    return pl.pallas_call(
        partial(mlp_data_kernel, depth, len(after)),
        out_shape=[
            shape((total, width), F32), shape((total, width), BF), shape((8, width), F32), shape((8, units), F32),
            shape((total, width), BF), shape((total, units), BF), shape((total, width), BF),
        ],
        in_specs=[VMEM] + [ANY] * 5 + [VMEM] * 2 + [ANY] * len(after),
        out_specs=[VMEM] * 7,
        scratch_shapes=[
            pltpu.VMEM((total, units), BF),
            pltpu.VMEM((width, units), BF), pltpu.VMEM((units, width), BF), pltpu.VMEM((width, width), BF),
            pltpu.VMEM((total, width), F32),
            pltpu.SemaphoreType.DMA((4,)), pltpu.SemaphoreType.DMA((total // ROWS,)),
        ],
        compiler_params=pltpu.CompilerParams(vmem_limit_bytes=40 << 20),
        cost_estimate=cost(10e9, 16e6),
        name="mlp_data",
    )(grad, middle, slope, up_w, down_w, out_w, gain2, bias2, *after)


def run_mlp_weight(depth, places, scalars, grad, saved, normed, grad_pre, rounded, after):
    hidden, qkv, probs, mixed, middle, act, slope = saved
    total, width = grad.shape
    units = grad_pre.shape[1]
    shape = jax.ShapeDtypeStruct
    return pl.pallas_call(
        partial(mlp_weight_kernel, depth, len(after), places),
        out_shape=[shape((width, units + width // 2), BF), shape((width, units + width // 2), BF)],
        in_specs=[SMEM, VMEM] + [ANY] * 5 + [ANY] * len(after),
        out_specs=[VMEM] * 2,
        scratch_shapes=[
            pltpu.VMEM((total, units), BF), pltpu.VMEM((total, width), BF), pltpu.VMEM((total, width), BF),
            pltpu.VMEM((total, units), BF), pltpu.VMEM((total, width), BF),
            pltpu.SemaphoreType.DMA((5,)),
        ],
        compiler_params=pltpu.CompilerParams(vmem_limit_bytes=40 << 20),
        cost_estimate=cost(8e9, 16e6),
        name="mlp_weight",
    )(scalars, grad, act, mixed, normed, grad_pre, rounded, *after)


def window_scratch(total, width, probs):
    reach = total + TILE + 32
    return [
        pltpu.VMEM((reach, 3 * width), BF), pltpu.VMEM(probs.shape[1:], BF),
        pltpu.VMEM((reach, width), BF), pltpu.VMEM((reach, 3 * width), BF),
    ]


def run_attention_back(depth, places, scalars, grad_mixed, grad_middle, saved, layers, after):
    hidden, qkv, probs, mixed, middle, act, slope = saved
    gain1, bias1, qkv_w = layers[:3]
    total, width = grad_mixed.shape
    shape = jax.ShapeDtypeStruct
    return pl.pallas_call(
        partial(attention_back_kernel, depth, len(after), places),
        out_shape=[
            shape((width, 3 * width // 2), BF), shape((width, 3 * width // 2), BF),
            shape((total, width), BF), shape((8, width), F32),
        ],
        in_specs=[SMEM] + [ANY] * 6 + [VMEM] * 2 + [ANY] * len(after),
        out_specs=[VMEM] * 4,
        scratch_shapes=[
            pltpu.VMEM((total, width), BF), pltpu.VMEM((total, width), F32), pltpu.VMEM(qkv_w.shape[1:], BF),
            pltpu.VMEM((total, width), BF), *window_scratch(total, width, probs),
            pltpu.SemaphoreType.DMA((6,)),
        ],
        compiler_params=pltpu.CompilerParams(vmem_limit_bytes=50 << 20),
        cost_estimate=cost(16e9, 24e6),
        name="attention_back",
    )(scalars, hidden, qkv, probs, grad_mixed, grad_middle, qkv_w, gain1, bias1, *after)


def run_attention_part(depth, part, parts, scalars, grad_mixed, saved, after):
    hidden, qkv, probs, mixed, middle, act, slope = saved
    total, width = grad_mixed.shape
    width = width // parts
    reach = total + TILE + 32
    return pl.pallas_call(
        partial(attention_part_kernel, depth, part, parts, len(after)),
        out_shape=jax.ShapeDtypeStruct((total, 3 * width), BF),
        in_specs=[SMEM] + [ANY] * 3 + [ANY] * len(after),
        out_specs=ANY,
        scratch_shapes=[
            pltpu.VMEM((reach, 3 * width), BF), pltpu.VMEM((width // TILE,) + probs.shape[2:], BF),
            pltpu.VMEM((reach, width), BF), pltpu.VMEM((reach, 3 * width), BF),
            pltpu.SemaphoreType.DMA((5,)), pltpu.SemaphoreType.DMA,
        ],
        compiler_params=pltpu.CompilerParams(vmem_limit_bytes=40 << 20),
        cost_estimate=cost(8e9, 8e6),
        name="attention_part",
    )(scalars, qkv, probs, grad_mixed, *after)


def run_table(depth, places, scalars, grad_mixed, grad_low, grad_middle, saved, layers, index, vectors, codes, steps, groups, after):
    hidden, qkv, probs, mixed, middle, act, slope = saved
    gain1, bias1, qkv_w = layers[:3]
    total, width = grad_middle.shape
    reach = total + TILE + 32
    columns = 3 * width // 2 + codes // 2 + TILE
    shape = jax.ShapeDtypeStruct
    return pl.pallas_call(
        partial(table_kernel, depth, len(after), places, groups),
        out_shape=[shape((width, columns), BF), shape((width, columns), BF), shape((steps, width), F32)],
        in_specs=[SMEM] + [ANY] * 7 + [VMEM] * 2 + [VMEM] * 7 + [ANY] * len(after),
        out_specs=[VMEM] * 3,
        scratch_shapes=[
            pltpu.VMEM((total, width), BF), pltpu.VMEM((width, total), BF), pltpu.VMEM((8, width), F32),
            pltpu.VMEM((TILE, width), F32), pltpu.VMEM((total, width), BF), pltpu.VMEM((total, width), BF),
            pltpu.VMEM((reach, 3 * width), BF), pltpu.VMEM(qkv_w.shape[1:], BF), pltpu.VMEM((total, width), F32),
            pltpu.VMEM((reach, 3 * width // 2), BF), pltpu.VMEM((probs.shape[1] // 2,) + probs.shape[2:], BF),
            pltpu.VMEM((reach, width // 2), BF),
            pltpu.SemaphoreType.DMA((6,)), pltpu.SemaphoreType.DMA((5,)),
        ],
        compiler_params=pltpu.CompilerParams(vmem_limit_bytes=40 << 20),
        cost_estimate=cost(12e9, 12e6),
        name="tables",
    )(scalars, qkv, probs, grad_mixed, grad_low, hidden, grad_middle, qkv_w, gain1, bias1, index, *vectors, *after)


def run_output(where, scalars, sources, width, units, codes, actions, positions):
    rows = sources[0].shape[0]
    wide, line = (2, rows), (1, rows)
    shapes = [
        (rows, codes), (actions, rows), (rows, positions), wide, wide, (2, rows, 3 * width), wide, wide, (2, rows, width),
        wide, wide, wide, (2, rows, units), (2, 4 * rows), (2, rows, units), wide, line, line,
    ]
    return pl.pallas_call(
        partial(output_kernel, where),
        out_shape=[jax.ShapeDtypeStruct(s, F32) for s in shapes],
        in_specs=[SMEM] + [VMEM] * len(sources),
        out_specs=[VMEM] * len(shapes),
        scratch_shapes=[pltpu.VMEM((TILE, TILE), F32)],
        compiler_params=pltpu.CompilerParams(vmem_limit_bytes=30 << 20),
        cost_estimate=cost(1e6, 6e6),
        name="outputs",
    )(scalars, *sources)


def meet(array, axis, by):
    size = lax.axis_size(axis)
    return lax.ppermute(array, axis, [(i, i ^ by) for i in range(size)])


def swap(array, axis, bit):
    return meet(array, axis, 1 << bit)


def bits_of(axis):
    return lax.axis_size(axis).bit_length() - 1


def own_bit(axis, bit):
    return (lax.axis_index(axis) >> bit) & 1


def take(array, dim, which):
    return lax.dynamic_index_in_dim(array, which, dim, keepdims=False)


def total_of(terms):
    return sum(term.astype(F32) for term in terms)


def settled(array):
    return lax.optimization_barrier(array.astype(BF))


def tied(array, token):
    return lax.optimization_barrier((array, token))[0]


def unit_places(count):
    first, second = [], []
    for unit in range(2 << count):
        bits = [(unit >> (1 + bit)) & 1 for bit in range(count)]
        for order, places in ((bits + [unit & 1], first), ([unit & 1] + bits, second)):
            place = 0
            for bit in order:
                place = 2 * place + bit
            places.append(place)
    return first, second


def reordered(array, which, count):
    rows, columns = array.shape
    ways = array.reshape((2,) * (count + 1) + (rows >> (count + 1), columns))
    dims = list(range(count - 1, -1, -1))
    first = ways.transpose(dims + [count, count + 1, count + 2])
    second = ways.transpose([count] + dims + [count + 1, count + 2])
    return jnp.where(which == 0, first, second).reshape(rows, columns)


class Chunk:
    def __init__(self, places):
        self.count = bits_of("dp")
        self.places = places
        self.pieces = []
        self.terms = []
        self.core = own_bit("section", 0)

    def add(self, mine, theirs):
        if self.places is None:
            mine, theirs = reordered(mine, self.core, self.count), reordered(theirs, 1 - self.core, self.count)
        self.pieces.append([mine, swap(theirs, "section", 0)])

    def hold(self, token):
        if self.terms:
            self.terms[-1] = tied(self.terms[-1], token)
        else:
            for piece in self.pieces:
                piece[1] = tied(piece[1], token)

    def step(self):
        if not self.terms:
            self.left = self.pieces[0][0].shape[0]
        k = len(self.terms)
        bits = [own_bit("dp", bit) for bit in range(self.count)]
        across = own_bit("section", 1)
        own = jnp.where(self.core == 0, (bits + [across])[k], ([across] + bits)[k])
        half = self.left // 2
        cut = lambda t, which: lax.dynamic_slice_in_dim(t, which * half, half, 0)
        if not self.terms:
            self.parts = [[[mine, arrived] for mine, arrived in self.pieces]]
        parts = self.parts[-1]
        sum_of = jnp.concatenate([total_of([cut(t, 1 - own) for t in part]) for part in parts], axis=1)
        for term in self.terms:
            sum_of = sum_of + cut(term, 1 - own).astype(F32)
        self.sent = settled(sum_of)
        sections = lax.axis_size("section")
        pairs = []
        for source in range(lax.axis_size("dp") * sections):
            at = k if source & 1 == 0 else (k - 1) % (self.count + 1)
            bit = sections << at if at < self.count else 2
            pairs.append((source, source ^ bit))
        self.parts = [[[cut(t, own) for t in part] for part in parts]]
        self.terms = [cut(t, own) for t in self.terms] + [lax.ppermute(self.sent, ("dp", "section"), pairs)]
        self.left = half
        return self

    def across(self):
        total = jnp.concatenate([total_of(part) for part in self.parts[-1]], axis=1)
        for term in self.terms:
            total = total + term.astype(F32)
        self.sent = settled(total)
        other = swap(self.sent, "section", 1)
        self.terms = [self.sent, other]

    def finish(self):
        rows = settled(jnp.concatenate(self.terms))
        arrived = swap(rows, "section", 0)
        return [rows, arrived]


def local(
    frames, actions, deltas, kinds, codebook, action_table, position_table, norm1_gain, norm1_bias, qkv_weight,
    query_bias, value_bias, out_weight, out_bias, norm2_gain, norm2_bias, up_weight, up_bias, down_weight, down_bias,
    final_gain, final_bias, cotangent,
):
    micro, steps, width = frames.shape
    units = up_weight.shape[2]
    codes = codebook.shape[0]
    slot = lax.axis_index("section") * micro // lax.axis_size("section")
    layers = (
        norm1_gain, norm1_bias, qkv_weight, query_bias, value_bias, out_weight, out_bias, norm2_gain, norm2_bias,
        up_weight, up_bias, down_weight, down_bias,
    )
    section = lax.axis_index("section")
    scalars = jnp.concatenate([jnp.stack([slot, section & 1]), kinds, section[None]]).astype(jnp.int32)
    groups = lax.axis_size("dp")
    count = bits_of("dp")
    places = unit_places(count) if width >> (count + 1) >= 16 else None
    chunk1, chunk2, chunk3 = Chunk(places), Chunk(places), Chunk(places)
    activations, index, final_grads, feed1, wide1, *saved, middle, mixed, mine, theirs = run_forward(
        places, scalars, actions[:, None], deltas.transpose(0, 2, 1), frames, codebook, action_table, position_table,
        layers, (final_gain, final_bias), cotangent,
    )
    chunk1.add(mine, theirs)
    mine, theirs, grad, attend1 = run_attention_back(1, places, scalars, mixed, middle, saved, layers, [])
    chunk1.hold(attend1)
    chunk2.add(mine, theirs)
    chunk1.step()
    middle, mixed, feed0, wide0, normed, grad_pre, rounded = run_mlp_data(0, grad, saved, layers, [chunk1.sent])
    chunk1.hold(normed)
    chunk1.step()
    mine, theirs = run_mlp_weight(0, places, scalars, grad, saved, normed, grad_pre, rounded, [chunk1.sent])
    chunk1.hold(theirs)
    chunk2.hold(theirs)
    chunk2.add(mine, theirs)
    chunk1.step()
    grad_low = run_attention_part(0, 0, 2, scalars, mixed, saved, [chunk1.sent])
    chunk1.hold(grad_low)
    chunk2.hold(grad_low)
    chunk2.step()
    chunk1.step()
    vectors = (final_grads, feed1, wide1, attend1, feed0, wide0)
    mine, theirs, frame_grad = run_table(
        0, places, scalars, mixed, grad_low, middle, saved, layers, index, vectors, codes, steps, groups,
        [chunk2.sent, chunk1.sent],
    )
    chunk3.add(mine, theirs)
    chunk2.hold(frame_grad)
    chunk1.hold(chunk2.terms[-1])
    chunk2.step()
    chunk3.hold(chunk2.sent)
    chunk3.step()
    chunk2.hold(chunk3.sent)
    chunk1.hold(chunk3.sent)
    for _ in range(3, count):
        chunk1.step()
    chunk1.across()
    for k in range(2, count + 3):
        if k <= count:
            chunk2.step()
        elif k == count + 1:
            chunk2.across()
        else:
            sources += chunk2.finish()
        chunk3.hold(chunk2.sent)
        if k == 2:
            chunk3.hold(chunk1.terms[-1])
            sources = chunk1.finish()
        if k <= count + 1:
            chunk3.step()
            chunk2.hold(chunk3.sent)
        else:
            chunk3.across()
    sources += chunk3.finish()
    split = 3 * width // 2
    where = {("feed", 1): (0, 0), ("attend", 1): (1, 0), ("feed", 0): (1, split), ("attend", 0): (2, 0)}
    (code, action, position, gain1, bias1, qkv, query, value, out, out_b, gain2, bias2, up, up_b, down, down_b, last_gain,
     last_bias) = run_output(
        where, scalars, sources, width, units, codes, action_table.shape[0], position_table.shape[0]
    )
    return (
        activations[None], frame_grad[None], code.T, action, position.T, gain1, bias1, qkv, query, value, out, out_b,
        gain2, bias2, up, up_b, down.transpose(0, 2, 1), down_b, last_gain[0], last_bias[0],
    )


def solution(mesh):
    rows, one = P("dp", None, None), P(None, "dp")
    weight = P(None, "dp", None)
    both = P(("dp", "section"), None, None)
    return jax.shard_map(
        local,
        mesh=mesh,
        in_specs=(rows, P("dp", None), rows, P("dp")) + (P(),) * 18 + (rows,),
        out_specs=(
            both, both, one, one, one, one, one, weight, one, one, weight, one, one, one, weight, one,
            P(None, None, "dp"), one, P("dp"), P("dp"),
        ),
        check_vma=False,
    )
```

```python
from functools import partial

import jax
import jax.numpy as jnp
from jax import lax
from jax.experimental import pallas as pl
from jax.experimental.pallas import tpu as pltpu
from jax.sharding import PartitionSpec as P

HEADS = 8
SHORT_STEPS = 8
LONG_STEPS = 21
EPSILON = 1e-05
MASKED = -1e30
TILE = 128
ROWS = 512
CHUNK = 512
STRIP = 256
VECTORS = 32
WINDOWS = 12
PER = 4
VMEM_PART = 58
BF = jnp.bfloat16
F32 = jnp.float32

NN = (((1,), (0,)), ((), ()))
NT = (((1,), (1,)), ((), ()))
TN = (((0,), (0,)), ((), ()))


def product(left, right, form=NN):
    return lax.dot_general(left, right, form, preferred_element_type=F32)


def normalized(x):
    center = x - jnp.mean(x, axis=-1, keepdims=True)
    spread = jnp.mean(center * center, axis=-1, keepdims=True)
    scale = lax.rsqrt(spread + EPSILON)
    return center * scale, scale


def norm_back(grad, xhat, scale, gain):
    inner = grad * gain
    first = jnp.mean(inner, axis=-1, keepdims=True)
    second = jnp.mean(inner * xhat, axis=-1, keepdims=True)
    back = (inner - first - xhat * second) * scale
    return back, jnp.sum(grad * xhat, axis=0, keepdims=True), jnp.sum(grad, axis=0, keepdims=True)


def gelu_pair(u):
    cdf = 0.5 + 0.5 * lax.erf(u * 0.7071067811865476)
    e = jnp.exp2(u * u * (-0.5 * 1.4426950408889634))
    return u * cdf, cdf + u * (e * 0.3989422804014327)


def row_tile(m):
    return pl.ds(pl.multiple_of(m * ROWS, ROWS), ROWS)


def lane_halves():
    lane = lax.broadcasted_iota(jnp.int32, (1, TILE), 1)
    low = (lane < TILE // 2).astype(F32)
    return low.astype(BF), (1.0 - low).astype(BF)


def both_heads(x, low, high):
    return jnp.concatenate([x * low, x * high], axis=0)


def side_by_side(x):
    return jnp.concatenate([x[:TILE], x[TILE:]], axis=1)


def write_mask(mask, stride):
    row = lax.broadcasted_iota(jnp.int32, (2 * TILE, TILE), 0)
    row = jnp.where(row >= TILE, row - TILE, row).astype(F32) + 0.5
    col = lax.broadcasted_iota(jnp.int32, (2 * TILE, TILE), 1).astype(F32) + 0.5
    step = jnp.floor(col * (1.0 / 6.0)) <= jnp.floor(row * (1.0 / 6.0))
    member = jnp.floor(col * (1.0 / 48.0)) == jnp.floor(row * (1.0 / 48.0))
    long = jnp.where(step, 0.0, MASKED)
    short = jnp.where(member, long, MASKED)
    mask[...] = jnp.where(stride == TILE, long, short)


def placed(scalars, total):
    long = scalars[2 + scalars[0]] == 1
    return jnp.where(long, TILE, 2 * SHORT_STEPS * 6), jnp.where(long, total // TILE, WINDOWS)


def fetch(source, target, sem):
    copy = pltpu.make_async_copy(source, target, sem)
    copy.start()
    return copy


def attention_forward(qkv, probs, mixed, mask, stride, windows, width):
    low, high = lane_halves()

    @pl.loop(0, windows // PER)
    def _(step):
        units = [(n, pair) for n in range(PER) for pair in range(width // TILE)]
        starts = [pl.multiple_of((PER * step + n) * stride, 32) for n in range(PER)]
        rows = [pl.ds(start, TILE) for start in starts]
        cut = lambda k, n, pair: qkv[rows[n], k * width + pair * TILE : k * width + (pair + 1) * TILE]
        scores = [product(both_heads(cut(0, n, pair), low, high), cut(1, n, pair), NT) + mask[...] for n, pair in units]
        shifted = [jnp.exp(s - jnp.max(s, axis=-1, keepdims=True)) for s in scores]
        p = [(s * (1.0 / jnp.sum(s, axis=-1, keepdims=True))).astype(BF) for s in shifted]
        for (n, pair), value in zip(units, p):
            kept = pl.ds(pl.multiple_of((PER * step + n) * 2 * TILE, 2 * TILE), 2 * TILE)
            probs[pair, kept, :] = value
        out = [product(side_by_side(value), both_heads(cut(2, n, pair), low, high)) for (n, pair), value in zip(units, p)]
        for (n, pair), value in zip(units, out):
            mixed[rows[n], pair * TILE : (pair + 1) * TILE] = value.astype(BF)


def build_index(index, actions, deltas, long):
    steps = actions.shape[-1]
    total = index.shape[1]
    step = lax.broadcasted_iota(jnp.int32, (steps, total), 0).astype(F32)
    start = step * 6.0 + jnp.where(long, 2.0, 0.0) * jnp.floor((step + 0.5) * (1.0 / LONG_STEPS))
    slot = lax.broadcasted_iota(jnp.int32, (steps, total), 1).astype(F32) - start
    line = lax.broadcasted_iota(jnp.int32, (8, steps), 0)

    def rows(**values):
        out = jnp.zeros((8, steps), F32)
        for name, value in values.items():
            out = jnp.where(line == int(name[1:]), value, out)
        return out.astype(BF)

    def spread(value, j):
        return product(value, (slot == float(j)).astype(F32).astype(BF))

    count = lax.broadcasted_iota(jnp.int32, (8, steps), 1).astype(F32)
    found = spread(rows(r5=count, r6=1.0), 0) + spread(rows(r3=actions.astype(F32), r4=1.0), 1)
    for j in range(deltas.shape[1]):
        code = deltas[0, j : j + 1, :].astype(F32)
        high = jnp.floor(code * (1.0 / 32.0))
        found = found + spread(rows(r0=high, r1=code - 32.0 * high, r2=1.0), 2 + j)
    found = found.astype(jnp.int32)
    none = jnp.full((1, total), -1, jnp.int32)
    row = lax.broadcasted_iota(jnp.int32, (1, total), 1)
    real = row.astype(F32) + 0.5
    apart = row - TILE * jnp.floor(real * (1.0 / TILE)).astype(jnp.int32)
    apart = jnp.where(apart < LONG_STEPS * 6, apart, none)
    close = row - SHORT_STEPS * 6 * jnp.floor(real * (1.0 / (SHORT_STEPS * 6))).astype(jnp.int32)
    close = jnp.where(row < steps * 6, close, none)
    index[0:1, :] = jnp.where(found[2:3] == 1, found[0:1] * 32 + found[1:2], none)
    index[1:2, :] = jnp.where(long, apart, close)
    index[2:3, :] = jnp.where(found[4:5] == 1, found[3:4] + TILE, none)
    index[3:4, :] = jnp.where(found[6:7] == 1, found[5:6], none)
    index[4:8, :] = jnp.full((4, total), -1, jnp.int32)


def forward_kernel(
    places, scalars, actions, deltas, frames, codebook, action_table, position_table,
    gain1, bias1, qkv_w, query_bias, value_bias, out_w, out_bias, gain2, bias2,
    up_w, up_bias, down_w, down_bias, final_gain, final_bias, cotangent,
    activations, index, final_grads, vectors, wide,
    hidden_out, qkv_out, probs_out, mixed_out, middle_out, act_out, slope_out,
    grad_middle_out, grad_mixed_out, mine_out, theirs_out,
    table, qkv_v, out_v, up_v, down_v, hidden, qkv, probs, mixed, middle, act, slope, mask, result, cot,
    grad, grad_mixed, normed_two, rounded, grad_pre, mine, theirs,
    weight_sem, save_sem, tile_sem, result_sem, part_sem,
):
    core = scalars[1]
    width = hidden.shape[-1]
    total = hidden.shape[1]
    stride, windows = placed(scalars, total)
    hidden_units = up_bias.shape[1]
    tiles = total // ROWS
    loads = []
    for depth in range(2):
        loads.append([
            fetch(qkv_w.at[depth], qkv_v.at[depth], weight_sem.at[depth, 0]),
            fetch(out_w.at[depth], out_v.at[depth], weight_sem.at[depth, 1]),
            fetch(up_w.at[depth], up_v.at[depth], weight_sem.at[depth, 2]),
            fetch(down_w.at[depth], down_v.at[depth], weight_sem.at[depth, 3]),
        ])
    write_mask(mask, stride)
    build_index(index, actions[pl.ds(scalars[0], 1), :], deltas, stride == TILE)
    positions = position_table.shape[0]
    action_count = action_table.shape[0]
    table[...] = jnp.zeros_like(table)
    table[:positions] = position_table[...]
    table[TILE : TILE + action_count] = action_table[...]
    qkv[total:, :] = jnp.zeros((qkv.shape[0] - total, qkv.shape[1]), BF)

    codes = codebook.shape[0]
    steps = frames.shape[1]

    @pl.loop(0, tiles)
    def _(m):
        rows = row_tile(m)
        code_hot = (lax.broadcasted_iota(jnp.int32, (codes, ROWS), 0) == index[0:1, rows]).astype(F32).astype(BF)
        line = lax.broadcasted_iota(jnp.int32, (2 * TILE, ROWS), 0)
        small_hot = ((line == index[1:2, rows]) | (line == index[2:3, rows])).astype(F32).astype(BF)
        frame_hot = (lax.broadcasted_iota(jnp.int32, (steps, ROWS), 0) == index[3:4, rows]).astype(F32).astype(BF)
        value = product(code_hot, codebook[...], TN) + product(small_hot, table[...], TN)
        value = value + product(frame_hot, frames[0], TN)
        hidden[0, rows, :] = value.astype(BF)

    def tile_copies(m):
        rows = row_tile(m)
        return (
            pltpu.make_async_copy(act.at[rows], act_out.at[rows], tile_sem.at[0, m]),
            pltpu.make_async_copy(slope.at[rows], slope_out.at[rows], tile_sem.at[1, m]),
        )

    saves = {}
    started = []

    def save(name, source, target):
        saves[name] = fetch(source, target, save_sem.at[len(started)])
        started.append(name)

    inside = pl.ds(0, total)
    for depth in range(2):
        save(("hidden", depth), hidden.at[depth], hidden_out.at[depth])
        loads[depth][0].wait()
        if depth:
            saves.pop(("qkv", 0)).wait()

        def normed_tile(m):
            xhat, _ = normalized(hidden[depth, m * ROWS : (m + 1) * ROWS, :].astype(F32))
            return (xhat * gain1[depth : depth + 1, :] + bias1[depth : depth + 1, :]).astype(BF)

        ready = normed_tile(0)
        for m in range(tiles):
            rows = slice(m * ROWS, (m + 1) * ROWS)
            normed = ready
            if m + 1 < tiles:
                ready = normed_tile(m + 1)
            q = product(normed, qkv_v[depth, :, :width]) + query_bias[depth : depth + 1, :]
            k = product(normed, qkv_v[depth, :, width : 2 * width])
            v = product(normed, qkv_v[depth, :, 2 * width :]) + value_bias[depth : depth + 1, :]
            qkv[rows, :width] = (q.astype(BF).astype(F32) * 0.125).astype(BF)
            qkv[rows, width : 2 * width] = k.astype(BF)
            qkv[rows, 2 * width :] = v.astype(BF)

        save(("qkv", depth), qkv.at[inside], qkv_out.at[depth])
        if depth:
            saves.pop(("probs", 0)).wait()
            saves.pop(("mixed", 0)).wait()
        attention_forward(qkv, probs, mixed, mask, stride, windows, width)
        save(("probs", depth), probs, probs_out.at[depth])
        if not depth:
            save(("mixed", depth), mixed.at[inside], mixed_out)
        for load in loads[depth][1:]:
            load.wait()
        if depth:
            saves.pop(("middle", 0)).wait()

        @pl.loop(0, tiles)
        def _(m):
            rows = row_tile(m)
            mid = hidden[depth, rows, :].astype(F32) + (
                product(mixed[rows, :], out_v[depth]) + out_bias[depth : depth + 1, :]
            )
            middle[rows, :] = mid
            xhat, _ = normalized(mid)
            normed = (xhat * gain2[depth : depth + 1, :] + bias2[depth : depth + 1, :]).astype(BF)
            if depth:
                normed_two[rows, :] = normed
                for copy in tile_copies(m):
                    copy.wait()
            parts = list(range(0, hidden_units, STRIP))
            up = lambda f: product(normed, up_v[depth, :, f : f + STRIP]) + up_bias[depth : depth + 1, f : f + STRIP]
            u = up(0)
            added = jnp.zeros((ROWS, width), F32)
            previous = None
            for f in parts:
                following = up(f + STRIP) if f + STRIP < hidden_units else None
                if previous is not None:
                    added = added + product(previous, down_v[depth, f - STRIP : f, :])
                z, d = gelu_pair(u)
                previous = z.astype(BF)
                act[rows, f : f + STRIP] = previous
                slope[rows, f : f + STRIP] = d.astype(BF)
                u = following
            added = added + product(previous, down_v[depth, hidden_units - STRIP :, :])
            hidden[depth + 1, rows, :] = (mid + (added + down_bias[depth : depth + 1, :])).astype(BF)
            if not depth:
                for copy in tile_copies(m):
                    copy.start()

        if not depth:
            save(("middle", depth), middle, middle_out)

    real = cotangent.shape[1]
    cot[:real] = cotangent[0].astype(F32)
    cot[real:] = jnp.zeros((cot.shape[0] - real, width), F32)
    final_grads[...] = jnp.zeros_like(final_grads)

    def finish(step):
        for g in range(total // TILE):
            xhat, scale = normalized(hidden[2, g * TILE : (g + 1) * TILE, :].astype(F32))
            result[g * step : g * step + TILE, :] = xhat * final_gain[...] + final_bias[...]
            arriving = cot[g * step : g * step + TILE, :]
            if step < TILE:
                line = lax.broadcasted_iota(jnp.int32, (TILE, 1), 0)
                arriving = jnp.where(line < step, arriving, 0.0)
            back, gain_sum, bias_sum = norm_back(arriving, xhat, scale, final_gain[...])
            grad[g * TILE : (g + 1) * TILE, :] = back.astype(BF)
            final_grads[0:1, :] += gain_sum
            final_grads[1:2, :] += bias_sum

    @pl.when(stride == TILE)
    def _():
        finish(LONG_STEPS * 6)

    @pl.when(stride != TILE)
    def _():
        finish(TILE)

    saves["out"] = fetch(result.at[pl.ds(0, real)], activations, result_sem)
    grad_middle = cot
    mlp_data_back(
        1, None, grad, grad_middle, grad_mixed, vectors, wide, slope, up_v.at[1], down_v.at[1], out_v.at[1], middle,
        normed_two, grad_pre, rounded, gain2, bias2,
    )
    save("grad_middle", grad_middle, grad_middle_out)
    save("grad_mixed", grad_mixed, grad_mixed_out)
    saves["parts"] = mlp_weight_back(
        core, places, (), mine, theirs, grad, act, mixed.at[inside], normed_two, grad_pre, rounded,
        (mine_out, theirs_out, part_sem),
    )
    for copy in saves.values():
        copy.wait()


def mlp_data_back(depth, loads, grad, grad_middle, grad_mixed, vectors, wide, slope_v, up_v, down_v, out_v, middle_v, normed, grad_pre, rounded, gain2, bias2):
    total, width = grad.shape
    hidden_units = grad_pre.shape[1]
    vectors[...] = jnp.zeros_like(vectors)
    wide[...] = jnp.zeros_like(wide)
    if loads:
        down, slopes, up, mid, out = loads
        down.wait()
    for m in range(total // ROWS):
        rows = slice(m * ROWS, (m + 1) * ROWS)
        g = grad[rows, :]
        if loads:
            slopes[m].wait()
        if loads and m == 0:
            up.wait()
        back = jnp.zeros((ROWS, width), F32)
        ahead = product(g, down_v[:CHUNK, :], NT)
        for f in range(0, hidden_units, CHUNK):
            grad_act = ahead
            if f + CHUNK < hidden_units:
                ahead = product(g, down_v[f + CHUNK : f + 2 * CHUNK, :], NT)
            pre = (grad_act * slope_v[rows, f : f + CHUNK].astype(F32)).astype(BF)
            grad_pre[rows, f : f + CHUNK] = pre
            wide[0:1, f : f + CHUNK] += jnp.sum(pre.astype(F32), axis=0, keepdims=True)
            back = back + product(pre, up_v[:, f : f + CHUNK], NT)
        if loads and m == 0:
            mid.wait()
            out.wait()
        xhat, scale = normalized(middle_v[rows, :])
        if loads:
            normed[rows, :] = (xhat * gain2[depth : depth + 1, :] + bias2[depth : depth + 1, :]).astype(BF)
        through, gain_sum, bias_sum = norm_back(back, xhat, scale, gain2[depth : depth + 1, :])
        g = g.astype(F32)
        total_grad = g + through
        grad_middle[rows, :] = total_grad
        r = total_grad.astype(BF)
        rounded[rows, :] = r
        vectors[0:1, :] += gain_sum
        vectors[1:2, :] += bias_sum
        vectors[2:3, :] += jnp.sum(g, axis=0, keepdims=True)
        vectors[3:4, :] += jnp.sum(r.astype(F32), axis=0, keepdims=True)
        grad_mixed[rows, :] = product(r, out_v[...], NT).astype(BF)


def store_units(out, at, value, which, places):
    width = value.shape[1]
    if places is None:
        out[:, at : at + width] = value.astype(BF)
        return
    first, second = places
    rows = value.shape[0] // len(first)
    for unit in range(len(first)):
        place = first[unit] + which * (second[unit] - first[unit])
        out[pl.ds(pl.multiple_of(place * rows, rows), rows), at : at + width] = value[unit * rows : (unit + 1) * rows].astype(BF)


class Several:
    def __init__(self, copies):
        self.copies = copies

    def wait(self):
        for copy in self.copies:
            copy.wait()


def mlp_weight_back(core, places, loads, mine, theirs, grad, act_v, mixed_v, normed, grad_pre, rounded, outside=None):
    width = grad.shape[1]
    half = grad_pre.shape[1] // 2
    copies = []
    normed_turned = normed[...].T
    grad_turned = grad[...].T

    def made(part, at, size):
        if outside:
            cols = pl.ds(at, size)
            copies.append(fetch((mine, theirs)[part].at[:, cols], outside[part].at[:, cols], outside[2].at[len(copies)]))

    for part in range(2):
        out = (mine, theirs)[part]
        which = core if part == 0 else 1 - core
        for at in range(0, half, CHUNK):
            cols = pl.ds(pl.multiple_of(which * half + at, CHUNK), CHUNK)
            store_units(out, at, product(normed_turned, grad_pre[:, cols]), which, places)
        made(part, 0, half)
        if part == 0:
            for load in loads:
                load.wait()
        for at in range(0, half, CHUNK):
            cols = pl.ds(pl.multiple_of(which * half + at, CHUNK), CHUNK)
            store_units(out, half + at, product(grad_turned, act_v[:, cols]), which, places)
        made(part, half, half)
        cols = pl.ds(pl.multiple_of(which * (width // 2), width // 2), width // 2)
        store_units(out, 2 * half, product(mixed_v[...], rounded[:, cols], TN), which, places)
        made(part, 2 * half, width // 2)
    return Several(copies)


def mlp_loads(depth, slope, up_w, down_w, middle, out_w, slope_v, up_v, down_v, middle_v, out_v, sems, tile_sems):
    tiles = slope_v.shape[0] // ROWS

    def slope_tile(m):
        rows = pl.ds(m * ROWS, ROWS)
        return fetch(slope.at[rows], slope_v.at[rows], tile_sems.at[m])

    down = fetch(down_w.at[depth], down_v, sems.at[0])
    slopes = [slope_tile(0)]
    up = fetch(up_w.at[depth], up_v, sems.at[1])
    mid = fetch(middle, middle_v, sems.at[2])
    out = fetch(out_w.at[depth], out_v, sems.at[3])
    slopes += [slope_tile(m) for m in range(1, tiles)]
    return down, slopes, up, mid, out


def mlp_data_kernel(depth, tokens, grad, middle, slope, up_w, down_w, out_w, gain2, bias2, *rest):
    (grad_middle, grad_mixed, vectors, wide, normed, grad_pre, rounded,
     slope_v, up_v, down_v, out_v, middle_v, sems, tile_sems) = rest[tokens:]
    loads = mlp_loads(depth, slope, up_w, down_w, middle, out_w, slope_v, up_v, down_v, middle_v, out_v, sems, tile_sems)
    mlp_data_back(
        depth, loads, grad, grad_middle, grad_mixed, vectors, wide, slope_v, up_v, down_v, out_v, middle_v, normed,
        grad_pre, rounded, gain2, bias2,
    )


def mlp_weight_kernel(depth, tokens, places, scalars, grad, act, mixed, normed, grad_pre, rounded, *rest):
    mine, theirs, act_v, mixed_v, normed_v, pre_v, rounded_v, sems = rest[tokens:]
    first = [fetch(normed, normed_v, sems.at[0]), fetch(grad_pre, pre_v, sems.at[1])]
    later = [
        fetch(act, act_v, sems.at[2]), fetch(mixed, mixed_v, sems.at[3]),
        fetch(rounded, rounded_v, sems.at[4]),
    ]
    for load in first:
        load.wait()
    mlp_weight_back(scalars[1], places, later, mine, theirs, grad, act_v, mixed_v, normed_v, pre_v, rounded_v)


def attention_backward(qkv, probs, grad_mixed, grad_qkv, stride, windows, width, whole=None, at=0):
    whole = whole or width
    low, high = lane_halves()

    @pl.loop(0, windows // PER)
    def _(step):
        units = [(n, pair) for n in range(PER) for pair in range(width // TILE)]
        rows = [pl.ds(pl.multiple_of((PER * step + n) * stride, 32), TILE) for n in range(PER)]
        kept = [pl.ds(pl.multiple_of((PER * step + n) * 2 * TILE, 2 * TILE), 2 * TILE) for n in range(PER)]
        count = range(len(units))
        cut = lambda k, n, pair: qkv[rows[n], k * width + pair * TILE : k * width + (pair + 1) * TILE]
        arriving = [both_heads(grad_mixed[rows[n], pair * TILE : (pair + 1) * TILE], low, high) for n, pair in units]
        grad_p = [product(arriving[i], cut(2, *units[i]), NT) for i in count]
        p = [probs[pair, kept[n], :] for n, pair in units]
        grad_v = [product(p[i], arriving[i], TN) for i in count]
        inner = [jnp.sum(grad_p[i] * p[i].astype(F32), axis=-1, keepdims=True) for i in count]
        grad_s = [(p[i].astype(F32) * (grad_p[i] - inner[i])).astype(BF) for i in count]
        grad_q = [product(side_by_side(grad_s[i]), both_heads(cut(1, *units[i]), low, high)) * 0.125 for i in count]
        grad_k = [product(grad_s[i], both_heads(cut(0, *units[i]), low, high), TN) for i in count]
        for k, grads in enumerate((grad_q, grad_k, grad_v)):
            for (n, pair), value in zip(units, grads):
                start = k * whole + at + pair * TILE
                grad_qkv[rows[n], start : start + TILE] = value.astype(BF)


def qkv_back(depth, core, places, grad_qkv, hidden_v, middle_v, weight_v, gain1, bias1, grad_in, normed, vectors, mine, theirs):
    total, width = hidden_v.shape

    @pl.loop(0, total // ROWS)
    def _(m):
        rows = row_tile(m)
        back = jnp.zeros((ROWS, width), F32)
        for f in range(0, 3 * width, width):
            back = back + product(grad_qkv[rows, f : f + width], weight_v[:, f : f + width], NT)
        xhat, scale = normalized(hidden_v[rows, :].astype(F32))
        normed[rows, :] = (xhat * gain1[depth : depth + 1, :] + bias1[depth : depth + 1, :]).astype(BF)
        through, gain_sum, bias_sum = norm_back(back, xhat, scale, gain1[depth : depth + 1, :])
        grad_in[rows, :] = (middle_v[rows, :] + through).astype(BF)
        vectors[0:1, :] += gain_sum
        vectors[1:2, :] += bias_sum
        vectors[2:3, :] += jnp.sum(grad_qkv[rows, :width].astype(F32), axis=0, keepdims=True)
        vectors[3:4, :] += jnp.sum(grad_qkv[rows, 2 * width :].astype(F32), axis=0, keepdims=True)

    half = 3 * width // 2
    for part in range(2):
        which = core if part == 0 else 1 - core
        cols = pl.ds(pl.multiple_of(which * half, half), half)
        store_units((mine, theirs)[part], 0, product(normed[...], grad_qkv[:total, cols], TN), which, places)


def attention_load(depth, qkv, probs, grad_mixed, qkv_v, probs_v, mixed_v, sems):
    total = grad_mixed.shape[0]
    loads = [
        fetch(qkv.at[depth], qkv_v.at[pl.ds(0, total)], sems.at[0]),
        fetch(grad_mixed, mixed_v.at[pl.ds(0, total)], sems.at[1]),
        fetch(probs.at[depth], probs_v, sems.at[2]),
    ]
    qkv_v[total:, :] = jnp.zeros((qkv_v.shape[0] - total, qkv_v.shape[1]), BF)
    mixed_v[total:, :] = jnp.zeros((mixed_v.shape[0] - total, mixed_v.shape[1]), BF)
    return loads


def attention_back_kernel(
    depth, tokens, places, scalars, hidden, qkv, probs, grad_mixed, grad_middle, qkv_w, gain1, bias1, *rest,
):
    (mine, theirs, grad_in, vectors,
     hidden_v, middle_v, weight_v, normed, qkv_v, probs_v, mixed_v, grad_qkv, sems) = rest[tokens:]
    loads = attention_load(depth, qkv, probs, grad_mixed, qkv_v, probs_v, mixed_v, sems)
    later = [
        fetch(qkv_w.at[depth], weight_v, sems.at[3]),
        fetch(hidden.at[depth], hidden_v, sems.at[4]),
        fetch(grad_middle, middle_v, sems.at[5]),
    ]
    vectors[...] = jnp.zeros_like(vectors)
    for load in loads:
        load.wait()
    attention_backward(qkv_v, probs_v, mixed_v, grad_qkv, *placed(scalars, grad_in.shape[0]), grad_in.shape[1])
    for load in later:
        load.wait()
    qkv_back(
        depth, scalars[1], places, grad_qkv, hidden_v, middle_v, weight_v, gain1, bias1, grad_in, normed, vectors, mine,
        theirs,
    )


def part_loads(depth, part, parts, qkv, probs, grad_mixed, qkv_v, probs_v, mixed_v, sems):
    total, whole = grad_mixed.shape
    width = whole // parts
    pairs = probs_v.shape[0]
    inside = pl.ds(0, total)
    loads = [
        fetch(qkv.at[depth, :, pl.ds(k * whole + part * width, width)], qkv_v.at[inside, pl.ds(k * width, width)], sems.at[k])
        for k in range(3)
    ]
    loads.append(fetch(grad_mixed.at[:, pl.ds(part * width, width)], mixed_v.at[inside], sems.at[3]))
    loads.append(fetch(probs.at[depth, pl.ds(part * pairs, pairs)], probs_v, sems.at[4]))
    qkv_v[total:, :] = jnp.zeros((qkv_v.shape[0] - total, qkv_v.shape[1]), BF)
    mixed_v[total:, :] = jnp.zeros((mixed_v.shape[0] - total, mixed_v.shape[1]), BF)
    return loads


def attention_part_kernel(depth, part, parts, tokens, scalars, qkv, probs, grad_mixed, *rest):
    out, qkv_v, probs_v, mixed_v, grad_qkv, sems, out_sem = rest[tokens:]
    total, whole = grad_mixed.shape
    for load in part_loads(depth, part, parts, qkv, probs, grad_mixed, qkv_v, probs_v, mixed_v, sems):
        load.wait()
    attention_backward(qkv_v, probs_v, mixed_v, grad_qkv, *placed(scalars, total), whole // parts)
    fetch(grad_qkv.at[pl.ds(0, total)], out, out_sem).wait()


def table_kernel(
    depth, tokens, places, groups, scalars, qkv, probs, grad_mixed, grad_low, hidden, grad_middle, qkv_w, gain1, bias1,
    index, final_grads, feed1, wide1, attend1, feed0, wide0, *rest,
):
    (mine, theirs, frame_grad, grad_in, turned, vectors, stage, hidden_v, normed, grad_qkv, weight_v, middle_v,
     qkv_v, probs_v, mixed_v, sems, part_sems) = rest[tokens:]
    total, width = grad_in.shape
    half = width // 2
    first = part_loads(depth, 1, 2, qkv, probs, grad_mixed, qkv_v, probs_v, mixed_v, part_sems)
    inside = pl.ds(0, total)
    loads = [
        fetch(grad_low.at[:, pl.ds(k * half, half)], grad_qkv.at[inside, pl.ds(k * width, half)], sems.at[k])
        for k in range(3)
    ]
    loads.append(fetch(qkv_w.at[depth], weight_v, sems.at[3]))
    loads.append(fetch(hidden.at[depth], hidden_v, sems.at[4]))
    loads.append(fetch(grad_middle, middle_v, sems.at[5]))
    core = scalars[1]
    steps = frame_grad.shape[0]
    qkv_width = 3 * width // 2
    code_width = mine.shape[1] - qkv_width - TILE
    vectors[...] = jnp.zeros_like(vectors)
    for load in first:
        load.wait()
    attention_backward(qkv_v, probs_v, mixed_v, grad_qkv, *placed(scalars, total), half, width, half)
    for load in loads:
        load.wait()
    qkv_back(
        depth, core, places, grad_qkv, hidden_v, middle_v, weight_v, gain1, bias1, grad_in, normed, vectors, mine, theirs,
    )

    stage[...] = jnp.zeros_like(stage)
    for k, block in enumerate((feed0, vectors, feed1, attend1, final_grads)):
        stage[VECTORS + 8 * k : VECTORS + 8 * k + 8, :] = block[...]
    each = width // groups
    for k, wide in enumerate((wide0, wide1)):
        for group in range(groups):
            for c in range(4):
                start = group * 4 * each + c * each
                at = VECTORS + 40 + 8 * k + c
                stage[at : at + 1, group * each : group * each + each] = wide[0:1, start : start + each]

    turned[...] = grad_in[...].T
    for part in range(2):
        out = (mine, theirs)[part]
        which = core if part == 0 else 1 - core
        line = lax.broadcasted_iota(jnp.int32, (code_width, total), 0) + which * code_width
        hot = (line == index[0:1, :]).astype(F32).astype(BF)
        store_units(out, qkv_width, product(turned[...], hot, NT), which, places)
        line = lax.broadcasted_iota(jnp.int32, (TILE, total), 0) + which * TILE
        hot = ((line == index[1:2, :]) | (line == index[2:3, :])).astype(F32).astype(BF)
        small = product(turned[...], hot, NT) + stage[...].T * which.astype(F32)
        store_units(out, qkv_width + code_width, small, which, places)
    hot = (lax.broadcasted_iota(jnp.int32, (steps, total), 0) == index[3:4, :]).astype(F32).astype(BF)
    frame_grad[...] = product(hot, grad_in[...])


def output_kernel(where, scalars, *refs):
    count = 1 + max(chunk for chunk, _ in where.values())
    sources = refs[: 2 * count]
    (code, action, position, gain1, bias1, qkv, query, value, out, out_bias, gain2, bias2, up, up_bias, down, down_bias,
     final_gain, final_bias) = refs[2 * count : -1]
    square = refs[-1]
    rows, units = up.shape[1:]
    half = units // 2
    small = qkv.shape[2] // 2 + code.shape[1] // 2

    def emit(own):
        def part(name, core, across, start, size):
            chunk, at = where[name]
            lines = slice((across ^ (own >> 1)) * rows // 2, ((across ^ (own >> 1)) + 1) * rows // 2)
            return sources[2 * chunk + (core ^ (own & 1))][lines, at + start : at + start + size].astype(F32)

        def place(target, name, start):
            size = target.shape[-1] // 2
            for across in range(2):
                lines = slice(across * rows // 2, (across + 1) * rows // 2)
                for core in range(2):
                    target[lines, core * size : (core + 1) * size] = part(name, core, across, start, size)

        for depth in range(2):
            place(up.at[depth], ("feed", depth), 0)
            place(down.at[depth], ("feed", depth), half)
            place(out.at[depth], ("feed", depth), units)
            place(qkv.at[depth], ("attend", depth), 0)
        place(code, ("attend", 0), qkv.shape[2] // 2)
        square[...] = jnp.zeros_like(square)
        for across in range(2):
            lines = slice(across * rows // 2, (across + 1) * rows // 2)
            position[lines, :] = part(("attend", 0), 0, across, small, TILE)[:, : position.shape[1]]
            square[lines, :] = part(("attend", 0), 1, across, small, TILE)
        lines = square[...].T[:, :rows]
        action[...] = lines[: action.shape[0]]

        def line(k):
            return lines[VECTORS + k : VECTORS + k + 1]

        for depth in range(2):
            at = slice(depth, depth + 1)
            base = 16 * depth
            for k, target in enumerate((gain2, bias2, down_bias, out_bias)):
                target[at, :] = line(base + k)
            for k, target in enumerate((gain1, bias1, query, value)):
                target[at, :] = line(base + 8 + k)
            for c in range(4):
                up_bias[at, c * rows : (c + 1) * rows] = line(40 + 8 * depth + c)
        final_gain[...] = line(32)
        final_bias[...] = line(33)

    for own in range(4):
        pl.when(scalars[scalars.shape[0] - 1] == own)(partial(emit, own))


VMEM = pl.BlockSpec(memory_space=pltpu.VMEM)
ANY = pl.BlockSpec(memory_space=pl.ANY)
SMEM = pl.BlockSpec(memory_space=pltpu.SMEM)


def cost(flops, moved, others=0):
    return pl.CostEstimate(flops=int(8 * flops), bytes_accessed=int(moved), transcendentals=int(others))


def run_forward(places, scalars, actions, deltas, frames, codebook, action_table, position_table, layers, finals, cotangent):
    gain1, bias1, qkv_w, query_bias, value_bias, out_w, out_bias, gain2, bias2, up_w, up_bias, down_w, down_bias = layers
    width = codebook.shape[1]
    units = up_bias.shape[1]
    real = cotangent.shape[1]
    total = -(-real // ROWS) * ROWS
    reach = total + TILE + 32
    columns = units + width // 2
    shape = jax.ShapeDtypeStruct
    once = dict(pipeline_mode=pl.Buffered(1))
    whole = lambda a: pl.BlockSpec(a.shape, lambda i, s, n=a.ndim: (0,) * n, **once)
    mine = lambda a: pl.BlockSpec((1,) + a.shape[1:], lambda i, s: (s[0], 0, 0), **once)
    kept = (width // TILE, WINDOWS * 2 * TILE, TILE)
    outs = [
        (shape((real, width), F32), ANY),
        (shape((8, total), jnp.int32), None),
        (shape((8, width), F32), None), (shape((8, width), F32), None), (shape((8, units), F32), None),
        (shape((2, total, width), BF), ANY),
        (shape((2, total, 3 * width), BF), ANY),
        (shape((2,) + kept, BF), ANY),
        (shape((total, width), BF), ANY),
        (shape((total, width), F32), ANY),
        (shape((total, units), BF), ANY),
        (shape((total, units), BF), ANY),
        (shape((total, width), F32), ANY), (shape((total, width), BF), ANY),
        (shape((width, columns), BF), ANY), (shape((width, columns), BF), ANY),
    ]
    args = [
        (actions, None), (deltas, mine(deltas)), (frames, mine(frames)),
        (codebook, None), (action_table, None), (position_table, None),
        (gain1, None), (bias1, None), (qkv_w, ANY), (query_bias, None), (value_bias, None), (out_w, ANY),
        (out_bias, None), (gain2, None), (bias2, None), (up_w, ANY), (up_bias, None), (down_w, ANY), (down_bias, None),
        (finals[0][None], None), (finals[1][None], None), (cotangent, mine(cotangent)),
    ]
    scratch = [
        pltpu.VMEM((2 * TILE, width), BF),
        pltpu.VMEM(qkv_w.shape, BF), pltpu.VMEM(out_w.shape, BF), pltpu.VMEM(up_w.shape, BF), pltpu.VMEM(down_w.shape, BF),
        pltpu.VMEM((3, total, width), BF), pltpu.VMEM((reach, 3 * width), BF), pltpu.VMEM(kept, BF),
        pltpu.VMEM((reach, width), BF), pltpu.VMEM((total, width), F32),
        pltpu.VMEM((total, units), BF), pltpu.VMEM((total, units), BF), pltpu.VMEM((2 * TILE, TILE), F32),
        pltpu.VMEM((total, width), F32), pltpu.VMEM((total, width), F32),
        pltpu.VMEM((total, width), BF), pltpu.VMEM((total, width), BF), pltpu.VMEM((total, width), BF),
        pltpu.VMEM((total, width), BF), pltpu.VMEM((total, units), BF),
        pltpu.VMEM((width, columns), BF), pltpu.VMEM((width, columns), BF),
        pltpu.SemaphoreType.DMA((2, 4)), pltpu.SemaphoreType.DMA((16,)), pltpu.SemaphoreType.DMA((2, total // ROWS)),
        pltpu.SemaphoreType.DMA, pltpu.SemaphoreType.DMA((6,)),
    ]
    return pl.pallas_call(
        partial(forward_kernel, places),
        out_shape=[o for o, _ in outs],
        grid_spec=pltpu.PrefetchScalarGridSpec(
            num_scalar_prefetch=1,
            grid=(1,),
            in_specs=[spec or whole(a) for a, spec in args],
            out_specs=[spec or whole(o) for o, spec in outs],
            scratch_shapes=scratch,
        ),
        compiler_params=pltpu.CompilerParams(vmem_limit_bytes=62 << 20),
        cost_estimate=cost(24e9, 50e6, 4e6),
        name="forward",
    )(scalars, *[a for a, _ in args])


def run_mlp_data(depth, grad, saved, layers, after):
    hidden, qkv, probs, mixed, middle, act, slope = saved
    gain1, bias1, qkv_w, query_bias, value_bias, out_w, out_bias, gain2, bias2, up_w, up_bias, down_w, down_bias = layers
    total, width = grad.shape
    units = up_bias.shape[1]
    shape = jax.ShapeDtypeStruct
    return pl.pallas_call(
        partial(mlp_data_kernel, depth, len(after)),
        out_shape=[
            shape((total, width), F32), shape((total, width), BF), shape((8, width), F32), shape((8, units), F32),
            shape((total, width), BF), shape((total, units), BF), shape((total, width), BF),
        ],
        in_specs=[VMEM] + [ANY] * 5 + [VMEM] * 2 + [ANY] * len(after),
        out_specs=[VMEM] * 7,
        scratch_shapes=[
            pltpu.VMEM((total, units), BF),
            pltpu.VMEM((width, units), BF), pltpu.VMEM((units, width), BF), pltpu.VMEM((width, width), BF),
            pltpu.VMEM((total, width), F32),
            pltpu.SemaphoreType.DMA((4,)), pltpu.SemaphoreType.DMA((total // ROWS,)),
        ],
        compiler_params=pltpu.CompilerParams(vmem_limit_bytes=40 << 20),
        cost_estimate=cost(10e9, 16e6),
        name="mlp_data",
    )(grad, middle, slope, up_w, down_w, out_w, gain2, bias2, *after)


def run_mlp_weight(depth, places, scalars, grad, saved, normed, grad_pre, rounded, after):
    hidden, qkv, probs, mixed, middle, act, slope = saved
    total, width = grad.shape
    units = grad_pre.shape[1]
    shape = jax.ShapeDtypeStruct
    return pl.pallas_call(
        partial(mlp_weight_kernel, depth, len(after), places),
        out_shape=[shape((width, units + width // 2), BF), shape((width, units + width // 2), BF)],
        in_specs=[SMEM, VMEM] + [ANY] * 5 + [ANY] * len(after),
        out_specs=[VMEM] * 2,
        scratch_shapes=[
            pltpu.VMEM((total, units), BF), pltpu.VMEM((total, width), BF), pltpu.VMEM((total, width), BF),
            pltpu.VMEM((total, units), BF), pltpu.VMEM((total, width), BF),
            pltpu.SemaphoreType.DMA((5,)),
        ],
        compiler_params=pltpu.CompilerParams(vmem_limit_bytes=40 << 20),
        cost_estimate=cost(8e9, 16e6),
        name="mlp_weight",
    )(scalars, grad, act, mixed, normed, grad_pre, rounded, *after)


def window_scratch(total, width, probs):
    reach = total + TILE + 32
    return [
        pltpu.VMEM((reach, 3 * width), BF), pltpu.VMEM(probs.shape[1:], BF),
        pltpu.VMEM((reach, width), BF), pltpu.VMEM((reach, 3 * width), BF),
    ]


def run_attention_back(depth, places, scalars, grad_mixed, grad_middle, saved, layers, after):
    hidden, qkv, probs, mixed, middle, act, slope = saved
    gain1, bias1, qkv_w = layers[:3]
    total, width = grad_mixed.shape
    shape = jax.ShapeDtypeStruct
    return pl.pallas_call(
        partial(attention_back_kernel, depth, len(after), places),
        out_shape=[
            shape((width, 3 * width // 2), BF), shape((width, 3 * width // 2), BF),
            shape((total, width), BF), shape((8, width), F32),
        ],
        in_specs=[SMEM] + [ANY] * 6 + [VMEM] * 2 + [ANY] * len(after),
        out_specs=[VMEM] * 4,
        scratch_shapes=[
            pltpu.VMEM((total, width), BF), pltpu.VMEM((total, width), F32), pltpu.VMEM(qkv_w.shape[1:], BF),
            pltpu.VMEM((total, width), BF), *window_scratch(total, width, probs),
            pltpu.SemaphoreType.DMA((6,)),
        ],
        compiler_params=pltpu.CompilerParams(vmem_limit_bytes=50 << 20),
        cost_estimate=cost(16e9, 24e6),
        name="attention_back",
    )(scalars, hidden, qkv, probs, grad_mixed, grad_middle, qkv_w, gain1, bias1, *after)


def run_attention_part(depth, part, parts, scalars, grad_mixed, saved, after):
    hidden, qkv, probs, mixed, middle, act, slope = saved
    total, width = grad_mixed.shape
    width = width // parts
    reach = total + TILE + 32
    return pl.pallas_call(
        partial(attention_part_kernel, depth, part, parts, len(after)),
        out_shape=jax.ShapeDtypeStruct((total, 3 * width), BF),
        in_specs=[SMEM] + [ANY] * 3 + [ANY] * len(after),
        out_specs=ANY,
        scratch_shapes=[
            pltpu.VMEM((reach, 3 * width), BF), pltpu.VMEM((width // TILE,) + probs.shape[2:], BF),
            pltpu.VMEM((reach, width), BF), pltpu.VMEM((reach, 3 * width), BF),
            pltpu.SemaphoreType.DMA((5,)), pltpu.SemaphoreType.DMA,
        ],
        compiler_params=pltpu.CompilerParams(vmem_limit_bytes=VMEM_PART << 20),
        cost_estimate=cost(8e9, 8e6),
        name="attention_part",
    )(scalars, qkv, probs, grad_mixed, *after)


def run_table(depth, places, scalars, grad_mixed, grad_low, grad_middle, saved, layers, index, vectors, codes, steps, groups, after):
    hidden, qkv, probs, mixed, middle, act, slope = saved
    gain1, bias1, qkv_w = layers[:3]
    total, width = grad_middle.shape
    reach = total + TILE + 32
    columns = 3 * width // 2 + codes // 2 + TILE
    shape = jax.ShapeDtypeStruct
    return pl.pallas_call(
        partial(table_kernel, depth, len(after), places, groups),
        out_shape=[shape((width, columns), BF), shape((width, columns), BF), shape((steps, width), F32)],
        in_specs=[SMEM] + [ANY] * 7 + [VMEM] * 2 + [VMEM] * 7 + [ANY] * len(after),
        out_specs=[VMEM] * 3,
        scratch_shapes=[
            pltpu.VMEM((total, width), BF), pltpu.VMEM((width, total), BF), pltpu.VMEM((8, width), F32),
            pltpu.VMEM((TILE, width), F32), pltpu.VMEM((total, width), BF), pltpu.VMEM((total, width), BF),
            pltpu.VMEM((reach, 3 * width), BF), pltpu.VMEM(qkv_w.shape[1:], BF), pltpu.VMEM((total, width), F32),
            pltpu.VMEM((reach, 3 * width // 2), BF), pltpu.VMEM((probs.shape[1] // 2,) + probs.shape[2:], BF),
            pltpu.VMEM((reach, width // 2), BF),
            pltpu.SemaphoreType.DMA((6,)), pltpu.SemaphoreType.DMA((5,)),
        ],
        compiler_params=pltpu.CompilerParams(vmem_limit_bytes=40 << 20),
        cost_estimate=cost(12e9, 12e6),
        name="tables",
    )(scalars, qkv, probs, grad_mixed, grad_low, hidden, grad_middle, qkv_w, gain1, bias1, index, *vectors, *after)


def run_output(where, scalars, sources, width, units, codes, actions, positions):
    rows = sources[0].shape[0]
    wide, line = (2, rows), (1, rows)
    shapes = [
        (rows, codes), (actions, rows), (rows, positions), wide, wide, (2, rows, 3 * width), wide, wide, (2, rows, width),
        wide, wide, wide, (2, rows, units), (2, 4 * rows), (2, rows, units), wide, line, line,
    ]
    return pl.pallas_call(
        partial(output_kernel, where),
        out_shape=[jax.ShapeDtypeStruct(s, F32) for s in shapes],
        in_specs=[SMEM] + [VMEM] * len(sources),
        out_specs=[VMEM] * len(shapes),
        scratch_shapes=[pltpu.VMEM((TILE, TILE), F32)],
        compiler_params=pltpu.CompilerParams(vmem_limit_bytes=30 << 20),
        cost_estimate=cost(1e6, 6e6),
        name="outputs",
    )(scalars, *sources)


def meet(array, axis, by):
    size = lax.axis_size(axis)
    return lax.ppermute(array, axis, [(i, i ^ by) for i in range(size)])


def swap(array, axis, bit):
    return meet(array, axis, 1 << bit)


def bits_of(axis):
    return lax.axis_size(axis).bit_length() - 1


def own_bit(axis, bit):
    return (lax.axis_index(axis) >> bit) & 1


def take(array, dim, which):
    return lax.dynamic_index_in_dim(array, which, dim, keepdims=False)


def total_of(terms):
    return sum(term.astype(F32) for term in terms)


def settled(array):
    return lax.optimization_barrier(array.astype(BF))


def tied(array, token):
    return lax.optimization_barrier((array, token))[0]


def unit_places(count):
    first, second = [], []
    for unit in range(2 << count):
        bits = [(unit >> (1 + bit)) & 1 for bit in range(count)]
        for order, places in ((bits + [unit & 1], first), ([unit & 1] + bits, second)):
            place = 0
            for bit in order:
                place = 2 * place + bit
            places.append(place)
    return first, second


def reordered(array, which, count):
    rows, columns = array.shape
    ways = array.reshape((2,) * (count + 1) + (rows >> (count + 1), columns))
    dims = list(range(count - 1, -1, -1))
    first = ways.transpose(dims + [count, count + 1, count + 2])
    second = ways.transpose([count] + dims + [count + 1, count + 2])
    return jnp.where(which == 0, first, second).reshape(rows, columns)


class Chunk:
    def __init__(self, places):
        self.count = bits_of("dp")
        self.places = places
        self.pieces = []
        self.terms = []
        self.core = own_bit("section", 0)

    def add(self, mine, theirs):
        if self.places is None:
            mine, theirs = reordered(mine, self.core, self.count), reordered(theirs, 1 - self.core, self.count)
        self.pieces.append([mine, swap(theirs, "section", 0)])

    def hold(self, token):
        if self.terms:
            self.terms[-1] = tied(self.terms[-1], token)
        else:
            for piece in self.pieces:
                piece[1] = tied(piece[1], token)

    def step(self):
        if not self.terms:
            self.left = self.pieces[0][0].shape[0]
        k = len(self.terms)
        bits = [own_bit("dp", bit) for bit in range(self.count)]
        across = own_bit("section", 1)
        own = jnp.where(self.core == 0, (bits + [across])[k], ([across] + bits)[k])
        half = self.left // 2
        cut = lambda t, which: lax.dynamic_slice_in_dim(t, which * half, half, 0)
        if not self.terms:
            self.parts = [[[mine, arrived] for mine, arrived in self.pieces]]
        parts = self.parts[-1]
        sum_of = jnp.concatenate([total_of([cut(t, 1 - own) for t in part]) for part in parts], axis=1)
        for term in self.terms:
            sum_of = sum_of + cut(term, 1 - own).astype(F32)
        self.sent = settled(sum_of)
        sections = lax.axis_size("section")
        pairs = []
        for source in range(lax.axis_size("dp") * sections):
            at = k if source & 1 == 0 else (k - 1) % (self.count + 1)
            bit = sections << at if at < self.count else 2
            pairs.append((source, source ^ bit))
        self.parts = [[[cut(t, own) for t in part] for part in parts]]
        self.terms = [cut(t, own) for t in self.terms] + [lax.ppermute(self.sent, ("dp", "section"), pairs)]
        self.left = half
        return self

    def across(self):
        total = jnp.concatenate([total_of(part) for part in self.parts[-1]], axis=1)
        for term in self.terms:
            total = total + term.astype(F32)
        self.sent = settled(total)
        other = swap(self.sent, "section", 1)
        self.terms = [self.sent, other]

    def finish(self):
        rows = settled(jnp.concatenate(self.terms))
        arrived = swap(rows, "section", 0)
        return [rows, arrived]


def local(
    frames, actions, deltas, kinds, codebook, action_table, position_table, norm1_gain, norm1_bias, qkv_weight,
    query_bias, value_bias, out_weight, out_bias, norm2_gain, norm2_bias, up_weight, up_bias, down_weight, down_bias,
    final_gain, final_bias, cotangent,
):
    micro, steps, width = frames.shape
    units = up_weight.shape[2]
    codes = codebook.shape[0]
    slot = lax.axis_index("section") * micro // lax.axis_size("section")
    layers = (
        norm1_gain, norm1_bias, qkv_weight, query_bias, value_bias, out_weight, out_bias, norm2_gain, norm2_bias,
        up_weight, up_bias, down_weight, down_bias,
    )
    section = lax.axis_index("section")
    scalars = jnp.concatenate([jnp.stack([slot, section & 1]), kinds, section[None]]).astype(jnp.int32)
    groups = lax.axis_size("dp")
    count = bits_of("dp")
    places = unit_places(count) if width >> (count + 1) >= 16 else None
    chunk1, chunk2, chunk3 = Chunk(places), Chunk(places), Chunk(places)
    activations, index, final_grads, feed1, wide1, *saved, middle, mixed, mine, theirs = run_forward(
        places, scalars, actions, deltas.transpose(0, 2, 1), frames, codebook, action_table, position_table,
        layers, (final_gain, final_bias), cotangent,
    )
    chunk1.add(mine, theirs)
    mine, theirs, grad, attend1 = run_attention_back(1, places, scalars, mixed, middle, saved, layers, [])
    chunk1.hold(attend1)
    chunk2.add(mine, theirs)
    chunk1.step()
    middle, mixed, feed0, wide0, normed, grad_pre, rounded = run_mlp_data(0, grad, saved, layers, [chunk1.sent])
    chunk1.hold(normed)
    chunk1.step()
    mine, theirs = run_mlp_weight(0, places, scalars, grad, saved, normed, grad_pre, rounded, [chunk1.sent])
    chunk1.hold(theirs)
    chunk2.hold(theirs)
    chunk2.add(mine, theirs)
    grad_low = run_attention_part(0, 0, 2, scalars, mixed, saved, [])
    chunk2.hold(grad_low)
    chunk2.step()
    chunk1.hold(chunk2.sent)
    chunk1.step()
    vectors = (final_grads, feed1, wide1, attend1, feed0, wide0)
    mine, theirs, frame_grad = run_table(
        0, places, scalars, mixed, grad_low, middle, saved, layers, index, vectors, codes, steps, groups,
        [chunk2.sent, chunk1.sent],
    )
    chunk3.add(mine, theirs)
    chunk2.hold(frame_grad)
    chunk1.hold(chunk2.terms[-1])
    chunk2.step()
    chunk3.hold(chunk2.sent)
    chunk3.step()
    chunk2.hold(chunk3.sent)
    chunk1.hold(chunk3.sent)
    for _ in range(3, count + 1):
        chunk1.step()
    for k in range(2, count + 3):
        if k <= count:
            chunk2.step()
        elif k == count + 1:
            chunk2.across()
        else:
            sources += chunk2.finish()
        chunk3.hold(chunk2.sent)
        if k == 2:
            chunk3.hold(chunk1.terms[-1])
            chunk1.across()
        if k == 3:
            chunk3.hold(chunk1.terms[-1])
            sources = chunk1.finish()
        if k <= count + 1:
            chunk3.step()
            chunk2.hold(chunk3.sent)
        else:
            chunk3.across()
    sources += chunk3.finish()
    split = 3 * width // 2
    where = {("feed", 1): (0, 0), ("attend", 1): (1, 0), ("feed", 0): (1, split), ("attend", 0): (2, 0)}
    (code, action, position, gain1, bias1, qkv, query, value, out, out_b, gain2, bias2, up, up_b, down, down_b, last_gain,
     last_bias) = run_output(
        where, scalars, sources, width, units, codes, action_table.shape[0], position_table.shape[0]
    )
    return (
        activations[None], frame_grad[None], code.T, action, position.T, gain1, bias1, qkv, query, value, out, out_b,
        gain2, bias2, up, up_b, down.transpose(0, 2, 1), down_b, last_gain[0], last_bias[0],
    )


def solution(mesh):
    rows, one = P("dp", None, None), P(None, "dp")
    weight = P(None, "dp", None)
    both = P(("dp", "section"), None, None)
    return jax.shard_map(
        local,
        mesh=mesh,
        in_specs=(rows, P("dp", None), rows, P("dp")) + (P(),) * 18 + (rows,),
        out_specs=(
            both, both, one, one, one, one, one, weight, one, one, weight, one, one, one, weight, one,
            P(None, None, "dp"), one, P("dp"), P("dp"),
        ),
        check_vma=False,
    )
```

```python
from functools import partial

import jax
import jax.numpy as jnp
from jax import lax
from jax.experimental import pallas as pl
from jax.experimental.pallas import tpu as pltpu
from jax.sharding import PartitionSpec as P

HEADS = 8
SHORT_STEPS = 8
LONG_STEPS = 21
EPSILON = 1e-05
MASKED = -1e30
TILE = 128
ROWS = 512
CHUNK = 512
STRIP = 256
VECTORS = 32
WINDOWS = 12
PER = 4
VMEM_PART = 58
BF = jnp.bfloat16
F32 = jnp.float32

NN = (((1,), (0,)), ((), ()))
NT = (((1,), (1,)), ((), ()))
TN = (((0,), (0,)), ((), ()))


def product(left, right, form=NN):
    return lax.dot_general(left, right, form, preferred_element_type=F32)


def normalized(x):
    center = x - jnp.mean(x, axis=-1, keepdims=True)
    spread = jnp.mean(center * center, axis=-1, keepdims=True)
    scale = lax.rsqrt(spread + EPSILON)
    return center * scale, scale


def norm_back(grad, xhat, scale, gain):
    inner = grad * gain
    first = jnp.mean(inner, axis=-1, keepdims=True)
    second = jnp.mean(inner * xhat, axis=-1, keepdims=True)
    back = (inner - first - xhat * second) * scale
    return back, jnp.sum(grad * xhat, axis=0, keepdims=True), jnp.sum(grad, axis=0, keepdims=True)


def gelu_pair(u):
    cdf = 0.5 + 0.5 * lax.erf(u * 0.7071067811865476)
    e = jnp.exp2(u * u * (-0.5 * 1.4426950408889634))
    return u * cdf, cdf + u * (e * 0.3989422804014327)


def row_tile(m):
    return pl.ds(pl.multiple_of(m * ROWS, ROWS), ROWS)


def lane_halves():
    lane = lax.broadcasted_iota(jnp.int32, (1, TILE), 1)
    low = (lane < TILE // 2).astype(F32)
    return low.astype(BF), (1.0 - low).astype(BF)


def both_heads(x, low, high):
    return jnp.concatenate([x * low, x * high], axis=0)


def side_by_side(x):
    return jnp.concatenate([x[:TILE], x[TILE:]], axis=1)


def write_mask(mask, stride):
    row = lax.broadcasted_iota(jnp.int32, (2 * TILE, TILE), 0)
    row = jnp.where(row >= TILE, row - TILE, row).astype(F32) + 0.5
    col = lax.broadcasted_iota(jnp.int32, (2 * TILE, TILE), 1).astype(F32) + 0.5
    step = jnp.floor(col * (1.0 / 6.0)) <= jnp.floor(row * (1.0 / 6.0))
    member = jnp.floor(col * (1.0 / 48.0)) == jnp.floor(row * (1.0 / 48.0))
    long = jnp.where(step, 0.0, MASKED)
    short = jnp.where(member, long, MASKED)
    mask[...] = jnp.where(stride == TILE, long, short)


def placed(scalars, total):
    long = scalars[2 + scalars[0]] == 1
    return jnp.where(long, TILE, 2 * SHORT_STEPS * 6), jnp.where(long, total // TILE, WINDOWS)


def fetch(source, target, sem):
    copy = pltpu.make_async_copy(source, target, sem)
    copy.start()
    return copy


def attention_forward(qkv, probs, mixed, mask, stride, windows, width):
    low, high = lane_halves()

    @pl.loop(0, windows // PER)
    def _(step):
        units = [(n, pair) for n in range(PER) for pair in range(width // TILE)]
        starts = [pl.multiple_of((PER * step + n) * stride, 32) for n in range(PER)]
        rows = [pl.ds(start, TILE) for start in starts]
        cut = lambda k, n, pair: qkv[rows[n], k * width + pair * TILE : k * width + (pair + 1) * TILE]
        scores = [product(both_heads(cut(0, n, pair), low, high), cut(1, n, pair), NT) + mask[...] for n, pair in units]
        shifted = [jnp.exp(s - jnp.max(s, axis=-1, keepdims=True)) for s in scores]
        p = [(s * (1.0 / jnp.sum(s, axis=-1, keepdims=True))).astype(BF) for s in shifted]
        for (n, pair), value in zip(units, p):
            kept = pl.ds(pl.multiple_of((PER * step + n) * 2 * TILE, 2 * TILE), 2 * TILE)
            probs[pair, kept, :] = value
        out = [product(side_by_side(value), both_heads(cut(2, n, pair), low, high)) for (n, pair), value in zip(units, p)]
        for (n, pair), value in zip(units, out):
            mixed[rows[n], pair * TILE : (pair + 1) * TILE] = value.astype(BF)


def build_index(index, actions, deltas, long):
    steps = actions.shape[-1]
    total = index.shape[1]
    step = lax.broadcasted_iota(jnp.int32, (steps, total), 0).astype(F32)
    start = step * 6.0 + jnp.where(long, 2.0, 0.0) * jnp.floor((step + 0.5) * (1.0 / LONG_STEPS))
    slot = lax.broadcasted_iota(jnp.int32, (steps, total), 1).astype(F32) - start
    line = lax.broadcasted_iota(jnp.int32, (8, steps), 0)

    def rows(**values):
        out = jnp.zeros((8, steps), F32)
        for name, value in values.items():
            out = jnp.where(line == int(name[1:]), value, out)
        return out.astype(BF)

    def spread(value, j):
        return product(value, (slot == float(j)).astype(F32).astype(BF))

    count = lax.broadcasted_iota(jnp.int32, (8, steps), 1).astype(F32)
    found = spread(rows(r5=count, r6=1.0), 0) + spread(rows(r3=actions.astype(F32), r4=1.0), 1)
    for j in range(deltas.shape[1]):
        code = deltas[0, j : j + 1, :].astype(F32)
        high = jnp.floor(code * (1.0 / 32.0))
        found = found + spread(rows(r0=high, r1=code - 32.0 * high, r2=1.0), 2 + j)
    found = found.astype(jnp.int32)
    none = jnp.full((1, total), -1, jnp.int32)
    row = lax.broadcasted_iota(jnp.int32, (1, total), 1)
    real = row.astype(F32) + 0.5
    apart = row - TILE * jnp.floor(real * (1.0 / TILE)).astype(jnp.int32)
    apart = jnp.where(apart < LONG_STEPS * 6, apart, none)
    close = row - SHORT_STEPS * 6 * jnp.floor(real * (1.0 / (SHORT_STEPS * 6))).astype(jnp.int32)
    close = jnp.where(row < steps * 6, close, none)
    index[0:1, :] = jnp.where(found[2:3] == 1, found[0:1] * 32 + found[1:2], none)
    index[1:2, :] = jnp.where(long, apart, close)
    index[2:3, :] = jnp.where(found[4:5] == 1, found[3:4] + TILE, none)
    index[3:4, :] = jnp.where(found[6:7] == 1, found[5:6], none)
    index[4:8, :] = jnp.full((4, total), -1, jnp.int32)


def forward_kernel(
    places, scalars, actions, deltas, frames, codebook, action_table, position_table,
    gain1, bias1, qkv_w, query_bias, value_bias, out_w, out_bias, gain2, bias2,
    up_w, up_bias, down_w, down_bias, final_gain, final_bias, cotangent,
    activations, index, final_grads, vectors, wide,
    hidden_out, qkv_out, probs_out, mixed_out, middle_out, act_out, slope_out,
    grad_middle_out, grad_mixed_out, mine_out, theirs_out,
    table, qkv_v, out_v, up_v, down_v, hidden, qkv, probs, mixed, middle, act, slope, mask, result, cot,
    grad, grad_mixed, normed_two, rounded, grad_pre, mine, theirs,
    weight_sem, save_sem, tile_sem, result_sem, part_sem,
):
    core = scalars[1]
    width = hidden.shape[-1]
    total = hidden.shape[1]
    stride, windows = placed(scalars, total)
    hidden_units = up_bias.shape[1]
    tiles = total // ROWS
    loads = []
    for depth in range(2):
        loads.append([
            fetch(qkv_w.at[depth], qkv_v.at[depth], weight_sem.at[depth, 0]),
            fetch(out_w.at[depth], out_v.at[depth], weight_sem.at[depth, 1]),
            fetch(up_w.at[depth], up_v.at[depth], weight_sem.at[depth, 2]),
            fetch(down_w.at[depth], down_v.at[depth], weight_sem.at[depth, 3]),
        ])
    write_mask(mask, stride)
    build_index(index, actions[pl.ds(scalars[0], 1), :], deltas, stride == TILE)
    positions = position_table.shape[0]
    action_count = action_table.shape[0]
    table[...] = jnp.zeros_like(table)
    table[:positions] = position_table[...]
    table[TILE : TILE + action_count] = action_table[...]
    qkv[total:, :] = jnp.zeros((qkv.shape[0] - total, qkv.shape[1]), BF)

    codes = codebook.shape[0]
    steps = frames.shape[1]

    @pl.loop(0, tiles)
    def _(m):
        rows = row_tile(m)
        code_hot = (lax.broadcasted_iota(jnp.int32, (codes, ROWS), 0) == index[0:1, rows]).astype(F32).astype(BF)
        line = lax.broadcasted_iota(jnp.int32, (2 * TILE, ROWS), 0)
        small_hot = ((line == index[1:2, rows]) | (line == index[2:3, rows])).astype(F32).astype(BF)
        frame_hot = (lax.broadcasted_iota(jnp.int32, (steps, ROWS), 0) == index[3:4, rows]).astype(F32).astype(BF)
        value = product(code_hot, codebook[...], TN) + product(small_hot, table[...], TN)
        value = value + product(frame_hot, frames[0], TN)
        hidden[0, rows, :] = value.astype(BF)

    def tile_copies(m):
        rows = row_tile(m)
        return (
            pltpu.make_async_copy(act.at[rows], act_out.at[rows], tile_sem.at[0, m]),
            pltpu.make_async_copy(slope.at[rows], slope_out.at[rows], tile_sem.at[1, m]),
        )

    saves = {}
    started = []

    def save(name, source, target):
        saves[name] = fetch(source, target, save_sem.at[len(started)])
        started.append(name)

    inside = pl.ds(0, total)
    for depth in range(2):
        save(("hidden", depth), hidden.at[depth], hidden_out.at[depth])
        loads[depth][0].wait()
        if depth:
            saves.pop(("qkv", 0)).wait()

        def normed_tile(m):
            xhat, _ = normalized(hidden[depth, m * ROWS : (m + 1) * ROWS, :].astype(F32))
            return (xhat * gain1[depth : depth + 1, :] + bias1[depth : depth + 1, :]).astype(BF)

        ready = normed_tile(0)
        for m in range(tiles):
            rows = slice(m * ROWS, (m + 1) * ROWS)
            normed = ready
            if m + 1 < tiles:
                ready = normed_tile(m + 1)
            q = product(normed, qkv_v[depth, :, :width]) + query_bias[depth : depth + 1, :]
            k = product(normed, qkv_v[depth, :, width : 2 * width])
            v = product(normed, qkv_v[depth, :, 2 * width :]) + value_bias[depth : depth + 1, :]
            qkv[rows, :width] = (q.astype(BF).astype(F32) * 0.125).astype(BF)
            qkv[rows, width : 2 * width] = k.astype(BF)
            qkv[rows, 2 * width :] = v.astype(BF)

        save(("qkv", depth), qkv.at[inside], qkv_out.at[depth])
        if depth:
            saves.pop(("probs", 0)).wait()
            saves.pop(("mixed", 0)).wait()
        attention_forward(qkv, probs, mixed, mask, stride, windows, width)
        save(("probs", depth), probs, probs_out.at[depth])
        if not depth:
            save(("mixed", depth), mixed.at[inside], mixed_out)
        for load in loads[depth][1:]:
            load.wait()
        if depth:
            saves.pop(("middle", 0)).wait()

        @pl.loop(0, tiles)
        def _(m):
            rows = row_tile(m)
            mid = hidden[depth, rows, :].astype(F32) + (
                product(mixed[rows, :], out_v[depth]) + out_bias[depth : depth + 1, :]
            )
            middle[rows, :] = mid
            xhat, _ = normalized(mid)
            normed = (xhat * gain2[depth : depth + 1, :] + bias2[depth : depth + 1, :]).astype(BF)
            if depth:
                normed_two[rows, :] = normed
                for copy in tile_copies(m):
                    copy.wait()
            parts = list(range(0, hidden_units, STRIP))
            up = lambda f: product(normed, up_v[depth, :, f : f + STRIP]) + up_bias[depth : depth + 1, f : f + STRIP]
            u = up(0)
            added = jnp.zeros((ROWS, width), F32)
            previous = None
            for f in parts:
                following = up(f + STRIP) if f + STRIP < hidden_units else None
                if previous is not None:
                    added = added + product(previous, down_v[depth, f - STRIP : f, :])
                z, d = gelu_pair(u)
                previous = z.astype(BF)
                act[rows, f : f + STRIP] = previous
                slope[rows, f : f + STRIP] = d.astype(BF)
                u = following
            added = added + product(previous, down_v[depth, hidden_units - STRIP :, :])
            hidden[depth + 1, rows, :] = (mid + (added + down_bias[depth : depth + 1, :])).astype(BF)
            if not depth:
                for copy in tile_copies(m):
                    copy.start()

        if not depth:
            save(("middle", depth), middle, middle_out)

    real = cotangent.shape[1]
    cot[:real] = cotangent[0].astype(F32)
    cot[real:] = jnp.zeros((cot.shape[0] - real, width), F32)
    final_grads[...] = jnp.zeros_like(final_grads)

    def finish(step):
        for g in range(total // TILE):
            xhat, scale = normalized(hidden[2, g * TILE : (g + 1) * TILE, :].astype(F32))
            result[g * step : g * step + TILE, :] = xhat * final_gain[...] + final_bias[...]
            arriving = cot[g * step : g * step + TILE, :]
            if step < TILE:
                line = lax.broadcasted_iota(jnp.int32, (TILE, 1), 0)
                arriving = jnp.where(line < step, arriving, 0.0)
            back, gain_sum, bias_sum = norm_back(arriving, xhat, scale, final_gain[...])
            grad[g * TILE : (g + 1) * TILE, :] = back.astype(BF)
            final_grads[0:1, :] += gain_sum
            final_grads[1:2, :] += bias_sum

    @pl.when(stride == TILE)
    def _():
        finish(LONG_STEPS * 6)

    @pl.when(stride != TILE)
    def _():
        finish(TILE)

    saves["out"] = fetch(result.at[pl.ds(0, real)], activations, result_sem)
    grad_middle = cot
    mlp_data_back(
        1, None, grad, grad_middle, grad_mixed, vectors, wide, slope, up_v.at[1], down_v.at[1], out_v.at[1], middle,
        normed_two, grad_pre, rounded, gain2, bias2,
    )
    save("grad_middle", grad_middle, grad_middle_out)
    save("grad_mixed", grad_mixed, grad_mixed_out)
    saves["parts"] = mlp_weight_back(
        core, places, (), mine, theirs, grad, act, mixed.at[inside], normed_two, grad_pre, rounded,
        (mine_out, theirs_out, part_sem),
    )
    for copy in saves.values():
        copy.wait()


def mlp_data_back(depth, loads, grad, grad_middle, grad_mixed, vectors, wide, slope_v, up_v, down_v, out_v, middle_v, normed, grad_pre, rounded, gain2, bias2):
    total, width = grad.shape
    hidden_units = grad_pre.shape[1]
    vectors[...] = jnp.zeros_like(vectors)
    wide[...] = jnp.zeros_like(wide)
    if loads:
        down, slopes, up, mid, out = loads
        down.wait()
    for m in range(total // ROWS):
        rows = slice(m * ROWS, (m + 1) * ROWS)
        g = grad[rows, :]
        if loads:
            slopes[m].wait()
        if loads and m == 0:
            up.wait()
        back = jnp.zeros((ROWS, width), F32)
        ahead = product(g, down_v[:CHUNK, :], NT)
        for f in range(0, hidden_units, CHUNK):
            grad_act = ahead
            if f + CHUNK < hidden_units:
                ahead = product(g, down_v[f + CHUNK : f + 2 * CHUNK, :], NT)
            pre = (grad_act * slope_v[rows, f : f + CHUNK].astype(F32)).astype(BF)
            grad_pre[rows, f : f + CHUNK] = pre
            wide[0:1, f : f + CHUNK] += jnp.sum(pre.astype(F32), axis=0, keepdims=True)
            back = back + product(pre, up_v[:, f : f + CHUNK], NT)
        if loads and m == 0:
            mid.wait()
            out.wait()
        xhat, scale = normalized(middle_v[rows, :])
        if loads:
            normed[rows, :] = (xhat * gain2[depth : depth + 1, :] + bias2[depth : depth + 1, :]).astype(BF)
        through, gain_sum, bias_sum = norm_back(back, xhat, scale, gain2[depth : depth + 1, :])
        g = g.astype(F32)
        total_grad = g + through
        grad_middle[rows, :] = total_grad
        r = total_grad.astype(BF)
        rounded[rows, :] = r
        vectors[0:1, :] += gain_sum
        vectors[1:2, :] += bias_sum
        vectors[2:3, :] += jnp.sum(g, axis=0, keepdims=True)
        vectors[3:4, :] += jnp.sum(r.astype(F32), axis=0, keepdims=True)
        grad_mixed[rows, :] = product(r, out_v[...], NT).astype(BF)


def store_units(out, at, value, which, places):
    width = value.shape[1]
    if places is None:
        out[:, at : at + width] = value.astype(BF)
        return
    first, second = places
    rows = value.shape[0] // len(first)
    for unit in range(len(first)):
        place = first[unit] + which * (second[unit] - first[unit])
        out[pl.ds(pl.multiple_of(place * rows, rows), rows), at : at + width] = value[unit * rows : (unit + 1) * rows].astype(BF)


class Several:
    def __init__(self, copies):
        self.copies = copies

    def wait(self):
        for copy in self.copies:
            copy.wait()


def mlp_weight_back(core, places, loads, mine, theirs, grad, act_v, mixed_v, normed, grad_pre, rounded, outside=None):
    width = grad.shape[1]
    half = grad_pre.shape[1] // 2
    copies = []
    normed_turned = normed[...].T
    grad_turned = grad[...].T

    def made(part, at, size):
        if outside:
            cols = pl.ds(at, size)
            copies.append(fetch((mine, theirs)[part].at[:, cols], outside[part].at[:, cols], outside[2].at[len(copies)]))

    for part in range(2):
        out = (mine, theirs)[part]
        which = core if part == 0 else 1 - core
        for at in range(0, half, CHUNK):
            cols = pl.ds(pl.multiple_of(which * half + at, CHUNK), CHUNK)
            store_units(out, at, product(normed_turned, grad_pre[:, cols]), which, places)
        made(part, 0, half)
        if part == 0:
            for load in loads:
                load.wait()
        for at in range(0, half, CHUNK):
            cols = pl.ds(pl.multiple_of(which * half + at, CHUNK), CHUNK)
            store_units(out, half + at, product(grad_turned, act_v[:, cols]), which, places)
        made(part, half, half)
        cols = pl.ds(pl.multiple_of(which * (width // 2), width // 2), width // 2)
        store_units(out, 2 * half, product(mixed_v[...], rounded[:, cols], TN), which, places)
        made(part, 2 * half, width // 2)
    return Several(copies)


def mlp_loads(depth, slope, up_w, down_w, middle, out_w, slope_v, up_v, down_v, middle_v, out_v, sems, tile_sems):
    tiles = slope_v.shape[0] // ROWS

    def slope_tile(m):
        rows = pl.ds(m * ROWS, ROWS)
        return fetch(slope.at[rows], slope_v.at[rows], tile_sems.at[m])

    down = fetch(down_w.at[depth], down_v, sems.at[0])
    slopes = [slope_tile(0)]
    up = fetch(up_w.at[depth], up_v, sems.at[1])
    mid = fetch(middle, middle_v, sems.at[2])
    out = fetch(out_w.at[depth], out_v, sems.at[3])
    slopes += [slope_tile(m) for m in range(1, tiles)]
    return down, slopes, up, mid, out


def mlp_data_kernel(depth, tokens, grad, middle, slope, up_w, down_w, out_w, gain2, bias2, *rest):
    (grad_middle, grad_mixed, vectors, wide, normed, grad_pre, rounded,
     slope_v, up_v, down_v, out_v, middle_v, sems, tile_sems) = rest[tokens:]
    loads = mlp_loads(depth, slope, up_w, down_w, middle, out_w, slope_v, up_v, down_v, middle_v, out_v, sems, tile_sems)
    mlp_data_back(
        depth, loads, grad, grad_middle, grad_mixed, vectors, wide, slope_v, up_v, down_v, out_v, middle_v, normed,
        grad_pre, rounded, gain2, bias2,
    )


def mlp_weight_kernel(depth, tokens, places, scalars, grad, act, mixed, normed, grad_pre, rounded, *rest):
    mine, theirs, act_v, mixed_v, normed_v, pre_v, rounded_v, sems = rest[tokens:]
    first = [fetch(normed, normed_v, sems.at[0]), fetch(grad_pre, pre_v, sems.at[1])]
    later = [
        fetch(act, act_v, sems.at[2]), fetch(mixed, mixed_v, sems.at[3]),
        fetch(rounded, rounded_v, sems.at[4]),
    ]
    for load in first:
        load.wait()
    mlp_weight_back(scalars[1], places, later, mine, theirs, grad, act_v, mixed_v, normed_v, pre_v, rounded_v)


def attention_backward(qkv, probs, grad_mixed, grad_qkv, stride, windows, width, whole=None, at=0):
    whole = whole or width
    low, high = lane_halves()

    @pl.loop(0, windows // PER)
    def _(step):
        units = [(n, pair) for n in range(PER) for pair in range(width // TILE)]
        rows = [pl.ds(pl.multiple_of((PER * step + n) * stride, 32), TILE) for n in range(PER)]
        kept = [pl.ds(pl.multiple_of((PER * step + n) * 2 * TILE, 2 * TILE), 2 * TILE) for n in range(PER)]
        count = range(len(units))
        cut = lambda k, n, pair: qkv[rows[n], k * width + pair * TILE : k * width + (pair + 1) * TILE]
        arriving = [both_heads(grad_mixed[rows[n], pair * TILE : (pair + 1) * TILE], low, high) for n, pair in units]
        grad_p = [product(arriving[i], cut(2, *units[i]), NT) for i in count]
        p = [probs[pair, kept[n], :] for n, pair in units]
        grad_v = [product(p[i], arriving[i], TN) for i in count]
        inner = [jnp.sum(grad_p[i] * p[i].astype(F32), axis=-1, keepdims=True) for i in count]
        grad_s = [(p[i].astype(F32) * (grad_p[i] - inner[i])).astype(BF) for i in count]
        grad_q = [product(side_by_side(grad_s[i]), both_heads(cut(1, *units[i]), low, high)) * 0.125 for i in count]
        grad_k = [product(grad_s[i], both_heads(cut(0, *units[i]), low, high), TN) for i in count]
        for k, grads in enumerate((grad_q, grad_k, grad_v)):
            for (n, pair), value in zip(units, grads):
                start = k * whole + at + pair * TILE
                grad_qkv[rows[n], start : start + TILE] = value.astype(BF)


def qkv_back(depth, core, places, grad_qkv, hidden_v, middle_v, weight_v, gain1, bias1, grad_in, normed, vectors, mine, theirs):
    total, width = hidden_v.shape

    @pl.loop(0, total // ROWS)
    def _(m):
        rows = row_tile(m)
        back = jnp.zeros((ROWS, width), F32)
        for f in range(0, 3 * width, width):
            back = back + product(grad_qkv[rows, f : f + width], weight_v[:, f : f + width], NT)
        xhat, scale = normalized(hidden_v[rows, :].astype(F32))
        normed[rows, :] = (xhat * gain1[depth : depth + 1, :] + bias1[depth : depth + 1, :]).astype(BF)
        through, gain_sum, bias_sum = norm_back(back, xhat, scale, gain1[depth : depth + 1, :])
        grad_in[rows, :] = (middle_v[rows, :] + through).astype(BF)
        vectors[0:1, :] += gain_sum
        vectors[1:2, :] += bias_sum
        vectors[2:3, :] += jnp.sum(grad_qkv[rows, :width].astype(F32), axis=0, keepdims=True)
        vectors[3:4, :] += jnp.sum(grad_qkv[rows, 2 * width :].astype(F32), axis=0, keepdims=True)

    half = 3 * width // 2
    for part in range(2):
        which = core if part == 0 else 1 - core
        cols = pl.ds(pl.multiple_of(which * half, half), half)
        store_units((mine, theirs)[part], 0, product(normed[...], grad_qkv[:total, cols], TN), which, places)


def attention_load(depth, qkv, probs, grad_mixed, qkv_v, probs_v, mixed_v, sems):
    total = grad_mixed.shape[0]
    loads = [
        fetch(qkv.at[depth], qkv_v.at[pl.ds(0, total)], sems.at[0]),
        fetch(grad_mixed, mixed_v.at[pl.ds(0, total)], sems.at[1]),
        fetch(probs.at[depth], probs_v, sems.at[2]),
    ]
    qkv_v[total:, :] = jnp.zeros((qkv_v.shape[0] - total, qkv_v.shape[1]), BF)
    mixed_v[total:, :] = jnp.zeros((mixed_v.shape[0] - total, mixed_v.shape[1]), BF)
    return loads


def attention_back_kernel(
    depth, tokens, places, scalars, hidden, qkv, probs, grad_mixed, grad_middle, qkv_w, gain1, bias1, *rest,
):
    (mine, theirs, grad_in, vectors,
     hidden_v, middle_v, weight_v, normed, qkv_v, probs_v, mixed_v, grad_qkv, sems) = rest[tokens:]
    loads = attention_load(depth, qkv, probs, grad_mixed, qkv_v, probs_v, mixed_v, sems)
    later = [
        fetch(qkv_w.at[depth], weight_v, sems.at[3]),
        fetch(hidden.at[depth], hidden_v, sems.at[4]),
        fetch(grad_middle, middle_v, sems.at[5]),
    ]
    vectors[...] = jnp.zeros_like(vectors)
    for load in loads:
        load.wait()
    attention_backward(qkv_v, probs_v, mixed_v, grad_qkv, *placed(scalars, grad_in.shape[0]), grad_in.shape[1])
    for load in later:
        load.wait()
    qkv_back(
        depth, scalars[1], places, grad_qkv, hidden_v, middle_v, weight_v, gain1, bias1, grad_in, normed, vectors, mine,
        theirs,
    )


def part_loads(depth, part, parts, qkv, probs, grad_mixed, qkv_v, probs_v, mixed_v, sems):
    total, whole = grad_mixed.shape
    width = whole // parts
    pairs = probs_v.shape[0]
    inside = pl.ds(0, total)
    loads = [
        fetch(qkv.at[depth, :, pl.ds(k * whole + part * width, width)], qkv_v.at[inside, pl.ds(k * width, width)], sems.at[k])
        for k in range(3)
    ]
    loads.append(fetch(grad_mixed.at[:, pl.ds(part * width, width)], mixed_v.at[inside], sems.at[3]))
    loads.append(fetch(probs.at[depth, pl.ds(part * pairs, pairs)], probs_v, sems.at[4]))
    qkv_v[total:, :] = jnp.zeros((qkv_v.shape[0] - total, qkv_v.shape[1]), BF)
    mixed_v[total:, :] = jnp.zeros((mixed_v.shape[0] - total, mixed_v.shape[1]), BF)
    return loads


def attention_part_kernel(depth, part, parts, tokens, scalars, qkv, probs, grad_mixed, *rest):
    out, qkv_v, probs_v, mixed_v, grad_qkv, sems, out_sem = rest[tokens:]
    total, whole = grad_mixed.shape
    for load in part_loads(depth, part, parts, qkv, probs, grad_mixed, qkv_v, probs_v, mixed_v, sems):
        load.wait()
    attention_backward(qkv_v, probs_v, mixed_v, grad_qkv, *placed(scalars, total), whole // parts)
    fetch(grad_qkv.at[pl.ds(0, total)], out, out_sem).wait()


def table_kernel(
    depth, tokens, places, groups, scalars, qkv, probs, grad_mixed, grad_low, hidden, grad_middle, qkv_w, gain1, bias1,
    index, final_grads, feed1, wide1, attend1, feed0, wide0, *rest,
):
    (mine, theirs, frame_grad, grad_in, turned, vectors, stage, hidden_v, normed, grad_qkv, weight_v, middle_v,
     qkv_v, probs_v, mixed_v, sems, part_sems) = rest[tokens:]
    total, width = grad_in.shape
    half = width // 2
    first = part_loads(depth, 1, 2, qkv, probs, grad_mixed, qkv_v, probs_v, mixed_v, part_sems)
    inside = pl.ds(0, total)
    loads = [
        fetch(grad_low.at[:, pl.ds(k * half, half)], grad_qkv.at[inside, pl.ds(k * width, half)], sems.at[k])
        for k in range(3)
    ]
    loads.append(fetch(qkv_w.at[depth], weight_v, sems.at[3]))
    loads.append(fetch(hidden.at[depth], hidden_v, sems.at[4]))
    loads.append(fetch(grad_middle, middle_v, sems.at[5]))
    core = scalars[1]
    steps = frame_grad.shape[0]
    qkv_width = 3 * width // 2
    code_width = mine.shape[1] - qkv_width - TILE
    vectors[...] = jnp.zeros_like(vectors)
    for load in first:
        load.wait()
    attention_backward(qkv_v, probs_v, mixed_v, grad_qkv, *placed(scalars, total), half, width, half)
    for load in loads:
        load.wait()
    qkv_back(
        depth, core, places, grad_qkv, hidden_v, middle_v, weight_v, gain1, bias1, grad_in, normed, vectors, mine, theirs,
    )

    stage[...] = jnp.zeros_like(stage)
    for k, block in enumerate((feed0, vectors, feed1, attend1, final_grads)):
        stage[VECTORS + 8 * k : VECTORS + 8 * k + 8, :] = block[...]
    each = width // groups
    for k, wide in enumerate((wide0, wide1)):
        for group in range(groups):
            for c in range(4):
                start = group * 4 * each + c * each
                at = VECTORS + 40 + 8 * k + c
                stage[at : at + 1, group * each : group * each + each] = wide[0:1, start : start + each]

    turned[...] = grad_in[...].T
    for part in range(2):
        out = (mine, theirs)[part]
        which = core if part == 0 else 1 - core
        line = lax.broadcasted_iota(jnp.int32, (code_width, total), 0) + which * code_width
        hot = (line == index[0:1, :]).astype(F32).astype(BF)
        store_units(out, qkv_width, product(turned[...], hot, NT), which, places)
        line = lax.broadcasted_iota(jnp.int32, (TILE, total), 0) + which * TILE
        hot = ((line == index[1:2, :]) | (line == index[2:3, :])).astype(F32).astype(BF)
        small = product(turned[...], hot, NT) + stage[...].T * which.astype(F32)
        store_units(out, qkv_width + code_width, small, which, places)
    hot = (lax.broadcasted_iota(jnp.int32, (steps, total), 0) == index[3:4, :]).astype(F32).astype(BF)
    frame_grad[...] = product(hot, grad_in[...])


def output_kernel(where, scalars, *refs):
    count = 1 + max(chunk for chunk, _ in where.values())
    sources = refs[: 2 * count]
    (code, action, position, gain1, bias1, qkv, query, value, out, out_bias, gain2, bias2, up, up_bias, down, down_bias,
     final_gain, final_bias) = refs[2 * count : -1]
    square = refs[-1]
    rows, units = up.shape[1:]
    half = units // 2
    small = qkv.shape[2] // 2 + code.shape[1] // 2

    def emit(own):
        def part(name, core, across, start, size):
            chunk, at = where[name]
            lines = slice((across ^ (own >> 1)) * rows // 2, ((across ^ (own >> 1)) + 1) * rows // 2)
            return sources[2 * chunk + (core ^ (own & 1))][lines, at + start : at + start + size].astype(F32)

        def place(target, name, start):
            size = target.shape[-1] // 2
            for across in range(2):
                lines = slice(across * rows // 2, (across + 1) * rows // 2)
                for core in range(2):
                    target[lines, core * size : (core + 1) * size] = part(name, core, across, start, size)

        for depth in range(2):
            place(up.at[depth], ("feed", depth), 0)
            place(down.at[depth], ("feed", depth), half)
            place(out.at[depth], ("feed", depth), units)
            place(qkv.at[depth], ("attend", depth), 0)
        place(code, ("attend", 0), qkv.shape[2] // 2)
        square[...] = jnp.zeros_like(square)
        for across in range(2):
            lines = slice(across * rows // 2, (across + 1) * rows // 2)
            position[lines, :] = part(("attend", 0), 0, across, small, TILE)[:, : position.shape[1]]
            square[lines, :] = part(("attend", 0), 1, across, small, TILE)
        lines = square[...].T[:, :rows]
        action[...] = lines[: action.shape[0]]

        def line(k):
            return lines[VECTORS + k : VECTORS + k + 1]

        for depth in range(2):
            at = slice(depth, depth + 1)
            base = 16 * depth
            for k, target in enumerate((gain2, bias2, down_bias, out_bias)):
                target[at, :] = line(base + k)
            for k, target in enumerate((gain1, bias1, query, value)):
                target[at, :] = line(base + 8 + k)
            for c in range(4):
                up_bias[at, c * rows : (c + 1) * rows] = line(40 + 8 * depth + c)
        final_gain[...] = line(32)
        final_bias[...] = line(33)

    for own in range(4):
        pl.when(scalars[scalars.shape[0] - 1] == own)(partial(emit, own))


VMEM = pl.BlockSpec(memory_space=pltpu.VMEM)
ANY = pl.BlockSpec(memory_space=pl.ANY)
SMEM = pl.BlockSpec(memory_space=pltpu.SMEM)


def cost(flops, moved, others=0):
    return pl.CostEstimate(flops=int(8 * flops), bytes_accessed=int(moved), transcendentals=int(others))


def run_forward(places, scalars, actions, deltas, frames, codebook, action_table, position_table, layers, finals, cotangent):
    gain1, bias1, qkv_w, query_bias, value_bias, out_w, out_bias, gain2, bias2, up_w, up_bias, down_w, down_bias = layers
    width = codebook.shape[1]
    units = up_bias.shape[1]
    real = cotangent.shape[1]
    total = -(-real // ROWS) * ROWS
    reach = total + TILE + 32
    columns = units + width // 2
    shape = jax.ShapeDtypeStruct
    once = dict(pipeline_mode=pl.Buffered(1))
    whole = lambda a: pl.BlockSpec(a.shape, lambda i, s, n=a.ndim: (0,) * n, **once)
    mine = lambda a: pl.BlockSpec((1,) + a.shape[1:], lambda i, s: (s[0], 0, 0), **once)
    kept = (width // TILE, WINDOWS * 2 * TILE, TILE)
    outs = [
        (shape((real, width), F32), ANY),
        (shape((8, total), jnp.int32), None),
        (shape((8, width), F32), None), (shape((8, width), F32), None), (shape((8, units), F32), None),
        (shape((2, total, width), BF), ANY),
        (shape((2, total, 3 * width), BF), ANY),
        (shape((2,) + kept, BF), ANY),
        (shape((total, width), BF), ANY),
        (shape((total, width), F32), ANY),
        (shape((total, units), BF), ANY),
        (shape((total, units), BF), ANY),
        (shape((total, width), F32), ANY), (shape((total, width), BF), ANY),
        (shape((width, columns), BF), ANY), (shape((width, columns), BF), ANY),
    ]
    args = [
        (actions, None), (deltas, mine(deltas)), (frames, mine(frames)),
        (codebook, None), (action_table, None), (position_table, None),
        (gain1, None), (bias1, None), (qkv_w, ANY), (query_bias, None), (value_bias, None), (out_w, ANY),
        (out_bias, None), (gain2, None), (bias2, None), (up_w, ANY), (up_bias, None), (down_w, ANY), (down_bias, None),
        (finals[0][None], None), (finals[1][None], None), (cotangent, mine(cotangent)),
    ]
    scratch = [
        pltpu.VMEM((2 * TILE, width), BF),
        pltpu.VMEM(qkv_w.shape, BF), pltpu.VMEM(out_w.shape, BF), pltpu.VMEM(up_w.shape, BF), pltpu.VMEM(down_w.shape, BF),
        pltpu.VMEM((3, total, width), BF), pltpu.VMEM((reach, 3 * width), BF), pltpu.VMEM(kept, BF),
        pltpu.VMEM((reach, width), BF), pltpu.VMEM((total, width), F32),
        pltpu.VMEM((total, units), BF), pltpu.VMEM((total, units), BF), pltpu.VMEM((2 * TILE, TILE), F32),
        pltpu.VMEM((total, width), F32), pltpu.VMEM((total, width), F32),
        pltpu.VMEM((total, width), BF), pltpu.VMEM((total, width), BF), pltpu.VMEM((total, width), BF),
        pltpu.VMEM((total, width), BF), pltpu.VMEM((total, units), BF),
        pltpu.VMEM((width, columns), BF), pltpu.VMEM((width, columns), BF),
        pltpu.SemaphoreType.DMA((2, 4)), pltpu.SemaphoreType.DMA((16,)), pltpu.SemaphoreType.DMA((2, total // ROWS)),
        pltpu.SemaphoreType.DMA, pltpu.SemaphoreType.DMA((6,)),
    ]
    return pl.pallas_call(
        partial(forward_kernel, places),
        out_shape=[o for o, _ in outs],
        grid_spec=pltpu.PrefetchScalarGridSpec(
            num_scalar_prefetch=1,
            grid=(1,),
            in_specs=[spec or whole(a) for a, spec in args],
            out_specs=[spec or whole(o) for o, spec in outs],
            scratch_shapes=scratch,
        ),
        compiler_params=pltpu.CompilerParams(vmem_limit_bytes=62 << 20),
        cost_estimate=cost(24e9, 50e6, 4e6),
        name="forward",
    )(scalars, *[a for a, _ in args])


def run_mlp_data(depth, grad, saved, layers, after):
    hidden, qkv, probs, mixed, middle, act, slope = saved
    gain1, bias1, qkv_w, query_bias, value_bias, out_w, out_bias, gain2, bias2, up_w, up_bias, down_w, down_bias = layers
    total, width = grad.shape
    units = up_bias.shape[1]
    shape = jax.ShapeDtypeStruct
    return pl.pallas_call(
        partial(mlp_data_kernel, depth, len(after)),
        out_shape=[
            shape((total, width), F32), shape((total, width), BF), shape((8, width), F32), shape((8, units), F32),
            shape((total, width), BF), shape((total, units), BF), shape((total, width), BF),
        ],
        in_specs=[VMEM] + [ANY] * 5 + [VMEM] * 2 + [ANY] * len(after),
        out_specs=[VMEM] * 7,
        scratch_shapes=[
            pltpu.VMEM((total, units), BF),
            pltpu.VMEM((width, units), BF), pltpu.VMEM((units, width), BF), pltpu.VMEM((width, width), BF),
            pltpu.VMEM((total, width), F32),
            pltpu.SemaphoreType.DMA((4,)), pltpu.SemaphoreType.DMA((total // ROWS,)),
        ],
        compiler_params=pltpu.CompilerParams(vmem_limit_bytes=40 << 20),
        cost_estimate=cost(10e9, 16e6),
        name="mlp_data",
    )(grad, middle, slope, up_w, down_w, out_w, gain2, bias2, *after)


def run_mlp_weight(depth, places, scalars, grad, saved, normed, grad_pre, rounded, after):
    hidden, qkv, probs, mixed, middle, act, slope = saved
    total, width = grad.shape
    units = grad_pre.shape[1]
    shape = jax.ShapeDtypeStruct
    return pl.pallas_call(
        partial(mlp_weight_kernel, depth, len(after), places),
        out_shape=[shape((width, units + width // 2), BF), shape((width, units + width // 2), BF)],
        in_specs=[SMEM, VMEM] + [ANY] * 5 + [ANY] * len(after),
        out_specs=[VMEM] * 2,
        scratch_shapes=[
            pltpu.VMEM((total, units), BF), pltpu.VMEM((total, width), BF), pltpu.VMEM((total, width), BF),
            pltpu.VMEM((total, units), BF), pltpu.VMEM((total, width), BF),
            pltpu.SemaphoreType.DMA((5,)),
        ],
        compiler_params=pltpu.CompilerParams(vmem_limit_bytes=40 << 20),
        cost_estimate=cost(8e9, 16e6),
        name="mlp_weight",
    )(scalars, grad, act, mixed, normed, grad_pre, rounded, *after)


def window_scratch(total, width, probs):
    reach = total + TILE + 32
    return [
        pltpu.VMEM((reach, 3 * width), BF), pltpu.VMEM(probs.shape[1:], BF),
        pltpu.VMEM((reach, width), BF), pltpu.VMEM((reach, 3 * width), BF),
    ]


def run_attention_back(depth, places, scalars, grad_mixed, grad_middle, saved, layers, after):
    hidden, qkv, probs, mixed, middle, act, slope = saved
    gain1, bias1, qkv_w = layers[:3]
    total, width = grad_mixed.shape
    shape = jax.ShapeDtypeStruct
    return pl.pallas_call(
        partial(attention_back_kernel, depth, len(after), places),
        out_shape=[
            shape((width, 3 * width // 2), BF), shape((width, 3 * width // 2), BF),
            shape((total, width), BF), shape((8, width), F32),
        ],
        in_specs=[SMEM] + [ANY] * 6 + [VMEM] * 2 + [ANY] * len(after),
        out_specs=[VMEM] * 4,
        scratch_shapes=[
            pltpu.VMEM((total, width), BF), pltpu.VMEM((total, width), F32), pltpu.VMEM(qkv_w.shape[1:], BF),
            pltpu.VMEM((total, width), BF), *window_scratch(total, width, probs),
            pltpu.SemaphoreType.DMA((6,)),
        ],
        compiler_params=pltpu.CompilerParams(vmem_limit_bytes=61 << 20),
        cost_estimate=cost(16e9, 24e6),
        name="attention_back",
    )(scalars, hidden, qkv, probs, grad_mixed, grad_middle, qkv_w, gain1, bias1, *after)


def run_attention_part(depth, part, parts, scalars, grad_mixed, saved, after):
    hidden, qkv, probs, mixed, middle, act, slope = saved
    total, width = grad_mixed.shape
    width = width // parts
    reach = total + TILE + 32
    return pl.pallas_call(
        partial(attention_part_kernel, depth, part, parts, len(after)),
        out_shape=jax.ShapeDtypeStruct((total, 3 * width), BF),
        in_specs=[SMEM] + [ANY] * 3 + [ANY] * len(after),
        out_specs=ANY,
        scratch_shapes=[
            pltpu.VMEM((reach, 3 * width), BF), pltpu.VMEM((width // TILE,) + probs.shape[2:], BF),
            pltpu.VMEM((reach, width), BF), pltpu.VMEM((reach, 3 * width), BF),
            pltpu.SemaphoreType.DMA((5,)), pltpu.SemaphoreType.DMA,
        ],
        compiler_params=pltpu.CompilerParams(vmem_limit_bytes=VMEM_PART << 20),
        cost_estimate=cost(8e9, 8e6),
        name="attention_part",
    )(scalars, qkv, probs, grad_mixed, *after)


def run_table(depth, places, scalars, grad_mixed, grad_low, grad_middle, saved, layers, index, vectors, codes, steps, groups, after):
    hidden, qkv, probs, mixed, middle, act, slope = saved
    gain1, bias1, qkv_w = layers[:3]
    total, width = grad_middle.shape
    reach = total + TILE + 32
    columns = 3 * width // 2 + codes // 2 + TILE
    shape = jax.ShapeDtypeStruct
    return pl.pallas_call(
        partial(table_kernel, depth, len(after), places, groups),
        out_shape=[shape((width, columns), BF), shape((width, columns), BF), shape((steps, width), F32)],
        in_specs=[SMEM] + [ANY] * 7 + [VMEM] * 2 + [VMEM] * 7 + [ANY] * len(after),
        out_specs=[VMEM] * 3,
        scratch_shapes=[
            pltpu.VMEM((total, width), BF), pltpu.VMEM((width, total), BF), pltpu.VMEM((8, width), F32),
            pltpu.VMEM((TILE, width), F32), pltpu.VMEM((total, width), BF), pltpu.VMEM((total, width), BF),
            pltpu.VMEM((reach, 3 * width), BF), pltpu.VMEM(qkv_w.shape[1:], BF), pltpu.VMEM((total, width), F32),
            pltpu.VMEM((reach, 3 * width // 2), BF), pltpu.VMEM((probs.shape[1] // 2,) + probs.shape[2:], BF),
            pltpu.VMEM((reach, width // 2), BF),
            pltpu.SemaphoreType.DMA((6,)), pltpu.SemaphoreType.DMA((5,)),
        ],
        compiler_params=pltpu.CompilerParams(vmem_limit_bytes=40 << 20),
        cost_estimate=cost(12e9, 12e6),
        name="tables",
    )(scalars, qkv, probs, grad_mixed, grad_low, hidden, grad_middle, qkv_w, gain1, bias1, index, *vectors, *after)


def run_output(where, scalars, sources, width, units, codes, actions, positions):
    rows = sources[0].shape[0]
    wide, line = (2, rows), (1, rows)
    shapes = [
        (rows, codes), (actions, rows), (rows, positions), wide, wide, (2, rows, 3 * width), wide, wide, (2, rows, width),
        wide, wide, wide, (2, rows, units), (2, 4 * rows), (2, rows, units), wide, line, line,
    ]
    return pl.pallas_call(
        partial(output_kernel, where),
        out_shape=[jax.ShapeDtypeStruct(s, F32) for s in shapes],
        in_specs=[SMEM] + [VMEM] * len(sources),
        out_specs=[VMEM] * len(shapes),
        scratch_shapes=[pltpu.VMEM((TILE, TILE), F32)],
        compiler_params=pltpu.CompilerParams(vmem_limit_bytes=30 << 20),
        cost_estimate=cost(1e6, 6e6),
        name="outputs",
    )(scalars, *sources)


def meet(array, axis, by):
    size = lax.axis_size(axis)
    return lax.ppermute(array, axis, [(i, i ^ by) for i in range(size)])


def swap(array, axis, bit):
    return meet(array, axis, 1 << bit)


def bits_of(axis):
    return lax.axis_size(axis).bit_length() - 1


def own_bit(axis, bit):
    return (lax.axis_index(axis) >> bit) & 1


def take(array, dim, which):
    return lax.dynamic_index_in_dim(array, which, dim, keepdims=False)


def total_of(terms):
    return sum(term.astype(F32) for term in terms)


def settled(array):
    return lax.optimization_barrier(array.astype(BF))


def tied(array, token):
    return lax.optimization_barrier((array, token))[0]


def unit_places(count):
    first, second = [], []
    for unit in range(2 << count):
        bits = [(unit >> (1 + bit)) & 1 for bit in range(count)]
        for order, places in ((bits + [unit & 1], first), ([unit & 1] + bits, second)):
            place = 0
            for bit in order:
                place = 2 * place + bit
            places.append(place)
    return first, second


def reordered(array, which, count):
    rows, columns = array.shape
    ways = array.reshape((2,) * (count + 1) + (rows >> (count + 1), columns))
    dims = list(range(count - 1, -1, -1))
    first = ways.transpose(dims + [count, count + 1, count + 2])
    second = ways.transpose([count] + dims + [count + 1, count + 2])
    return jnp.where(which == 0, first, second).reshape(rows, columns)


class Chunk:
    def __init__(self, places):
        self.count = bits_of("dp")
        self.places = places
        self.pieces = []
        self.terms = []
        self.core = own_bit("section", 0)

    def add(self, mine, theirs):
        if self.places is None:
            mine, theirs = reordered(mine, self.core, self.count), reordered(theirs, 1 - self.core, self.count)
        self.pieces.append([mine, swap(theirs, "section", 0)])

    def hold(self, token):
        if self.terms:
            self.terms[-1] = tied(self.terms[-1], token)
        else:
            for piece in self.pieces:
                piece[1] = tied(piece[1], token)

    def step(self):
        if not self.terms:
            self.left = self.pieces[0][0].shape[0]
        k = len(self.terms)
        bits = [own_bit("dp", bit) for bit in range(self.count)]
        across = own_bit("section", 1)
        own = jnp.where(self.core == 0, (bits + [across])[k], ([across] + bits)[k])
        half = self.left // 2
        cut = lambda t, which: lax.dynamic_slice_in_dim(t, which * half, half, 0)
        if not self.terms:
            self.parts = [[[mine, arrived] for mine, arrived in self.pieces]]
        parts = self.parts[-1]
        sum_of = jnp.concatenate([total_of([cut(t, 1 - own) for t in part]) for part in parts], axis=1)
        for term in self.terms:
            sum_of = sum_of + cut(term, 1 - own).astype(F32)
        self.sent = settled(sum_of)
        sections = lax.axis_size("section")
        pairs = []
        for source in range(lax.axis_size("dp") * sections):
            at = k if source & 1 == 0 else (k - 1) % (self.count + 1)
            bit = sections << at if at < self.count else 2
            pairs.append((source, source ^ bit))
        self.parts = [[[cut(t, own) for t in part] for part in parts]]
        self.terms = [cut(t, own) for t in self.terms] + [lax.ppermute(self.sent, ("dp", "section"), pairs)]
        self.left = half
        return self

    def across(self):
        total = jnp.concatenate([total_of(part) for part in self.parts[-1]], axis=1)
        for term in self.terms:
            total = total + term.astype(F32)
        self.sent = settled(total)
        other = swap(self.sent, "section", 1)
        self.terms = [self.sent, other]

    def finish(self):
        rows = settled(jnp.concatenate(self.terms))
        arrived = swap(rows, "section", 0)
        return [rows, arrived]


def local(
    frames, actions, deltas, kinds, codebook, action_table, position_table, norm1_gain, norm1_bias, qkv_weight,
    query_bias, value_bias, out_weight, out_bias, norm2_gain, norm2_bias, up_weight, up_bias, down_weight, down_bias,
    final_gain, final_bias, cotangent,
):
    micro, steps, width = frames.shape
    units = up_weight.shape[2]
    codes = codebook.shape[0]
    slot = lax.axis_index("section") * micro // lax.axis_size("section")
    layers = (
        norm1_gain, norm1_bias, qkv_weight, query_bias, value_bias, out_weight, out_bias, norm2_gain, norm2_bias,
        up_weight, up_bias, down_weight, down_bias,
    )
    section = lax.axis_index("section")
    scalars = jnp.concatenate([jnp.stack([slot, section & 1]), kinds, section[None]]).astype(jnp.int32)
    groups = lax.axis_size("dp")
    count = bits_of("dp")
    places = unit_places(count) if width >> (count + 1) >= 16 else None
    chunk1, chunk2, chunk3 = Chunk(places), Chunk(places), Chunk(places)
    activations, index, final_grads, feed1, wide1, *saved, middle, mixed, mine, theirs = run_forward(
        places, scalars, actions, deltas.transpose(0, 2, 1), frames, codebook, action_table, position_table,
        layers, (final_gain, final_bias), cotangent,
    )
    chunk1.add(mine, theirs)
    mine, theirs, grad, attend1 = run_attention_back(1, places, scalars, mixed, middle, saved, layers, [])
    chunk1.hold(attend1)
    chunk2.add(mine, theirs)
    chunk1.step()
    middle, mixed, feed0, wide0, normed, grad_pre, rounded = run_mlp_data(0, grad, saved, layers, [chunk1.sent])
    chunk1.hold(normed)
    chunk1.step()
    mine, theirs = run_mlp_weight(0, places, scalars, grad, saved, normed, grad_pre, rounded, [chunk1.sent])
    chunk1.hold(theirs)
    chunk2.hold(theirs)
    chunk2.add(mine, theirs)
    grad_low = run_attention_part(0, 0, 2, scalars, mixed, saved, [])
    chunk2.hold(grad_low)
    chunk2.step()
    chunk1.hold(chunk2.sent)
    chunk1.step()
    vectors = (final_grads, feed1, wide1, attend1, feed0, wide0)
    mine, theirs, frame_grad = run_table(
        0, places, scalars, mixed, grad_low, middle, saved, layers, index, vectors, codes, steps, groups,
        [chunk2.sent, chunk1.sent],
    )
    chunk3.add(mine, theirs)
    chunk2.hold(frame_grad)
    chunk1.hold(chunk2.terms[-1])
    chunk2.step()
    chunk3.hold(chunk2.sent)
    chunk3.step()
    chunk2.hold(chunk3.sent)
    chunk1.hold(chunk3.sent)
    for _ in range(3, count + 1):
        chunk1.step()
    for k in range(2, count + 3):
        if k <= count:
            chunk2.step()
        elif k == count + 1:
            chunk2.across()
        else:
            sources += chunk2.finish()
        chunk3.hold(chunk2.sent)
        if k == 2:
            chunk3.hold(chunk1.terms[-1])
            chunk1.across()
        if k == 3:
            chunk3.hold(chunk1.terms[-1])
            sources = chunk1.finish()
        if k <= count + 1:
            chunk3.step()
            chunk2.hold(chunk3.sent)
        else:
            chunk3.across()
    sources += chunk3.finish()
    split = 3 * width // 2
    where = {("feed", 1): (0, 0), ("attend", 1): (1, 0), ("feed", 0): (1, split), ("attend", 0): (2, 0)}
    (code, action, position, gain1, bias1, qkv, query, value, out, out_b, gain2, bias2, up, up_b, down, down_b, last_gain,
     last_bias) = run_output(
        where, scalars, sources, width, units, codes, action_table.shape[0], position_table.shape[0]
    )
    return (
        activations[None], frame_grad[None], code.T, action, position.T, gain1, bias1, qkv, query, value, out, out_b,
        gain2, bias2, up, up_b, down.transpose(0, 2, 1), down_b, last_gain[0], last_bias[0],
    )


def solution(mesh):
    rows, one = P("dp", None, None), P(None, "dp")
    weight = P(None, "dp", None)
    both = P(("dp", "section"), None, None)
    return jax.shard_map(
        local,
        mesh=mesh,
        in_specs=(rows, P("dp", None), rows, P("dp")) + (P(),) * 18 + (rows,),
        out_specs=(
            both, both, one, one, one, one, one, weight, one, one, weight, one, one, one, weight, one,
            P(None, None, "dp"), one, P("dp"), P("dp"),
        ),
        check_vma=False,
    )
```

```python
from functools import partial

import jax
import jax.numpy as jnp
from jax import lax
from jax.experimental import pallas as pl
from jax.experimental.pallas import tpu as pltpu
from jax.sharding import PartitionSpec as P

HEADS = 8
SHORT_STEPS = 8
LONG_STEPS = 21
EPSILON = 1e-05
MASKED = -1e30
TILE = 128
ROWS = 512
CHUNK = 512
STRIP = 256
VECTORS = 32
WINDOWS = 12
PER = 4
VMEM_PART = 58
BF = jnp.bfloat16
F32 = jnp.float32

NN = (((1,), (0,)), ((), ()))
NT = (((1,), (1,)), ((), ()))
TN = (((0,), (0,)), ((), ()))


def product(left, right, form=NN):
    return lax.dot_general(left, right, form, preferred_element_type=F32)


def normalized(x):
    center = x - jnp.mean(x, axis=-1, keepdims=True)
    spread = jnp.mean(center * center, axis=-1, keepdims=True)
    scale = lax.rsqrt(spread + EPSILON)
    return center * scale, scale


def norm_back(grad, xhat, scale, gain):
    inner = grad * gain
    first = jnp.mean(inner, axis=-1, keepdims=True)
    second = jnp.mean(inner * xhat, axis=-1, keepdims=True)
    back = (inner - first - xhat * second) * scale
    return back, jnp.sum(grad * xhat, axis=0, keepdims=True), jnp.sum(grad, axis=0, keepdims=True)


def gelu_pair(u):
    cdf = 0.5 + 0.5 * lax.erf(u * 0.7071067811865476)
    e = jnp.exp2(u * u * (-0.5 * 1.4426950408889634))
    return u * cdf, cdf + u * (e * 0.3989422804014327)


def row_tile(m):
    return pl.ds(pl.multiple_of(m * ROWS, ROWS), ROWS)


def lane_halves():
    lane = lax.broadcasted_iota(jnp.int32, (1, TILE), 1)
    low = (lane < TILE // 2).astype(F32)
    return low.astype(BF), (1.0 - low).astype(BF)


def both_heads(x, low, high):
    return jnp.concatenate([x * low, x * high], axis=0)


def side_by_side(x):
    return jnp.concatenate([x[:TILE], x[TILE:]], axis=1)


def write_mask(mask, stride):
    row = lax.broadcasted_iota(jnp.int32, (2 * TILE, TILE), 0)
    row = jnp.where(row >= TILE, row - TILE, row).astype(F32) + 0.5
    col = lax.broadcasted_iota(jnp.int32, (2 * TILE, TILE), 1).astype(F32) + 0.5
    step = jnp.floor(col * (1.0 / 6.0)) <= jnp.floor(row * (1.0 / 6.0))
    member = jnp.floor(col * (1.0 / 48.0)) == jnp.floor(row * (1.0 / 48.0))
    long = jnp.where(step, 0.0, MASKED)
    short = jnp.where(member, long, MASKED)
    mask[...] = jnp.where(stride == TILE, long, short)


def placed(scalars, total):
    long = scalars[2 + scalars[0]] == 1
    return jnp.where(long, TILE, 2 * SHORT_STEPS * 6), jnp.where(long, total // TILE, WINDOWS)


def fetch(source, target, sem):
    copy = pltpu.make_async_copy(source, target, sem)
    copy.start()
    return copy


def attention_forward(qkv, probs, mixed, mask, stride, windows, width):
    low, high = lane_halves()

    @pl.loop(0, windows // PER)
    def _(step):
        units = [(n, pair) for n in range(PER) for pair in range(width // TILE)]
        starts = [pl.multiple_of((PER * step + n) * stride, 32) for n in range(PER)]
        rows = [pl.ds(start, TILE) for start in starts]
        cut = lambda k, n, pair: qkv[rows[n], k * width + pair * TILE : k * width + (pair + 1) * TILE]
        scores = [product(both_heads(cut(0, n, pair), low, high), cut(1, n, pair), NT) + mask[...] for n, pair in units]
        shifted = [jnp.exp(s - jnp.max(s, axis=-1, keepdims=True)) for s in scores]
        p = [(s * (1.0 / jnp.sum(s, axis=-1, keepdims=True))).astype(BF) for s in shifted]
        for (n, pair), value in zip(units, p):
            kept = pl.ds(pl.multiple_of((PER * step + n) * 2 * TILE, 2 * TILE), 2 * TILE)
            probs[pair, kept, :] = value
        out = [product(side_by_side(value), both_heads(cut(2, n, pair), low, high)) for (n, pair), value in zip(units, p)]
        for (n, pair), value in zip(units, out):
            mixed[rows[n], pair * TILE : (pair + 1) * TILE] = value.astype(BF)


def build_index(index, actions, deltas, long):
    steps = actions.shape[-1]
    total = index.shape[1]
    step = lax.broadcasted_iota(jnp.int32, (steps, total), 0).astype(F32)
    start = step * 6.0 + jnp.where(long, 2.0, 0.0) * jnp.floor((step + 0.5) * (1.0 / LONG_STEPS))
    slot = lax.broadcasted_iota(jnp.int32, (steps, total), 1).astype(F32) - start
    line = lax.broadcasted_iota(jnp.int32, (8, steps), 0)

    def rows(**values):
        out = jnp.zeros((8, steps), F32)
        for name, value in values.items():
            out = jnp.where(line == int(name[1:]), value, out)
        return out.astype(BF)

    def spread(value, j):
        return product(value, (slot == float(j)).astype(F32).astype(BF))

    count = lax.broadcasted_iota(jnp.int32, (8, steps), 1).astype(F32)
    found = spread(rows(r5=count, r6=1.0), 0) + spread(rows(r3=actions.astype(F32), r4=1.0), 1)
    for j in range(deltas.shape[1]):
        code = deltas[0, j : j + 1, :].astype(F32)
        high = jnp.floor(code * (1.0 / 32.0))
        found = found + spread(rows(r0=high, r1=code - 32.0 * high, r2=1.0), 2 + j)
    found = found.astype(jnp.int32)
    none = jnp.full((1, total), -1, jnp.int32)
    row = lax.broadcasted_iota(jnp.int32, (1, total), 1)
    real = row.astype(F32) + 0.5
    apart = row - TILE * jnp.floor(real * (1.0 / TILE)).astype(jnp.int32)
    apart = jnp.where(apart < LONG_STEPS * 6, apart, none)
    close = row - SHORT_STEPS * 6 * jnp.floor(real * (1.0 / (SHORT_STEPS * 6))).astype(jnp.int32)
    close = jnp.where(row < steps * 6, close, none)
    index[0:1, :] = jnp.where(found[2:3] == 1, found[0:1] * 32 + found[1:2], none)
    index[1:2, :] = jnp.where(long, apart, close)
    index[2:3, :] = jnp.where(found[4:5] == 1, found[3:4] + TILE, none)
    index[3:4, :] = jnp.where(found[6:7] == 1, found[5:6], none)
    index[4:8, :] = jnp.full((4, total), -1, jnp.int32)


def forward_kernel(
    places, scalars, actions, deltas, frames, codebook, action_table, position_table,
    gain1, bias1, qkv_w, query_bias, value_bias, out_w, out_bias, gain2, bias2,
    up_w, up_bias, down_w, down_bias, final_gain, final_bias, cotangent,
    activations, index, final_grads, vectors, wide,
    hidden_out, qkv_out, probs_out, mixed_out, middle_out, act_out, slope_out,
    grad_middle_out, grad_mixed_out, mine_out, theirs_out,
    table, qkv_v, out_v, up_v, down_v, hidden, qkv, probs, mixed, middle, act, slope, mask, result, cot,
    grad, grad_mixed, normed_two, rounded, grad_pre, mine, theirs,
    weight_sem, save_sem, tile_sem, result_sem, part_sem,
):
    core = scalars[1]
    width = hidden.shape[-1]
    total = hidden.shape[1]
    stride, windows = placed(scalars, total)
    hidden_units = up_bias.shape[1]
    tiles = total // ROWS
    loads = []
    for depth in range(2):
        loads.append([
            fetch(qkv_w.at[depth], qkv_v.at[depth], weight_sem.at[depth, 0]),
            fetch(out_w.at[depth], out_v.at[depth], weight_sem.at[depth, 1]),
            fetch(up_w.at[depth], up_v.at[depth], weight_sem.at[depth, 2]),
            fetch(down_w.at[depth], down_v.at[depth], weight_sem.at[depth, 3]),
        ])
    write_mask(mask, stride)
    build_index(index, actions[pl.ds(scalars[0], 1), :], deltas, stride == TILE)
    positions = position_table.shape[0]
    action_count = action_table.shape[0]
    table[...] = jnp.zeros_like(table)
    table[:positions] = position_table[...]
    table[TILE : TILE + action_count] = action_table[...]
    qkv[total:, :] = jnp.zeros((qkv.shape[0] - total, qkv.shape[1]), BF)

    codes = codebook.shape[0]
    steps = frames.shape[1]

    @pl.loop(0, tiles)
    def _(m):
        rows = row_tile(m)
        code_hot = (lax.broadcasted_iota(jnp.int32, (codes, ROWS), 0) == index[0:1, rows]).astype(F32).astype(BF)
        line = lax.broadcasted_iota(jnp.int32, (2 * TILE, ROWS), 0)
        small_hot = ((line == index[1:2, rows]) | (line == index[2:3, rows])).astype(F32).astype(BF)
        frame_hot = (lax.broadcasted_iota(jnp.int32, (steps, ROWS), 0) == index[3:4, rows]).astype(F32).astype(BF)
        value = product(code_hot, codebook[...], TN) + product(small_hot, table[...], TN)
        value = value + product(frame_hot, frames[0], TN)
        hidden[0, rows, :] = value.astype(BF)

    def tile_copies(m):
        rows = row_tile(m)
        return (
            pltpu.make_async_copy(act.at[rows], act_out.at[rows], tile_sem.at[0, m]),
            pltpu.make_async_copy(slope.at[rows], slope_out.at[rows], tile_sem.at[1, m]),
        )

    saves = {}
    started = []

    def save(name, source, target):
        saves[name] = fetch(source, target, save_sem.at[len(started)])
        started.append(name)

    inside = pl.ds(0, total)
    for depth in range(2):
        save(("hidden", depth), hidden.at[depth], hidden_out.at[depth])
        loads[depth][0].wait()
        if depth:
            saves.pop(("qkv", 0)).wait()

        def normed_tile(m):
            xhat, _ = normalized(hidden[depth, m * ROWS : (m + 1) * ROWS, :].astype(F32))
            return (xhat * gain1[depth : depth + 1, :] + bias1[depth : depth + 1, :]).astype(BF)

        ready = normed_tile(0)
        for m in range(tiles):
            rows = slice(m * ROWS, (m + 1) * ROWS)
            normed = ready
            if m + 1 < tiles:
                ready = normed_tile(m + 1)
            q = product(normed, qkv_v[depth, :, :width]) + query_bias[depth : depth + 1, :]
            k = product(normed, qkv_v[depth, :, width : 2 * width])
            v = product(normed, qkv_v[depth, :, 2 * width :]) + value_bias[depth : depth + 1, :]
            qkv[rows, :width] = (q.astype(BF).astype(F32) * 0.125).astype(BF)
            qkv[rows, width : 2 * width] = k.astype(BF)
            qkv[rows, 2 * width :] = v.astype(BF)

        save(("qkv", depth), qkv.at[inside], qkv_out.at[depth])
        if depth:
            saves.pop(("probs", 0)).wait()
            saves.pop(("mixed", 0)).wait()
        attention_forward(qkv, probs, mixed, mask, stride, windows, width)
        save(("probs", depth), probs, probs_out.at[depth])
        if not depth:
            save(("mixed", depth), mixed.at[inside], mixed_out)
        for load in loads[depth][1:]:
            load.wait()
        if depth:
            saves.pop(("middle", 0)).wait()

        @pl.loop(0, tiles)
        def _(m):
            rows = row_tile(m)
            mid = hidden[depth, rows, :].astype(F32) + (
                product(mixed[rows, :], out_v[depth]) + out_bias[depth : depth + 1, :]
            )
            middle[rows, :] = mid
            xhat, _ = normalized(mid)
            normed = (xhat * gain2[depth : depth + 1, :] + bias2[depth : depth + 1, :]).astype(BF)
            if depth:
                normed_two[rows, :] = normed
                for copy in tile_copies(m):
                    copy.wait()
            parts = list(range(0, hidden_units, STRIP))
            up = lambda f: product(normed, up_v[depth, :, f : f + STRIP]) + up_bias[depth : depth + 1, f : f + STRIP]
            u = up(0)
            added = jnp.zeros((ROWS, width), F32)
            previous = None
            for f in parts:
                following = up(f + STRIP) if f + STRIP < hidden_units else None
                if previous is not None:
                    added = added + product(previous, down_v[depth, f - STRIP : f, :])
                z, d = gelu_pair(u)
                previous = z.astype(BF)
                act[rows, f : f + STRIP] = previous
                slope[rows, f : f + STRIP] = d.astype(BF)
                u = following
            added = added + product(previous, down_v[depth, hidden_units - STRIP :, :])
            hidden[depth + 1, rows, :] = (mid + (added + down_bias[depth : depth + 1, :])).astype(BF)
            if not depth:
                for copy in tile_copies(m):
                    copy.start()

        if not depth:
            save(("middle", depth), middle, middle_out)

    real = cotangent.shape[1]
    cot[:real] = cotangent[0].astype(F32)
    cot[real:] = jnp.zeros((cot.shape[0] - real, width), F32)
    final_grads[...] = jnp.zeros_like(final_grads)

    def finish(step):
        for g in range(total // TILE):
            xhat, scale = normalized(hidden[2, g * TILE : (g + 1) * TILE, :].astype(F32))
            result[g * step : g * step + TILE, :] = xhat * final_gain[...] + final_bias[...]
            arriving = cot[g * step : g * step + TILE, :]
            if step < TILE:
                line = lax.broadcasted_iota(jnp.int32, (TILE, 1), 0)
                arriving = jnp.where(line < step, arriving, 0.0)
            back, gain_sum, bias_sum = norm_back(arriving, xhat, scale, final_gain[...])
            grad[g * TILE : (g + 1) * TILE, :] = back.astype(BF)
            final_grads[0:1, :] += gain_sum
            final_grads[1:2, :] += bias_sum

    @pl.when(stride == TILE)
    def _():
        finish(LONG_STEPS * 6)

    @pl.when(stride != TILE)
    def _():
        finish(TILE)

    saves["out"] = fetch(result.at[pl.ds(0, real)], activations, result_sem)
    grad_middle = cot
    mlp_data_back(
        1, None, grad, grad_middle, grad_mixed, vectors, wide, slope, up_v.at[1], down_v.at[1], out_v.at[1], middle,
        normed_two, grad_pre, rounded, gain2, bias2,
    )
    save("grad_middle", grad_middle, grad_middle_out)
    save("grad_mixed", grad_mixed, grad_mixed_out)
    saves["parts"] = mlp_weight_back(
        core, places, (), mine, theirs, grad, act, mixed.at[inside], normed_two, grad_pre, rounded,
        (mine_out, theirs_out, part_sem),
    )
    for copy in saves.values():
        copy.wait()


def mlp_data_back(depth, loads, grad, grad_middle, grad_mixed, vectors, wide, slope_v, up_v, down_v, out_v, middle_v, normed, grad_pre, rounded, gain2, bias2):
    total, width = grad.shape
    hidden_units = grad_pre.shape[1]
    vectors[...] = jnp.zeros_like(vectors)
    wide[...] = jnp.zeros_like(wide)
    if loads:
        down, slopes, up, mid, out = loads
    for m in range(total // ROWS):
        rows = slice(m * ROWS, (m + 1) * ROWS)
        g = grad[rows, :]
        back = jnp.zeros((ROWS, width), F32)
        if loads and m == 0:
            down[0].wait()
        ahead = product(g, down_v[:CHUNK, :], NT)
        if loads:
            slopes[m].wait()
        for f in range(0, hidden_units, CHUNK):
            grad_act = ahead
            if loads and m == 0:
                for load in (down[f // CHUNK + 1 :][:1] + ([] if f else [up])):
                    load.wait()
            if f + CHUNK < hidden_units:
                ahead = product(g, down_v[f + CHUNK : f + 2 * CHUNK, :], NT)
            pre = (grad_act * slope_v[rows, f : f + CHUNK].astype(F32)).astype(BF)
            grad_pre[rows, f : f + CHUNK] = pre
            wide[0:1, f : f + CHUNK] += jnp.sum(pre.astype(F32), axis=0, keepdims=True)
            back = back + product(pre, up_v[:, f : f + CHUNK], NT)
        if loads and m == 0:
            mid.wait()
            out.wait()
        xhat, scale = normalized(middle_v[rows, :])
        if loads:
            normed[rows, :] = (xhat * gain2[depth : depth + 1, :] + bias2[depth : depth + 1, :]).astype(BF)
        through, gain_sum, bias_sum = norm_back(back, xhat, scale, gain2[depth : depth + 1, :])
        g = g.astype(F32)
        total_grad = g + through
        grad_middle[rows, :] = total_grad
        r = total_grad.astype(BF)
        rounded[rows, :] = r
        vectors[0:1, :] += gain_sum
        vectors[1:2, :] += bias_sum
        vectors[2:3, :] += jnp.sum(g, axis=0, keepdims=True)
        vectors[3:4, :] += jnp.sum(r.astype(F32), axis=0, keepdims=True)
        grad_mixed[rows, :] = product(r, out_v[...], NT).astype(BF)


def store_units(out, at, value, which, places):
    width = value.shape[1]
    if places is None:
        out[:, at : at + width] = value.astype(BF)
        return
    first, second = places
    rows = value.shape[0] // len(first)
    for unit in range(len(first)):
        place = first[unit] + which * (second[unit] - first[unit])
        out[pl.ds(pl.multiple_of(place * rows, rows), rows), at : at + width] = value[unit * rows : (unit + 1) * rows].astype(BF)


class Several:
    def __init__(self, copies):
        self.copies = copies

    def wait(self):
        for copy in self.copies:
            copy.wait()


def mlp_weight_back(core, places, loads, mine, theirs, grad, act_v, mixed_v, normed, grad_pre, rounded, outside=None):
    width = grad.shape[1]
    half = grad_pre.shape[1] // 2
    copies = []
    normed_turned = normed[...].T
    grad_turned = grad[...].T

    def made(part, at, size):
        if outside:
            cols = pl.ds(at, size)
            copies.append(fetch((mine, theirs)[part].at[:, cols], outside[part].at[:, cols], outside[2].at[len(copies)]))

    for part in range(2):
        out = (mine, theirs)[part]
        which = core if part == 0 else 1 - core
        for at in range(0, half, CHUNK):
            cols = pl.ds(pl.multiple_of(which * half + at, CHUNK), CHUNK)
            store_units(out, at, product(normed_turned, grad_pre[:, cols]), which, places)
        made(part, 0, half)
        if part == 0:
            for load in loads:
                load.wait()
        for at in range(0, half, CHUNK):
            cols = pl.ds(pl.multiple_of(which * half + at, CHUNK), CHUNK)
            store_units(out, half + at, product(grad_turned, act_v[:, cols]), which, places)
        made(part, half, half)
        cols = pl.ds(pl.multiple_of(which * (width // 2), width // 2), width // 2)
        store_units(out, 2 * half, product(mixed_v[...], rounded[:, cols], TN), which, places)
        made(part, 2 * half, width // 2)
    return Several(copies)


def mlp_loads(depth, slope, up_w, down_w, middle, out_w, slope_v, up_v, down_v, middle_v, out_v, sems, tile_sems):
    tiles = slope_v.shape[0] // ROWS

    def slope_tile(m):
        rows = pl.ds(m * ROWS, ROWS)
        return fetch(slope.at[rows], slope_v.at[rows], tile_sems.at[m])

    def down_part(f):
        lines = pl.ds(f * CHUNK, CHUNK)
        return fetch(down_w.at[depth, lines], down_v.at[lines], sems.at[4 + f])

    down = [down_part(0)]
    slopes = [slope_tile(0)]
    down += [down_part(f) for f in range(1, down_v.shape[0] // CHUNK)]
    up = fetch(up_w.at[depth], up_v, sems.at[1])
    mid = fetch(middle, middle_v, sems.at[2])
    out = fetch(out_w.at[depth], out_v, sems.at[3])
    slopes += [slope_tile(m) for m in range(1, tiles)]
    return down, slopes, up, mid, out


def mlp_data_kernel(depth, tokens, grad, middle, slope, up_w, down_w, out_w, gain2, bias2, *rest):
    (grad_middle, grad_mixed, vectors, wide, normed, grad_pre, rounded,
     slope_v, up_v, down_v, out_v, middle_v, sems, tile_sems) = rest[tokens:]
    loads = mlp_loads(depth, slope, up_w, down_w, middle, out_w, slope_v, up_v, down_v, middle_v, out_v, sems, tile_sems)
    mlp_data_back(
        depth, loads, grad, grad_middle, grad_mixed, vectors, wide, slope_v, up_v, down_v, out_v, middle_v, normed,
        grad_pre, rounded, gain2, bias2,
    )


def mlp_weight_kernel(depth, tokens, places, scalars, grad, act, mixed, normed, grad_pre, rounded, *rest):
    mine, theirs, act_v, mixed_v, normed_v, pre_v, rounded_v, sems = rest[tokens:]
    first = [fetch(normed, normed_v, sems.at[0]), fetch(grad_pre, pre_v, sems.at[1])]
    later = [
        fetch(act, act_v, sems.at[2]), fetch(mixed, mixed_v, sems.at[3]),
        fetch(rounded, rounded_v, sems.at[4]),
    ]
    for load in first:
        load.wait()
    mlp_weight_back(scalars[1], places, later, mine, theirs, grad, act_v, mixed_v, normed_v, pre_v, rounded_v)


def attention_backward(qkv, probs, grad_mixed, grad_qkv, stride, windows, width, whole=None, at=0):
    whole = whole or width
    low, high = lane_halves()

    @pl.loop(0, windows // PER)
    def _(step):
        units = [(n, pair) for n in range(PER) for pair in range(width // TILE)]
        rows = [pl.ds(pl.multiple_of((PER * step + n) * stride, 32), TILE) for n in range(PER)]
        kept = [pl.ds(pl.multiple_of((PER * step + n) * 2 * TILE, 2 * TILE), 2 * TILE) for n in range(PER)]
        count = range(len(units))
        cut = lambda k, n, pair: qkv[rows[n], k * width + pair * TILE : k * width + (pair + 1) * TILE]
        arriving = [both_heads(grad_mixed[rows[n], pair * TILE : (pair + 1) * TILE], low, high) for n, pair in units]
        grad_p = [product(arriving[i], cut(2, *units[i]), NT) for i in count]
        p = [probs[pair, kept[n], :] for n, pair in units]
        grad_v = [product(p[i], arriving[i], TN) for i in count]
        inner = [jnp.sum(grad_p[i] * p[i].astype(F32), axis=-1, keepdims=True) for i in count]
        grad_s = [(p[i].astype(F32) * (grad_p[i] - inner[i])).astype(BF) for i in count]
        grad_q = [product(side_by_side(grad_s[i]), both_heads(cut(1, *units[i]), low, high)) * 0.125 for i in count]
        grad_k = [product(grad_s[i], both_heads(cut(0, *units[i]), low, high), TN) for i in count]
        for k, grads in enumerate((grad_q, grad_k, grad_v)):
            for (n, pair), value in zip(units, grads):
                start = k * whole + at + pair * TILE
                grad_qkv[rows[n], start : start + TILE] = value.astype(BF)


def qkv_back(depth, core, places, grad_qkv, hidden_v, middle_v, weight_v, gain1, bias1, grad_in, normed, vectors, mine, theirs):
    total, width = hidden_v.shape

    @pl.loop(0, total // ROWS)
    def _(m):
        rows = row_tile(m)
        back = jnp.zeros((ROWS, width), F32)
        for f in range(0, 3 * width, width):
            back = back + product(grad_qkv[rows, f : f + width], weight_v[:, f : f + width], NT)
        xhat, scale = normalized(hidden_v[rows, :].astype(F32))
        normed[rows, :] = (xhat * gain1[depth : depth + 1, :] + bias1[depth : depth + 1, :]).astype(BF)
        through, gain_sum, bias_sum = norm_back(back, xhat, scale, gain1[depth : depth + 1, :])
        grad_in[rows, :] = (middle_v[rows, :] + through).astype(BF)
        vectors[0:1, :] += gain_sum
        vectors[1:2, :] += bias_sum
        vectors[2:3, :] += jnp.sum(grad_qkv[rows, :width].astype(F32), axis=0, keepdims=True)
        vectors[3:4, :] += jnp.sum(grad_qkv[rows, 2 * width :].astype(F32), axis=0, keepdims=True)

    half = 3 * width // 2
    for part in range(2):
        which = core if part == 0 else 1 - core
        cols = pl.ds(pl.multiple_of(which * half, half), half)
        store_units((mine, theirs)[part], 0, product(normed[...], grad_qkv[:total, cols], TN), which, places)


def attention_load(depth, qkv, probs, grad_mixed, qkv_v, probs_v, mixed_v, sems):
    total = grad_mixed.shape[0]
    loads = [
        fetch(qkv.at[depth], qkv_v.at[pl.ds(0, total)], sems.at[0]),
        fetch(grad_mixed, mixed_v.at[pl.ds(0, total)], sems.at[1]),
        fetch(probs.at[depth], probs_v, sems.at[2]),
    ]
    qkv_v[total:, :] = jnp.zeros((qkv_v.shape[0] - total, qkv_v.shape[1]), BF)
    mixed_v[total:, :] = jnp.zeros((mixed_v.shape[0] - total, mixed_v.shape[1]), BF)
    return loads


def attention_back_kernel(
    depth, tokens, places, scalars, hidden, qkv, probs, grad_mixed, grad_middle, qkv_w, gain1, bias1, *rest,
):
    (mine, theirs, grad_in, vectors,
     hidden_v, middle_v, weight_v, normed, qkv_v, probs_v, mixed_v, grad_qkv, sems) = rest[tokens:]
    loads = attention_load(depth, qkv, probs, grad_mixed, qkv_v, probs_v, mixed_v, sems)
    later = [
        fetch(qkv_w.at[depth], weight_v, sems.at[3]),
        fetch(hidden.at[depth], hidden_v, sems.at[4]),
        fetch(grad_middle, middle_v, sems.at[5]),
    ]
    vectors[...] = jnp.zeros_like(vectors)
    for load in loads:
        load.wait()
    attention_backward(qkv_v, probs_v, mixed_v, grad_qkv, *placed(scalars, grad_in.shape[0]), grad_in.shape[1])
    for load in later:
        load.wait()
    qkv_back(
        depth, scalars[1], places, grad_qkv, hidden_v, middle_v, weight_v, gain1, bias1, grad_in, normed, vectors, mine,
        theirs,
    )


def part_loads(depth, part, parts, qkv, probs, grad_mixed, qkv_v, probs_v, mixed_v, sems):
    total, whole = grad_mixed.shape
    width = whole // parts
    pairs = probs_v.shape[0]
    inside = pl.ds(0, total)
    loads = [
        fetch(qkv.at[depth, :, pl.ds(k * whole + part * width, width)], qkv_v.at[inside, pl.ds(k * width, width)], sems.at[k])
        for k in range(3)
    ]
    loads.append(fetch(grad_mixed.at[:, pl.ds(part * width, width)], mixed_v.at[inside], sems.at[3]))
    loads.append(fetch(probs.at[depth, pl.ds(part * pairs, pairs)], probs_v, sems.at[4]))
    qkv_v[total:, :] = jnp.zeros((qkv_v.shape[0] - total, qkv_v.shape[1]), BF)
    mixed_v[total:, :] = jnp.zeros((mixed_v.shape[0] - total, mixed_v.shape[1]), BF)
    return loads


def attention_part_kernel(depth, part, parts, tokens, scalars, qkv, probs, grad_mixed, *rest):
    out, qkv_v, probs_v, mixed_v, grad_qkv, sems, out_sem = rest[tokens:]
    total, whole = grad_mixed.shape
    for load in part_loads(depth, part, parts, qkv, probs, grad_mixed, qkv_v, probs_v, mixed_v, sems):
        load.wait()
    attention_backward(qkv_v, probs_v, mixed_v, grad_qkv, *placed(scalars, total), whole // parts)
    fetch(grad_qkv.at[pl.ds(0, total)], out, out_sem).wait()


def table_kernel(
    depth, tokens, places, groups, scalars, qkv, probs, grad_mixed, grad_low, hidden, grad_middle, qkv_w, gain1, bias1,
    index, final_grads, feed1, wide1, attend1, feed0, wide0, *rest,
):
    (mine, theirs, frame_grad, grad_in, turned, vectors, stage, hidden_v, normed, grad_qkv, weight_v, middle_v,
     qkv_v, probs_v, mixed_v, sems, part_sems) = rest[tokens:]
    total, width = grad_in.shape
    half = width // 2
    first = part_loads(depth, 1, 2, qkv, probs, grad_mixed, qkv_v, probs_v, mixed_v, part_sems)
    inside = pl.ds(0, total)
    loads = [
        fetch(grad_low.at[:, pl.ds(k * half, half)], grad_qkv.at[inside, pl.ds(k * width, half)], sems.at[k])
        for k in range(3)
    ]
    loads.append(fetch(qkv_w.at[depth], weight_v, sems.at[3]))
    loads.append(fetch(hidden.at[depth], hidden_v, sems.at[4]))
    loads.append(fetch(grad_middle, middle_v, sems.at[5]))
    core = scalars[1]
    steps = frame_grad.shape[0]
    qkv_width = 3 * width // 2
    code_width = mine.shape[1] - qkv_width - TILE
    vectors[...] = jnp.zeros_like(vectors)
    for load in first:
        load.wait()
    attention_backward(qkv_v, probs_v, mixed_v, grad_qkv, *placed(scalars, total), half, width, half)
    for load in loads:
        load.wait()
    qkv_back(
        depth, core, places, grad_qkv, hidden_v, middle_v, weight_v, gain1, bias1, grad_in, normed, vectors, mine, theirs,
    )

    stage[...] = jnp.zeros_like(stage)
    for k, block in enumerate((feed0, vectors, feed1, attend1, final_grads)):
        stage[VECTORS + 8 * k : VECTORS + 8 * k + 8, :] = block[...]
    each = width // groups
    for k, wide in enumerate((wide0, wide1)):
        for group in range(groups):
            for c in range(4):
                start = group * 4 * each + c * each
                at = VECTORS + 40 + 8 * k + c
                stage[at : at + 1, group * each : group * each + each] = wide[0:1, start : start + each]

    turned[...] = grad_in[...].T
    for part in range(2):
        out = (mine, theirs)[part]
        which = core if part == 0 else 1 - core
        line = lax.broadcasted_iota(jnp.int32, (code_width, total), 0) + which * code_width
        hot = (line == index[0:1, :]).astype(F32).astype(BF)
        store_units(out, qkv_width, product(turned[...], hot, NT), which, places)
        line = lax.broadcasted_iota(jnp.int32, (TILE, total), 0) + which * TILE
        hot = ((line == index[1:2, :]) | (line == index[2:3, :])).astype(F32).astype(BF)
        small = product(turned[...], hot, NT) + stage[...].T * which.astype(F32)
        store_units(out, qkv_width + code_width, small, which, places)
    hot = (lax.broadcasted_iota(jnp.int32, (steps, total), 0) == index[3:4, :]).astype(F32).astype(BF)
    frame_grad[...] = product(hot, grad_in[...])


def output_kernel(where, scalars, *refs):
    count = 1 + max(chunk for chunk, _ in where.values())
    sources = refs[: 2 * count]
    (code, action, position, gain1, bias1, qkv, query, value, out, out_bias, gain2, bias2, up, up_bias, down, down_bias,
     final_gain, final_bias) = refs[2 * count : -1]
    square = refs[-1]
    rows, units = up.shape[1:]
    half = units // 2
    small = qkv.shape[2] // 2 + code.shape[1] // 2

    def emit(own):
        def part(name, core, across, start, size):
            chunk, at = where[name]
            lines = slice((across ^ (own >> 1)) * rows // 2, ((across ^ (own >> 1)) + 1) * rows // 2)
            return sources[2 * chunk + (core ^ (own & 1))][lines, at + start : at + start + size].astype(F32)

        def place(target, name, start):
            size = target.shape[-1] // 2
            for across in range(2):
                lines = slice(across * rows // 2, (across + 1) * rows // 2)
                for core in range(2):
                    target[lines, core * size : (core + 1) * size] = part(name, core, across, start, size)

        for depth in range(2):
            place(up.at[depth], ("feed", depth), 0)
            place(down.at[depth], ("feed", depth), half)
            place(out.at[depth], ("feed", depth), units)
            place(qkv.at[depth], ("attend", depth), 0)
        place(code, ("attend", 0), qkv.shape[2] // 2)
        square[...] = jnp.zeros_like(square)
        for across in range(2):
            lines = slice(across * rows // 2, (across + 1) * rows // 2)
            position[lines, :] = part(("attend", 0), 0, across, small, TILE)[:, : position.shape[1]]
            square[lines, :] = part(("attend", 0), 1, across, small, TILE)
        lines = square[...].T[:, :rows]
        action[...] = lines[: action.shape[0]]

        def line(k):
            return lines[VECTORS + k : VECTORS + k + 1]

        for depth in range(2):
            at = slice(depth, depth + 1)
            base = 16 * depth
            for k, target in enumerate((gain2, bias2, down_bias, out_bias)):
                target[at, :] = line(base + k)
            for k, target in enumerate((gain1, bias1, query, value)):
                target[at, :] = line(base + 8 + k)
            for c in range(4):
                up_bias[at, c * rows : (c + 1) * rows] = line(40 + 8 * depth + c)
        final_gain[...] = line(32)
        final_bias[...] = line(33)

    for own in range(4):
        pl.when(scalars[scalars.shape[0] - 1] == own)(partial(emit, own))


VMEM = pl.BlockSpec(memory_space=pltpu.VMEM)
ANY = pl.BlockSpec(memory_space=pl.ANY)
SMEM = pl.BlockSpec(memory_space=pltpu.SMEM)


def cost(flops, moved, others=0):
    return pl.CostEstimate(flops=int(8 * flops), bytes_accessed=int(moved), transcendentals=int(others))


def run_forward(places, scalars, actions, deltas, frames, codebook, action_table, position_table, layers, finals, cotangent):
    gain1, bias1, qkv_w, query_bias, value_bias, out_w, out_bias, gain2, bias2, up_w, up_bias, down_w, down_bias = layers
    width = codebook.shape[1]
    units = up_bias.shape[1]
    real = cotangent.shape[1]
    total = -(-real // ROWS) * ROWS
    reach = total + TILE + 32
    columns = units + width // 2
    shape = jax.ShapeDtypeStruct
    once = dict(pipeline_mode=pl.Buffered(1))
    whole = lambda a: pl.BlockSpec(a.shape, lambda i, s, n=a.ndim: (0,) * n, **once)
    mine = lambda a: pl.BlockSpec((1,) + a.shape[1:], lambda i, s: (s[0], 0, 0), **once)
    kept = (width // TILE, WINDOWS * 2 * TILE, TILE)
    outs = [
        (shape((real, width), F32), ANY),
        (shape((8, total), jnp.int32), None),
        (shape((8, width), F32), None), (shape((8, width), F32), None), (shape((8, units), F32), None),
        (shape((2, total, width), BF), ANY),
        (shape((2, total, 3 * width), BF), ANY),
        (shape((2,) + kept, BF), ANY),
        (shape((total, width), BF), ANY),
        (shape((total, width), F32), ANY),
        (shape((total, units), BF), ANY),
        (shape((total, units), BF), ANY),
        (shape((total, width), F32), ANY), (shape((total, width), BF), ANY),
        (shape((width, columns), BF), ANY), (shape((width, columns), BF), ANY),
    ]
    args = [
        (actions, None), (deltas, mine(deltas)), (frames, mine(frames)),
        (codebook, None), (action_table, None), (position_table, None),
        (gain1, None), (bias1, None), (qkv_w, ANY), (query_bias, None), (value_bias, None), (out_w, ANY),
        (out_bias, None), (gain2, None), (bias2, None), (up_w, ANY), (up_bias, None), (down_w, ANY), (down_bias, None),
        (finals[0][None], None), (finals[1][None], None), (cotangent, mine(cotangent)),
    ]
    scratch = [
        pltpu.VMEM((2 * TILE, width), BF),
        pltpu.VMEM(qkv_w.shape, BF), pltpu.VMEM(out_w.shape, BF), pltpu.VMEM(up_w.shape, BF), pltpu.VMEM(down_w.shape, BF),
        pltpu.VMEM((3, total, width), BF), pltpu.VMEM((reach, 3 * width), BF), pltpu.VMEM(kept, BF),
        pltpu.VMEM((reach, width), BF), pltpu.VMEM((total, width), F32),
        pltpu.VMEM((total, units), BF), pltpu.VMEM((total, units), BF), pltpu.VMEM((2 * TILE, TILE), F32),
        pltpu.VMEM((total, width), F32), pltpu.VMEM((total, width), F32),
        pltpu.VMEM((total, width), BF), pltpu.VMEM((total, width), BF), pltpu.VMEM((total, width), BF),
        pltpu.VMEM((total, width), BF), pltpu.VMEM((total, units), BF),
        pltpu.VMEM((width, columns), BF), pltpu.VMEM((width, columns), BF),
        pltpu.SemaphoreType.DMA((2, 4)), pltpu.SemaphoreType.DMA((16,)), pltpu.SemaphoreType.DMA((2, total // ROWS)),
        pltpu.SemaphoreType.DMA, pltpu.SemaphoreType.DMA((6,)),
    ]
    return pl.pallas_call(
        partial(forward_kernel, places),
        out_shape=[o for o, _ in outs],
        grid_spec=pltpu.PrefetchScalarGridSpec(
            num_scalar_prefetch=1,
            grid=(1,),
            in_specs=[spec or whole(a) for a, spec in args],
            out_specs=[spec or whole(o) for o, spec in outs],
            scratch_shapes=scratch,
        ),
        compiler_params=pltpu.CompilerParams(vmem_limit_bytes=62 << 20),
        cost_estimate=cost(24e9, 50e6, 4e6),
        name="forward",
    )(scalars, *[a for a, _ in args])


def run_mlp_data(depth, grad, saved, layers, after):
    hidden, qkv, probs, mixed, middle, act, slope = saved
    gain1, bias1, qkv_w, query_bias, value_bias, out_w, out_bias, gain2, bias2, up_w, up_bias, down_w, down_bias = layers
    total, width = grad.shape
    units = up_bias.shape[1]
    shape = jax.ShapeDtypeStruct
    return pl.pallas_call(
        partial(mlp_data_kernel, depth, len(after)),
        out_shape=[
            shape((total, width), F32), shape((total, width), BF), shape((8, width), F32), shape((8, units), F32),
            shape((total, width), BF), shape((total, units), BF), shape((total, width), BF),
        ],
        in_specs=[VMEM] + [ANY] * 5 + [VMEM] * 2 + [ANY] * len(after),
        out_specs=[VMEM] * 7,
        scratch_shapes=[
            pltpu.VMEM((total, units), BF),
            pltpu.VMEM((width, units), BF), pltpu.VMEM((units, width), BF), pltpu.VMEM((width, width), BF),
            pltpu.VMEM((total, width), F32),
            pltpu.SemaphoreType.DMA((4 + units // CHUNK,)), pltpu.SemaphoreType.DMA((total // ROWS,)),
        ],
        compiler_params=pltpu.CompilerParams(vmem_limit_bytes=40 << 20),
        cost_estimate=cost(10e9, 16e6),
        name="mlp_data",
    )(grad, middle, slope, up_w, down_w, out_w, gain2, bias2, *after)


def run_mlp_weight(depth, places, scalars, grad, saved, normed, grad_pre, rounded, after):
    hidden, qkv, probs, mixed, middle, act, slope = saved
    total, width = grad.shape
    units = grad_pre.shape[1]
    shape = jax.ShapeDtypeStruct
    return pl.pallas_call(
        partial(mlp_weight_kernel, depth, len(after), places),
        out_shape=[shape((width, units + width // 2), BF), shape((width, units + width // 2), BF)],
        in_specs=[SMEM, VMEM] + [ANY] * 5 + [ANY] * len(after),
        out_specs=[VMEM] * 2,
        scratch_shapes=[
            pltpu.VMEM((total, units), BF), pltpu.VMEM((total, width), BF), pltpu.VMEM((total, width), BF),
            pltpu.VMEM((total, units), BF), pltpu.VMEM((total, width), BF),
            pltpu.SemaphoreType.DMA((5,)),
        ],
        compiler_params=pltpu.CompilerParams(vmem_limit_bytes=40 << 20),
        cost_estimate=cost(8e9, 16e6),
        name="mlp_weight",
    )(scalars, grad, act, mixed, normed, grad_pre, rounded, *after)


def window_scratch(total, width, probs):
    reach = total + TILE + 32
    return [
        pltpu.VMEM((reach, 3 * width), BF), pltpu.VMEM(probs.shape[1:], BF),
        pltpu.VMEM((reach, width), BF), pltpu.VMEM((reach, 3 * width), BF),
    ]


def run_attention_back(depth, places, scalars, grad_mixed, grad_middle, saved, layers, after):
    hidden, qkv, probs, mixed, middle, act, slope = saved
    gain1, bias1, qkv_w = layers[:3]
    total, width = grad_mixed.shape
    shape = jax.ShapeDtypeStruct
    return pl.pallas_call(
        partial(attention_back_kernel, depth, len(after), places),
        out_shape=[
            shape((width, 3 * width // 2), BF), shape((width, 3 * width // 2), BF),
            shape((total, width), BF), shape((8, width), F32),
        ],
        in_specs=[SMEM] + [ANY] * 6 + [VMEM] * 2 + [ANY] * len(after),
        out_specs=[VMEM] * 4,
        scratch_shapes=[
            pltpu.VMEM((total, width), BF), pltpu.VMEM((total, width), F32), pltpu.VMEM(qkv_w.shape[1:], BF),
            pltpu.VMEM((total, width), BF), *window_scratch(total, width, probs),
            pltpu.SemaphoreType.DMA((6,)),
        ],
        compiler_params=pltpu.CompilerParams(vmem_limit_bytes=61 << 20),
        cost_estimate=cost(16e9, 24e6),
        name="attention_back",
    )(scalars, hidden, qkv, probs, grad_mixed, grad_middle, qkv_w, gain1, bias1, *after)


def run_attention_part(depth, part, parts, scalars, grad_mixed, saved, after):
    hidden, qkv, probs, mixed, middle, act, slope = saved
    total, width = grad_mixed.shape
    width = width // parts
    reach = total + TILE + 32
    return pl.pallas_call(
        partial(attention_part_kernel, depth, part, parts, len(after)),
        out_shape=jax.ShapeDtypeStruct((total, 3 * width), BF),
        in_specs=[SMEM] + [ANY] * 3 + [ANY] * len(after),
        out_specs=ANY,
        scratch_shapes=[
            pltpu.VMEM((reach, 3 * width), BF), pltpu.VMEM((width // TILE,) + probs.shape[2:], BF),
            pltpu.VMEM((reach, width), BF), pltpu.VMEM((reach, 3 * width), BF),
            pltpu.SemaphoreType.DMA((5,)), pltpu.SemaphoreType.DMA,
        ],
        compiler_params=pltpu.CompilerParams(vmem_limit_bytes=VMEM_PART << 20),
        cost_estimate=cost(8e9, 8e6),
        name="attention_part",
    )(scalars, qkv, probs, grad_mixed, *after)


def run_table(depth, places, scalars, grad_mixed, grad_low, grad_middle, saved, layers, index, vectors, codes, steps, groups, after):
    hidden, qkv, probs, mixed, middle, act, slope = saved
    gain1, bias1, qkv_w = layers[:3]
    total, width = grad_middle.shape
    reach = total + TILE + 32
    columns = 3 * width // 2 + codes // 2 + TILE
    shape = jax.ShapeDtypeStruct
    return pl.pallas_call(
        partial(table_kernel, depth, len(after), places, groups),
        out_shape=[shape((width, columns), BF), shape((width, columns), BF), shape((steps, width), F32)],
        in_specs=[SMEM] + [ANY] * 7 + [VMEM] * 2 + [VMEM] * 7 + [ANY] * len(after),
        out_specs=[VMEM] * 3,
        scratch_shapes=[
            pltpu.VMEM((total, width), BF), pltpu.VMEM((width, total), BF), pltpu.VMEM((8, width), F32),
            pltpu.VMEM((TILE, width), F32), pltpu.VMEM((total, width), BF), pltpu.VMEM((total, width), BF),
            pltpu.VMEM((reach, 3 * width), BF), pltpu.VMEM(qkv_w.shape[1:], BF), pltpu.VMEM((total, width), F32),
            pltpu.VMEM((reach, 3 * width // 2), BF), pltpu.VMEM((probs.shape[1] // 2,) + probs.shape[2:], BF),
            pltpu.VMEM((reach, width // 2), BF),
            pltpu.SemaphoreType.DMA((6,)), pltpu.SemaphoreType.DMA((5,)),
        ],
        compiler_params=pltpu.CompilerParams(vmem_limit_bytes=40 << 20),
        cost_estimate=cost(12e9, 12e6),
        name="tables",
    )(scalars, qkv, probs, grad_mixed, grad_low, hidden, grad_middle, qkv_w, gain1, bias1, index, *vectors, *after)


def run_output(where, scalars, sources, width, units, codes, actions, positions):
    rows = sources[0].shape[0]
    wide, line = (2, rows), (1, rows)
    shapes = [
        (rows, codes), (actions, rows), (rows, positions), wide, wide, (2, rows, 3 * width), wide, wide, (2, rows, width),
        wide, wide, wide, (2, rows, units), (2, 4 * rows), (2, rows, units), wide, line, line,
    ]
    return pl.pallas_call(
        partial(output_kernel, where),
        out_shape=[jax.ShapeDtypeStruct(s, F32) for s in shapes],
        in_specs=[SMEM] + [VMEM] * len(sources),
        out_specs=[VMEM] * len(shapes),
        scratch_shapes=[pltpu.VMEM((TILE, TILE), F32)],
        compiler_params=pltpu.CompilerParams(vmem_limit_bytes=30 << 20),
        cost_estimate=cost(1e6, 6e6),
        name="outputs",
    )(scalars, *sources)


def meet(array, axis, by):
    size = lax.axis_size(axis)
    return lax.ppermute(array, axis, [(i, i ^ by) for i in range(size)])


def swap(array, axis, bit):
    return meet(array, axis, 1 << bit)


def bits_of(axis):
    return lax.axis_size(axis).bit_length() - 1


def own_bit(axis, bit):
    return (lax.axis_index(axis) >> bit) & 1


def take(array, dim, which):
    return lax.dynamic_index_in_dim(array, which, dim, keepdims=False)


def total_of(terms):
    return sum(term.astype(F32) for term in terms)


def settled(array):
    return lax.optimization_barrier(array.astype(BF))


def tied(array, token):
    return lax.optimization_barrier((array, token))[0]


def unit_places(count):
    first, second = [], []
    for unit in range(2 << count):
        bits = [(unit >> (1 + bit)) & 1 for bit in range(count)]
        for order, places in ((bits + [unit & 1], first), ([unit & 1] + bits, second)):
            place = 0
            for bit in order:
                place = 2 * place + bit
            places.append(place)
    return first, second


def reordered(array, which, count):
    rows, columns = array.shape
    ways = array.reshape((2,) * (count + 1) + (rows >> (count + 1), columns))
    dims = list(range(count - 1, -1, -1))
    first = ways.transpose(dims + [count, count + 1, count + 2])
    second = ways.transpose([count] + dims + [count + 1, count + 2])
    return jnp.where(which == 0, first, second).reshape(rows, columns)


class Chunk:
    def __init__(self, places):
        self.count = bits_of("dp")
        self.places = places
        self.pieces = []
        self.terms = []
        self.core = own_bit("section", 0)

    def add(self, mine, theirs):
        if self.places is None:
            mine, theirs = reordered(mine, self.core, self.count), reordered(theirs, 1 - self.core, self.count)
        self.pieces.append([mine, swap(theirs, "section", 0)])

    def hold(self, token):
        if self.terms:
            self.terms[-1] = tied(self.terms[-1], token)
        else:
            for piece in self.pieces:
                piece[1] = tied(piece[1], token)

    def step(self):
        if not self.terms:
            self.left = self.pieces[0][0].shape[0]
        k = len(self.terms)
        bits = [own_bit("dp", bit) for bit in range(self.count)]
        across = own_bit("section", 1)
        own = jnp.where(self.core == 0, (bits + [across])[k], ([across] + bits)[k])
        half = self.left // 2
        cut = lambda t, which: lax.dynamic_slice_in_dim(t, which * half, half, 0)
        if not self.terms:
            self.parts = [[[mine, arrived] for mine, arrived in self.pieces]]
        parts = self.parts[-1]
        sum_of = jnp.concatenate([total_of([cut(t, 1 - own) for t in part]) for part in parts], axis=1)
        for term in self.terms:
            sum_of = sum_of + cut(term, 1 - own).astype(F32)
        self.sent = settled(sum_of)
        sections = lax.axis_size("section")
        pairs = []
        for source in range(lax.axis_size("dp") * sections):
            at = k if source & 1 == 0 else (k - 1) % (self.count + 1)
            bit = sections << at if at < self.count else 2
            pairs.append((source, source ^ bit))
        self.parts = [[[cut(t, own) for t in part] for part in parts]]
        self.terms = [cut(t, own) for t in self.terms] + [lax.ppermute(self.sent, ("dp", "section"), pairs)]
        self.left = half
        return self

    def across(self):
        total = jnp.concatenate([total_of(part) for part in self.parts[-1]], axis=1)
        for term in self.terms:
            total = total + term.astype(F32)
        self.sent = settled(total)
        other = swap(self.sent, "section", 1)
        self.terms = [self.sent, other]

    def finish(self):
        rows = settled(jnp.concatenate(self.terms))
        arrived = swap(rows, "section", 0)
        return [rows, arrived]


def local(
    frames, actions, deltas, kinds, codebook, action_table, position_table, norm1_gain, norm1_bias, qkv_weight,
    query_bias, value_bias, out_weight, out_bias, norm2_gain, norm2_bias, up_weight, up_bias, down_weight, down_bias,
    final_gain, final_bias, cotangent,
):
    micro, steps, width = frames.shape
    units = up_weight.shape[2]
    codes = codebook.shape[0]
    slot = lax.axis_index("section") * micro // lax.axis_size("section")
    layers = (
        norm1_gain, norm1_bias, qkv_weight, query_bias, value_bias, out_weight, out_bias, norm2_gain, norm2_bias,
        up_weight, up_bias, down_weight, down_bias,
    )
    section = lax.axis_index("section")
    scalars = jnp.concatenate([jnp.stack([slot, section & 1]), kinds, section[None]]).astype(jnp.int32)
    groups = lax.axis_size("dp")
    count = bits_of("dp")
    places = unit_places(count) if width >> (count + 1) >= 16 else None
    chunk1, chunk2, chunk3 = Chunk(places), Chunk(places), Chunk(places)
    activations, index, final_grads, feed1, wide1, *saved, middle, mixed, mine, theirs = run_forward(
        places, scalars, actions, deltas.transpose(0, 2, 1), frames, codebook, action_table, position_table,
        layers, (final_gain, final_bias), cotangent,
    )
    chunk1.add(mine, theirs)
    mine, theirs, grad, attend1 = run_attention_back(1, places, scalars, mixed, middle, saved, layers, [])
    chunk1.hold(attend1)
    chunk2.add(mine, theirs)
    chunk1.step()
    middle, mixed, feed0, wide0, normed, grad_pre, rounded = run_mlp_data(0, grad, saved, layers, [chunk1.sent])
    chunk1.hold(normed)
    chunk1.step()
    mine, theirs = run_mlp_weight(0, places, scalars, grad, saved, normed, grad_pre, rounded, [chunk1.sent])
    chunk1.hold(theirs)
    chunk2.hold(theirs)
    chunk2.add(mine, theirs)
    grad_low = run_attention_part(0, 0, 2, scalars, mixed, saved, [])
    chunk2.hold(grad_low)
    chunk2.step()
    chunk1.hold(chunk2.sent)
    chunk1.step()
    vectors = (final_grads, feed1, wide1, attend1, feed0, wide0)
    mine, theirs, frame_grad = run_table(
        0, places, scalars, mixed, grad_low, middle, saved, layers, index, vectors, codes, steps, groups,
        [chunk2.sent, chunk1.sent],
    )
    chunk3.add(mine, theirs)
    chunk2.hold(frame_grad)
    chunk1.hold(chunk2.terms[-1])
    chunk2.step()
    chunk3.hold(chunk2.sent)
    chunk3.step()
    chunk2.hold(chunk3.sent)
    chunk1.hold(chunk3.sent)
    for _ in range(3, count + 1):
        chunk1.step()
    for k in range(2, count + 3):
        if k <= count:
            chunk2.step()
        elif k == count + 1:
            chunk2.across()
        else:
            sources += chunk2.finish()
        chunk3.hold(chunk2.sent)
        if k == 2:
            chunk3.hold(chunk1.terms[-1])
            chunk1.across()
        if k == 3:
            chunk3.hold(chunk1.terms[-1])
            sources = chunk1.finish()
        if k <= count + 1:
            chunk3.step()
            chunk2.hold(chunk3.sent)
        else:
            chunk3.across()
    sources += chunk3.finish()
    split = 3 * width // 2
    where = {("feed", 1): (0, 0), ("attend", 1): (1, 0), ("feed", 0): (1, split), ("attend", 0): (2, 0)}
    (code, action, position, gain1, bias1, qkv, query, value, out, out_b, gain2, bias2, up, up_b, down, down_b, last_gain,
     last_bias) = run_output(
        where, scalars, sources, width, units, codes, action_table.shape[0], position_table.shape[0]
    )
    return (
        activations[None], frame_grad[None], code.T, action, position.T, gain1, bias1, qkv, query, value, out, out_b,
        gain2, bias2, up, up_b, down.transpose(0, 2, 1), down_b, last_gain[0], last_bias[0],
    )


def solution(mesh):
    rows, one = P("dp", None, None), P(None, "dp")
    weight = P(None, "dp", None)
    both = P(("dp", "section"), None, None)
    return jax.shard_map(
        local,
        mesh=mesh,
        in_specs=(rows, P("dp", None), rows, P("dp")) + (P(),) * 18 + (rows,),
        out_specs=(
            both, both, one, one, one, one, one, weight, one, one, weight, one, one, one, weight, one,
            P(None, None, "dp"), one, P("dp"), P("dp"),
        ),
        check_vma=False,
    )
```
